32 devices in a mesh: seq: 8 (over y, x, core), tp: 4 (over z).
Axes of the slice: x: 2, y: 2, z: 4, core: 2. Of those that a mesh axis runs over, the one named last changes fastest.
Arguments:
- tokens: bfloat16 [4, 1024, 768], P(None, 'seq'), may hold values from -6 to 6
- norm_gain: float32 [768], replicated, may hold values from 0.5 to 1.5
- norm_bias: float32 [768], replicated, may hold values from -1.75 to 1.75
- in_right: bfloat16 [4, 192, 192], replicated, may hold values from -0.4375 to 0.4375
- in_left: bfloat16 [4, 192, 576], replicated, may hold values from -0.4375 to 0.4375
- short_kernel: bfloat16 [3, 768, 3], replicated, may hold values from -3.5 to 3.5
- filter_first: bfloat16 [5, 128], replicated, may hold values from -12 to 12
- filter_second: bfloat16 [128, 128], replicated, may hold values from -2.5 to 2.5
- filter_third: bfloat16 [128, 768], replicated, may hold values from -0.75 to 0.75
- conv_bias: float32 [768], replicated, may hold values from -6 to 6
- out_right: bfloat16 [4, 192, 192], replicated, may hold values from -0.4375 to 0.4375
- out_left: bfloat16 [4, 192, 192], replicated, may hold values from -0.4375 to 0.4375
- ffn_gain: float32 [768], replicated, may hold values from 0.5 to 1.5
- ffn_bias: float32 [768], replicated, may hold values from -1.75 to 1.75
- gate_weight: bfloat16 [768, 3072], P(None, 'tp'), may hold values from -0.21875 to 0.21875
- up_weight: bfloat16 [768, 3072], P(None, 'tp'), may hold values from -0.21875 to 0.21875
- down_weight: bfloat16 [3072, 768], P('tp'), may hold values from -0.21875 to 0.21875
- cotangent: bfloat16 [4, 1024, 768], P(None, ('seq', 'tp')), may hold values from -6 to 6
Outputs:
- output: bfloat16 [4, 1024, 768], P(None, ('seq', 'tp'))
- grad_tokens: float32 [4, 1024, 768], P(None, 'seq')
- grad_norm_gain: float32 [768], replicated
- grad_norm_bias: float32 [768], replicated
- grad_in_right: float32 [4, 192, 192], replicated
- grad_in_left: float32 [4, 192, 576], replicated
- grad_short_kernel: float32 [3, 768, 3], replicated
- grad_filter_first: float32 [5, 128], replicated
- grad_filter_second: float32 [128, 128], replicated
- grad_filter_third: float32 [128, 768], replicated
- grad_conv_bias: float32 [768], replicated
- grad_out_right: float32 [4, 192, 192], replicated
- grad_out_left: float32 [4, 192, 192], replicated
- grad_ffn_gain: float32 [768], replicated
- grad_ffn_bias: float32 [768], replicated
- grad_gate_weight: float32 [768, 3072], P(None, 'tp')
- grad_up_weight: float32 [768, 3072], P(None, 'tp')
- grad_down_weight: float32 [3072, 768], P('tp')
The draws below stay inside these ranges and needn't reach their ends.
All inputs are finite; a program needn't handle non-finite values.
Results may differ from the reference program's by a relative error of at most 0.022.
Values may be sent and summed in bfloat16 or wider, within the bound.
A program may use at most 128 MiB of HBM per device.

```python
import math
import jax
import jax.numpy as jnp
from jax import lax

D = 768
FF = 3072
HID = 128
NB = 4
FEAT = 5
SEQS = 4
LENGTH = 1024


def level_of(own_key, shape, split, least, high):
    loudness = 1.0
    for axis_at, parts in split:
        draws = jax.random.uniform(jax.random.fold_in(jax.random.fold_in(own_key, 6), axis_at), (parts,), jnp.float32, least / len(split), high / len(split))
        loudness = loudness * jnp.repeat(jnp.exp(draws), shape[axis_at] // parts).reshape((-1,) + (1,) * (len(shape) - 1 - axis_at))
    return loudness


def normal_values(stream_key, shape, width, bound, shards=(), kind=jnp.bfloat16):
    entries = jax.random.normal(stream_key, shape, jnp.float32) * width
    if len(shards) > 0:
        entries = level_of(stream_key, shape, shards, -0.22, 0.18) * entries
    return jnp.clip(entries, min=-bound, max=bound).astype(kind)


def setup_inputs(seed: int = 0) -> dict:
    splits = jax.random.split(jax.random.key(seed), 19)
    tokens = normal_values(splits[0], (SEQS, LENGTH, D), 1.0, 6.0, ((1, 8),))
    norm_gain = jnp.clip(1.0 + 0.1 * jax.random.normal(splits[1], (D,), jnp.float32), 0.5, 1.5)
    norm_bias = normal_values(splits[2], (D,), 0.3, 1.75, (), jnp.float32)
    in_right = normal_values(splits[3], (NB, D // NB, D // NB), (D // NB) ** -0.5, 0.4375)
    in_left = normal_values(splits[4], (NB, D // NB, 3 * D // NB), (D // NB) ** -0.5, 0.4375)
    short_kernel = normal_values(splits[5], (3, D, 3), 3 ** -0.5, 3.5)
    filter_first = normal_values(splits[6], (FEAT, HID), 3.0, 12.0)
    filter_second = normal_values(splits[7], (HID, HID), 6 ** -0.5, 2.5)
    filter_third = normal_values(splits[8], (HID, D), (HID // 2) ** -0.5, 0.75)
    conv_bias = normal_values(splits[9], (D,), 1.0, 6.0, (), jnp.float32)
    out_right = normal_values(splits[10], (NB, D // NB, D // NB), (D // NB) ** -0.5, 0.4375)
    out_left = normal_values(splits[11], (NB, D // NB, D // NB), (D // NB) ** -0.5, 0.4375)
    ffn_gain = jnp.clip(1.0 + 0.1 * jax.random.normal(splits[12], (D,), jnp.float32), 0.5, 1.5)
    ffn_bias = normal_values(splits[13], (D,), 0.3, 1.75, (), jnp.float32)
    gate_weight = normal_values(splits[14], (D, FF), D ** -0.5, 0.21875, ((1, 4),))
    up_weight = normal_values(splits[15], (D, FF), D ** -0.5, 0.21875, ((1, 4),))
    down_weight = normal_values(splits[16], (FF, D), (FF // 4) ** -0.5, 0.21875, ((0, 4),))
    cotangent = normal_values(splits[17], (SEQS, LENGTH, D), 1.0, 6.0, ((1, 32),))
    return dict(tokens=tokens, norm_gain=norm_gain, norm_bias=norm_bias, in_right=in_right, in_left=in_left, short_kernel=short_kernel, filter_first=filter_first, filter_second=filter_second, filter_third=filter_third, conv_bias=conv_bias, out_right=out_right, out_left=out_left, ffn_gain=ffn_gain, ffn_bias=ffn_bias, gate_weight=gate_weight, up_weight=up_weight, down_weight=down_weight, cotangent=cotangent)


highest = lax.Precision.HIGHEST

@jax.custom_vjp
def low(v):
    return lax.optimization_barrier(v.astype(jnp.bfloat16)).astype(jnp.float32)

@jax.custom_vjp
def low_back(v):
    return v

def low_keep(v):
    return (low(v), None)

def low_pass(kept, grad):
    return (grad,)

def back_keep(v):
    return (v, None)

def back_low(kept, grad):
    return (low(grad),)
low.defvjp(low_keep, low_pass)
low_back.defvjp(back_keep, back_low)

def norm_rows(values, gain, bias):
    centre = lax.optimization_barrier(jnp.mean(values, axis=-1, keepdims=True))
    shifted = values - centre
    variance = lax.optimization_barrier(jnp.mean(shifted * shifted, axis=-1, keepdims=True))
    return shifted * lax.rsqrt(variance + 1e-05) * gain + bias

def monarch(operand, right_factor, left_factor):
    row_count = operand.shape[0]
    block_count = right_factor.shape[0]
    blocked = operand.reshape(row_count, block_count, -1)
    middle = jnp.einsum('tbi,bij->tbj', blocked, right_factor, precision=highest)
    middle = low(low_back(middle))
    breadth = middle.shape[-1]
    shuffled = middle.reshape(row_count, block_count, block_count, breadth // block_count).transpose(0, 2, 1, 3).reshape(row_count, block_count, breadth)
    return jnp.einsum('tbi,bij->tbj', shuffled, left_factor, precision=highest).reshape(row_count, -1)

def filter_taps(filter_first, filter_second, filter_third):
    total = 2 * LENGTH
    index = jnp.arange(total)
    offset = jnp.where(index < LENGTH, index, index - total).astype(jnp.float32)
    scaled = offset / LENGTH
    features = jnp.stack([scaled, jnp.sin(math.pi * scaled), jnp.cos(math.pi * scaled), jnp.sin(7.0 * math.pi * scaled), jnp.cos(7.0 * math.pi * scaled)], axis=1)
    hidden_one = jnp.sin(jnp.dot(features, filter_first, precision=highest))
    hidden_two = jnp.sin(jnp.dot(hidden_one, filter_second, precision=highest))
    keep_mask = (index != LENGTH).astype(jnp.float32)[:, None]
    return jnp.dot(hidden_two, filter_third, precision=highest) * (keep_mask * LENGTH ** (-0.5))

def forward(params, tokens):
    norm_gain, norm_bias, in_right, in_left, short_kernel, filter_first, filter_second, filter_third, conv_bias, out_right, out_left, ffn_gain, ffn_bias, gate_weight, up_weight, down_weight = params
    normed = low(norm_rows(tokens, norm_gain, norm_bias))
    projected = low(low_back(monarch(normed, in_right, in_left)))
    signals = projected.reshape(LENGTH, 3, D)
    padded = jnp.pad(signals, ((1, 1), (0, 0), (0, 0)))
    kernel = jnp.transpose(short_kernel, (2, 0, 1))
    shorted = padded[:-2] * kernel[0] + padded[1:-1] * kernel[1] + padded[2:] * kernel[2]
    product = shorted[:, 0] * shorted[:, 2]
    taps = filter_taps(filter_first, filter_second, filter_third)
    spectrum = jnp.fft.rfft(jnp.pad(product, ((0, LENGTH), (0, 0))), axis=0) * jnp.fft.rfft(taps, axis=0)
    convolved = jnp.fft.irfft(spectrum, n=2 * LENGTH, axis=0)[:LENGTH] + conv_bias * product
    mixed = low(low_back(shorted[:, 1] * convolved))
    branch = low_back(monarch(mixed, out_right, out_left))
    residual = tokens + branch
    normed_two = low(norm_rows(residual, ffn_gain, ffn_bias))
    gate = low_back(jnp.dot(normed_two, gate_weight, precision=highest))
    upward = low_back(jnp.dot(normed_two, up_weight, precision=highest))
    hidden = low(jax.nn.silu(gate) * upward)
    return residual + low_back(jnp.dot(hidden, down_weight, precision=highest))

def add_pair(first_term, second_term):
    return first_term + second_term

def reference(tokens, norm_gain, norm_bias, in_right, in_left, short_kernel, filter_first, filter_second, filter_third, conv_bias, out_right, out_left, ffn_gain, ffn_bias, gate_weight, up_weight, down_weight, cotangent):
    params = tuple((weight.astype(jnp.float32) for weight in (norm_gain, norm_bias, in_right, in_left, short_kernel, filter_first, filter_second, filter_third, conv_bias, out_right, out_left, ffn_gain, ffn_bias, gate_weight, up_weight, down_weight)))

    def one_sequence(totals, pair):
        seq_tokens, seq_cot = pair
        result, pullback = jax.vjp(forward, params, seq_tokens.astype(jnp.float32))
        grad_params, grad_input = pullback(seq_cot.astype(jnp.float32))
        totals = jax.tree.map(add_pair, totals, grad_params)
        return (totals, (result.astype(jnp.bfloat16), grad_input))
    zeros = jax.tree.map(jnp.zeros_like, params)
    totals, (output, grad_tokens) = lax.scan(one_sequence, zeros, (tokens, cotangent))
    return (output, grad_tokens, totals[0], totals[1], totals[2], totals[3], totals[4], totals[5], totals[6], totals[7], totals[8], totals[9], totals[10], totals[11], totals[12], totals[13], totals[14], totals[15])
```

```python
import functools
import math

import numpy as np
import jax
import jax.numpy as jnp
from jax import lax
from jax.experimental import pallas as pl
from jax.experimental.pallas import tpu as pltpu
from jax.sharding import PartitionSpec as P

BF = jnp.bfloat16
F32 = jnp.float32
MESH = pl.DeviceIdType.MESH
NN = ((1,), (0,))
NT = ((1,), (1,))
TN = ((0,), (0,))
LIMIT = 56 * 1024 * 1024


def dot(first, second, form=NN):
    return lax.dot_general(first, second, (form, ((), ())), preferred_element_type=F32)


def any_spec():
    return pl.BlockSpec(memory_space=pl.ANY)


def vmem_spec():
    return pl.BlockSpec(memory_space=pltpu.VMEM)


def sin_cos(value):
    turns = jnp.floor(value * (1.0 / math.pi) + 0.5)
    rest = value - turns * 3.140625
    rest = rest - turns * 9.67502593994140625e-4
    rest = rest - turns * 1.509957990978376432e-7
    half = turns * 0.5
    sign = 1.0 - 4.0 * (half - jnp.floor(half))
    square = rest * rest
    sine = 1.0 / 362880 - square * (1.0 / 39916800)
    sine = -1.0 / 5040 + square * sine
    sine = 1.0 / 120 + square * sine
    sine = -1.0 / 6 + square * sine
    sine = rest + rest * square * sine
    cosine = 1.0 / 40320 - square * (1.0 / 3628800 - square * (1.0 / 479001600))
    cosine = -1.0 / 720 + square * cosine
    cosine = 1.0 / 24 + square * cosine
    cosine = -0.5 + square * cosine
    cosine = 1.0 + square * cosine
    return sign * sine, sign * cosine


def flip(index, bits):
    result = 0
    for place in range(3):
        digit = lax.rem(index // (1 << place), 2)
        if (bits >> place) & 1:
            digit = 1 - digit
        result = result + digit * (1 << place)
    return result


def greet(n_seq, n_tp):
    me, plane = lax.axis_index("seq"), lax.axis_index("tp")
    barrier = pltpu.get_barrier_semaphore()
    for k in range(1, n_seq):
        pl.semaphore_signal(barrier, inc=1, device_id={"seq": flip(me, k)}, device_id_type=MESH)
    for k in range(1, n_tp):
        pl.semaphore_signal(barrier, inc=1, device_id={"tp": flip(plane, k)}, device_id_type=MESH)
    return lambda: pl.semaphore_wait(barrier, n_seq + n_tp - 2)


def sign_rows(count, width):
    row = lax.broadcasted_iota(jnp.int32, (count, width), 0)
    return (1 - 2 * lax.rem(row, 2)).astype(F32)


def sign_lanes(count, width):
    lane = lax.broadcasted_iota(jnp.int32, (count, width), 1)
    return (1 - 2 * lax.rem(lane, 2)).astype(F32)


def previous(values):
    lane = lax.broadcasted_iota(jnp.int32, values.shape, 1)
    return jnp.where(lane == 0, 0.0, pltpu.roll(values, 1, 1))


def following(values):
    last = values.shape[1] - 1
    lane = lax.broadcasted_iota(jnp.int32, values.shape, 1)
    return jnp.where(lane == last, 0.0, pltpu.roll(values, last, 1))


def monarch_forward(load, right, left, shuffled, store):
    groups, width, _ = right.shape
    part = width // groups
    for b in range(groups):
        middle = dot(right[b], load(b), TN).astype(BF)
        for g in range(groups):
            shuffled[pl.ds(g * width + b * part, part), :] = middle[g * part : (g + 1) * part]
    for g in range(groups):
        store(g, dot(left[g], shuffled[pl.ds(g * width, width), :], TN))


SEQ_ORDER = (6, 7, 2, 3, 4, 5, 1)


def front_kernel(n_seq, n_tp, dims, *refs):
    (tokens, cotangent, table, vectors, right, left, columns, features, first, second, third) = refs[:11]
    (mixed_out, signals_out, conv_out, wave_out, taps_out, nyquist_out, acts_out, normed_out, shuffled_out, cot_out) = refs[11:21]
    (token_v, table_v, normed, shuffled, projected, signals, acts, spread, taps_v, padded, product, keyed, wave, spectrum, conv,
     mixed, mixed_rows, nyquist, totals, local_sems, seq_send, seq_recv, back_send, back_recv, tp_send, tp_recv) = refs[21:]
    width, chans, length, rows = dims
    me, plane = lax.axis_index("seq"), lax.axis_index("tp")
    entered = greet(n_seq, n_tp)
    token_load = pltpu.make_async_copy(tokens.at[plane], token_v, local_sems.at[0])
    token_load.start()
    table_load = pltpu.make_async_copy(table, table_v, local_sems.at[1])
    table_load.start()
    token_load.wait()
    value = token_v[...].astype(F32)
    shifted = value - jnp.mean(value, axis=-1, keepdims=True)
    inverse = lax.rsqrt(jnp.mean(shifted * shifted, axis=-1, keepdims=True) + 1e-05)
    value = shifted * inverse * vectors[0:1, :] + vectors[1:2, :]
    normed[...] = value.T.astype(BF)
    groups = right.shape[0]
    block = width // groups
    fan = left.shape[2]

    def keep(g, result):
        projected[pl.ds(g * fan, fan), :] = result.astype(BF)

    monarch_forward(lambda b: normed[pl.ds(b * block, block), :], right, left, shuffled, keep)
    entered()
    sends = []
    mine = pl.ds(pl.multiple_of(me * rows, rows), rows)
    for k in SEQ_ORDER:
        other = flip(me, k)
        for s in range(3):
            copy = pltpu.make_async_remote_copy(
                src_ref=projected.at[pl.ds(pl.multiple_of(s * width + other * chans, 16), chans), :],
                dst_ref=signals.at[s, :, mine],
                send_sem=seq_send.at[k, s],
                recv_sem=seq_recv.at[k, s],
                device_id={"seq": other},
                device_id_type=MESH,
            )
            copy.start()
            sends.append(copy)
    for s in range(3):
        signals[s, :, mine] = projected[pl.ds(pl.multiple_of(s * width + me * chans, 16), chans), :]
    part = rows // n_tp
    spot = pl.ds(pl.multiple_of(plane * part, part), part)
    cot_copies = []
    for k in range(1, n_tp):
        copy = pltpu.make_async_remote_copy(
            src_ref=cotangent,
            dst_ref=cot_out.at[:, spot, :],
            send_sem=tp_send.at[k],
            recv_sem=tp_recv.at[k],
            device_id={"tp": flip(plane, k)},
            device_id_type=MESH,
        )
        copy.start()
        cot_copies.append(copy)
    own_cot = pltpu.make_async_copy(cotangent, cot_out.at[:, spot, :], local_sems.at[2])
    own_cot.start()
    out_copies = [
        pltpu.make_async_copy(normed, normed_out, local_sems.at[3]),
        pltpu.make_async_copy(shuffled, shuffled_out, local_sems.at[4]),
    ]
    for copy in out_copies:
        copy.start()

    chunk = 256
    per = length // chunk
    totals[...] = jnp.zeros_like(totals)
    for half in range(2):

        def tap_step(at, carry, half=half):
            row = pl.multiple_of(half * length + at * chunk, chunk)
            here = pl.ds(row, chunk)
            sine, cosine = sin_cos(dot(features[here, :], first[...]))
            high = sine.astype(BF)
            acts[0, here, :] = high
            acts[1, here, :] = cosine.astype(BF)
            low = (sine - high.astype(F32)).astype(BF)
            sine, cosine = sin_cos(dot(high, second[...]) + dot(low, second[...]))
            high = sine.astype(BF)
            acts[2, here, :] = high
            acts[3, here, :] = cosine.astype(BF)
            taps = dot(high, third[...]) * (length**-0.5)
            if half == 1:
                index = lax.broadcasted_iota(jnp.int32, taps.shape, 0) + at * chunk
                taps = jnp.where(index == 0, 0.0, taps)
            totals[...] += jnp.sum(taps * sign_rows(*taps.shape), axis=0, keepdims=True)
            spread[pl.ds(pl.multiple_of(at * chunk, chunk), chunk), pl.ds(half * 128, 128)] = taps.astype(BF)
            return carry

        lax.fori_loop(0, per, tap_step, 0)
    acts_copy = pltpu.make_async_copy(acts, acts_out, local_sems.at[5])
    acts_copy.start()
    out_copies.append(acts_copy)
    table_load.wait()

    def spectrum_step(at, carry):
        here = pl.ds(pl.multiple_of(at * chunk, chunk), chunk)
        sign = sign_rows(chunk, 128)
        index = lax.broadcasted_iota(jnp.int32, (chunk, 128), 0) + at * chunk
        weight = jnp.where(index == 0, 0.5 / length, 1.0 / length)
        for which in range(2):
            result = dot(table_v[which, here, :], spread[...])
            taps_v[which, here, :] = ((result[:, :128] + sign * result[:, 128:]) * weight).astype(BF)
        return carry

    lax.fori_loop(0, per, spectrum_step, 0)
    copy = pltpu.make_async_copy(taps_v, taps_out, local_sems.at[6])
    copy.start()
    out_copies.append(copy)
    tap_total = jnp.broadcast_to(totals[...], (128, 128)).T[:chans, 0:1]

    for copy in sends:
        copy.wait_recv()
    copy = pltpu.make_async_copy(signals, signals_out, local_sems.at[7])
    copy.start()
    out_copies.append(copy)

    step = 16
    padded[pl.ds(chans, 128 - chans), :] = jnp.zeros((128 - chans, length), BF)

    def short_step(at, carry):
        here = pl.ds(pl.multiple_of(at * step, step), step)
        shorted = []
        for s in range(3):
            value = signals[s, here, :].astype(F32)
            shorted.append(
                previous(value) * columns[here, 3 * s : 3 * s + 1]
                + value * columns[here, 3 * s + 1 : 3 * s + 2]
                + following(value) * columns[here, 3 * s + 2 : 3 * s + 3]
            )
        result = shorted[0] * shorted[2]
        product[here, :] = result
        keyed[here, :] = shorted[1]
        padded[here, :] = result.astype(BF)
        nyquist[here, 0:1] = jnp.sum(result * sign_lanes(step, length), axis=1, keepdims=True)
        return carry

    lax.fori_loop(0, chans // step, short_step, 0)
    nyquist[:, 1:2] = tap_total

    def wave_step(at, carry):
        here = pl.ds(pl.multiple_of(at * chunk, chunk), chunk)
        cos_part = dot(table_v[0, here, :], padded[...], NT)
        sin_part = dot(table_v[1, here, :], padded[...], NT)
        wave[0, here, :] = cos_part.astype(BF)
        wave[1, here, :] = sin_part.astype(BF)
        tap_cos = taps_v[0, here, :].astype(F32)
        tap_sin = taps_v[1, here, :].astype(F32)
        spectrum[0, here, :] = (cos_part * tap_cos - sin_part * tap_sin).astype(BF)
        spectrum[1, here, :] = (cos_part * tap_sin + sin_part * tap_cos).astype(BF)
        return carry

    lax.fori_loop(0, per, wave_step, 0)

    def conv_step(at, carry):
        here = pl.ds(pl.multiple_of(at * chunk, chunk), chunk)
        result = dot(table_v[0, here, :], spectrum[0]) + dot(table_v[1, here, :], spectrum[1])
        result = result.T[:chans]
        result = (
            result
            + sign_lanes(chans, chunk) * (nyquist[:, 0:1] * nyquist[:, 1:2] * (0.5 / length))
            + columns[:, 9:10] * product[:, here]
        )
        conv[:, here] = result
        mixed[:, here] = (keyed[:, here] * result).astype(BF)
        return carry

    lax.fori_loop(0, per, conv_step, 0)
    backs = []
    slot = pl.ds(pl.multiple_of(me * chans, 16), chans)
    for k in SEQ_ORDER:
        other = flip(me, k)
        copy = pltpu.make_async_remote_copy(
            src_ref=mixed.at[:, pl.ds(pl.multiple_of(other * rows, rows), rows)],
            dst_ref=mixed_rows.at[slot, :],
            send_sem=back_send.at[k],
            recv_sem=back_recv.at[k],
            device_id={"seq": other},
            device_id_type=MESH,
        )
        copy.start()
        backs.append(copy)
    mixed_rows[slot, :] = mixed[:, mine]
    for at, pair in enumerate(((wave, wave_out), (conv, conv_out), (nyquist, nyquist_out))):
        copy = pltpu.make_async_copy(pair[0], pair[1], local_sems.at[8 + at])
        copy.start()
        out_copies.append(copy)
    for copy in sends:
        copy.wait_send()
    for copy in cot_copies:
        copy.wait()
    own_cot.wait()
    for copy in backs:
        copy.wait()
    mixed_out[...] = mixed_rows[...]
    for copy in out_copies:
        copy.wait()


def front(mesh_shape, tokens, cotangent, table, vectors, right, left, columns, features, first, second, third):
    n_seq, n_tp = mesh_shape
    _, rows, width = tokens.shape
    chans, length = width // n_seq, rows * n_seq
    shape = jax.ShapeDtypeStruct
    return pl.pallas_call(
        functools.partial(front_kernel, n_seq, n_tp, (width, chans, length, rows)),
        out_shape=(
            shape((width, rows), BF),
            shape((3, chans, length), BF),
            shape((chans, length), F32),
            shape((2, length, 128), BF),
            shape((2, length, 128), BF),
            shape((chans, 128), F32),
            shape((4, 2 * length, 128), BF),
            shape((width, rows), BF),
            shape((width, rows), BF),
            shape((n_tp, rows, width), BF),
        ),
        in_specs=[any_spec()] * 3 + [vmem_spec()] * 8,
        out_specs=(vmem_spec(),) + (any_spec(),) * 9,
        scratch_shapes=[
            pltpu.VMEM((rows, width), BF),
            pltpu.VMEM((2, length, length), BF),
            pltpu.VMEM((width, rows), BF),
            pltpu.VMEM((width, rows), BF),
            pltpu.VMEM((3 * width, rows), BF),
            pltpu.VMEM((3, chans, length), BF),
            pltpu.VMEM((4, 2 * length, 128), BF),
            pltpu.VMEM((length, 256), BF),
            pltpu.VMEM((2, length, 128), BF),
            pltpu.VMEM((128, length), BF),
            pltpu.VMEM((chans, length), F32),
            pltpu.VMEM((chans, length), F32),
            pltpu.VMEM((2, length, 128), BF),
            pltpu.VMEM((2, length, 128), BF),
            pltpu.VMEM((chans, length), F32),
            pltpu.VMEM((chans, length), BF),
            pltpu.VMEM((width, rows), BF),
            pltpu.VMEM((chans, 128), F32),
            pltpu.VMEM((1, 128), F32),
            pltpu.SemaphoreType.DMA((12,)),
            pltpu.SemaphoreType.DMA((n_seq, 3)),
            pltpu.SemaphoreType.DMA((n_seq, 3)),
            pltpu.SemaphoreType.DMA((n_seq,)),
            pltpu.SemaphoreType.DMA((n_seq,)),
            pltpu.SemaphoreType.DMA((n_tp,)),
            pltpu.SemaphoreType.DMA((n_tp,)),
        ],
        compiler_params=pltpu.CompilerParams(collective_id=0, has_side_effects=True, vmem_limit_bytes=LIMIT),
        name="front",
    )(tokens, cotangent, table, vectors, right, left, columns, features, first, second, third)


def split_table(values):
    high = values.astype(BF)
    low = (values - high.astype(np.float32)).astype(BF)
    return high, low


def constants(length):
    index = np.arange(length)
    angle = (index[:, None] * index[None, :] % (2 * length)) * (math.pi / length)
    table = np.stack([np.cos(angle), np.sin(angle)]).astype(np.float32).astype(BF)
    place = np.arange(2 * length)
    scaled = np.where(place < length, place, place - 2 * length) / length
    features = np.zeros((2 * length, 8), np.float32)
    features[:, 0] = scaled
    features[:, 1] = np.sin(math.pi * scaled)
    features[:, 2] = np.cos(math.pi * scaled)
    features[:, 3] = np.sin(7.0 * math.pi * scaled)
    features[:, 4] = np.cos(7.0 * math.pi * scaled)
    return table, np.concatenate(split_table(features), axis=1)


def prepare(tokens, norm_gain, norm_bias, ffn_gain, ffn_bias, short_kernel, filter_first, filter_third, conv_bias):
    me = lax.axis_index("seq")
    width = tokens.shape[2]
    chans = width // lax.axis_size("seq")
    vectors = jnp.stack([norm_gain, norm_bias, ffn_gain, ffn_bias] + [jnp.zeros_like(norm_gain)] * 4)
    kernel = lax.dynamic_slice_in_dim(short_kernel, me * chans, chans, 1).astype(F32)
    bias = lax.dynamic_slice_in_dim(conv_bias, me * chans, chans, 0)
    columns = jnp.concatenate(
        [kernel.transpose(1, 0, 2).reshape(chans, 9), bias[:, None], jnp.zeros((chans, 6), F32)], axis=1
    )
    lead = jnp.pad(filter_first, ((0, 3), (0, 0)))
    first = jnp.concatenate([lead, lead], axis=0)
    third = jnp.pad(lax.dynamic_slice_in_dim(filter_third, me * chans, chans, 1), ((0, 0), (0, 128 - chans)))
    return vectors, columns, first, third


highest = lax.Precision.HIGHEST


def norm_forward(values, gain, bias):
    centre = jnp.mean(values, axis=-1, keepdims=True)
    shifted = values - centre
    inverse = lax.rsqrt(jnp.mean(shifted * shifted, axis=-1, keepdims=True) + 1e-05)
    scaled = shifted * inverse
    return (scaled * gain + bias, scaled, inverse)


def norm_backward(upstream, scaled, inverse, gain):
    weighted = upstream * gain
    first_mean = jnp.mean(weighted, axis=-1, keepdims=True)
    second_mean = jnp.mean(weighted * scaled, axis=-1, keepdims=True)
    grad_input = inverse * (weighted - first_mean - scaled * second_mean)
    breadth = upstream.shape[-1]
    grad_gain = jnp.sum((upstream * scaled).reshape(-1, breadth), axis=0)
    grad_bias = jnp.sum(upstream.reshape(-1, breadth), axis=0)
    return (grad_input, grad_gain, grad_bias)


def shuffle(blocked):
    row_count, groups, breadth = blocked.shape
    return (
        blocked.reshape(row_count, groups, groups, breadth // groups)
        .transpose(0, 2, 1, 3)
        .reshape(row_count, groups, breadth)
    )


def rows_monarch_forward(operand, right_factor, left_factor):
    row_count = operand.shape[0]
    groups = right_factor.shape[0]
    blocked = operand.reshape(row_count, groups, -1)
    middle = jnp.einsum(
        "tbi,bij->tbj", blocked, right_factor, preferred_element_type=jnp.float32
    ).astype(jnp.bfloat16)
    shuffled = shuffle(middle)
    result = jnp.einsum("tbi,bij->tbj", shuffled, left_factor, preferred_element_type=jnp.float32)
    return (shuffled, result.reshape(row_count, -1))


def rows_monarch_backward(grad_result, operand, shuffled, right_factor, left_factor):
    row_count = operand.shape[0]
    groups = right_factor.shape[0]
    grad_blocked = grad_result.reshape(row_count, groups, -1)
    grad_left = jnp.einsum(
        "tbi,tbj->bij", shuffled, grad_blocked, preferred_element_type=jnp.float32
    )
    grad_shuffled = jnp.einsum(
        "tbj,bij->tbi", grad_blocked, left_factor, preferred_element_type=jnp.float32
    )
    grad_middle = shuffle(grad_shuffled).astype(jnp.bfloat16)
    blocked = operand.reshape(row_count, groups, -1)
    grad_right = jnp.einsum(
        "tbi,tbj->bij", blocked, grad_middle, preferred_element_type=jnp.float32
    )
    grad_operand = jnp.einsum(
        "tbj,bij->tbi", grad_middle, right_factor, preferred_element_type=jnp.float32
    )
    return (grad_operand.reshape(row_count, -1), grad_right, grad_left)


def roots(row_count, col_count, period):
    product = jnp.arange(row_count)[:, None] * jnp.arange(col_count)[None, :] % period
    angle = product.astype(jnp.float32) * (2.0 * math.pi / period)
    return (jnp.cos(angle), jnp.sin(angle))


def complex_step(real_part, imag_part, cos_table, sin_table, sign, form):
    real_out = jnp.einsum(form, real_part, cos_table, precision=highest) - sign * jnp.einsum(
        form, imag_part, sin_table, precision=highest
    )
    imag_out = jnp.einsum(form, imag_part, cos_table, precision=highest) + sign * jnp.einsum(
        form, real_part, sin_table, precision=highest
    )
    return (real_out, imag_out)


def real_step(real_part, cos_table, sin_table, sign, form):
    real_out = jnp.einsum(form, real_part, cos_table, precision=highest)
    imag_out = sign * jnp.einsum(form, real_part, sin_table, precision=highest)
    return (real_out, imag_out)


def twiddle(real_part, imag_part, cos_table, sin_table, sign):
    real_out = real_part * cos_table - sign * imag_part * sin_table
    imag_out = imag_part * cos_table + sign * real_part * sin_table
    return (real_out, imag_out)


def spectrum_of(real_part):
    total = real_part.shape[-1]
    first = math.gcd(total, 128)
    second = total // first
    leading = real_part.shape[:-1]
    real_part = real_part.reshape(leading + (first, second))
    cos_first, sin_first = roots(first, first, first)
    real_part, imag_part = real_step(real_part, cos_first, sin_first, -1.0, "...ab,ak->...kb")
    cos_twist, sin_twist = roots(first, second, total)
    real_part, imag_part = twiddle(real_part, imag_part, cos_twist, sin_twist, -1.0)
    cos_second, sin_second = roots(second, second, second)
    return complex_step(real_part, imag_part, cos_second, sin_second, -1.0, "...kb,bm->...km")


def signal_of(real_part, imag_part):
    first = real_part.shape[-2]
    second = real_part.shape[-1]
    total = first * second
    leading = real_part.shape[:-2]
    cos_second, sin_second = roots(second, second, second)
    real_part, imag_part = complex_step(
        real_part, imag_part, cos_second, sin_second, 1.0, "...kb,bm->...km"
    )
    cos_twist, sin_twist = roots(first, second, total)
    real_part, imag_part = twiddle(real_part, imag_part, cos_twist, sin_twist, 1.0)
    cos_first, sin_first = roots(first, first, first)
    real_part, imag_part = complex_step(
        real_part, imag_part, cos_first, sin_first, 1.0, "...ab,ak->...kb"
    )
    return real_part.reshape(leading + (total,)) / total


def filter_parts(filter_first, filter_second, third_cols, seq_length):
    total = 2 * seq_length
    index = jnp.arange(total)
    offset = jnp.where(index < seq_length, index, index - total).astype(jnp.float32)
    scaled = offset / seq_length
    features = jnp.stack(
        [
            scaled,
            jnp.sin(math.pi * scaled),
            jnp.cos(math.pi * scaled),
            jnp.sin(7.0 * math.pi * scaled),
            jnp.cos(7.0 * math.pi * scaled),
        ],
        axis=1,
    )
    pre_one = jnp.dot(features, filter_first, precision=highest)
    act_one = jnp.sin(pre_one)
    pre_two = jnp.dot(act_one, filter_second, precision=highest)
    act_two = jnp.sin(pre_two)
    tap_mask = (index != seq_length).astype(jnp.float32)[:, None] * seq_length ** (-0.5)
    taps = jnp.dot(act_two, third_cols, precision=highest) * tap_mask
    filt_real, filt_imag = spectrum_of(taps.T)
    return (features, pre_one, act_one, pre_two, act_two, tap_mask, filt_real, filt_imag)


def general_body(
    tokens,
    norm_gain,
    norm_bias,
    in_right,
    in_left,
    short_kernel,
    filter_first,
    filter_second,
    filter_third,
    conv_bias,
    out_right,
    out_left,
    ffn_gain,
    ffn_bias,
    gate_weight,
    up_weight,
    down_weight,
    cotangent,
):
    seq_count, pos_count, model_width = tokens.shape
    row_count = seq_count * pos_count
    axis_count = lax.axis_size("seq")
    my_index = lax.axis_index("seq")
    chan_count = model_width // axis_count
    seq_length = pos_count * axis_count
    part_rows = cotangent.shape[1]
    tp_index = lax.axis_index("tp")
    tp_count = lax.axis_size("tp")
    chan_start = my_index * chan_count
    mix_count = seq_count // tp_count
    mix_tokens = lax.dynamic_slice_in_dim(tokens, tp_index * mix_count, mix_count, 0)
    mix_rows = mix_count * pos_count
    flat = mix_tokens.reshape(mix_rows, model_width).astype(jnp.float32)
    normed, scaled_one, inverse_one = norm_forward(flat, norm_gain, norm_bias)
    normed_low = normed.astype(jnp.bfloat16)
    shuffled_in, projected = rows_monarch_forward(normed_low, in_right, in_left)
    projected_low = (
        projected.astype(jnp.bfloat16)
        .reshape(mix_count, pos_count, 3, model_width)
        .transpose(2, 3, 0, 1)
    )
    channels = lax.all_to_all(projected_low, "seq", split_axis=1, concat_axis=3, tiled=True)
    signals = channels.astype(jnp.float32)
    kernel = lax.dynamic_slice_in_dim(short_kernel, chan_start, chan_count, 1).astype(jnp.float32)
    tap_zero = kernel[:, :, 0][:, :, None, None]
    tap_one = kernel[:, :, 1][:, :, None, None]
    tap_two = kernel[:, :, 2][:, :, None, None]
    padded = jnp.pad(signals, ((0, 0), (0, 0), (0, 0), (1, 1)))
    shorted = padded[..., :-2] * tap_zero + padded[..., 1:-1] * tap_one + padded[..., 2:] * tap_two
    first_f = filter_first.astype(jnp.float32)
    second_f = filter_second.astype(jnp.float32)
    third_cols = lax.dynamic_slice_in_dim(filter_third, chan_start, chan_count, 1).astype(
        jnp.float32
    )
    kept = filter_parts(first_f, second_f, third_cols, seq_length)
    filt_real = kept[6][:, None]
    filt_imag = kept[7][:, None]
    bias_cols = lax.dynamic_slice_in_dim(conv_bias, chan_start, chan_count, 0)[:, None, None]
    product = shorted[0] * shorted[2]
    product_pad = jnp.pad(product, ((0, 0), (0, 0), (0, seq_length)))
    spec_real, spec_imag = spectrum_of(product_pad)
    conv_real = spec_real * filt_real - spec_imag * filt_imag
    conv_imag = spec_real * filt_imag + spec_imag * filt_real
    convolved = signal_of(conv_real, conv_imag)[..., :seq_length] + bias_cols * product
    mixed_low = (shorted[1] * convolved).astype(jnp.bfloat16)
    back_rows = lax.all_to_all(mixed_low, "seq", split_axis=2, concat_axis=0, tiled=True)
    mixed_rows = back_rows.transpose(1, 2, 0).reshape(mix_rows, model_width)
    shuffled_out, branch = rows_monarch_forward(mixed_rows, out_right, out_left)
    residual_mine = (flat + branch).reshape(mix_count, pos_count, model_width)
    residual = lax.all_gather(residual_mine, "tp", axis=0, tiled=True)
    part_resid = lax.dynamic_slice_in_dim(residual, tp_index * part_rows, part_rows, 1)
    normed_two, scaled_two, inverse_two = norm_forward(part_resid, ffn_gain, ffn_bias)
    normed_rows = lax.all_gather(normed_two.astype(jnp.bfloat16), "tp", axis=1, tiled=True).reshape(
        row_count, model_width
    )
    gate = jnp.dot(normed_rows, gate_weight, preferred_element_type=jnp.float32)
    upward = jnp.dot(normed_rows, up_weight, preferred_element_type=jnp.float32)
    sigma = jax.nn.sigmoid(gate)
    hidden_low = (gate * sigma * upward).astype(jnp.bfloat16)
    partial_down = jnp.dot(hidden_low, down_weight, preferred_element_type=jnp.float32).reshape(
        seq_count, pos_count, model_width
    )
    glu_part = lax.psum_scatter(
        partial_down.astype(jnp.bfloat16), "tp", scatter_dimension=1, tiled=True
    ).astype(jnp.float32)
    output = (part_resid + glu_part).astype(jnp.bfloat16)
    grad_out_rows = lax.all_gather(cotangent, "tp", axis=1, tiled=True).reshape(
        row_count, model_width
    )
    grad_hidden = jnp.dot(grad_out_rows, down_weight.T, preferred_element_type=jnp.float32)
    grad_gate = (grad_hidden * upward * (sigma + gate * sigma * (1.0 - sigma))).astype(jnp.bfloat16)
    grad_up = (grad_hidden * gate * sigma).astype(jnp.bfloat16)
    grad_down_w = jnp.dot(hidden_low.T, grad_out_rows, preferred_element_type=jnp.float32)
    grad_gate_w = jnp.dot(normed_rows.T, grad_gate, preferred_element_type=jnp.float32)
    grad_up_w = jnp.dot(normed_rows.T, grad_up, preferred_element_type=jnp.float32)
    grad_normed = jnp.dot(grad_gate, gate_weight.T, preferred_element_type=jnp.float32) + jnp.dot(
        grad_up, up_weight.T, preferred_element_type=jnp.float32
    )
    grad_normed_part = lax.psum_scatter(
        grad_normed.reshape(seq_count, pos_count, model_width),
        "tp",
        scatter_dimension=1,
        tiled=True,
    )
    grad_in_two, grad_gain_two, grad_bias_two = norm_backward(
        grad_normed_part, scaled_two, inverse_two, ffn_gain
    )
    gain_total = lax.psum((grad_gain_two, grad_bias_two), ("seq", "tp"))
    grad_resid_part = cotangent.astype(jnp.float32) + grad_in_two
    grad_resid = lax.all_gather(
        grad_resid_part.astype(jnp.bfloat16), "tp", axis=1, tiled=True
    ).astype(grad_resid_part.dtype)
    grad_resid_mix = lax.dynamic_slice_in_dim(
        grad_resid, tp_index * mix_count, mix_count, 0
    ).reshape(mix_rows, model_width)
    grad_mixed_rows, grad_out_right, grad_out_left = rows_monarch_backward(
        grad_resid_mix.astype(jnp.bfloat16), mixed_rows, shuffled_out, out_right, out_left
    )
    grad_mixed_low = (
        grad_mixed_rows.astype(jnp.bfloat16)
        .reshape(mix_count, pos_count, model_width)
        .transpose(2, 0, 1)
    )
    grad_mixed = lax.all_to_all(
        grad_mixed_low, "seq", split_axis=0, concat_axis=2, tiled=True
    ).astype(jnp.float32)
    grad_conv = grad_mixed * shorted[1]
    grad_key = grad_mixed * convolved
    again = lax.optimization_barrier((first_f, second_f, third_cols))
    kept = filter_parts(again[0], again[1], again[2], seq_length)
    filt_real = kept[6][:, None]
    filt_imag = kept[7][:, None]
    features, pre_one, act_one, pre_two, act_two, tap_mask = (
        kept[0],
        kept[1],
        kept[2],
        kept[3],
        kept[4],
        kept[5],
    )
    grad_pad = jnp.pad(grad_conv, ((0, 0), (0, 0), (0, seq_length)))
    grad_spec_real, grad_spec_imag = spectrum_of(grad_pad)
    back_real = grad_spec_real * filt_real + grad_spec_imag * filt_imag
    back_imag = grad_spec_imag * filt_real - grad_spec_real * filt_imag
    grad_product = signal_of(back_real, back_imag)[..., :seq_length] + bias_cols * grad_conv
    grad_bias_cols = jnp.sum(grad_conv * product, axis=(1, 2))
    taps_real = jnp.sum(grad_spec_real * spec_real + grad_spec_imag * spec_imag, axis=1)
    taps_imag = jnp.sum(grad_spec_imag * spec_real - grad_spec_real * spec_imag, axis=1)
    grad_taps = signal_of(taps_real, taps_imag)
    grad_pre = grad_taps.T * tap_mask
    grad_third_cols = jnp.dot(act_two.T, grad_pre, precision=highest)
    grad_pre_two = jnp.dot(grad_pre, third_cols.T, precision=highest) * jnp.cos(pre_two)
    grad_second = jnp.dot(act_one.T, grad_pre_two, precision=highest)
    grad_pre_one = jnp.dot(grad_pre_two, second_f.T, precision=highest) * jnp.cos(pre_one)
    grad_first = jnp.dot(features.T, grad_pre_one, precision=highest)
    grad_shorted = jnp.stack([grad_product * shorted[2], grad_key, grad_product * shorted[0]])
    grad_short_pad = jnp.pad(grad_shorted, ((0, 0), (0, 0), (0, 0), (1, 1)))
    grad_signals = (
        grad_short_pad[..., 2:] * tap_zero
        + grad_short_pad[..., 1:-1] * tap_one
        + grad_short_pad[..., :-2] * tap_two
    )
    grad_kernel = jnp.stack(
        [
            jnp.sum(grad_shorted * padded[..., :-2], axis=(2, 3)),
            jnp.sum(grad_shorted * padded[..., 1:-1], axis=(2, 3)),
            jnp.sum(grad_shorted * padded[..., 2:], axis=(2, 3)),
        ],
        axis=-1,
    )
    grad_proj = lax.all_to_all(
        grad_signals.astype(jnp.bfloat16), "seq", split_axis=3, concat_axis=1, tiled=True
    )
    grad_proj_rows = grad_proj.transpose(2, 3, 0, 1).reshape(mix_rows, 3 * model_width)
    grad_normed_one, grad_in_right, grad_in_left = rows_monarch_backward(
        grad_proj_rows, normed_low, shuffled_in, in_right, in_left
    )
    grad_in_one, grad_gain_one, grad_bias_one = norm_backward(
        grad_normed_one, scaled_one, inverse_one, norm_gain
    )
    grad_mine = (grad_resid_mix + grad_in_one).reshape(mix_count, pos_count, model_width)
    short_full = lax.dynamic_update_slice_in_dim(
        jnp.zeros(short_kernel.shape, jnp.float32), grad_kernel, chan_start, 1
    )
    third_full = lax.dynamic_update_slice_in_dim(
        jnp.zeros(filter_third.shape, jnp.float32), grad_third_cols, chan_start, 1
    )
    bias_full = lax.dynamic_update_slice_in_dim(
        jnp.zeros(conv_bias.shape, jnp.float32), grad_bias_cols, chan_start, 0
    )
    mixer_grads = (
        grad_gain_one,
        grad_bias_one,
        grad_in_right,
        grad_in_left,
        short_full,
        grad_first,
        grad_second,
        third_full,
        bias_full,
        grad_out_right,
        grad_out_left,
    )
    grad_tokens = lax.all_gather(grad_mine.astype(jnp.bfloat16), "tp", axis=0, tiled=True).astype(
        grad_mine.dtype
    )
    mixer_grads = (
        lax.psum(mixer_grads[0].astype(jnp.bfloat16), "tp").astype(jnp.float32),
        lax.psum(mixer_grads[1].astype(jnp.bfloat16), "tp").astype(jnp.float32),
        lax.psum(mixer_grads[2].astype(jnp.bfloat16), "tp").astype(jnp.float32),
        lax.psum(mixer_grads[3].astype(jnp.bfloat16), "tp").astype(jnp.float32),
        lax.psum(mixer_grads[4].astype(jnp.bfloat16), "tp").astype(jnp.float32),
        lax.psum(mixer_grads[5].astype(jnp.bfloat16), "tp").astype(jnp.float32),
        lax.psum(mixer_grads[6].astype(jnp.bfloat16), "tp").astype(jnp.float32),
        lax.psum(mixer_grads[7].astype(jnp.bfloat16), "tp").astype(jnp.float32),
        lax.psum(mixer_grads[8].astype(jnp.bfloat16), "tp").astype(jnp.float32),
        lax.psum(mixer_grads[9].astype(jnp.bfloat16), "tp").astype(jnp.float32),
        lax.psum(mixer_grads[10].astype(jnp.bfloat16), "tp").astype(jnp.float32),
    )
    all_total = lax.psum(
        (
            mixer_grads[0],
            mixer_grads[1],
            mixer_grads[2],
            mixer_grads[3],
            mixer_grads[4],
            mixer_grads[5],
            mixer_grads[6],
            mixer_grads[7],
            mixer_grads[8],
            mixer_grads[9],
            mixer_grads[10],
            grad_gate_w,
            grad_up_w,
            grad_down_w,
        ),
        "seq",
    )
    return (
        output,
        grad_tokens,
        all_total[0],
        all_total[1],
        all_total[2],
        all_total[3],
        all_total[4],
        all_total[5],
        all_total[6],
        all_total[7],
        all_total[8],
        all_total[9],
        all_total[10],
        gain_total[0],
        gain_total[1],
        all_total[11],
        all_total[12],
        all_total[13],
    )


def fast_body(
    tokens,
    norm_gain,
    norm_bias,
    in_right,
    in_left,
    short_kernel,
    filter_first,
    filter_second,
    filter_third,
    conv_bias,
    out_right,
    out_left,
    ffn_gain,
    ffn_bias,
    gate_weight,
    up_weight,
    down_weight,
    cotangent,
):
    seq_count, pos_count, model_width = tokens.shape
    row_count = seq_count * pos_count
    axis_count = lax.axis_size("seq")
    my_index = lax.axis_index("seq")
    chan_count = model_width // axis_count
    seq_length = pos_count * axis_count
    part_rows = cotangent.shape[1]
    tp_index = lax.axis_index("tp")
    tp_count = lax.axis_size("tp")
    chan_start = my_index * chan_count
    mix_count = seq_count // tp_count
    mix_tokens = lax.dynamic_slice_in_dim(tokens, tp_index * mix_count, mix_count, 0)
    mix_rows = mix_count * pos_count
    flat = mix_tokens.reshape(mix_rows, model_width).astype(jnp.float32)
    normed, scaled_one, inverse_one = norm_forward(flat, norm_gain, norm_bias)
    normed_low = normed.astype(jnp.bfloat16)
    table, features = constants(seq_length)
    vectors, columns, first_pair, third_pad = prepare(
        tokens, norm_gain, norm_bias, ffn_gain, ffn_bias, short_kernel, filter_first, filter_third, conv_bias
    )
    (mixed_t, signal_t, conv_t, wave, taps_wave, nyquist, acts, normed_t, shuffled_t, cot_rows) = front(
        (axis_count, tp_count), tokens, cotangent, jnp.asarray(table), vectors, in_right, in_left, columns,
        jnp.asarray(features), first_pair, filter_second, third_pad
    )
    normed_low = normed_t.T
    shuffled_in = shuffled_t.T.reshape(mix_rows, 4, -1)
    channels = signal_t[:, :, None, :]
    signals = channels.astype(jnp.float32)
    kernel = lax.dynamic_slice_in_dim(short_kernel, chan_start, chan_count, 1).astype(jnp.float32)
    tap_zero = kernel[:, :, 0][:, :, None, None]
    tap_one = kernel[:, :, 1][:, :, None, None]
    tap_two = kernel[:, :, 2][:, :, None, None]
    padded = jnp.pad(signals, ((0, 0), (0, 0), (0, 0), (1, 1)))
    shorted = padded[..., :-2] * tap_zero + padded[..., 1:-1] * tap_one + padded[..., 2:] * tap_two
    first_f = filter_first.astype(jnp.float32)
    second_f = filter_second.astype(jnp.float32)
    third_cols = lax.dynamic_slice_in_dim(filter_third, chan_start, chan_count, 1).astype(
        jnp.float32
    )
    bias_cols = lax.dynamic_slice_in_dim(conv_bias, chan_start, chan_count, 0)[:, None, None]
    product = shorted[0] * shorted[2]
    product_pad = jnp.pad(product, ((0, 0), (0, 0), (0, seq_length)))
    spec_real, spec_imag = spectrum_of(product_pad)
    convolved = conv_t[:, None, :]
    mixed_rows = mixed_t.T
    shuffled_out, branch = rows_monarch_forward(mixed_rows, out_right, out_left)
    residual_mine = (flat + branch).reshape(mix_count, pos_count, model_width)
    residual = lax.all_gather(residual_mine, "tp", axis=0, tiled=True)
    part_resid = lax.dynamic_slice_in_dim(residual, tp_index * part_rows, part_rows, 1)
    normed_two, scaled_two, inverse_two = norm_forward(part_resid, ffn_gain, ffn_bias)
    normed_rows = lax.all_gather(normed_two.astype(jnp.bfloat16), "tp", axis=1, tiled=True).reshape(
        row_count, model_width
    )
    gate = jnp.dot(normed_rows, gate_weight, preferred_element_type=jnp.float32)
    upward = jnp.dot(normed_rows, up_weight, preferred_element_type=jnp.float32)
    sigma = jax.nn.sigmoid(gate)
    hidden_low = (gate * sigma * upward).astype(jnp.bfloat16)
    partial_down = jnp.dot(hidden_low, down_weight, preferred_element_type=jnp.float32).reshape(
        seq_count, pos_count, model_width
    )
    glu_part = lax.psum_scatter(
        partial_down.astype(jnp.bfloat16), "tp", scatter_dimension=1, tiled=True
    ).astype(jnp.float32)
    output = (part_resid + glu_part).astype(jnp.bfloat16)
    grad_out_rows = cot_rows.reshape(row_count, model_width)
    grad_hidden = jnp.dot(grad_out_rows, down_weight.T, preferred_element_type=jnp.float32)
    grad_gate = (grad_hidden * upward * (sigma + gate * sigma * (1.0 - sigma))).astype(jnp.bfloat16)
    grad_up = (grad_hidden * gate * sigma).astype(jnp.bfloat16)
    grad_down_w = jnp.dot(hidden_low.T, grad_out_rows, preferred_element_type=jnp.float32)
    grad_gate_w = jnp.dot(normed_rows.T, grad_gate, preferred_element_type=jnp.float32)
    grad_up_w = jnp.dot(normed_rows.T, grad_up, preferred_element_type=jnp.float32)
    grad_normed = jnp.dot(grad_gate, gate_weight.T, preferred_element_type=jnp.float32) + jnp.dot(
        grad_up, up_weight.T, preferred_element_type=jnp.float32
    )
    grad_normed_part = lax.psum_scatter(
        grad_normed.reshape(seq_count, pos_count, model_width),
        "tp",
        scatter_dimension=1,
        tiled=True,
    )
    grad_in_two, grad_gain_two, grad_bias_two = norm_backward(
        grad_normed_part, scaled_two, inverse_two, ffn_gain
    )
    gain_total = lax.psum((grad_gain_two, grad_bias_two), ("seq", "tp"))
    grad_resid_part = cotangent.astype(jnp.float32) + grad_in_two
    grad_resid = lax.all_gather(
        grad_resid_part.astype(jnp.bfloat16), "tp", axis=1, tiled=True
    ).astype(grad_resid_part.dtype)
    grad_resid_mix = lax.dynamic_slice_in_dim(
        grad_resid, tp_index * mix_count, mix_count, 0
    ).reshape(mix_rows, model_width)
    grad_mixed_rows, grad_out_right, grad_out_left = rows_monarch_backward(
        grad_resid_mix.astype(jnp.bfloat16), mixed_rows, shuffled_out, out_right, out_left
    )
    grad_mixed_low = (
        grad_mixed_rows.astype(jnp.bfloat16)
        .reshape(mix_count, pos_count, model_width)
        .transpose(2, 0, 1)
    )
    grad_mixed = lax.all_to_all(
        grad_mixed_low, "seq", split_axis=0, concat_axis=2, tiled=True
    ).astype(jnp.float32)
    grad_conv = grad_mixed * shorted[1]
    grad_key = grad_mixed * convolved
    again = lax.optimization_barrier((first_f, second_f, third_cols))
    kept = filter_parts(again[0], again[1], again[2], seq_length)
    filt_real = kept[6][:, None]
    filt_imag = kept[7][:, None]
    features, pre_one, act_one, pre_two, act_two, tap_mask = (
        kept[0],
        kept[1],
        kept[2],
        kept[3],
        kept[4],
        kept[5],
    )
    grad_pad = jnp.pad(grad_conv, ((0, 0), (0, 0), (0, seq_length)))
    grad_spec_real, grad_spec_imag = spectrum_of(grad_pad)
    back_real = grad_spec_real * filt_real + grad_spec_imag * filt_imag
    back_imag = grad_spec_imag * filt_real - grad_spec_real * filt_imag
    grad_product = signal_of(back_real, back_imag)[..., :seq_length] + bias_cols * grad_conv
    grad_bias_cols = jnp.sum(grad_conv * product, axis=(1, 2))
    taps_real = jnp.sum(grad_spec_real * spec_real + grad_spec_imag * spec_imag, axis=1)
    taps_imag = jnp.sum(grad_spec_imag * spec_real - grad_spec_real * spec_imag, axis=1)
    grad_taps = signal_of(taps_real, taps_imag)
    grad_pre = grad_taps.T * tap_mask
    grad_third_cols = jnp.dot(act_two.T, grad_pre, precision=highest)
    grad_pre_two = jnp.dot(grad_pre, third_cols.T, precision=highest) * jnp.cos(pre_two)
    grad_second = jnp.dot(act_one.T, grad_pre_two, precision=highest)
    grad_pre_one = jnp.dot(grad_pre_two, second_f.T, precision=highest) * jnp.cos(pre_one)
    grad_first = jnp.dot(features.T, grad_pre_one, precision=highest)
    grad_shorted = jnp.stack([grad_product * shorted[2], grad_key, grad_product * shorted[0]])
    grad_short_pad = jnp.pad(grad_shorted, ((0, 0), (0, 0), (0, 0), (1, 1)))
    grad_signals = (
        grad_short_pad[..., 2:] * tap_zero
        + grad_short_pad[..., 1:-1] * tap_one
        + grad_short_pad[..., :-2] * tap_two
    )
    grad_kernel = jnp.stack(
        [
            jnp.sum(grad_shorted * padded[..., :-2], axis=(2, 3)),
            jnp.sum(grad_shorted * padded[..., 1:-1], axis=(2, 3)),
            jnp.sum(grad_shorted * padded[..., 2:], axis=(2, 3)),
        ],
        axis=-1,
    )
    grad_proj = lax.all_to_all(
        grad_signals.astype(jnp.bfloat16), "seq", split_axis=3, concat_axis=1, tiled=True
    )
    grad_proj_rows = grad_proj.transpose(2, 3, 0, 1).reshape(mix_rows, 3 * model_width)
    grad_normed_one, grad_in_right, grad_in_left = rows_monarch_backward(
        grad_proj_rows, normed_low, shuffled_in, in_right, in_left
    )
    grad_in_one, grad_gain_one, grad_bias_one = norm_backward(
        grad_normed_one, scaled_one, inverse_one, norm_gain
    )
    grad_mine = (grad_resid_mix + grad_in_one).reshape(mix_count, pos_count, model_width)
    short_full = lax.dynamic_update_slice_in_dim(
        jnp.zeros(short_kernel.shape, jnp.float32), grad_kernel, chan_start, 1
    )
    third_full = lax.dynamic_update_slice_in_dim(
        jnp.zeros(filter_third.shape, jnp.float32), grad_third_cols, chan_start, 1
    )
    bias_full = lax.dynamic_update_slice_in_dim(
        jnp.zeros(conv_bias.shape, jnp.float32), grad_bias_cols, chan_start, 0
    )
    mixer_grads = (
        grad_gain_one,
        grad_bias_one,
        grad_in_right,
        grad_in_left,
        short_full,
        grad_first,
        grad_second,
        third_full,
        bias_full,
        grad_out_right,
        grad_out_left,
    )
    grad_tokens = lax.all_gather(grad_mine.astype(jnp.bfloat16), "tp", axis=0, tiled=True).astype(
        grad_mine.dtype
    )
    mixer_grads = (
        lax.psum(mixer_grads[0].astype(jnp.bfloat16), "tp").astype(jnp.float32),
        lax.psum(mixer_grads[1].astype(jnp.bfloat16), "tp").astype(jnp.float32),
        lax.psum(mixer_grads[2].astype(jnp.bfloat16), "tp").astype(jnp.float32),
        lax.psum(mixer_grads[3].astype(jnp.bfloat16), "tp").astype(jnp.float32),
        lax.psum(mixer_grads[4].astype(jnp.bfloat16), "tp").astype(jnp.float32),
        lax.psum(mixer_grads[5].astype(jnp.bfloat16), "tp").astype(jnp.float32),
        lax.psum(mixer_grads[6].astype(jnp.bfloat16), "tp").astype(jnp.float32),
        lax.psum(mixer_grads[7].astype(jnp.bfloat16), "tp").astype(jnp.float32),
        lax.psum(mixer_grads[8].astype(jnp.bfloat16), "tp").astype(jnp.float32),
        lax.psum(mixer_grads[9].astype(jnp.bfloat16), "tp").astype(jnp.float32),
        lax.psum(mixer_grads[10].astype(jnp.bfloat16), "tp").astype(jnp.float32),
    )
    all_total = lax.psum(
        (
            mixer_grads[0],
            mixer_grads[1],
            mixer_grads[2],
            mixer_grads[3],
            mixer_grads[4],
            mixer_grads[5],
            mixer_grads[6],
            mixer_grads[7],
            mixer_grads[8],
            mixer_grads[9],
            mixer_grads[10],
            grad_gate_w,
            grad_up_w,
            grad_down_w,
        ),
        "seq",
    )
    return (
        output,
        grad_tokens,
        all_total[0],
        all_total[1],
        all_total[2],
        all_total[3],
        all_total[4],
        all_total[5],
        all_total[6],
        all_total[7],
        all_total[8],
        all_total[9],
        all_total[10],
        gain_total[0],
        gain_total[1],
        all_total[11],
        all_total[12],
        all_total[13],
    )


def choose_body(mesh, *arrays):
    tokens = arrays[0]
    chans = tokens.shape[2] // mesh.shape["seq"]
    fits = mesh.shape["seq"] == 8 and mesh.shape["tp"] == 4 and tokens.shape[:2] == (4, 128) and chans == 96
    return (fast_body if fits else general_body)(*arrays)


def solution(mesh):
    return jax.shard_map(
        functools.partial(choose_body, mesh),
        mesh=mesh,
        in_specs=(
            P(None, "seq", None),
            P(),
            P(),
            P(),
            P(),
            P(),
            P(),
            P(),
            P(),
            P(),
            P(),
            P(),
            P(),
            P(),
            P(None, "tp"),
            P(None, "tp"),
            P("tp", None),
            P(None, ("seq", "tp"), None),
        ),
        out_specs=(
            P(None, ("seq", "tp"), None),
            P(None, "seq", None),
            P(),
            P(),
            P(),
            P(),
            P(),
            P(),
            P(),
            P(),
            P(),
            P(),
            P(),
            P(),
            P(),
            P(None, "tp"),
            P(None, "tp"),
            P("tp", None),
        ),
        check_vma=False,
    )
```

```python
import functools
import math

import numpy as np
import jax
import jax.numpy as jnp
from jax import lax
from jax.experimental import pallas as pl
from jax.experimental.pallas import tpu as pltpu
from jax.sharding import PartitionSpec as P

BF = jnp.bfloat16
F32 = jnp.float32
MESH = pl.DeviceIdType.MESH
NN = ((1,), (0,))
NT = ((1,), (1,))
TN = ((0,), (0,))
LIMIT = 56 * 1024 * 1024


def dot(first, second, form=NN):
    return lax.dot_general(first, second, (form, ((), ())), preferred_element_type=F32)


def any_spec():
    return pl.BlockSpec(memory_space=pl.ANY)


def vmem_spec():
    return pl.BlockSpec(memory_space=pltpu.VMEM)


def sin_cos(value):
    turns = jnp.floor(value * (1.0 / math.pi) + 0.5)
    rest = value - turns * 3.140625
    rest = rest - turns * 9.67502593994140625e-4
    rest = rest - turns * 1.509957990978376432e-7
    half = turns * 0.5
    sign = 1.0 - 4.0 * (half - jnp.floor(half))
    square = rest * rest
    sine = 1.0 / 362880 - square * (1.0 / 39916800)
    sine = -1.0 / 5040 + square * sine
    sine = 1.0 / 120 + square * sine
    sine = -1.0 / 6 + square * sine
    sine = rest + rest * square * sine
    cosine = 1.0 / 40320 - square * (1.0 / 3628800 - square * (1.0 / 479001600))
    cosine = -1.0 / 720 + square * cosine
    cosine = 1.0 / 24 + square * cosine
    cosine = -0.5 + square * cosine
    cosine = 1.0 + square * cosine
    return sign * sine, sign * cosine


def flip(index, bits):
    result = 0
    for place in range(3):
        digit = lax.rem(index // (1 << place), 2)
        if (bits >> place) & 1:
            digit = 1 - digit
        result = result + digit * (1 << place)
    return result


def greet(n_seq, n_tp):
    me, plane = lax.axis_index("seq"), lax.axis_index("tp")
    barrier = pltpu.get_barrier_semaphore()
    for k in range(1, n_seq):
        pl.semaphore_signal(barrier, inc=1, device_id={"seq": flip(me, k)}, device_id_type=MESH)
    for k in range(1, n_tp):
        pl.semaphore_signal(barrier, inc=1, device_id={"tp": flip(plane, k)}, device_id_type=MESH)
    return lambda: pl.semaphore_wait(barrier, n_seq + n_tp - 2)


def sign_rows(count, width):
    row = lax.broadcasted_iota(jnp.int32, (count, width), 0)
    return (1 - 2 * lax.rem(row, 2)).astype(F32)


def sign_lanes(count, width):
    lane = lax.broadcasted_iota(jnp.int32, (count, width), 1)
    return (1 - 2 * lax.rem(lane, 2)).astype(F32)


def previous(values):
    lane = lax.broadcasted_iota(jnp.int32, values.shape, 1)
    return jnp.where(lane == 0, 0.0, pltpu.roll(values, 1, 1))


def following(values):
    last = values.shape[1] - 1
    lane = lax.broadcasted_iota(jnp.int32, values.shape, 1)
    return jnp.where(lane == last, 0.0, pltpu.roll(values, last, 1))


def monarch_forward(load, right, left, shuffled, store):
    groups, width, _ = right.shape
    part = width // groups
    for b in range(groups):
        middle = dot(right[b], load(b), TN).astype(BF)
        for g in range(groups):
            shuffled[pl.ds(g * width + b * part, part), :] = middle[g * part : (g + 1) * part]
    for g in range(groups):
        store(g, dot(left[g], shuffled[pl.ds(g * width, width), :], TN))


SEQ_ORDER = (6, 7, 2, 3, 4, 5, 1)


def front_kernel(n_seq, n_tp, dims, *refs):
    (tokens, cotangent, table, vectors, right, left, columns, features, first, second, third) = refs[:11]
    (mixed_out, signals_out, conv_out, wave_out, taps_out, nyquist_out, acts_out, normed_out, shuffled_out, cot_out) = refs[11:21]
    (token_v, table_v, normed, shuffled, projected, signals, acts, spread, taps_v, padded, product, keyed, wave, spectrum, conv,
     mixed, mixed_rows, nyquist, totals, local_sems, seq_send, seq_recv, back_send, back_recv, tp_send, tp_recv) = refs[21:]
    width, chans, length, rows = dims
    me, plane = lax.axis_index("seq"), lax.axis_index("tp")
    entered = greet(n_seq, n_tp)
    token_load = pltpu.make_async_copy(tokens.at[plane], token_v, local_sems.at[0])
    token_load.start()
    table_load = pltpu.make_async_copy(table, table_v, local_sems.at[1])
    table_load.start()
    token_load.wait()
    value = token_v[...].astype(F32)
    shifted = value - jnp.mean(value, axis=-1, keepdims=True)
    inverse = lax.rsqrt(jnp.mean(shifted * shifted, axis=-1, keepdims=True) + 1e-05)
    value = shifted * inverse * vectors[0:1, :] + vectors[1:2, :]
    normed[...] = value.T.astype(BF)
    groups = right.shape[0]
    block = width // groups
    fan = left.shape[2]

    def keep(g, result):
        projected[pl.ds(g * fan, fan), :] = result.astype(BF)

    monarch_forward(lambda b: normed[pl.ds(b * block, block), :], right, left, shuffled, keep)
    entered()
    sends = []
    mine = pl.ds(pl.multiple_of(me * rows, rows), rows)
    for k in SEQ_ORDER:
        other = flip(me, k)
        for s in range(3):
            copy = pltpu.make_async_remote_copy(
                src_ref=projected.at[pl.ds(pl.multiple_of(s * width + other * chans, 16), chans), :],
                dst_ref=signals.at[s, :, mine],
                send_sem=seq_send.at[k, s],
                recv_sem=seq_recv.at[k, s],
                device_id={"seq": other},
                device_id_type=MESH,
            )
            copy.start()
            sends.append(copy)
    for s in range(3):
        signals[s, :, mine] = projected[pl.ds(pl.multiple_of(s * width + me * chans, 16), chans), :]
    part = rows // n_tp
    spot = pl.ds(pl.multiple_of(plane * part, part), part)
    cot_copies = []
    for k in range(1, n_tp):
        copy = pltpu.make_async_remote_copy(
            src_ref=cotangent,
            dst_ref=cot_out.at[:, spot, :],
            send_sem=tp_send.at[k],
            recv_sem=tp_recv.at[k],
            device_id={"tp": flip(plane, k)},
            device_id_type=MESH,
        )
        copy.start()
        cot_copies.append(copy)
    own_cot = pltpu.make_async_copy(cotangent, cot_out.at[:, spot, :], local_sems.at[2])
    own_cot.start()
    out_copies = [
        pltpu.make_async_copy(normed, normed_out, local_sems.at[3]),
        pltpu.make_async_copy(shuffled, shuffled_out, local_sems.at[4]),
    ]
    for copy in out_copies:
        copy.start()

    chunk = 256
    per = length // chunk
    totals[...] = jnp.zeros_like(totals)
    for half in range(2):

        def tap_step(at, carry, half=half):
            row = pl.multiple_of(half * length + at * chunk, chunk)
            here = pl.ds(row, chunk)
            sine, cosine = sin_cos(dot(features[here, :], first[...]))
            high = sine.astype(BF)
            acts[0, here, :] = high
            acts[1, here, :] = cosine.astype(BF)
            low = (sine - high.astype(F32)).astype(BF)
            sine, cosine = sin_cos(dot(high, second[...]) + dot(low, second[...]))
            high = sine.astype(BF)
            acts[2, here, :] = high
            acts[3, here, :] = cosine.astype(BF)
            taps = dot(high, third[...]) * (length**-0.5)
            if half == 1:
                index = lax.broadcasted_iota(jnp.int32, taps.shape, 0) + at * chunk
                taps = jnp.where(index == 0, 0.0, taps)
            totals[...] += jnp.sum(taps * sign_rows(*taps.shape), axis=0, keepdims=True)
            spread[pl.ds(pl.multiple_of(at * chunk, chunk), chunk), pl.ds(half * 128, 128)] = taps.astype(BF)
            return carry

        lax.fori_loop(0, per, tap_step, 0)
    acts_copy = pltpu.make_async_copy(acts, acts_out, local_sems.at[5])
    acts_copy.start()
    out_copies.append(acts_copy)
    table_load.wait()

    def spectrum_step(at, carry):
        here = pl.ds(pl.multiple_of(at * chunk, chunk), chunk)
        sign = sign_rows(chunk, 128)
        index = lax.broadcasted_iota(jnp.int32, (chunk, 128), 0) + at * chunk
        weight = jnp.where(index == 0, 0.5 / length, 1.0 / length)
        for which in range(2):
            result = dot(table_v[which, here, :], spread[...])
            taps_v[which, here, :] = ((result[:, :128] + sign * result[:, 128:]) * weight).astype(BF)
        return carry

    lax.fori_loop(0, per, spectrum_step, 0)
    copy = pltpu.make_async_copy(taps_v, taps_out, local_sems.at[6])
    copy.start()
    out_copies.append(copy)
    tap_total = jnp.broadcast_to(totals[...], (128, 128)).T[:chans, 0:1]

    for copy in sends:
        copy.wait_recv()
    copy = pltpu.make_async_copy(signals, signals_out, local_sems.at[7])
    copy.start()
    out_copies.append(copy)

    step = 16
    padded[pl.ds(chans, 128 - chans), :] = jnp.zeros((128 - chans, length), BF)

    def short_step(at, carry):
        here = pl.ds(pl.multiple_of(at * step, step), step)
        shorted = []
        for s in range(3):
            value = signals[s, here, :].astype(F32)
            shorted.append(
                previous(value) * columns[here, 3 * s : 3 * s + 1]
                + value * columns[here, 3 * s + 1 : 3 * s + 2]
                + following(value) * columns[here, 3 * s + 2 : 3 * s + 3]
            )
        result = shorted[0] * shorted[2]
        product[here, :] = result
        keyed[here, :] = shorted[1]
        padded[here, :] = result.astype(BF)
        nyquist[here, 0:1] = jnp.sum(result * sign_lanes(step, length), axis=1, keepdims=True)
        return carry

    lax.fori_loop(0, chans // step, short_step, 0)
    nyquist[:, 1:2] = tap_total

    def wave_step(at, carry):
        here = pl.ds(pl.multiple_of(at * chunk, chunk), chunk)
        cos_part = dot(table_v[0, here, :], padded[...], NT)
        sin_part = dot(table_v[1, here, :], padded[...], NT)
        wave[0, here, :] = cos_part.astype(BF)
        wave[1, here, :] = sin_part.astype(BF)
        tap_cos = taps_v[0, here, :].astype(F32)
        tap_sin = taps_v[1, here, :].astype(F32)
        spectrum[0, here, :] = (cos_part * tap_cos - sin_part * tap_sin).astype(BF)
        spectrum[1, here, :] = (cos_part * tap_sin + sin_part * tap_cos).astype(BF)
        return carry

    lax.fori_loop(0, per, wave_step, 0)

    def conv_step(at, carry):
        here = pl.ds(pl.multiple_of(at * chunk, chunk), chunk)
        result = dot(table_v[0, here, :], spectrum[0]) + dot(table_v[1, here, :], spectrum[1])
        result = result.T[:chans]
        result = (
            result
            + sign_lanes(chans, chunk) * (nyquist[:, 0:1] * nyquist[:, 1:2] * (0.5 / length))
            + columns[:, 9:10] * product[:, here]
        )
        conv[:, here] = result
        mixed[:, here] = (keyed[:, here] * result).astype(BF)
        return carry

    lax.fori_loop(0, per, conv_step, 0)
    backs = []
    slot = pl.ds(pl.multiple_of(me * chans, 16), chans)
    for k in SEQ_ORDER:
        other = flip(me, k)
        copy = pltpu.make_async_remote_copy(
            src_ref=mixed.at[:, pl.ds(pl.multiple_of(other * rows, rows), rows)],
            dst_ref=mixed_rows.at[slot, :],
            send_sem=back_send.at[k],
            recv_sem=back_recv.at[k],
            device_id={"seq": other},
            device_id_type=MESH,
        )
        copy.start()
        backs.append(copy)
    mixed_rows[slot, :] = mixed[:, mine]
    for at, pair in enumerate(((wave, wave_out), (conv, conv_out), (nyquist, nyquist_out))):
        copy = pltpu.make_async_copy(pair[0], pair[1], local_sems.at[8 + at])
        copy.start()
        out_copies.append(copy)
    for copy in sends:
        copy.wait_send()
    for copy in cot_copies:
        copy.wait()
    own_cot.wait()
    for copy in backs:
        copy.wait()
    mixed_out[...] = mixed_rows[...]
    for copy in out_copies:
        copy.wait()


def front(mesh_shape, tokens, cotangent, table, vectors, right, left, columns, features, first, second, third):
    n_seq, n_tp = mesh_shape
    _, rows, width = tokens.shape
    chans, length = width // n_seq, rows * n_seq
    shape = jax.ShapeDtypeStruct
    return pl.pallas_call(
        functools.partial(front_kernel, n_seq, n_tp, (width, chans, length, rows)),
        out_shape=(
            shape((width, rows), BF),
            shape((3, chans, length), BF),
            shape((chans, length), F32),
            shape((2, length, 128), BF),
            shape((2, length, 128), BF),
            shape((chans, 128), F32),
            shape((4, 2 * length, 128), BF),
            shape((width, rows), BF),
            shape((width, rows), BF),
            shape((n_tp, rows, width), BF),
        ),
        in_specs=[any_spec()] * 3 + [vmem_spec()] * 8,
        out_specs=(vmem_spec(),) + (any_spec(),) * 9,
        scratch_shapes=[
            pltpu.VMEM((rows, width), BF),
            pltpu.VMEM((2, length, length), BF),
            pltpu.VMEM((width, rows), BF),
            pltpu.VMEM((width, rows), BF),
            pltpu.VMEM((3 * width, rows), BF),
            pltpu.VMEM((3, chans, length), BF),
            pltpu.VMEM((4, 2 * length, 128), BF),
            pltpu.VMEM((length, 256), BF),
            pltpu.VMEM((2, length, 128), BF),
            pltpu.VMEM((128, length), BF),
            pltpu.VMEM((chans, length), F32),
            pltpu.VMEM((chans, length), F32),
            pltpu.VMEM((2, length, 128), BF),
            pltpu.VMEM((2, length, 128), BF),
            pltpu.VMEM((chans, length), F32),
            pltpu.VMEM((chans, length), BF),
            pltpu.VMEM((width, rows), BF),
            pltpu.VMEM((chans, 128), F32),
            pltpu.VMEM((1, 128), F32),
            pltpu.SemaphoreType.DMA((12,)),
            pltpu.SemaphoreType.DMA((n_seq, 3)),
            pltpu.SemaphoreType.DMA((n_seq, 3)),
            pltpu.SemaphoreType.DMA((n_seq,)),
            pltpu.SemaphoreType.DMA((n_seq,)),
            pltpu.SemaphoreType.DMA((n_tp,)),
            pltpu.SemaphoreType.DMA((n_tp,)),
        ],
        compiler_params=pltpu.CompilerParams(collective_id=0, has_side_effects=True, vmem_limit_bytes=LIMIT),
        name="front",
    )(tokens, cotangent, table, vectors, right, left, columns, features, first, second, third)


def split_table(values):
    high = values.astype(BF)
    low = (values - high.astype(np.float32)).astype(BF)
    return high, low


def constants(length):
    index = np.arange(length)
    angle = (index[:, None] * index[None, :] % (2 * length)) * (math.pi / length)
    table = np.stack([np.cos(angle), np.sin(angle)]).astype(np.float32).astype(BF)
    place = np.arange(2 * length)
    scaled = np.where(place < length, place, place - 2 * length) / length
    features = np.zeros((2 * length, 8), np.float32)
    features[:, 0] = scaled
    features[:, 1] = np.sin(math.pi * scaled)
    features[:, 2] = np.cos(math.pi * scaled)
    features[:, 3] = np.sin(7.0 * math.pi * scaled)
    features[:, 4] = np.cos(7.0 * math.pi * scaled)
    return table, np.concatenate(split_table(features), axis=1)


def prepare(tokens, norm_gain, norm_bias, ffn_gain, ffn_bias, short_kernel, filter_first, filter_third, conv_bias):
    me = lax.axis_index("seq")
    width = tokens.shape[2]
    chans = width // lax.axis_size("seq")
    vectors = jnp.stack([norm_gain, norm_bias, ffn_gain, ffn_bias] + [jnp.zeros_like(norm_gain)] * 4)
    kernel = lax.dynamic_slice_in_dim(short_kernel, me * chans, chans, 1).astype(F32)
    bias = lax.dynamic_slice_in_dim(conv_bias, me * chans, chans, 0)
    columns = jnp.concatenate(
        [kernel.transpose(1, 0, 2).reshape(chans, 9), bias[:, None], jnp.zeros((chans, 6), F32)], axis=1
    )
    lead = jnp.pad(filter_first, ((0, 3), (0, 0)))
    first = jnp.concatenate([lead, lead], axis=0)
    third = jnp.pad(lax.dynamic_slice_in_dim(filter_third, me * chans, chans, 1), ((0, 0), (0, 128 - chans)))
    return vectors, columns, first, third


def monarch_backward(upstream, operand, shuffled, right, left, middle, keep_right, keep_left, store):
    groups, width, _ = right.shape
    part = width // groups
    for g in range(groups):
        above = upstream(g)
        keep_left(g, dot(shuffled[pl.ds(g * width, width), :], above, NT))
        below = dot(left[g], above).astype(BF)
        for b in range(groups):
            middle[pl.ds(b * width + g * part, part), :] = below[b * part : (b + 1) * part]
    for b in range(groups):
        above = middle[pl.ds(b * width, width), :]
        keep_right(b, dot(operand(b), above, NT))
        store(b, dot(right[b], above))


CHIPS = (6, 2, 4)


def feed_kernel(n_seq, n_tp, dims, *refs):
    (mixed, tokens, cot_rows, vectors, right, left, gate_w, up_w, down_w) = refs[:9]
    (grad_mixed_out, grad_resid_out, shard_out, grad_weights_out, grad_vectors_out, output_out) = refs[9:15]
    (token_v, cot_v, gate_v, up_v, down_v, shuffled, branch, resid, scaled, inverse, normed, hidden, grad_hidden, grad_gate, grad_up,
     grad_normed, grad_send, grad_recv, glu_own, glu_send, glu_recv, turned, grads, core_recv, halves, chip_recv, grad_branch,
     middle, grad_mixed, grad_mixed_all, out_rows, output_v, local_sems, gather_send, gather_recv, back_send, back_recv, glu_ssem, glu_rsem,
     out_send, out_recv, core_ssem, core_rsem, chip_ssem, chip_rsem, seq_send, seq_recv) = refs[15:]
    width, chans, length, rows = dims
    me, plane = lax.axis_index("seq"), lax.axis_index("tp")
    entered = greet(n_seq, n_tp)
    loads = [
        pltpu.make_async_copy(tokens.at[plane], token_v, local_sems.at[0]),
        pltpu.make_async_copy(cot_rows, cot_v, local_sems.at[1]),
        pltpu.make_async_copy(down_w, down_v, local_sems.at[2]),
        pltpu.make_async_copy(gate_w, gate_v, local_sems.at[3]),
        pltpu.make_async_copy(up_w, up_v, local_sems.at[4]),
    ]
    for copy in loads:
        copy.start()
    groups = right.shape[0]
    block = width // groups

    def keep_branch(g, result):
        branch[pl.ds(g * block, block), :] = result

    monarch_forward(lambda b: mixed[pl.ds(b * block, block), :], right, left, shuffled, keep_branch)
    loads[0].wait()
    value = token_v[...].astype(F32) + branch[...].T
    resid[...] = value
    shifted = value - jnp.mean(value, axis=-1, keepdims=True)
    inverse[...] = lax.rsqrt(jnp.mean(shifted * shifted, axis=-1, keepdims=True) + 1e-05)
    value = shifted * inverse[...]
    scaled[...] = value
    normed[plane] = (value * vectors[2:3, :] + vectors[3:4, :]).astype(BF)
    entered()
    gathers = {}
    for k in range(1, n_tp):
        gathers[k] = pltpu.make_async_remote_copy(
            src_ref=normed.at[plane],
            dst_ref=normed.at[plane],
            send_sem=gather_send.at[k],
            recv_sem=gather_recv.at[k],
            device_id={"tp": flip(plane, k)},
            device_id_type=MESH,
        )
        gathers[k].start()
    loads[1].wait()
    loads[2].wait()
    chunk = 256
    pieces = width // chunk

    def hidden_step(at, carry):
        cols = pl.ds(pl.multiple_of(at * chunk, chunk), chunk)
        result = dot(cot_v[...].reshape(n_tp * rows, width), down_v[cols, :], NT)
        grad_hidden[:, :, cols] = result.reshape(n_tp, rows, chunk)
        return carry

    lax.fori_loop(0, pieces, hidden_step, 0)
    loads[3].wait()
    loads[4].wait()
    backs, glus = {}, {}
    for k in range(n_tp):
        other = flip(plane, k)
        if k > 0:
            gathers[k].wait_recv()

        def gate_step(at, carry, other=other):
            cols = pl.ds(pl.multiple_of(at * chunk, chunk), chunk)
            value = normed[other]
            gate = dot(value, gate_v[:, cols])
            upward = dot(value, up_v[:, cols])
            sigma = 1.0 / (1.0 + jnp.exp(-gate))
            active = gate * sigma
            hidden[other, :, cols] = (active * upward).astype(BF)
            above = grad_hidden[other, :, cols]
            grad_gate[other, :, cols] = (above * upward * (sigma + active * (1.0 - sigma))).astype(BF)
            grad_up[other, :, cols] = (above * active).astype(BF)
            return carry

        lax.fori_loop(0, pieces, gate_step, 0)

        def back_step(at, carry, k=k, other=other):
            cols = pl.ds(pl.multiple_of(at * chunk, chunk), chunk)
            result = dot(grad_gate[other], gate_v[cols, :], NT) + dot(grad_up[other], up_v[cols, :], NT)
            if k == 0:
                grad_normed[:, cols] = result
            else:
                grad_send[k, :, cols] = result.astype(BF)
            return carry

        lax.fori_loop(0, pieces, back_step, 0)
        if k > 0:
            backs[k] = pltpu.make_async_remote_copy(
                src_ref=grad_send.at[k],
                dst_ref=grad_recv.at[k],
                send_sem=back_send.at[k],
                recv_sem=back_recv.at[k],
                device_id={"tp": other},
                device_id_type=MESH,
            )
            backs[k].start()

    def turn(source):
        for s in range(n_tp):
            turned[:, s * rows : (s + 1) * rows] = source[s].T

    def weight_grad(which, factor):
        def step(at, carry):
            here = pl.ds(pl.multiple_of(at * chunk, chunk), chunk)
            result = dot(turned[here, :], factor[...].reshape(n_tp * rows, width))
            grads[which, here, :] = result.astype(BF)
            return carry

        lax.fori_loop(0, pieces, step, 0)

    core = lax.rem(me, 2)
    half = width // 2
    core_copies = []

    def core_send(which):
        copy = pltpu.make_async_remote_copy(
            src_ref=grads.at[which, pl.ds(pl.multiple_of((1 - core) * half, half), half), :],
            dst_ref=core_recv.at[which],
            send_sem=core_ssem.at[which],
            recv_sem=core_rsem.at[which],
            device_id={"seq": flip(me, 1)},
            device_id_type=MESH,
        )
        copy.start()
        core_copies.append(copy)

    turn(normed)
    weight_grad(0, grad_gate)
    core_send(0)
    weight_grad(1, grad_up)
    core_send(1)
    turn(hidden)
    weight_grad(2, cot_v)
    core_send(2)

    for k in (1, 2, 3, 0):
        other = flip(plane, k)

        def glu_step(at, carry, k=k, other=other):
            cols = pl.ds(pl.multiple_of(at * chunk, chunk), chunk)
            result = dot(hidden[other], down_v[:, cols])
            if k == 0:
                glu_own[:, cols] = result
            else:
                glu_send[k, :, cols] = result.astype(BF)
            return carry

        lax.fori_loop(0, pieces, glu_step, 0)
        if k > 0:
            glus[k] = pltpu.make_async_remote_copy(
                src_ref=glu_send.at[k],
                dst_ref=glu_recv.at[k],
                send_sem=glu_ssem.at[k],
                recv_sem=glu_rsem.at[k],
                device_id={"tp": other},
                device_id_type=MESH,
            )
            glus[k].start()

    quarter = half // (n_seq // 2)
    chip_copies = []
    for which in range(3):
        core_copies[which].wait_recv()
        own = grads[which, pl.ds(pl.multiple_of(core * half, half), half), :]
        halves[which] = (own.astype(F32) + core_recv[which].astype(F32)).astype(BF)
        for k in CHIPS:
            other = flip(me, k)
            copy = pltpu.make_async_remote_copy(
                src_ref=halves.at[which, pl.ds(pl.multiple_of(other // 2 * quarter, 16), quarter), :],
                dst_ref=chip_recv.at[which, k // 2],
                send_sem=chip_ssem.at[which, k // 2],
                recv_sem=chip_rsem.at[which, k // 2],
                device_id={"seq": other},
                device_id_type=MESH,
            )
            copy.start()
            chip_copies.append(copy)

    for k in range(1, n_tp):
        backs[k].wait_recv()
    total = grad_normed[...]
    for k in range(1, n_tp):
        total = total + grad_recv[k].astype(F32)
    value = scaled[...]
    grad_vectors_out[0:1, :] = jnp.sum(total * value, axis=0, keepdims=True)
    grad_vectors_out[1:2, :] = jnp.sum(total, axis=0, keepdims=True)
    total = total * vectors[2:3, :]
    first_mean = jnp.mean(total, axis=-1, keepdims=True)
    second_mean = jnp.mean(total * value, axis=-1, keepdims=True)
    total = cot_v[plane].astype(F32) + inverse[...] * (total - first_mean - value * second_mean)
    grad_resid_out[...] = total
    grad_branch[...] = total.T.astype(BF)

    def keep_right(b, result):
        grad_weights_out[0, pl.ds(b * block, block), :] = result.astype(BF)

    def keep_left(g, result):
        grad_weights_out[1, pl.ds(g * block, block), :] = result.astype(BF)

    def keep_mixed(b, result):
        grad_mixed[pl.ds(b * block, block), :] = result.astype(BF)

    monarch_backward(
        lambda g: grad_branch[pl.ds(g * block, block), :],
        lambda b: mixed[pl.ds(b * block, block), :],
        shuffled, right, left, middle, keep_right, keep_left, keep_mixed,
    )
    mine = pl.ds(pl.multiple_of(me * rows, rows), rows)
    seq_copies = []
    for k in SEQ_ORDER:
        other = flip(me, k)
        copy = pltpu.make_async_remote_copy(
            src_ref=grad_mixed.at[pl.ds(pl.multiple_of(other * chans, 16), chans), :],
            dst_ref=grad_mixed_all.at[:, mine],
            send_sem=seq_send.at[k],
            recv_sem=seq_recv.at[k],
            device_id={"seq": other},
            device_id_type=MESH,
        )
        copy.start()
        seq_copies.append(copy)
    grad_mixed_all[:, mine] = grad_mixed[pl.ds(pl.multiple_of(me * chans, 16), chans), :]

    for k in range(1, n_tp):
        glus[k].wait_recv()
    total = resid[...] + glu_own[...]
    for k in range(1, n_tp):
        total = total + glu_recv[k].astype(F32)
    out_rows[...] = total.astype(BF)
    part = rows // n_tp
    out_copies = []
    for k in range(1, n_tp):
        other = flip(plane, k)
        copy = pltpu.make_async_remote_copy(
            src_ref=out_rows.at[pl.ds(pl.multiple_of(other * part, part), part), :],
            dst_ref=output_v.at[plane],
            send_sem=out_send.at[k],
            recv_sem=out_recv.at[k],
            device_id={"tp": other},
            device_id_type=MESH,
        )
        copy.start()
        out_copies.append(copy)
    output_v[plane] = out_rows[pl.ds(pl.multiple_of(plane * part, part), part), :]

    chip = me // 2
    for which in range(3):
        for at in range(3):
            chip_copies[3 * which + at].wait_recv()
        total = halves[which, pl.ds(pl.multiple_of(chip * quarter, 16), quarter), :].astype(F32)
        for k in CHIPS:
            total = total + chip_recv[which, k // 2].astype(F32)
        shard_out[which] = total.astype(BF)
    for copy in seq_copies:
        copy.wait()
    grad_mixed_out[...] = grad_mixed_all[...]
    for copy in out_copies:
        copy.wait()
    output_out[...] = output_v[...]
    for k in range(1, n_tp):
        gathers[k].wait_send()
        backs[k].wait_send()
        glus[k].wait_send()
    for copy in core_copies + chip_copies:
        copy.wait_send()


def feed(mesh_shape, mixed, tokens, cot_rows, vectors, right, left, gate_w, up_w, down_w):
    n_seq, n_tp = mesh_shape
    _, rows, width = tokens.shape
    chans, length = width // n_seq, rows * n_seq
    part = rows // n_tp
    shape = jax.ShapeDtypeStruct
    dma = pltpu.SemaphoreType.DMA
    return pl.pallas_call(
        functools.partial(feed_kernel, n_seq, n_tp, (width, chans, length, rows)),
        out_shape=(
            shape((chans, length), BF),
            shape((rows, width), F32),
            shape((3, width // n_seq, width), BF),
            shape((2, width, width // 4), BF),
            shape((2, width), F32),
            shape((n_tp, part, width), BF),
        ),
        in_specs=[vmem_spec(), any_spec(), any_spec(), vmem_spec(), vmem_spec(), vmem_spec(), any_spec(), any_spec(), any_spec()],
        out_specs=(vmem_spec(),) * 6,
        scratch_shapes=[
            pltpu.VMEM((rows, width), BF),
            pltpu.VMEM((n_tp, rows, width), BF),
            pltpu.VMEM((width, width), BF),
            pltpu.VMEM((width, width), BF),
            pltpu.VMEM((width, width), BF),
            pltpu.VMEM((width, rows), BF),
            pltpu.VMEM((width, rows), F32),
            pltpu.VMEM((rows, width), F32),
            pltpu.VMEM((rows, width), F32),
            pltpu.VMEM((rows, 1), F32),
            pltpu.VMEM((n_tp, rows, width), BF),
            pltpu.VMEM((n_tp, rows, width), BF),
            pltpu.VMEM((n_tp, rows, width), F32),
            pltpu.VMEM((n_tp, rows, width), BF),
            pltpu.VMEM((n_tp, rows, width), BF),
            pltpu.VMEM((rows, width), F32),
            pltpu.VMEM((n_tp, rows, width), BF),
            pltpu.VMEM((n_tp, rows, width), BF),
            pltpu.VMEM((rows, width), F32),
            pltpu.VMEM((n_tp, rows, width), BF),
            pltpu.VMEM((n_tp, rows, width), BF),
            pltpu.VMEM((width, n_tp * rows), BF),
            pltpu.VMEM((3, width, width), BF),
            pltpu.VMEM((3, width // 2, width), BF),
            pltpu.VMEM((3, width // 2, width), BF),
            pltpu.VMEM((3, n_seq // 2, width // n_seq, width), BF),
            pltpu.VMEM((width, rows), BF),
            pltpu.VMEM((width, rows), BF),
            pltpu.VMEM((width, rows), BF),
            pltpu.VMEM((chans, length), BF),
            pltpu.VMEM((rows, width), BF),
            pltpu.VMEM((n_tp, part, width), BF),
            dma((5,)),
            dma((n_tp,)), dma((n_tp,)), dma((n_tp,)), dma((n_tp,)), dma((n_tp,)), dma((n_tp,)), dma((n_tp,)), dma((n_tp,)),
            dma((3,)), dma((3,)), dma((3, n_seq // 2)), dma((3, n_seq // 2)), dma((n_seq,)), dma((n_seq,)),
        ],
        compiler_params=pltpu.CompilerParams(collective_id=1, has_side_effects=True, vmem_limit_bytes=LIMIT),
        name="feed",
    )(mixed, tokens, cot_rows, vectors, right, left, gate_w, up_w, down_w)


class Reduce:
    def __init__(self, n_seq, n_tp, own, full, core_in, halves, chip_in, quarter, plane_in, send, recv):
        self.own, self.full, self.core_in, self.halves = own, full, core_in, halves
        self.chip_in, self.quarter, self.plane_in = chip_in, quarter, plane_in
        self.send, self.recv, self.n_tp = send, recv, n_tp
        rows, width = own.shape
        self.rows, self.width = rows, width
        self.per_chip, self.per_plane = rows // (n_seq // 2), rows // (n_seq // 2) // n_tp
        self.me, self.plane = lax.axis_index("seq"), lax.axis_index("tp")
        core = lax.rem(self.me, 2)
        self.mine = pl.ds(pl.multiple_of(core * (width // 2), 128), width // 2)
        self.theirs = pl.ds(pl.multiple_of((1 - core) * (width // 2), 128), width // 2)
        self.started = []

    def chip_rows(self, index):
        return pl.ds(pl.multiple_of(index // 2 * self.per_chip, 16), self.per_chip)

    def copy(self, source, target, at, where):
        result = pltpu.make_async_remote_copy(
            src_ref=source, dst_ref=target, send_sem=self.send.at[at], recv_sem=self.recv.at[at],
            device_id=where, device_id_type=MESH,
        )
        result.start()
        self.started.append(result)
        return result

    def start_core(self):
        self.phase = [self.copy(self.own.at[:, self.theirs], self.core_in, 0, {"seq": flip(self.me, 1)})]

    def arrived(self):
        for copy in self.phase:
            copy.wait_recv()
        self.phase = []

    def start_chip(self):
        self.arrived()
        self.halves[...] = (self.own[:, self.mine].astype(F32) + self.core_in[...].astype(F32)).astype(BF)
        for k in CHIPS:
            other = flip(self.me, k)
            self.phase.append(
                self.copy(self.halves.at[self.chip_rows(other), :], self.chip_in.at[k // 2], k // 2, {"seq": other})
            )

    def start_plane(self):
        self.arrived()
        total = self.halves[self.chip_rows(self.me), :].astype(F32)
        for k in CHIPS:
            total = total + self.chip_in[k // 2].astype(F32)
        self.quarter[...] = total.astype(BF)
        for k in range(1, self.n_tp):
            other = flip(self.plane, k)
            here = pl.ds(pl.multiple_of(other * self.per_plane, 16), self.per_plane)
            self.phase.append(self.copy(self.quarter.at[here, :], self.plane_in.at[k], 3 + k, {"tp": other}))

    def start_plane_back(self):
        self.arrived()
        here = pl.ds(pl.multiple_of(self.plane * self.per_plane, 16), self.per_plane)
        total = self.quarter[here, :].astype(F32)
        for k in range(1, self.n_tp):
            total = total + self.plane_in[k].astype(F32)
        rows = pl.ds(
            pl.multiple_of(self.me // 2 * self.per_chip + self.plane * self.per_plane, 16), self.per_plane
        )
        self.full[rows, self.mine] = total.astype(BF)
        spot = self.full.at[rows, self.mine]
        for k in range(1, self.n_tp):
            self.phase.append(self.copy(spot, spot, 6 + k, {"tp": flip(self.plane, k)}))

    def start_chip_back(self):
        self.arrived()
        spot = self.full.at[self.chip_rows(self.me), self.mine]
        for k in CHIPS:
            self.phase.append(self.copy(spot, spot, 9 + k // 2, {"seq": flip(self.me, k)}))

    def start_core_back(self):
        self.arrived()
        spot = self.full.at[:, self.mine]
        self.phase.append(self.copy(spot, spot, 13, {"seq": flip(self.me, 1)}))

    def finish(self):
        self.arrived()
        for copy in self.started:
            copy.wait_send()


def reduce_scratch(n_seq, n_tp, rows, width):
    half, chip, plane = width // 2, rows // (n_seq // 2), rows // (n_seq // 2) // n_tp
    return [
        pltpu.VMEM((rows, width), BF),
        pltpu.VMEM((rows, width), BF),
        pltpu.VMEM((rows, half), BF),
        pltpu.VMEM((rows, half), BF),
        pltpu.VMEM((n_seq // 2, chip, half), BF),
        pltpu.VMEM((chip, half), BF),
        pltpu.VMEM((n_tp, plane, half), BF),
        pltpu.SemaphoreType.DMA((14,)),
        pltpu.SemaphoreType.DMA((14,)),
    ]


def back_kernel(n_seq, n_tp, dims, *refs):
    (grad_mixed, columns, vectors, right, left, first, second, third, nyquist, shard, grad_weights, grad_vectors,
     features, tokens, table, signals_in, conv_in, wave_in, taps_in, acts_in, normed_in, shuffled_in, resid_in) = refs[:23]
    (ffn_out, tokens_out, late_out, early_out, small_out) = refs[23:28]
    (table_v, signals, conv, wave, taps_v, acts, token_v, normed, shuffled, grad_resid, grad_short, query, value_v, grad_conv,
     padded, back_wave, cross, sums, grad_signals, grad_proj, middle, grad_rows, grad_tok, grad_second, grad_first, grad_third,
     local_sems, ffn_ssem, ffn_rsem, seq_send, seq_recv, tp_send, tp_recv) = refs[28:61]
    width, chans, length, rows = dims
    late = Reduce(n_seq, n_tp, *refs[61:70])
    early = Reduce(n_seq, n_tp, *refs[70:79])
    small = Reduce(n_seq, n_tp, *refs[79:88])
    me, plane = lax.axis_index("seq"), lax.axis_index("tp")
    entered = greet(n_seq, n_tp)
    loads = [
        pltpu.make_async_copy(source, target, local_sems.at[at])
        for at, (source, target) in enumerate(
            (
                (signals_in, signals), (conv_in, conv), (table, table_v), (wave_in, wave), (taps_in, taps_v), (acts_in, acts),
                (tokens.at[plane], token_v), (normed_in, normed), (shuffled_in, shuffled), (resid_in, grad_resid),
            )
        )
    ]
    for copy in loads:
        copy.start()
    half, quarter = width // 2, width // n_seq
    own_rows = pl.ds(pl.multiple_of(lax.rem(me, 2) * half + me // 2 * quarter, 16), quarter)
    entered()
    ffn_copies = []
    for which in range(3):
        for k in CHIPS:
            copy = pltpu.make_async_remote_copy(
                src_ref=shard.at[which],
                dst_ref=ffn_out.at[which, own_rows, :],
                send_sem=ffn_ssem.at[which, k // 2],
                recv_sem=ffn_rsem.at[which, k // 2],
                device_id={"seq": flip(me, k)},
                device_id_type=MESH,
            )
            copy.start()
            ffn_copies.append(copy)
    own_shard = pltpu.make_async_copy(shard, ffn_out.at[:, own_rows, :], local_sems.at[10])
    own_shard.start()
    sums[...] = jnp.zeros_like(sums)
    small.own[...] = jnp.zeros_like(small.own)
    early.own[...] = jnp.zeros_like(early.own)
    loads[0].wait()
    loads[1].wait()
    step = 16
    padded[pl.ds(chans, 128 - chans), :] = jnp.zeros((128 - chans, length), BF)

    def short_step(at, carry):
        here = pl.ds(pl.multiple_of(at * step, step), step)
        shorted = []
        for s in range(3):
            value = signals[s, here, :].astype(F32)
            shorted.append(
                previous(value) * columns[here, 3 * s : 3 * s + 1]
                + value * columns[here, 3 * s + 1 : 3 * s + 2]
                + following(value) * columns[here, 3 * s + 2 : 3 * s + 3]
            )
        query[here, :] = shorted[0]
        value_v[here, :] = shorted[2]
        above = grad_mixed[here, :].astype(F32)
        grad_short[1, here, :] = above * conv[here, :]
        above = above * shorted[1]
        grad_conv[here, :] = above
        padded[here, :] = above.astype(BF)
        sums[here, 9:10] = jnp.sum(above * shorted[0] * shorted[2], axis=1, keepdims=True)
        sums[here, 10:11] = jnp.sum(above * sign_lanes(step, length), axis=1, keepdims=True)
        return carry

    lax.fori_loop(0, chans // step, short_step, 0)
    for at in (2, 3, 4):
        loads[at].wait()
    chunk = 256
    per = length // chunk

    def wave_step(at, carry):
        here = pl.ds(pl.multiple_of(at * chunk, chunk), chunk)
        sign = sign_rows(chunk, 128)
        index = lax.broadcasted_iota(jnp.int32, (chunk, 128), 0) + at * chunk
        weight = jnp.where(index == 0, 0.5 / length, 1.0 / length)
        cos_part = dot(table_v[0, here, :], padded[...], NT)
        sin_part = dot(table_v[1, here, :], padded[...], NT)
        tap_cos = taps_v[0, here, :].astype(F32)
        tap_sin = taps_v[1, here, :].astype(F32)
        back_wave[0, here, :] = (cos_part * tap_cos + sin_part * tap_sin).astype(BF)
        back_wave[1, here, :] = (sin_part * tap_cos - cos_part * tap_sin).astype(BF)
        wave_cos = wave[0, here, :].astype(F32) * weight
        wave_sin = wave[1, here, :].astype(F32) * weight
        result = cos_part * wave_cos + sin_part * wave_sin
        cross[0, here, 0:128] = result.astype(BF)
        cross[0, here, 128:256] = (result * sign).astype(BF)
        result = sin_part * wave_cos - cos_part * wave_sin
        cross[1, here, 0:128] = result.astype(BF)
        cross[1, here, 128:256] = (result * sign).astype(BF)
        return carry

    lax.fori_loop(0, per, wave_step, 0)

    def product_step(at, carry):
        here = pl.ds(pl.multiple_of(at * chunk, chunk), chunk)
        result = dot(table_v[0, here, :], back_wave[0]) + dot(table_v[1, here, :], back_wave[1])
        result = (
            result.T[:chans]
            + sign_lanes(chans, chunk) * (sums[:chans, 10:11] * nyquist[:, 1:2] * (0.5 / length))
            + columns[:, 9:10] * grad_conv[:, here]
        )
        grad_short[0, :, here] = result * value_v[:, here]
        grad_short[2, :, here] = result * query[:, here]
        return carry

    lax.fori_loop(0, per, product_step, 0)

    def signal_step(at, carry):
        here = pl.ds(pl.multiple_of(at * step, step), step)
        for s in range(3):
            above = grad_short[s, here, :]
            value = signals[s, here, :].astype(F32)
            before, after = previous(above), following(above)
            grad_signals[s, here, :] = (
                after * columns[here, 3 * s : 3 * s + 1]
                + above * columns[here, 3 * s + 1 : 3 * s + 2]
                + before * columns[here, 3 * s + 2 : 3 * s + 3]
            ).astype(BF)
            sums[here, 3 * s : 3 * s + 1] = jnp.sum(after * value, axis=1, keepdims=True)
            sums[here, 3 * s + 1 : 3 * s + 2] = jnp.sum(above * value, axis=1, keepdims=True)
            sums[here, 3 * s + 2 : 3 * s + 3] = jnp.sum(before * value, axis=1, keepdims=True)
        return carry

    lax.fori_loop(0, chans // step, signal_step, 0)
    mine = pl.ds(pl.multiple_of(me * rows, rows), rows)
    seq_copies = []
    for k in SEQ_ORDER:
        other = flip(me, k)
        for s in range(3):
            copy = pltpu.make_async_remote_copy(
                src_ref=grad_signals.at[s, :, pl.ds(pl.multiple_of(other * rows, rows), rows)],
                dst_ref=grad_proj.at[pl.ds(pl.multiple_of(s * width + me * chans, 16), chans), :],
                send_sem=seq_send.at[k, s],
                recv_sem=seq_recv.at[k, s],
                device_id={"seq": other},
                device_id_type=MESH,
            )
            copy.start()
            seq_copies.append(copy)
    for s in range(3):
        grad_proj[pl.ds(pl.multiple_of(s * width + me * chans, 16), chans), :] = grad_signals[s, :, mine]

    loads[5].wait()
    tap_total = jnp.broadcast_to(sums[:, 10:11], (128, 128)).T[0:1, :]
    pad_nyquist = jnp.concatenate([nyquist[:, 0:1], jnp.zeros((128 - chans, 1), F32)], axis=0)
    tap_total = tap_total * jnp.broadcast_to(pad_nyquist, (128, 128)).T[0:1, :] * (0.5 / length)
    grad_second[...] = jnp.zeros_like(grad_second)
    grad_first[...] = jnp.zeros_like(grad_first)
    grad_third[...] = jnp.zeros_like(grad_third)

    def filter_step(at, carry):
        here = pl.ds(pl.multiple_of(at * chunk, chunk), chunk)
        result = dot(table_v[0, here, :], cross[0]) + dot(table_v[1, here, :], cross[1])
        sign = sign_rows(chunk, 128)
        for part in range(2):
            above = (result[:, part * 128 : (part + 1) * 128] + sign * tap_total) * (length**-0.5)
            if part == 1:
                index = lax.broadcasted_iota(jnp.int32, above.shape, 0) + at * chunk
                above = jnp.where(index == 0, 0.0, above)
            above = above.astype(BF)
            spot = pl.ds(pl.multiple_of(part * length + at * chunk, chunk), chunk)
            grad_third[...] += dot(above, acts[2, spot, :], TN)
            below = (dot(above, third[...], NT) * acts[3, spot, :].astype(F32)).astype(BF)
            grad_second[...] += dot(acts[0, spot, :], below, TN)
            below = (dot(below, second[...], NT) * acts[1, spot, :].astype(F32)).astype(BF)
            grad_first[...] += dot(features[spot, :], below, TN)
        return carry

    lax.fori_loop(0, per, filter_step, 0)
    early.own[:, 0:384] = jnp.concatenate([grad_weights[0], grad_weights[1]], axis=1)
    early.own[pl.ds(pl.multiple_of(me * chans, 16), chans), 384:512] = grad_third[:chans, :].astype(BF)
    small.own[0:128, 0:128] = grad_second[...].astype(BF)
    small.own[128:136, 0:128] = (grad_first[0:8, :] + grad_first[8:16, :]).astype(BF)
    small.own[pl.ds(pl.multiple_of(me * 16, 16), 16), 128:256] = sums[...].T[0:16, :].astype(BF)
    early.start_core()
    for copy in ffn_copies:
        copy.wait_recv()
    own_shard.wait()
    own_half = pl.ds(pl.multiple_of(lax.rem(me, 2) * half, half), half)
    ffn_last = []
    for which in range(3):
        copy = pltpu.make_async_remote_copy(
            src_ref=ffn_out.at[which, own_half, :],
            dst_ref=ffn_out.at[which, own_half, :],
            send_sem=ffn_ssem.at[which, 0],
            recv_sem=ffn_rsem.at[which, 0],
            device_id={"seq": flip(me, 1)},
            device_id_type=MESH,
        )
        copy.start()
        ffn_last.append(copy)
    early.start_chip()

    for at in range(6, 10):
        loads[at].wait()
    value = token_v[...].astype(F32)
    shifted = value - jnp.mean(value, axis=-1, keepdims=True)
    inverse = lax.rsqrt(jnp.mean(shifted * shifted, axis=-1, keepdims=True) + 1e-05)
    scaled = shifted * inverse

    groups = right.shape[0]
    block = width // groups
    fan = left.shape[2]
    for copy in seq_copies:
        copy.wait_recv()

    def keep_left(g, result):
        late.own[pl.ds(g * block, block), 0:512] = result[:, 0:512].astype(BF)
        middle_left[g] = result[:, 512:576].astype(BF)

    def keep_right(b, result):
        late.own[pl.ds(b * block, block), 512:768] = jnp.concatenate([middle_left[b], result.astype(BF)], axis=1)

    def keep_rows(b, result):
        grad_rows[pl.ds(b * block, block), :] = result

    middle_left = {}
    monarch_backward(
        lambda g: grad_proj[pl.ds(g * fan, fan), :],
        lambda b: normed[pl.ds(b * block, block), :],
        shuffled, right, left, middle, keep_right, keep_left, keep_rows,
    )
    late.start_core()
    early.start_plane()
    total = grad_rows[...].T
    norm_grads = [jnp.sum(total * scaled, axis=0, keepdims=True), jnp.sum(total, axis=0, keepdims=True)]
    total = total * vectors[0:1, :]
    first_mean = jnp.mean(total, axis=-1, keepdims=True)
    second_mean = jnp.mean(total * scaled, axis=-1, keepdims=True)
    total = grad_resid[...] + inverse * (total - first_mean - scaled * second_mean)
    grad_tok[...] = total.astype(BF)
    norm_grads += [grad_vectors[0:1, :], grad_vectors[1:2, :]]
    lines = []
    for line in norm_grads:
        for at in range(width // 128):
            lines.append(line[:, at * 128 : (at + 1) * 128])
    small.own[128:160, 128:256] = jnp.concatenate(lines + [jnp.zeros((8, 128), F32)], axis=0).astype(BF)
    small.start_core()
    tok_copies = []
    for k in range(1, n_tp):
        copy = pltpu.make_async_remote_copy(
            src_ref=grad_tok,
            dst_ref=tokens_out.at[plane],
            send_sem=tp_send.at[k],
            recv_sem=tp_recv.at[k],
            device_id={"tp": flip(plane, k)},
            device_id_type=MESH,
        )
        copy.start()
        tok_copies.append(copy)
    own_tok = pltpu.make_async_copy(grad_tok, tokens_out.at[plane], local_sems.at[11])
    own_tok.start()
    late.start_chip()
    small.start_chip()
    early.start_plane_back()
    late.start_plane()
    small.start_plane()
    early.start_chip_back()
    late.start_plane_back()
    small.start_plane_back()
    early.start_core_back()
    late.start_chip_back()
    small.start_chip_back()
    late.start_core_back()
    small.start_core_back()
    early.finish()
    early_out[...] = early.full[...]
    small.finish()
    small_out[...] = small.full[...]
    late.finish()
    late_out[...] = late.full[...]
    for copy in ffn_copies + seq_copies:
        copy.wait_send()
    for copy in ffn_last + tok_copies:
        copy.wait()
    own_tok.wait()


def back(mesh_shape, *operands):
    n_seq, n_tp = mesh_shape
    tokens = operands[13]
    _, rows, width = tokens.shape
    chans, length = width // n_seq, rows * n_seq
    shape = jax.ShapeDtypeStruct
    dma = pltpu.SemaphoreType.DMA
    return pl.pallas_call(
        functools.partial(back_kernel, n_seq, n_tp, (width, chans, length, rows)),
        out_shape=(
            shape((3, width, width), BF),
            shape((n_tp, rows, width), BF),
            shape((width, width), BF),
            shape((width, 512), BF),
            shape((256, 256), BF),
        ),
        in_specs=[vmem_spec()] * 13 + [any_spec()] * 10,
        out_specs=(any_spec(), any_spec(), vmem_spec(), vmem_spec(), vmem_spec()),
        scratch_shapes=[
            pltpu.VMEM((2, length, length), BF),
            pltpu.VMEM((3, chans, length), BF),
            pltpu.VMEM((chans, length), F32),
            pltpu.VMEM((2, length, 128), BF),
            pltpu.VMEM((2, length, 128), BF),
            pltpu.VMEM((4, 2 * length, 128), BF),
            pltpu.VMEM((rows, width), BF),
            pltpu.VMEM((width, rows), BF),
            pltpu.VMEM((width, rows), BF),
            pltpu.VMEM((rows, width), F32),
            pltpu.VMEM((3, chans, length), F32),
            pltpu.VMEM((chans, length), F32),
            pltpu.VMEM((chans, length), F32),
            pltpu.VMEM((chans, length), F32),
            pltpu.VMEM((128, length), BF),
            pltpu.VMEM((2, length, 128), BF),
            pltpu.VMEM((2, length, 256), BF),
            pltpu.VMEM((128, 128), F32),
            pltpu.VMEM((3, chans, length), BF),
            pltpu.VMEM((3 * width, rows), BF),
            pltpu.VMEM((width, rows), BF),
            pltpu.VMEM((width, rows), F32),
            pltpu.VMEM((rows, width), BF),
            pltpu.VMEM((128, 128), F32),
            pltpu.VMEM((16, 128), F32),
            pltpu.VMEM((128, 128), F32),
            dma((12,)),
            dma((3, n_seq // 2)), dma((3, n_seq // 2)), dma((n_seq, 3)), dma((n_seq, 3)), dma((n_tp,)), dma((n_tp,)),
        ]
        + reduce_scratch(n_seq, n_tp, width, width)
        + reduce_scratch(n_seq, n_tp, width, 512)
        + reduce_scratch(n_seq, n_tp, 256, 256),
        compiler_params=pltpu.CompilerParams(collective_id=2, has_side_effects=True, vmem_limit_bytes=LIMIT),
        name="back",
    )(*operands)


def fast_body(
    tokens,
    norm_gain,
    norm_bias,
    in_right,
    in_left,
    short_kernel,
    filter_first,
    filter_second,
    filter_third,
    conv_bias,
    out_right,
    out_left,
    ffn_gain,
    ffn_bias,
    gate_weight,
    up_weight,
    down_weight,
    cotangent,
):
    n_seq, n_tp = lax.axis_size("seq"), lax.axis_size("tp")
    _, rows, width = tokens.shape
    chans, length = width // n_seq, rows * n_seq
    shape = (n_seq, n_tp)
    table, features = (jnp.asarray(array) for array in constants(length))
    vectors, columns, first, third = prepare(
        tokens, norm_gain, norm_bias, ffn_gain, ffn_bias, short_kernel, filter_first, filter_third, conv_bias
    )
    mixed, signals, conv, wave, taps, nyquist, acts, normed, shuffled, cot_rows = front(
        shape, tokens, cotangent, table, vectors, in_right, in_left, columns, features, first, filter_second, third
    )
    grad_mixed, grad_resid, shard, grad_weights, grad_vectors, output = feed(
        shape, mixed, tokens, cot_rows, vectors, out_right, out_left, gate_weight, up_weight, down_weight
    )
    ffn, grad_tokens, late, early, small = back(
        shape, grad_mixed, columns, vectors, in_right, in_left, first, filter_second, third, nyquist, shard, grad_weights,
        grad_vectors, features, tokens, table, signals, conv, wave, taps, acts, normed, shuffled, grad_resid,
    )
    ffn, late, early, small = (array.astype(F32) for array in (ffn, late, early, small))
    channel = small[:128, 128:].reshape(n_seq, 16, 128)[:, :10, :chans]
    lines = small[128:152, 128:].reshape(4, width)
    return (
        output,
        grad_tokens.astype(F32),
        lines[0],
        lines[1],
        late[:, 576:].reshape(in_right.shape),
        late[:, :576].reshape(in_left.shape),
        channel[:, :9].reshape(n_seq, 3, 3, chans).transpose(1, 0, 3, 2).reshape(3, width, 3),
        small[128:133, :128],
        small[:128, :128],
        early[:, 384:].T,
        channel[:, 9].reshape(width),
        early[:, :192].reshape(out_right.shape),
        early[:, 192:384].reshape(out_left.shape),
        lines[2],
        lines[3],
        ffn[0],
        ffn[1],
        ffn[2],
    )


highest = lax.Precision.HIGHEST


def norm_forward(values, gain, bias):
    centre = jnp.mean(values, axis=-1, keepdims=True)
    shifted = values - centre
    inverse = lax.rsqrt(jnp.mean(shifted * shifted, axis=-1, keepdims=True) + 1e-05)
    scaled = shifted * inverse
    return (scaled * gain + bias, scaled, inverse)


def norm_backward(upstream, scaled, inverse, gain):
    weighted = upstream * gain
    first_mean = jnp.mean(weighted, axis=-1, keepdims=True)
    second_mean = jnp.mean(weighted * scaled, axis=-1, keepdims=True)
    grad_input = inverse * (weighted - first_mean - scaled * second_mean)
    breadth = upstream.shape[-1]
    grad_gain = jnp.sum((upstream * scaled).reshape(-1, breadth), axis=0)
    grad_bias = jnp.sum(upstream.reshape(-1, breadth), axis=0)
    return (grad_input, grad_gain, grad_bias)


def shuffle(blocked):
    row_count, groups, breadth = blocked.shape
    return (
        blocked.reshape(row_count, groups, groups, breadth // groups)
        .transpose(0, 2, 1, 3)
        .reshape(row_count, groups, breadth)
    )


def rows_monarch_forward(operand, right_factor, left_factor):
    row_count = operand.shape[0]
    groups = right_factor.shape[0]
    blocked = operand.reshape(row_count, groups, -1)
    middle = jnp.einsum(
        "tbi,bij->tbj", blocked, right_factor, preferred_element_type=jnp.float32
    ).astype(jnp.bfloat16)
    shuffled = shuffle(middle)
    result = jnp.einsum("tbi,bij->tbj", shuffled, left_factor, preferred_element_type=jnp.float32)
    return (shuffled, result.reshape(row_count, -1))


def rows_monarch_backward(grad_result, operand, shuffled, right_factor, left_factor):
    row_count = operand.shape[0]
    groups = right_factor.shape[0]
    grad_blocked = grad_result.reshape(row_count, groups, -1)
    grad_left = jnp.einsum(
        "tbi,tbj->bij", shuffled, grad_blocked, preferred_element_type=jnp.float32
    )
    grad_shuffled = jnp.einsum(
        "tbj,bij->tbi", grad_blocked, left_factor, preferred_element_type=jnp.float32
    )
    grad_middle = shuffle(grad_shuffled).astype(jnp.bfloat16)
    blocked = operand.reshape(row_count, groups, -1)
    grad_right = jnp.einsum(
        "tbi,tbj->bij", blocked, grad_middle, preferred_element_type=jnp.float32
    )
    grad_operand = jnp.einsum(
        "tbj,bij->tbi", grad_middle, right_factor, preferred_element_type=jnp.float32
    )
    return (grad_operand.reshape(row_count, -1), grad_right, grad_left)


def roots(row_count, col_count, period):
    product = jnp.arange(row_count)[:, None] * jnp.arange(col_count)[None, :] % period
    angle = product.astype(jnp.float32) * (2.0 * math.pi / period)
    return (jnp.cos(angle), jnp.sin(angle))


def complex_step(real_part, imag_part, cos_table, sin_table, sign, form):
    real_out = jnp.einsum(form, real_part, cos_table, precision=highest) - sign * jnp.einsum(
        form, imag_part, sin_table, precision=highest
    )
    imag_out = jnp.einsum(form, imag_part, cos_table, precision=highest) + sign * jnp.einsum(
        form, real_part, sin_table, precision=highest
    )
    return (real_out, imag_out)


def real_step(real_part, cos_table, sin_table, sign, form):
    real_out = jnp.einsum(form, real_part, cos_table, precision=highest)
    imag_out = sign * jnp.einsum(form, real_part, sin_table, precision=highest)
    return (real_out, imag_out)


def twiddle(real_part, imag_part, cos_table, sin_table, sign):
    real_out = real_part * cos_table - sign * imag_part * sin_table
    imag_out = imag_part * cos_table + sign * real_part * sin_table
    return (real_out, imag_out)


def spectrum_of(real_part):
    total = real_part.shape[-1]
    first = math.gcd(total, 128)
    second = total // first
    leading = real_part.shape[:-1]
    real_part = real_part.reshape(leading + (first, second))
    cos_first, sin_first = roots(first, first, first)
    real_part, imag_part = real_step(real_part, cos_first, sin_first, -1.0, "...ab,ak->...kb")
    cos_twist, sin_twist = roots(first, second, total)
    real_part, imag_part = twiddle(real_part, imag_part, cos_twist, sin_twist, -1.0)
    cos_second, sin_second = roots(second, second, second)
    return complex_step(real_part, imag_part, cos_second, sin_second, -1.0, "...kb,bm->...km")


def signal_of(real_part, imag_part):
    first = real_part.shape[-2]
    second = real_part.shape[-1]
    total = first * second
    leading = real_part.shape[:-2]
    cos_second, sin_second = roots(second, second, second)
    real_part, imag_part = complex_step(
        real_part, imag_part, cos_second, sin_second, 1.0, "...kb,bm->...km"
    )
    cos_twist, sin_twist = roots(first, second, total)
    real_part, imag_part = twiddle(real_part, imag_part, cos_twist, sin_twist, 1.0)
    cos_first, sin_first = roots(first, first, first)
    real_part, imag_part = complex_step(
        real_part, imag_part, cos_first, sin_first, 1.0, "...ab,ak->...kb"
    )
    return real_part.reshape(leading + (total,)) / total


def filter_parts(filter_first, filter_second, third_cols, seq_length):
    total = 2 * seq_length
    index = jnp.arange(total)
    offset = jnp.where(index < seq_length, index, index - total).astype(jnp.float32)
    scaled = offset / seq_length
    features = jnp.stack(
        [
            scaled,
            jnp.sin(math.pi * scaled),
            jnp.cos(math.pi * scaled),
            jnp.sin(7.0 * math.pi * scaled),
            jnp.cos(7.0 * math.pi * scaled),
        ],
        axis=1,
    )
    pre_one = jnp.dot(features, filter_first, precision=highest)
    act_one = jnp.sin(pre_one)
    pre_two = jnp.dot(act_one, filter_second, precision=highest)
    act_two = jnp.sin(pre_two)
    tap_mask = (index != seq_length).astype(jnp.float32)[:, None] * seq_length ** (-0.5)
    taps = jnp.dot(act_two, third_cols, precision=highest) * tap_mask
    filt_real, filt_imag = spectrum_of(taps.T)
    return (features, pre_one, act_one, pre_two, act_two, tap_mask, filt_real, filt_imag)


def general_body(
    tokens,
    norm_gain,
    norm_bias,
    in_right,
    in_left,
    short_kernel,
    filter_first,
    filter_second,
    filter_third,
    conv_bias,
    out_right,
    out_left,
    ffn_gain,
    ffn_bias,
    gate_weight,
    up_weight,
    down_weight,
    cotangent,
):
    seq_count, pos_count, model_width = tokens.shape
    row_count = seq_count * pos_count
    axis_count = lax.axis_size("seq")
    my_index = lax.axis_index("seq")
    chan_count = model_width // axis_count
    seq_length = pos_count * axis_count
    part_rows = cotangent.shape[1]
    tp_index = lax.axis_index("tp")
    tp_count = lax.axis_size("tp")
    chan_start = my_index * chan_count
    mix_count = seq_count // tp_count
    mix_tokens = lax.dynamic_slice_in_dim(tokens, tp_index * mix_count, mix_count, 0)
    mix_rows = mix_count * pos_count
    flat = mix_tokens.reshape(mix_rows, model_width).astype(jnp.float32)
    normed, scaled_one, inverse_one = norm_forward(flat, norm_gain, norm_bias)
    normed_low = normed.astype(jnp.bfloat16)
    shuffled_in, projected = rows_monarch_forward(normed_low, in_right, in_left)
    projected_low = (
        projected.astype(jnp.bfloat16)
        .reshape(mix_count, pos_count, 3, model_width)
        .transpose(2, 3, 0, 1)
    )
    channels = lax.all_to_all(projected_low, "seq", split_axis=1, concat_axis=3, tiled=True)
    signals = channels.astype(jnp.float32)
    kernel = lax.dynamic_slice_in_dim(short_kernel, chan_start, chan_count, 1).astype(jnp.float32)
    tap_zero = kernel[:, :, 0][:, :, None, None]
    tap_one = kernel[:, :, 1][:, :, None, None]
    tap_two = kernel[:, :, 2][:, :, None, None]
    padded = jnp.pad(signals, ((0, 0), (0, 0), (0, 0), (1, 1)))
    shorted = padded[..., :-2] * tap_zero + padded[..., 1:-1] * tap_one + padded[..., 2:] * tap_two
    first_f = filter_first.astype(jnp.float32)
    second_f = filter_second.astype(jnp.float32)
    third_cols = lax.dynamic_slice_in_dim(filter_third, chan_start, chan_count, 1).astype(
        jnp.float32
    )
    kept = filter_parts(first_f, second_f, third_cols, seq_length)
    filt_real = kept[6][:, None]
    filt_imag = kept[7][:, None]
    bias_cols = lax.dynamic_slice_in_dim(conv_bias, chan_start, chan_count, 0)[:, None, None]
    product = shorted[0] * shorted[2]
    product_pad = jnp.pad(product, ((0, 0), (0, 0), (0, seq_length)))
    spec_real, spec_imag = spectrum_of(product_pad)
    conv_real = spec_real * filt_real - spec_imag * filt_imag
    conv_imag = spec_real * filt_imag + spec_imag * filt_real
    convolved = signal_of(conv_real, conv_imag)[..., :seq_length] + bias_cols * product
    mixed_low = (shorted[1] * convolved).astype(jnp.bfloat16)
    back_rows = lax.all_to_all(mixed_low, "seq", split_axis=2, concat_axis=0, tiled=True)
    mixed_rows = back_rows.transpose(1, 2, 0).reshape(mix_rows, model_width)
    shuffled_out, branch = rows_monarch_forward(mixed_rows, out_right, out_left)
    residual_mine = (flat + branch).reshape(mix_count, pos_count, model_width)
    residual = lax.all_gather(residual_mine, "tp", axis=0, tiled=True)
    part_resid = lax.dynamic_slice_in_dim(residual, tp_index * part_rows, part_rows, 1)
    normed_two, scaled_two, inverse_two = norm_forward(part_resid, ffn_gain, ffn_bias)
    normed_rows = lax.all_gather(normed_two.astype(jnp.bfloat16), "tp", axis=1, tiled=True).reshape(
        row_count, model_width
    )
    gate = jnp.dot(normed_rows, gate_weight, preferred_element_type=jnp.float32)
    upward = jnp.dot(normed_rows, up_weight, preferred_element_type=jnp.float32)
    sigma = jax.nn.sigmoid(gate)
    hidden_low = (gate * sigma * upward).astype(jnp.bfloat16)
    partial_down = jnp.dot(hidden_low, down_weight, preferred_element_type=jnp.float32).reshape(
        seq_count, pos_count, model_width
    )
    glu_part = lax.psum_scatter(
        partial_down.astype(jnp.bfloat16), "tp", scatter_dimension=1, tiled=True
    ).astype(jnp.float32)
    output = (part_resid + glu_part).astype(jnp.bfloat16)
    grad_out_rows = lax.all_gather(cotangent, "tp", axis=1, tiled=True).reshape(
        row_count, model_width
    )
    grad_hidden = jnp.dot(grad_out_rows, down_weight.T, preferred_element_type=jnp.float32)
    grad_gate = (grad_hidden * upward * (sigma + gate * sigma * (1.0 - sigma))).astype(jnp.bfloat16)
    grad_up = (grad_hidden * gate * sigma).astype(jnp.bfloat16)
    grad_down_w = jnp.dot(hidden_low.T, grad_out_rows, preferred_element_type=jnp.float32)
    grad_gate_w = jnp.dot(normed_rows.T, grad_gate, preferred_element_type=jnp.float32)
    grad_up_w = jnp.dot(normed_rows.T, grad_up, preferred_element_type=jnp.float32)
    grad_normed = jnp.dot(grad_gate, gate_weight.T, preferred_element_type=jnp.float32) + jnp.dot(
        grad_up, up_weight.T, preferred_element_type=jnp.float32
    )
    grad_normed_part = lax.psum_scatter(
        grad_normed.reshape(seq_count, pos_count, model_width),
        "tp",
        scatter_dimension=1,
        tiled=True,
    )
    grad_in_two, grad_gain_two, grad_bias_two = norm_backward(
        grad_normed_part, scaled_two, inverse_two, ffn_gain
    )
    gain_total = lax.psum((grad_gain_two, grad_bias_two), ("seq", "tp"))
    grad_resid_part = cotangent.astype(jnp.float32) + grad_in_two
    grad_resid = lax.all_gather(
        grad_resid_part.astype(jnp.bfloat16), "tp", axis=1, tiled=True
    ).astype(grad_resid_part.dtype)
    grad_resid_mix = lax.dynamic_slice_in_dim(
        grad_resid, tp_index * mix_count, mix_count, 0
    ).reshape(mix_rows, model_width)
    grad_mixed_rows, grad_out_right, grad_out_left = rows_monarch_backward(
        grad_resid_mix.astype(jnp.bfloat16), mixed_rows, shuffled_out, out_right, out_left
    )
    grad_mixed_low = (
        grad_mixed_rows.astype(jnp.bfloat16)
        .reshape(mix_count, pos_count, model_width)
        .transpose(2, 0, 1)
    )
    grad_mixed = lax.all_to_all(
        grad_mixed_low, "seq", split_axis=0, concat_axis=2, tiled=True
    ).astype(jnp.float32)
    grad_conv = grad_mixed * shorted[1]
    grad_key = grad_mixed * convolved
    again = lax.optimization_barrier((first_f, second_f, third_cols))
    kept = filter_parts(again[0], again[1], again[2], seq_length)
    filt_real = kept[6][:, None]
    filt_imag = kept[7][:, None]
    features, pre_one, act_one, pre_two, act_two, tap_mask = (
        kept[0],
        kept[1],
        kept[2],
        kept[3],
        kept[4],
        kept[5],
    )
    grad_pad = jnp.pad(grad_conv, ((0, 0), (0, 0), (0, seq_length)))
    grad_spec_real, grad_spec_imag = spectrum_of(grad_pad)
    back_real = grad_spec_real * filt_real + grad_spec_imag * filt_imag
    back_imag = grad_spec_imag * filt_real - grad_spec_real * filt_imag
    grad_product = signal_of(back_real, back_imag)[..., :seq_length] + bias_cols * grad_conv
    grad_bias_cols = jnp.sum(grad_conv * product, axis=(1, 2))
    taps_real = jnp.sum(grad_spec_real * spec_real + grad_spec_imag * spec_imag, axis=1)
    taps_imag = jnp.sum(grad_spec_imag * spec_real - grad_spec_real * spec_imag, axis=1)
    grad_taps = signal_of(taps_real, taps_imag)
    grad_pre = grad_taps.T * tap_mask
    grad_third_cols = jnp.dot(act_two.T, grad_pre, precision=highest)
    grad_pre_two = jnp.dot(grad_pre, third_cols.T, precision=highest) * jnp.cos(pre_two)
    grad_second = jnp.dot(act_one.T, grad_pre_two, precision=highest)
    grad_pre_one = jnp.dot(grad_pre_two, second_f.T, precision=highest) * jnp.cos(pre_one)
    grad_first = jnp.dot(features.T, grad_pre_one, precision=highest)
    grad_shorted = jnp.stack([grad_product * shorted[2], grad_key, grad_product * shorted[0]])
    grad_short_pad = jnp.pad(grad_shorted, ((0, 0), (0, 0), (0, 0), (1, 1)))
    grad_signals = (
        grad_short_pad[..., 2:] * tap_zero
        + grad_short_pad[..., 1:-1] * tap_one
        + grad_short_pad[..., :-2] * tap_two
    )
    grad_kernel = jnp.stack(
        [
            jnp.sum(grad_shorted * padded[..., :-2], axis=(2, 3)),
            jnp.sum(grad_shorted * padded[..., 1:-1], axis=(2, 3)),
            jnp.sum(grad_shorted * padded[..., 2:], axis=(2, 3)),
        ],
        axis=-1,
    )
    grad_proj = lax.all_to_all(
        grad_signals.astype(jnp.bfloat16), "seq", split_axis=3, concat_axis=1, tiled=True
    )
    grad_proj_rows = grad_proj.transpose(2, 3, 0, 1).reshape(mix_rows, 3 * model_width)
    grad_normed_one, grad_in_right, grad_in_left = rows_monarch_backward(
        grad_proj_rows, normed_low, shuffled_in, in_right, in_left
    )
    grad_in_one, grad_gain_one, grad_bias_one = norm_backward(
        grad_normed_one, scaled_one, inverse_one, norm_gain
    )
    grad_mine = (grad_resid_mix + grad_in_one).reshape(mix_count, pos_count, model_width)
    short_full = lax.dynamic_update_slice_in_dim(
        jnp.zeros(short_kernel.shape, jnp.float32), grad_kernel, chan_start, 1
    )
    third_full = lax.dynamic_update_slice_in_dim(
        jnp.zeros(filter_third.shape, jnp.float32), grad_third_cols, chan_start, 1
    )
    bias_full = lax.dynamic_update_slice_in_dim(
        jnp.zeros(conv_bias.shape, jnp.float32), grad_bias_cols, chan_start, 0
    )
    mixer_grads = (
        grad_gain_one,
        grad_bias_one,
        grad_in_right,
        grad_in_left,
        short_full,
        grad_first,
        grad_second,
        third_full,
        bias_full,
        grad_out_right,
        grad_out_left,
    )
    grad_tokens = lax.all_gather(grad_mine.astype(jnp.bfloat16), "tp", axis=0, tiled=True).astype(
        grad_mine.dtype
    )
    mixer_grads = (
        lax.psum(mixer_grads[0].astype(jnp.bfloat16), "tp").astype(jnp.float32),
        lax.psum(mixer_grads[1].astype(jnp.bfloat16), "tp").astype(jnp.float32),
        lax.psum(mixer_grads[2].astype(jnp.bfloat16), "tp").astype(jnp.float32),
        lax.psum(mixer_grads[3].astype(jnp.bfloat16), "tp").astype(jnp.float32),
        lax.psum(mixer_grads[4].astype(jnp.bfloat16), "tp").astype(jnp.float32),
        lax.psum(mixer_grads[5].astype(jnp.bfloat16), "tp").astype(jnp.float32),
        lax.psum(mixer_grads[6].astype(jnp.bfloat16), "tp").astype(jnp.float32),
        lax.psum(mixer_grads[7].astype(jnp.bfloat16), "tp").astype(jnp.float32),
        lax.psum(mixer_grads[8].astype(jnp.bfloat16), "tp").astype(jnp.float32),
        lax.psum(mixer_grads[9].astype(jnp.bfloat16), "tp").astype(jnp.float32),
        lax.psum(mixer_grads[10].astype(jnp.bfloat16), "tp").astype(jnp.float32),
    )
    all_total = lax.psum(
        (
            mixer_grads[0],
            mixer_grads[1],
            mixer_grads[2],
            mixer_grads[3],
            mixer_grads[4],
            mixer_grads[5],
            mixer_grads[6],
            mixer_grads[7],
            mixer_grads[8],
            mixer_grads[9],
            mixer_grads[10],
            grad_gate_w,
            grad_up_w,
            grad_down_w,
        ),
        "seq",
    )
    return (
        output,
        grad_tokens,
        all_total[0],
        all_total[1],
        all_total[2],
        all_total[3],
        all_total[4],
        all_total[5],
        all_total[6],
        all_total[7],
        all_total[8],
        all_total[9],
        all_total[10],
        gain_total[0],
        gain_total[1],
        all_total[11],
        all_total[12],
        all_total[13],
    )


def choose_body(mesh, *arrays):
    tokens = arrays[0]
    chans = tokens.shape[2] // mesh.shape["seq"]
    fits = mesh.shape["seq"] == 8 and mesh.shape["tp"] == 4 and tokens.shape[:2] == (4, 128) and chans == 96
    return (fast_body if fits else general_body)(*arrays)


def solution(mesh):
    return jax.shard_map(
        functools.partial(choose_body, mesh),
        mesh=mesh,
        in_specs=(
            P(None, "seq", None),
            P(),
            P(),
            P(),
            P(),
            P(),
            P(),
            P(),
            P(),
            P(),
            P(),
            P(),
            P(),
            P(),
            P(None, "tp"),
            P(None, "tp"),
            P("tp", None),
            P(None, ("seq", "tp"), None),
        ),
        out_specs=(
            P(None, ("seq", "tp"), None),
            P(None, "seq", None),
            P(),
            P(),
            P(),
            P(),
            P(),
            P(),
            P(),
            P(),
            P(),
            P(),
            P(),
            P(),
            P(),
            P(None, "tp"),
            P(None, "tp"),
            P("tp", None),
        ),
        check_vma=False,
    )
```

```python
import functools
import math

import numpy as np
import jax
import jax.numpy as jnp
from jax import lax
from jax.experimental import pallas as pl
from jax.experimental.pallas import tpu as pltpu
from jax.sharding import PartitionSpec as P

BF = jnp.bfloat16
F32 = jnp.float32
MESH = pl.DeviceIdType.MESH
NN = ((1,), (0,))
NT = ((1,), (1,))
TN = ((0,), (0,))
LIMIT = 56 * 1024 * 1024


def dot(first, second, form=NN):
    return lax.dot_general(first, second, (form, ((), ())), preferred_element_type=F32)


def any_spec():
    return pl.BlockSpec(memory_space=pl.ANY)


def vmem_spec():
    return pl.BlockSpec(memory_space=pltpu.VMEM)


def sin_cos(value):
    turns = jnp.floor(value * (1.0 / math.pi) + 0.5)
    rest = value - turns * 3.140625
    rest = rest - turns * 9.67502593994140625e-4
    rest = rest - turns * 1.509957990978376432e-7
    half = turns * 0.5
    sign = 1.0 - 4.0 * (half - jnp.floor(half))
    square = rest * rest
    sine = 1.0 / 362880 - square * (1.0 / 39916800)
    sine = -1.0 / 5040 + square * sine
    sine = 1.0 / 120 + square * sine
    sine = -1.0 / 6 + square * sine
    sine = rest + rest * square * sine
    cosine = 1.0 / 40320 - square * (1.0 / 3628800 - square * (1.0 / 479001600))
    cosine = -1.0 / 720 + square * cosine
    cosine = 1.0 / 24 + square * cosine
    cosine = -0.5 + square * cosine
    cosine = 1.0 + square * cosine
    return sign * sine, sign * cosine


def flip(index, bits):
    result = 0
    for place in range(3):
        digit = lax.rem(index // (1 << place), 2)
        if (bits >> place) & 1:
            digit = 1 - digit
        result = result + digit * (1 << place)
    return result


def greet(n_seq, n_tp):
    me, plane = lax.axis_index("seq"), lax.axis_index("tp")
    barrier = pltpu.get_barrier_semaphore()
    for k in range(1, n_seq):
        pl.semaphore_signal(barrier, inc=1, device_id={"seq": flip(me, k)}, device_id_type=MESH)
    for k in range(1, n_tp):
        pl.semaphore_signal(barrier, inc=1, device_id={"tp": flip(plane, k)}, device_id_type=MESH)
    return lambda: pl.semaphore_wait(barrier, n_seq + n_tp - 2)


def sign_rows(count, width):
    row = lax.broadcasted_iota(jnp.int32, (count, width), 0)
    return (1 - 2 * lax.rem(row, 2)).astype(F32)


def sign_lanes(count, width):
    lane = lax.broadcasted_iota(jnp.int32, (count, width), 1)
    return (1 - 2 * lax.rem(lane, 2)).astype(F32)


def previous(values):
    lane = lax.broadcasted_iota(jnp.int32, values.shape, 1)
    return jnp.where(lane == 0, 0.0, pltpu.roll(values, 1, 1))


def following(values):
    last = values.shape[1] - 1
    lane = lax.broadcasted_iota(jnp.int32, values.shape, 1)
    return jnp.where(lane == last, 0.0, pltpu.roll(values, last, 1))


def monarch_forward(load, right, left, shuffled, store):
    groups, width, _ = right.shape
    part = width // groups
    for b in range(groups):
        middle = dot(right[b], load(b), TN).astype(BF)
        for g in range(groups):
            shuffled[pl.ds(g * width + b * part, part), :] = middle[g * part : (g + 1) * part]
    for g in range(groups):
        store(g, dot(left[g], shuffled[pl.ds(g * width, width), :], TN))


SEQ_ORDER = (6, 7, 2, 3, 4, 5, 1)


def front_kernel(n_seq, n_tp, dims, *refs):
    (tokens, cotangent, table, gain, bias, right, left, short, conv_bias, features, first, second, third) = refs[:13]
    (mixed_out, signals_out, conv_out, wave_out, taps_out, nyquist_out, acts_out, normed_out, shuffled_out, cot_out,
     columns_out, third_out) = refs[13:25]
    (token_v, table_v, normed, shuffled, projected, signals, acts, spread, taps_v, padded, product, keyed, wave, spectrum, conv,
     mixed, mixed_rows, nyquist, totals, columns, tall, turned, third_v,
     local_sems, seq_send, seq_recv, back_send, back_recv, tp_send, tp_recv) = refs[25:]
    width, chans, length, rows = dims
    me, plane = lax.axis_index("seq"), lax.axis_index("tp")
    entered = greet(n_seq, n_tp)
    token_load = pltpu.make_async_copy(tokens.at[plane], token_v, local_sems.at[0])
    token_load.start()
    table_load = pltpu.make_async_copy(table, table_v, local_sems.at[1])
    table_load.start()
    token_load.wait()
    value = token_v[...].astype(F32)
    shifted = value - jnp.mean(value, axis=-1, keepdims=True)
    inverse = lax.rsqrt(jnp.mean(shifted * shifted, axis=-1, keepdims=True) + 1e-05)
    value = shifted * inverse * gain[...].reshape(1, width) + bias[...].reshape(1, width)
    normed[...] = value.T.astype(BF)
    groups = right.shape[0]
    block = width // groups
    fan = left.shape[2]

    def keep(g, result):
        projected[pl.ds(g * fan, fan), :] = result.astype(BF)

    monarch_forward(lambda b: normed[pl.ds(b * block, block), :], right, left, shuffled, keep)
    entered()
    sends = []
    mine = pl.ds(pl.multiple_of(me * rows, rows), rows)
    for k in SEQ_ORDER:
        other = flip(me, k)
        for s in range(3):
            copy = pltpu.make_async_remote_copy(
                src_ref=projected.at[pl.ds(pl.multiple_of(s * width + other * chans, 16), chans), :],
                dst_ref=signals.at[s, :, mine],
                send_sem=seq_send.at[k, s],
                recv_sem=seq_recv.at[k, s],
                device_id={"seq": other},
                device_id_type=MESH,
            )
            copy.start()
            sends.append(copy)
    for s in range(3):
        signals[s, :, mine] = projected[pl.ds(pl.multiple_of(s * width + me * chans, 16), chans), :]
    part = rows // n_tp
    spot = pl.ds(pl.multiple_of(plane * part, part), part)
    cot_copies = []
    for k in range(1, n_tp):
        copy = pltpu.make_async_remote_copy(
            src_ref=cotangent,
            dst_ref=cot_out.at[:, spot, :],
            send_sem=tp_send.at[k],
            recv_sem=tp_recv.at[k],
            device_id={"tp": flip(plane, k)},
            device_id_type=MESH,
        )
        copy.start()
        cot_copies.append(copy)
    own_cot = pltpu.make_async_copy(cotangent, cot_out.at[:, spot, :], local_sems.at[2])
    own_cot.start()
    out_copies = [
        pltpu.make_async_copy(normed, normed_out, local_sems.at[3]),
        pltpu.make_async_copy(shuffled, shuffled_out, local_sems.at[4]),
    ]
    for copy in out_copies:
        copy.start()

    own = pl.ds(pl.multiple_of(me * chans, 16), chans)
    lines = [short[s].astype(F32) for s in range(3)]
    lines += [conv_bias[...].reshape(1, width), jnp.zeros((6, width), F32)]
    tall[...] = jnp.concatenate(lines, axis=0).T
    columns[...] = tall[own, :]
    columns_out[...] = columns[...]
    turned[...] = third[...].T
    third_v[pl.ds(0, chans), :] = turned[own, :]
    third_v[pl.ds(chans, 128 - chans), :] = jnp.zeros((128 - chans, 128), BF)
    third_out[...] = third_v[...]
    lead = jnp.concatenate([first[...].astype(F32), jnp.zeros((3, 128), F32)], axis=0)
    lead = jnp.concatenate([lead, lead], axis=0).astype(BF)

    chunk = 256
    per = length // chunk
    totals[...] = jnp.zeros_like(totals)
    for half in range(2):

        def tap_step(at, carry, half=half):
            row = pl.multiple_of(half * length + at * chunk, chunk)
            here = pl.ds(row, chunk)
            sine, cosine = sin_cos(dot(features[here, :], lead))
            high = sine.astype(BF)
            acts[0, here, :] = high
            acts[1, here, :] = cosine.astype(BF)
            low = (sine - high.astype(F32)).astype(BF)
            sine, cosine = sin_cos(dot(high, second[...]) + dot(low, second[...]))
            high = sine.astype(BF)
            acts[2, here, :] = high
            acts[3, here, :] = cosine.astype(BF)
            taps = dot(high, third_v[...], NT) * (length**-0.5)
            if half == 1:
                index = lax.broadcasted_iota(jnp.int32, taps.shape, 0) + at * chunk
                taps = jnp.where(index == 0, 0.0, taps)
            totals[...] += jnp.sum(taps * sign_rows(*taps.shape), axis=0, keepdims=True)
            spread[pl.ds(pl.multiple_of(at * chunk, chunk), chunk), pl.ds(half * 128, 128)] = taps.astype(BF)
            return carry

        lax.fori_loop(0, per, tap_step, 0)
    acts_copy = pltpu.make_async_copy(acts, acts_out, local_sems.at[5])
    acts_copy.start()
    out_copies.append(acts_copy)
    table_load.wait()

    def spectrum_step(at, carry):
        here = pl.ds(pl.multiple_of(at * chunk, chunk), chunk)
        sign = sign_rows(chunk, 128)
        index = lax.broadcasted_iota(jnp.int32, (chunk, 128), 0) + at * chunk
        weight = jnp.where(index == 0, 0.5 / length, 1.0 / length)
        for which in range(2):
            result = dot(table_v[which, here, :], spread[...])
            taps_v[which, here, :] = ((result[:, :128] + sign * result[:, 128:]) * weight).astype(BF)
        return carry

    lax.fori_loop(0, per, spectrum_step, 0)
    copy = pltpu.make_async_copy(taps_v, taps_out, local_sems.at[6])
    copy.start()
    out_copies.append(copy)
    tap_total = jnp.broadcast_to(totals[...], (128, 128)).T[:chans, 0:1]

    for copy in sends:
        copy.wait_recv()
    copy = pltpu.make_async_copy(signals, signals_out, local_sems.at[7])
    copy.start()
    out_copies.append(copy)

    step = 16
    padded[pl.ds(chans, 128 - chans), :] = jnp.zeros((128 - chans, length), BF)

    def short_step(at, carry):
        here = pl.ds(pl.multiple_of(at * step, step), step)
        shorted = []
        for s in range(3):
            value = signals[s, here, :].astype(F32)
            shorted.append(
                previous(value) * columns[here, 3 * s : 3 * s + 1]
                + value * columns[here, 3 * s + 1 : 3 * s + 2]
                + following(value) * columns[here, 3 * s + 2 : 3 * s + 3]
            )
        result = shorted[0] * shorted[2]
        product[here, :] = result
        keyed[here, :] = shorted[1]
        padded[here, :] = result.astype(BF)
        nyquist[here, 0:1] = jnp.sum(result * sign_lanes(step, length), axis=1, keepdims=True)
        return carry

    lax.fori_loop(0, chans // step, short_step, 0)
    nyquist[:, 1:2] = tap_total

    def wave_step(at, carry):
        here = pl.ds(pl.multiple_of(at * chunk, chunk), chunk)
        cos_part = dot(table_v[0, here, :], padded[...], NT)
        sin_part = dot(table_v[1, here, :], padded[...], NT)
        wave[0, here, :] = cos_part.astype(BF)
        wave[1, here, :] = sin_part.astype(BF)
        tap_cos = taps_v[0, here, :].astype(F32)
        tap_sin = taps_v[1, here, :].astype(F32)
        spectrum[0, here, :] = (cos_part * tap_cos - sin_part * tap_sin).astype(BF)
        spectrum[1, here, :] = (cos_part * tap_sin + sin_part * tap_cos).astype(BF)
        return carry

    lax.fori_loop(0, per, wave_step, 0)

    def conv_step(at, carry):
        here = pl.ds(pl.multiple_of(at * chunk, chunk), chunk)
        result = dot(table_v[0, here, :], spectrum[0]) + dot(table_v[1, here, :], spectrum[1])
        result = result.T[:chans]
        result = (
            result
            + sign_lanes(chans, chunk) * (nyquist[:, 0:1] * nyquist[:, 1:2] * (0.5 / length))
            + columns[:, 9:10] * product[:, here]
        )
        conv[:, here] = result
        mixed[:, here] = (keyed[:, here] * result).astype(BF)
        return carry

    lax.fori_loop(0, per, conv_step, 0)
    backs = []
    slot = pl.ds(pl.multiple_of(me * chans, 16), chans)
    for k in SEQ_ORDER:
        other = flip(me, k)
        copy = pltpu.make_async_remote_copy(
            src_ref=mixed.at[:, pl.ds(pl.multiple_of(other * rows, rows), rows)],
            dst_ref=mixed_rows.at[slot, :],
            send_sem=back_send.at[k],
            recv_sem=back_recv.at[k],
            device_id={"seq": other},
            device_id_type=MESH,
        )
        copy.start()
        backs.append(copy)
    mixed_rows[slot, :] = mixed[:, mine]
    for at, pair in enumerate(((wave, wave_out), (conv, conv_out), (nyquist, nyquist_out))):
        copy = pltpu.make_async_copy(pair[0], pair[1], local_sems.at[8 + at])
        copy.start()
        out_copies.append(copy)
    for copy in sends:
        copy.wait_send()
    for copy in cot_copies:
        copy.wait()
    own_cot.wait()
    for copy in backs:
        copy.wait()
    mixed_out[...] = mixed_rows[...]
    for copy in out_copies:
        copy.wait()


def front(mesh_shape, *operands):
    n_seq, n_tp = mesh_shape
    _, rows, width = operands[0].shape
    chans, length = width // n_seq, rows * n_seq
    shape = jax.ShapeDtypeStruct
    return pl.pallas_call(
        functools.partial(front_kernel, n_seq, n_tp, (width, chans, length, rows)),
        out_shape=(
            shape((width, rows), BF),
            shape((3, chans, length), BF),
            shape((chans, length), F32),
            shape((2, length, 128), BF),
            shape((2, length, 128), BF),
            shape((chans, 128), F32),
            shape((4, 2 * length, 128), BF),
            shape((width, rows), BF),
            shape((width, rows), BF),
            shape((n_tp, rows, width), BF),
            shape((chans, 16), F32),
            shape((128, 128), BF),
        ),
        in_specs=[any_spec()] * 3 + [vmem_spec()] * 10,
        out_specs=(vmem_spec(),) + (any_spec(),) * 9 + (vmem_spec(),) * 2,
        scratch_shapes=[
            pltpu.VMEM((rows, width), BF),
            pltpu.VMEM((2, length, length), BF),
            pltpu.VMEM((width, rows), BF),
            pltpu.VMEM((width, rows), BF),
            pltpu.VMEM((3 * width, rows), BF),
            pltpu.VMEM((3, chans, length), BF),
            pltpu.VMEM((4, 2 * length, 128), BF),
            pltpu.VMEM((length, 256), BF),
            pltpu.VMEM((2, length, 128), BF),
            pltpu.VMEM((128, length), BF),
            pltpu.VMEM((chans, length), F32),
            pltpu.VMEM((chans, length), F32),
            pltpu.VMEM((2, length, 128), BF),
            pltpu.VMEM((2, length, 128), BF),
            pltpu.VMEM((chans, length), F32),
            pltpu.VMEM((chans, length), BF),
            pltpu.VMEM((width, rows), BF),
            pltpu.VMEM((chans, 128), F32),
            pltpu.VMEM((1, 128), F32),
            pltpu.VMEM((chans, 16), F32),
            pltpu.VMEM((width, 16), F32),
            pltpu.VMEM((width, 128), BF),
            pltpu.VMEM((128, 128), BF),
            pltpu.SemaphoreType.DMA((12,)),
            pltpu.SemaphoreType.DMA((n_seq, 3)),
            pltpu.SemaphoreType.DMA((n_seq, 3)),
            pltpu.SemaphoreType.DMA((n_seq,)),
            pltpu.SemaphoreType.DMA((n_seq,)),
            pltpu.SemaphoreType.DMA((n_tp,)),
            pltpu.SemaphoreType.DMA((n_tp,)),
        ],
        compiler_params=pltpu.CompilerParams(collective_id=0, has_side_effects=True, vmem_limit_bytes=LIMIT),
        name="front",
    )(*operands)


def split_table(values):
    high = values.astype(BF)
    low = (values - high.astype(np.float32)).astype(BF)
    return high, low


def constants(length):
    index = np.arange(length)
    angle = (index[:, None] * index[None, :] % (2 * length)) * (math.pi / length)
    table = np.stack([np.cos(angle), np.sin(angle)]).astype(np.float32).astype(BF)
    place = np.arange(2 * length)
    scaled = np.where(place < length, place, place - 2 * length) / length
    features = np.zeros((2 * length, 8), np.float32)
    features[:, 0] = scaled
    features[:, 1] = np.sin(math.pi * scaled)
    features[:, 2] = np.cos(math.pi * scaled)
    features[:, 3] = np.sin(7.0 * math.pi * scaled)
    features[:, 4] = np.cos(7.0 * math.pi * scaled)
    return table, np.concatenate(split_table(features), axis=1)


def monarch_backward(upstream, operand, shuffled, right, left, middle, keep_right, keep_left, store):
    groups, width, _ = right.shape
    part = width // groups
    for g in range(groups):
        above = upstream(g)
        keep_left(g, dot(shuffled[pl.ds(g * width, width), :], above, NT))
        below = dot(left[g], above).astype(BF)
        for b in range(groups):
            middle[pl.ds(b * width + g * part, part), :] = below[b * part : (b + 1) * part]
    for b in range(groups):
        above = middle[pl.ds(b * width, width), :]
        keep_right(b, dot(operand(b), above, NT))
        store(b, dot(right[b], above))


CHIPS = (6, 2, 4)


def feed_kernel(n_seq, n_tp, dims, *refs):
    (mixed, tokens, cot_rows, gain, bias, right, left, gate_w, up_w, down_w) = refs[:10]
    (grad_mixed_out, grad_resid_out, shard_out, grad_weights_out, grad_vectors_out, output_out) = refs[10:16]
    (token_v, cot_v, gate_v, up_v, down_v, shuffled, branch, resid, scaled, inverse, normed, hidden, grad_hidden, grad_gate, grad_up,
     grad_normed, grad_send, grad_recv, glu_own, glu_send, glu_recv, turned, grads, core_recv, halves, chip_recv, grad_branch,
     middle, grad_mixed, grad_mixed_all, out_rows, output_v, local_sems, gather_send, gather_recv, back_send, back_recv, glu_ssem, glu_rsem,
     out_send, out_recv, core_ssem, core_rsem, chip_ssem, chip_rsem, seq_send, seq_recv) = refs[16:]
    width, chans, length, rows = dims
    me, plane = lax.axis_index("seq"), lax.axis_index("tp")
    entered = greet(n_seq, n_tp)
    loads = [
        pltpu.make_async_copy(tokens.at[plane], token_v, local_sems.at[0]),
        pltpu.make_async_copy(cot_rows, cot_v, local_sems.at[1]),
        pltpu.make_async_copy(down_w, down_v, local_sems.at[2]),
        pltpu.make_async_copy(gate_w, gate_v, local_sems.at[3]),
        pltpu.make_async_copy(up_w, up_v, local_sems.at[4]),
    ]
    for copy in loads:
        copy.start()
    groups = right.shape[0]
    block = width // groups

    def keep_branch(g, result):
        branch[pl.ds(g * block, block), :] = result

    monarch_forward(lambda b: mixed[pl.ds(b * block, block), :], right, left, shuffled, keep_branch)
    loads[0].wait()
    value = token_v[...].astype(F32) + branch[...].T
    resid[...] = value
    shifted = value - jnp.mean(value, axis=-1, keepdims=True)
    inverse[...] = lax.rsqrt(jnp.mean(shifted * shifted, axis=-1, keepdims=True) + 1e-05)
    value = shifted * inverse[...]
    scaled[...] = value
    normed[plane] = (value * gain[...].reshape(1, width) + bias[...].reshape(1, width)).astype(BF)
    entered()
    gathers = {}
    for k in range(1, n_tp):
        gathers[k] = pltpu.make_async_remote_copy(
            src_ref=normed.at[plane],
            dst_ref=normed.at[plane],
            send_sem=gather_send.at[k],
            recv_sem=gather_recv.at[k],
            device_id={"tp": flip(plane, k)},
            device_id_type=MESH,
        )
        gathers[k].start()
    loads[1].wait()
    loads[2].wait()
    chunk = 256
    pieces = width // chunk

    def hidden_step(at, carry):
        cols = pl.ds(pl.multiple_of(at * chunk, chunk), chunk)
        result = dot(cot_v[...].reshape(n_tp * rows, width), down_v[cols, :], NT)
        grad_hidden[:, :, cols] = result.reshape(n_tp, rows, chunk)
        return carry

    lax.fori_loop(0, pieces, hidden_step, 0)
    loads[3].wait()
    loads[4].wait()
    backs, glus = {}, {}
    for k in range(n_tp):
        other = flip(plane, k)
        if k > 0:
            gathers[k].wait_recv()

        def gate_step(at, carry, other=other):
            cols = pl.ds(pl.multiple_of(at * chunk, chunk), chunk)
            value = normed[other]
            gate = dot(value, gate_v[:, cols])
            upward = dot(value, up_v[:, cols])
            sigma = 1.0 / (1.0 + jnp.exp(-gate))
            active = gate * sigma
            hidden[other, :, cols] = (active * upward).astype(BF)
            above = grad_hidden[other, :, cols]
            grad_gate[other, :, cols] = (above * upward * (sigma + active * (1.0 - sigma))).astype(BF)
            grad_up[other, :, cols] = (above * active).astype(BF)
            return carry

        lax.fori_loop(0, pieces, gate_step, 0)

        def back_step(at, carry, k=k, other=other):
            cols = pl.ds(pl.multiple_of(at * chunk, chunk), chunk)
            result = dot(grad_gate[other], gate_v[cols, :], NT) + dot(grad_up[other], up_v[cols, :], NT)
            if k == 0:
                grad_normed[:, cols] = result
            else:
                grad_send[k, :, cols] = result.astype(BF)
            return carry

        lax.fori_loop(0, pieces, back_step, 0)
        if k > 0:
            backs[k] = pltpu.make_async_remote_copy(
                src_ref=grad_send.at[k],
                dst_ref=grad_recv.at[k],
                send_sem=back_send.at[k],
                recv_sem=back_recv.at[k],
                device_id={"tp": other},
                device_id_type=MESH,
            )
            backs[k].start()

    def turn(source):
        for s in range(n_tp):
            turned[:, s * rows : (s + 1) * rows] = source[s].T

    def weight_grad(which, factor):
        def step(at, carry):
            here = pl.ds(pl.multiple_of(at * chunk, chunk), chunk)
            result = dot(turned[here, :], factor[...].reshape(n_tp * rows, width))
            grads[which, here, :] = result.astype(BF)
            return carry

        lax.fori_loop(0, pieces, step, 0)

    core = lax.rem(me, 2)
    half = width // 2
    core_copies = []

    def core_send(which):
        copy = pltpu.make_async_remote_copy(
            src_ref=grads.at[which, pl.ds(pl.multiple_of((1 - core) * half, half), half), :],
            dst_ref=core_recv.at[which],
            send_sem=core_ssem.at[which],
            recv_sem=core_rsem.at[which],
            device_id={"seq": flip(me, 1)},
            device_id_type=MESH,
        )
        copy.start()
        core_copies.append(copy)

    turn(normed)
    weight_grad(0, grad_gate)
    core_send(0)
    weight_grad(1, grad_up)
    core_send(1)
    turn(hidden)
    weight_grad(2, cot_v)
    core_send(2)

    for k in (1, 2, 3, 0):
        other = flip(plane, k)

        def glu_step(at, carry, k=k, other=other):
            cols = pl.ds(pl.multiple_of(at * chunk, chunk), chunk)
            result = dot(hidden[other], down_v[:, cols])
            if k == 0:
                glu_own[:, cols] = result
            else:
                glu_send[k, :, cols] = result.astype(BF)
            return carry

        lax.fori_loop(0, pieces, glu_step, 0)
        if k > 0:
            glus[k] = pltpu.make_async_remote_copy(
                src_ref=glu_send.at[k],
                dst_ref=glu_recv.at[k],
                send_sem=glu_ssem.at[k],
                recv_sem=glu_rsem.at[k],
                device_id={"tp": other},
                device_id_type=MESH,
            )
            glus[k].start()

    quarter = half // (n_seq // 2)
    chip_copies = []
    for which in range(3):
        core_copies[which].wait_recv()
        own = grads[which, pl.ds(pl.multiple_of(core * half, half), half), :]
        halves[which] = (own.astype(F32) + core_recv[which].astype(F32)).astype(BF)
        for k in CHIPS:
            other = flip(me, k)
            copy = pltpu.make_async_remote_copy(
                src_ref=halves.at[which, pl.ds(pl.multiple_of(other // 2 * quarter, 16), quarter), :],
                dst_ref=chip_recv.at[which, k // 2],
                send_sem=chip_ssem.at[which, k // 2],
                recv_sem=chip_rsem.at[which, k // 2],
                device_id={"seq": other},
                device_id_type=MESH,
            )
            copy.start()
            chip_copies.append(copy)

    for k in range(1, n_tp):
        backs[k].wait_recv()
    total = grad_normed[...]
    for k in range(1, n_tp):
        total = total + grad_recv[k].astype(F32)
    value = scaled[...]
    grad_vectors_out[0:1, :] = jnp.sum(total * value, axis=0, keepdims=True)
    grad_vectors_out[1:2, :] = jnp.sum(total, axis=0, keepdims=True)
    total = total * gain[...].reshape(1, width)
    first_mean = jnp.mean(total, axis=-1, keepdims=True)
    second_mean = jnp.mean(total * value, axis=-1, keepdims=True)
    total = cot_v[plane].astype(F32) + inverse[...] * (total - first_mean - value * second_mean)
    grad_resid_out[...] = total
    grad_branch[...] = total.T.astype(BF)

    def keep_right(b, result):
        grad_weights_out[0, pl.ds(b * block, block), :] = result.astype(BF)

    def keep_left(g, result):
        grad_weights_out[1, pl.ds(g * block, block), :] = result.astype(BF)

    def keep_mixed(b, result):
        grad_mixed[pl.ds(b * block, block), :] = result.astype(BF)

    monarch_backward(
        lambda g: grad_branch[pl.ds(g * block, block), :],
        lambda b: mixed[pl.ds(b * block, block), :],
        shuffled, right, left, middle, keep_right, keep_left, keep_mixed,
    )
    mine = pl.ds(pl.multiple_of(me * rows, rows), rows)
    seq_copies = []
    for k in SEQ_ORDER:
        other = flip(me, k)
        copy = pltpu.make_async_remote_copy(
            src_ref=grad_mixed.at[pl.ds(pl.multiple_of(other * chans, 16), chans), :],
            dst_ref=grad_mixed_all.at[:, mine],
            send_sem=seq_send.at[k],
            recv_sem=seq_recv.at[k],
            device_id={"seq": other},
            device_id_type=MESH,
        )
        copy.start()
        seq_copies.append(copy)
    grad_mixed_all[:, mine] = grad_mixed[pl.ds(pl.multiple_of(me * chans, 16), chans), :]

    for k in range(1, n_tp):
        glus[k].wait_recv()
    total = resid[...] + glu_own[...]
    for k in range(1, n_tp):
        total = total + glu_recv[k].astype(F32)
    out_rows[...] = total.astype(BF)
    part = rows // n_tp
    out_copies = []
    for k in range(1, n_tp):
        other = flip(plane, k)
        copy = pltpu.make_async_remote_copy(
            src_ref=out_rows.at[pl.ds(pl.multiple_of(other * part, part), part), :],
            dst_ref=output_v.at[plane],
            send_sem=out_send.at[k],
            recv_sem=out_recv.at[k],
            device_id={"tp": other},
            device_id_type=MESH,
        )
        copy.start()
        out_copies.append(copy)
    output_v[plane] = out_rows[pl.ds(pl.multiple_of(plane * part, part), part), :]

    chip = me // 2
    for which in range(3):
        for at in range(3):
            chip_copies[3 * which + at].wait_recv()
        total = halves[which, pl.ds(pl.multiple_of(chip * quarter, 16), quarter), :].astype(F32)
        for k in CHIPS:
            total = total + chip_recv[which, k // 2].astype(F32)
        shard_out[which] = total.astype(BF)
    for copy in seq_copies:
        copy.wait()
    grad_mixed_out[...] = grad_mixed_all[...]
    for copy in out_copies:
        copy.wait()
    output_out[...] = output_v[...]
    for k in range(1, n_tp):
        gathers[k].wait_send()
        backs[k].wait_send()
        glus[k].wait_send()
    for copy in core_copies + chip_copies:
        copy.wait_send()


def feed(mesh_shape, mixed, tokens, cot_rows, gain, bias, right, left, gate_w, up_w, down_w):
    n_seq, n_tp = mesh_shape
    _, rows, width = tokens.shape
    chans, length = width // n_seq, rows * n_seq
    part = rows // n_tp
    shape = jax.ShapeDtypeStruct
    dma = pltpu.SemaphoreType.DMA
    return pl.pallas_call(
        functools.partial(feed_kernel, n_seq, n_tp, (width, chans, length, rows)),
        out_shape=(
            shape((chans, length), BF),
            shape((rows, width), F32),
            shape((3, width // n_seq, width), BF),
            shape((2, width, width // 4), BF),
            shape((2, width), F32),
            shape((n_tp, part, width), BF),
        ),
        in_specs=[vmem_spec(), any_spec(), any_spec()] + [vmem_spec()] * 4 + [any_spec()] * 3,
        out_specs=(vmem_spec(),) * 6,
        scratch_shapes=[
            pltpu.VMEM((rows, width), BF),
            pltpu.VMEM((n_tp, rows, width), BF),
            pltpu.VMEM((width, width), BF),
            pltpu.VMEM((width, width), BF),
            pltpu.VMEM((width, width), BF),
            pltpu.VMEM((width, rows), BF),
            pltpu.VMEM((width, rows), F32),
            pltpu.VMEM((rows, width), F32),
            pltpu.VMEM((rows, width), F32),
            pltpu.VMEM((rows, 1), F32),
            pltpu.VMEM((n_tp, rows, width), BF),
            pltpu.VMEM((n_tp, rows, width), BF),
            pltpu.VMEM((n_tp, rows, width), F32),
            pltpu.VMEM((n_tp, rows, width), BF),
            pltpu.VMEM((n_tp, rows, width), BF),
            pltpu.VMEM((rows, width), F32),
            pltpu.VMEM((n_tp, rows, width), BF),
            pltpu.VMEM((n_tp, rows, width), BF),
            pltpu.VMEM((rows, width), F32),
            pltpu.VMEM((n_tp, rows, width), BF),
            pltpu.VMEM((n_tp, rows, width), BF),
            pltpu.VMEM((width, n_tp * rows), BF),
            pltpu.VMEM((3, width, width), BF),
            pltpu.VMEM((3, width // 2, width), BF),
            pltpu.VMEM((3, width // 2, width), BF),
            pltpu.VMEM((3, n_seq // 2, width // n_seq, width), BF),
            pltpu.VMEM((width, rows), BF),
            pltpu.VMEM((width, rows), BF),
            pltpu.VMEM((width, rows), BF),
            pltpu.VMEM((chans, length), BF),
            pltpu.VMEM((rows, width), BF),
            pltpu.VMEM((n_tp, part, width), BF),
            dma((5,)),
            dma((n_tp,)), dma((n_tp,)), dma((n_tp,)), dma((n_tp,)), dma((n_tp,)), dma((n_tp,)), dma((n_tp,)), dma((n_tp,)),
            dma((3,)), dma((3,)), dma((3, n_seq // 2)), dma((3, n_seq // 2)), dma((n_seq,)), dma((n_seq,)),
        ],
        compiler_params=pltpu.CompilerParams(collective_id=1, has_side_effects=True, vmem_limit_bytes=LIMIT),
        name="feed",
    )(mixed, tokens, cot_rows, gain, bias, right, left, gate_w, up_w, down_w)


class Reduce:
    def __init__(self, n_seq, n_tp, own, full, core_in, halves, chip_in, quarter, plane_in, send, recv):
        self.own, self.full, self.core_in, self.halves = own, full, core_in, halves
        self.chip_in, self.quarter, self.plane_in = chip_in, quarter, plane_in
        self.send, self.recv, self.n_tp = send, recv, n_tp
        rows, width = own.shape
        self.rows, self.width = rows, width
        self.per_chip, self.per_plane = rows // (n_seq // 2), rows // (n_seq // 2) // n_tp
        self.me, self.plane = lax.axis_index("seq"), lax.axis_index("tp")
        core = lax.rem(self.me, 2)
        self.mine = pl.ds(pl.multiple_of(core * (width // 2), 128), width // 2)
        self.theirs = pl.ds(pl.multiple_of((1 - core) * (width // 2), 128), width // 2)
        self.started = []

    def chip_rows(self, index):
        return pl.ds(pl.multiple_of(index // 2 * self.per_chip, 16), self.per_chip)

    def copy(self, source, target, at, where):
        result = pltpu.make_async_remote_copy(
            src_ref=source, dst_ref=target, send_sem=self.send.at[at], recv_sem=self.recv.at[at],
            device_id=where, device_id_type=MESH,
        )
        result.start()
        self.started.append(result)
        return result

    def start_core(self):
        self.phase = [self.copy(self.own.at[:, self.theirs], self.core_in, 0, {"seq": flip(self.me, 1)})]

    def arrived(self):
        for copy in self.phase:
            copy.wait_recv()
        self.phase = []

    def start_chip(self):
        self.arrived()
        self.halves[...] = (self.own[:, self.mine].astype(F32) + self.core_in[...].astype(F32)).astype(BF)
        for k in CHIPS:
            other = flip(self.me, k)
            self.phase.append(
                self.copy(self.halves.at[self.chip_rows(other), :], self.chip_in.at[k // 2], k // 2, {"seq": other})
            )

    def start_plane(self):
        self.arrived()
        total = self.halves[self.chip_rows(self.me), :].astype(F32)
        for k in CHIPS:
            total = total + self.chip_in[k // 2].astype(F32)
        self.quarter[...] = total.astype(BF)
        for k in range(1, self.n_tp):
            other = flip(self.plane, k)
            here = pl.ds(pl.multiple_of(other * self.per_plane, 16), self.per_plane)
            self.phase.append(self.copy(self.quarter.at[here, :], self.plane_in.at[k], 3 + k, {"tp": other}))

    def start_plane_back(self):
        self.arrived()
        here = pl.ds(pl.multiple_of(self.plane * self.per_plane, 16), self.per_plane)
        total = self.quarter[here, :].astype(F32)
        for k in range(1, self.n_tp):
            total = total + self.plane_in[k].astype(F32)
        rows = pl.ds(
            pl.multiple_of(self.me // 2 * self.per_chip + self.plane * self.per_plane, 16), self.per_plane
        )
        self.full[rows, self.mine] = total.astype(BF)
        spot = self.full.at[rows, self.mine]
        for k in range(1, self.n_tp):
            self.phase.append(self.copy(spot, spot, 6 + k, {"tp": flip(self.plane, k)}))

    def start_chip_back(self):
        self.arrived()
        spot = self.full.at[self.chip_rows(self.me), self.mine]
        for k in CHIPS:
            self.phase.append(self.copy(spot, spot, 9 + k // 2, {"seq": flip(self.me, k)}))

    def start_core_back(self):
        self.arrived()
        spot = self.full.at[:, self.mine]
        self.phase.append(self.copy(spot, spot, 13, {"seq": flip(self.me, 1)}))

    def finish(self):
        self.arrived()
        for copy in self.started:
            copy.wait_send()


def reduce_scratch(n_seq, n_tp, rows, width):
    half, chip, plane = width // 2, rows // (n_seq // 2), rows // (n_seq // 2) // n_tp
    return [
        pltpu.VMEM((rows, width), BF),
        pltpu.VMEM((rows, width), BF),
        pltpu.VMEM((rows, half), BF),
        pltpu.VMEM((rows, half), BF),
        pltpu.VMEM((n_seq // 2, chip, half), BF),
        pltpu.VMEM((chip, half), BF),
        pltpu.VMEM((n_tp, plane, half), BF),
        pltpu.SemaphoreType.DMA((14,)),
        pltpu.SemaphoreType.DMA((14,)),
    ]


def back_kernel(n_seq, n_tp, dims, *refs):
    (grad_mixed, columns, gain, right, left, second, third, nyquist, shard, grad_weights, grad_vectors,
     features, tokens, table, signals_in, conv_in, wave_in, taps_in, acts_in, normed_in, shuffled_in, resid_in) = refs[:22]
    (ffn_out, tokens_out, late_out, early_out, small_out) = refs[22:27]
    (table_v, signals, conv, wave, taps_v, acts, token_v, normed, shuffled, grad_resid, grad_short, query, value_v, grad_conv,
     padded, back_wave, cross, sums, grad_signals, grad_proj, middle, grad_rows, grad_tok, grad_second, grad_first, grad_third,
     local_sems, ffn_ssem, ffn_rsem, seq_send, seq_recv, tp_send, tp_recv) = refs[27:60]
    width, chans, length, rows = dims
    late = Reduce(n_seq, n_tp, *refs[60:69])
    early = Reduce(n_seq, n_tp, *refs[69:78])
    small = Reduce(n_seq, n_tp, *refs[78:87])
    me, plane = lax.axis_index("seq"), lax.axis_index("tp")
    entered = greet(n_seq, n_tp)
    loads = [
        pltpu.make_async_copy(source, target, local_sems.at[at])
        for at, (source, target) in enumerate(
            (
                (signals_in, signals), (conv_in, conv), (table, table_v), (wave_in, wave), (taps_in, taps_v), (acts_in, acts),
                (tokens.at[plane], token_v), (normed_in, normed), (shuffled_in, shuffled), (resid_in, grad_resid),
            )
        )
    ]
    for copy in loads:
        copy.start()
    half, quarter = width // 2, width // n_seq
    own_rows = pl.ds(pl.multiple_of(lax.rem(me, 2) * half + me // 2 * quarter, 16), quarter)
    entered()
    ffn_copies = []
    for which in range(3):
        for k in CHIPS:
            copy = pltpu.make_async_remote_copy(
                src_ref=shard.at[which],
                dst_ref=ffn_out.at[which, own_rows, :],
                send_sem=ffn_ssem.at[which, k // 2],
                recv_sem=ffn_rsem.at[which, k // 2],
                device_id={"seq": flip(me, k)},
                device_id_type=MESH,
            )
            copy.start()
            ffn_copies.append(copy)
    own_shard = pltpu.make_async_copy(shard, ffn_out.at[:, own_rows, :], local_sems.at[10])
    own_shard.start()
    sums[...] = jnp.zeros_like(sums)
    small.own[...] = jnp.zeros_like(small.own)
    early.own[...] = jnp.zeros_like(early.own)
    loads[0].wait()
    loads[1].wait()
    step = 16
    padded[pl.ds(chans, 128 - chans), :] = jnp.zeros((128 - chans, length), BF)

    def short_step(at, carry):
        here = pl.ds(pl.multiple_of(at * step, step), step)
        shorted = []
        for s in range(3):
            value = signals[s, here, :].astype(F32)
            shorted.append(
                previous(value) * columns[here, 3 * s : 3 * s + 1]
                + value * columns[here, 3 * s + 1 : 3 * s + 2]
                + following(value) * columns[here, 3 * s + 2 : 3 * s + 3]
            )
        query[here, :] = shorted[0]
        value_v[here, :] = shorted[2]
        above = grad_mixed[here, :].astype(F32)
        grad_short[1, here, :] = above * conv[here, :]
        above = above * shorted[1]
        grad_conv[here, :] = above
        padded[here, :] = above.astype(BF)
        sums[here, 9:10] = jnp.sum(above * shorted[0] * shorted[2], axis=1, keepdims=True)
        sums[here, 10:11] = jnp.sum(above * sign_lanes(step, length), axis=1, keepdims=True)
        return carry

    lax.fori_loop(0, chans // step, short_step, 0)
    for at in (2, 3, 4):
        loads[at].wait()
    chunk = 256
    per = length // chunk

    def wave_step(at, carry):
        here = pl.ds(pl.multiple_of(at * chunk, chunk), chunk)
        sign = sign_rows(chunk, 128)
        index = lax.broadcasted_iota(jnp.int32, (chunk, 128), 0) + at * chunk
        weight = jnp.where(index == 0, 0.5 / length, 1.0 / length)
        cos_part = dot(table_v[0, here, :], padded[...], NT)
        sin_part = dot(table_v[1, here, :], padded[...], NT)
        tap_cos = taps_v[0, here, :].astype(F32)
        tap_sin = taps_v[1, here, :].astype(F32)
        back_wave[0, here, :] = (cos_part * tap_cos + sin_part * tap_sin).astype(BF)
        back_wave[1, here, :] = (sin_part * tap_cos - cos_part * tap_sin).astype(BF)
        wave_cos = wave[0, here, :].astype(F32) * weight
        wave_sin = wave[1, here, :].astype(F32) * weight
        result = cos_part * wave_cos + sin_part * wave_sin
        cross[0, here, 0:128] = result.astype(BF)
        cross[0, here, 128:256] = (result * sign).astype(BF)
        result = sin_part * wave_cos - cos_part * wave_sin
        cross[1, here, 0:128] = result.astype(BF)
        cross[1, here, 128:256] = (result * sign).astype(BF)
        return carry

    lax.fori_loop(0, per, wave_step, 0)

    def product_step(at, carry):
        here = pl.ds(pl.multiple_of(at * chunk, chunk), chunk)
        result = dot(table_v[0, here, :], back_wave[0]) + dot(table_v[1, here, :], back_wave[1])
        result = (
            result.T[:chans]
            + sign_lanes(chans, chunk) * (sums[:chans, 10:11] * nyquist[:, 1:2] * (0.5 / length))
            + columns[:, 9:10] * grad_conv[:, here]
        )
        grad_short[0, :, here] = result * value_v[:, here]
        grad_short[2, :, here] = result * query[:, here]
        return carry

    lax.fori_loop(0, per, product_step, 0)

    def signal_step(at, carry):
        here = pl.ds(pl.multiple_of(at * step, step), step)
        for s in range(3):
            above = grad_short[s, here, :]
            value = signals[s, here, :].astype(F32)
            before, after = previous(above), following(above)
            grad_signals[s, here, :] = (
                after * columns[here, 3 * s : 3 * s + 1]
                + above * columns[here, 3 * s + 1 : 3 * s + 2]
                + before * columns[here, 3 * s + 2 : 3 * s + 3]
            ).astype(BF)
            sums[here, 3 * s : 3 * s + 1] = jnp.sum(after * value, axis=1, keepdims=True)
            sums[here, 3 * s + 1 : 3 * s + 2] = jnp.sum(above * value, axis=1, keepdims=True)
            sums[here, 3 * s + 2 : 3 * s + 3] = jnp.sum(before * value, axis=1, keepdims=True)
        return carry

    lax.fori_loop(0, chans // step, signal_step, 0)
    mine = pl.ds(pl.multiple_of(me * rows, rows), rows)
    seq_copies = []
    for k in SEQ_ORDER:
        other = flip(me, k)
        for s in range(3):
            copy = pltpu.make_async_remote_copy(
                src_ref=grad_signals.at[s, :, pl.ds(pl.multiple_of(other * rows, rows), rows)],
                dst_ref=grad_proj.at[pl.ds(pl.multiple_of(s * width + me * chans, 16), chans), :],
                send_sem=seq_send.at[k, s],
                recv_sem=seq_recv.at[k, s],
                device_id={"seq": other},
                device_id_type=MESH,
            )
            copy.start()
            seq_copies.append(copy)
    for s in range(3):
        grad_proj[pl.ds(pl.multiple_of(s * width + me * chans, 16), chans), :] = grad_signals[s, :, mine]

    loads[5].wait()
    tap_total = jnp.broadcast_to(sums[:, 10:11], (128, 128)).T[0:1, :]
    pad_nyquist = jnp.concatenate([nyquist[:, 0:1], jnp.zeros((128 - chans, 1), F32)], axis=0)
    tap_total = tap_total * jnp.broadcast_to(pad_nyquist, (128, 128)).T[0:1, :] * (0.5 / length)
    grad_second[...] = jnp.zeros_like(grad_second)
    grad_first[...] = jnp.zeros_like(grad_first)
    grad_third[...] = jnp.zeros_like(grad_third)

    def filter_step(at, carry):
        here = pl.ds(pl.multiple_of(at * chunk, chunk), chunk)
        result = dot(table_v[0, here, :], cross[0]) + dot(table_v[1, here, :], cross[1])
        sign = sign_rows(chunk, 128)
        for part in range(2):
            above = (result[:, part * 128 : (part + 1) * 128] + sign * tap_total) * (length**-0.5)
            if part == 1:
                index = lax.broadcasted_iota(jnp.int32, above.shape, 0) + at * chunk
                above = jnp.where(index == 0, 0.0, above)
            above = above.astype(BF)
            spot = pl.ds(pl.multiple_of(part * length + at * chunk, chunk), chunk)
            grad_third[...] += dot(above, acts[2, spot, :], TN)
            below = (dot(above, third[...]) * acts[3, spot, :].astype(F32)).astype(BF)
            grad_second[...] += dot(acts[0, spot, :], below, TN)
            below = (dot(below, second[...], NT) * acts[1, spot, :].astype(F32)).astype(BF)
            grad_first[...] += dot(features[spot, :], below, TN)
        return carry

    lax.fori_loop(0, per, filter_step, 0)
    early.own[:, 0:384] = jnp.concatenate([grad_weights[0], grad_weights[1]], axis=1)
    early.own[pl.ds(pl.multiple_of(me * chans, 16), chans), 384:512] = grad_third[:chans, :].astype(BF)
    small.own[0:128, 0:128] = grad_second[...].astype(BF)
    small.own[128:136, 0:128] = (grad_first[0:8, :] + grad_first[8:16, :]).astype(BF)
    small.own[pl.ds(pl.multiple_of(me * 16, 16), 16), 128:256] = sums[...].T[0:16, :].astype(BF)
    early.start_core()
    for copy in ffn_copies:
        copy.wait_recv()
    own_shard.wait()
    own_half = pl.ds(pl.multiple_of(lax.rem(me, 2) * half, half), half)
    ffn_last = []
    for which in range(3):
        copy = pltpu.make_async_remote_copy(
            src_ref=ffn_out.at[which, own_half, :],
            dst_ref=ffn_out.at[which, own_half, :],
            send_sem=ffn_ssem.at[which, 0],
            recv_sem=ffn_rsem.at[which, 0],
            device_id={"seq": flip(me, 1)},
            device_id_type=MESH,
        )
        copy.start()
        ffn_last.append(copy)
    early.start_chip()

    for at in range(6, 10):
        loads[at].wait()
    value = token_v[...].astype(F32)
    shifted = value - jnp.mean(value, axis=-1, keepdims=True)
    inverse = lax.rsqrt(jnp.mean(shifted * shifted, axis=-1, keepdims=True) + 1e-05)
    scaled = shifted * inverse

    groups = right.shape[0]
    block = width // groups
    fan = left.shape[2]
    for copy in seq_copies:
        copy.wait_recv()

    def keep_left(g, result):
        late.own[pl.ds(g * block, block), 0:512] = result[:, 0:512].astype(BF)
        middle_left[g] = result[:, 512:576].astype(BF)

    def keep_right(b, result):
        late.own[pl.ds(b * block, block), 512:768] = jnp.concatenate([middle_left[b], result.astype(BF)], axis=1)

    def keep_rows(b, result):
        grad_rows[pl.ds(b * block, block), :] = result

    middle_left = {}
    monarch_backward(
        lambda g: grad_proj[pl.ds(g * fan, fan), :],
        lambda b: normed[pl.ds(b * block, block), :],
        shuffled, right, left, middle, keep_right, keep_left, keep_rows,
    )
    late.start_core()
    early.start_plane()
    total = grad_rows[...].T
    norm_grads = [jnp.sum(total * scaled, axis=0, keepdims=True), jnp.sum(total, axis=0, keepdims=True)]
    total = total * gain[...].reshape(1, width)
    first_mean = jnp.mean(total, axis=-1, keepdims=True)
    second_mean = jnp.mean(total * scaled, axis=-1, keepdims=True)
    total = grad_resid[...] + inverse * (total - first_mean - scaled * second_mean)
    grad_tok[...] = total.astype(BF)
    norm_grads += [grad_vectors[0:1, :], grad_vectors[1:2, :]]
    lines = []
    for line in norm_grads:
        for at in range(width // 128):
            lines.append(line[:, at * 128 : (at + 1) * 128])
    small.own[128:160, 128:256] = jnp.concatenate(lines + [jnp.zeros((8, 128), F32)], axis=0).astype(BF)
    small.start_core()
    tok_copies = []
    for k in range(1, n_tp):
        copy = pltpu.make_async_remote_copy(
            src_ref=grad_tok,
            dst_ref=tokens_out.at[plane],
            send_sem=tp_send.at[k],
            recv_sem=tp_recv.at[k],
            device_id={"tp": flip(plane, k)},
            device_id_type=MESH,
        )
        copy.start()
        tok_copies.append(copy)
    own_tok = pltpu.make_async_copy(grad_tok, tokens_out.at[plane], local_sems.at[11])
    own_tok.start()
    late.start_chip()
    small.start_chip()
    early.start_plane_back()
    late.start_plane()
    small.start_plane()
    early.start_chip_back()
    late.start_plane_back()
    small.start_plane_back()
    early.start_core_back()
    late.start_chip_back()
    small.start_chip_back()
    late.start_core_back()
    small.start_core_back()
    early.finish()
    early_out[...] = early.full[...]
    small.finish()
    small_out[...] = small.full[...]
    late.finish()
    late_out[...] = late.full[...]
    for copy in ffn_copies + seq_copies:
        copy.wait_send()
    for copy in ffn_last + tok_copies:
        copy.wait()
    own_tok.wait()


def back(mesh_shape, *operands):
    n_seq, n_tp = mesh_shape
    tokens = operands[12]
    _, rows, width = tokens.shape
    chans, length = width // n_seq, rows * n_seq
    shape = jax.ShapeDtypeStruct
    dma = pltpu.SemaphoreType.DMA
    return pl.pallas_call(
        functools.partial(back_kernel, n_seq, n_tp, (width, chans, length, rows)),
        out_shape=(
            shape((3, width, width), BF),
            shape((n_tp, rows, width), BF),
            shape((width, width), BF),
            shape((width, 512), BF),
            shape((256, 256), BF),
        ),
        in_specs=[vmem_spec()] * 12 + [any_spec()] * 10,
        out_specs=(any_spec(), any_spec(), vmem_spec(), vmem_spec(), vmem_spec()),
        scratch_shapes=[
            pltpu.VMEM((2, length, length), BF),
            pltpu.VMEM((3, chans, length), BF),
            pltpu.VMEM((chans, length), F32),
            pltpu.VMEM((2, length, 128), BF),
            pltpu.VMEM((2, length, 128), BF),
            pltpu.VMEM((4, 2 * length, 128), BF),
            pltpu.VMEM((rows, width), BF),
            pltpu.VMEM((width, rows), BF),
            pltpu.VMEM((width, rows), BF),
            pltpu.VMEM((rows, width), F32),
            pltpu.VMEM((3, chans, length), F32),
            pltpu.VMEM((chans, length), F32),
            pltpu.VMEM((chans, length), F32),
            pltpu.VMEM((chans, length), F32),
            pltpu.VMEM((128, length), BF),
            pltpu.VMEM((2, length, 128), BF),
            pltpu.VMEM((2, length, 256), BF),
            pltpu.VMEM((128, 128), F32),
            pltpu.VMEM((3, chans, length), BF),
            pltpu.VMEM((3 * width, rows), BF),
            pltpu.VMEM((width, rows), BF),
            pltpu.VMEM((width, rows), F32),
            pltpu.VMEM((rows, width), BF),
            pltpu.VMEM((128, 128), F32),
            pltpu.VMEM((16, 128), F32),
            pltpu.VMEM((128, 128), F32),
            dma((12,)),
            dma((3, n_seq // 2)), dma((3, n_seq // 2)), dma((n_seq, 3)), dma((n_seq, 3)), dma((n_tp,)), dma((n_tp,)),
        ]
        + reduce_scratch(n_seq, n_tp, width, width)
        + reduce_scratch(n_seq, n_tp, width, 512)
        + reduce_scratch(n_seq, n_tp, 256, 256),
        compiler_params=pltpu.CompilerParams(collective_id=2, has_side_effects=True, vmem_limit_bytes=LIMIT),
        name="back",
    )(*operands)


def finish_kernel(width, chans, *refs):
    (ffn, tokens, late, early, small) = refs[:5]
    (grad_tokens, norm_gain, norm_bias, in_right, in_left, short, first, second, third, conv_bias, out_right, out_left,
     ffn_gain, ffn_bias, gate, up, down) = refs[5:22]
    (ffn_v, ffn_f, token_v, token_f, in_sems, out_sems) = refs[22:]
    loads = [pltpu.make_async_copy(ffn.at[which], ffn_v.at[which], in_sems.at[which]) for which in range(3)]
    loads.append(pltpu.make_async_copy(tokens, token_v, in_sems.at[3]))
    for copy in loads:
        copy.start()
    stores = [
        pltpu.make_async_copy(ffn_f.at[which], target, out_sems.at[which]) for which, target in enumerate((gate, up, down))
    ]
    stores.append(pltpu.make_async_copy(token_f, grad_tokens, out_sems.at[3]))
    chunk = 64
    for which in range(3):
        loads[which].wait()

        def step(at, carry, which=which):
            here = pl.ds(pl.multiple_of(at * chunk, chunk), chunk)
            ffn_f[which, here, :] = ffn_v[which, here, :].astype(F32)
            return carry

        lax.fori_loop(0, width // chunk, step, 0)
        stores[which].start()
    loads[3].wait()

    def token_step(at, carry):
        token_f[at] = token_v[at].astype(F32)
        return carry

    lax.fori_loop(0, token_v.shape[0], token_step, 0)
    stores[3].start()
    groups, block, _ = in_right.shape
    for b in range(groups):
        here = pl.ds(b * block, block)
        in_left[b] = late[here, 0 : 3 * block].astype(F32)
        in_right[b] = late[here, 3 * block : 4 * block].astype(F32)
        out_right[b] = early[here, 0:block].astype(F32)
        out_left[b] = early[here, block : 2 * block].astype(F32)
    third[...] = early[:, 384:512].astype(F32).T
    values = small[...].astype(F32)
    second[...] = values[0:128, 0:128]
    first[...] = values[128:133, 0:128]
    for at, target in enumerate((norm_gain, norm_bias, ffn_gain, ffn_bias)):
        row = 128 + at * (width // 128)
        target[...] = jnp.concatenate([values[row + k : row + k + 1, 128:256] for k in range(width // 128)], axis=1).reshape(width)
    parts = [values[16 * at : 16 * at + 16, 128 : 128 + chans] for at in range(width // chans)]
    lines = jnp.concatenate(parts, axis=1)
    for s in range(3):
        short[s] = lines[3 * s : 3 * s + 3]
    conv_bias[...] = lines[9:10].reshape(width)
    for copy in stores:
        copy.wait()


def finish(chans, ffn, tokens, late, early, small):
    width = ffn.shape[1]
    block = width // 4
    shape = jax.ShapeDtypeStruct
    vector = shape((width,), F32)
    square = shape((4, block, block), F32)
    return pl.pallas_call(
        functools.partial(finish_kernel, width, chans),
        out_shape=(
            shape(tokens.shape, F32), vector, vector, square, shape((4, block, 3 * block), F32), shape((3, 3, width), F32),
            shape((5, 128), F32), shape((128, 128), F32), shape((128, width), F32), vector, square, square, vector, vector,
        )
        + (shape((width, width), F32),) * 3,
        in_specs=[any_spec()] * 2 + [vmem_spec()] * 3,
        out_specs=(any_spec(),) + (vmem_spec(),) * 13 + (any_spec(),) * 3,
        scratch_shapes=[
            pltpu.VMEM(ffn.shape, BF),
            pltpu.VMEM(ffn.shape, F32),
            pltpu.VMEM(tokens.shape, BF),
            pltpu.VMEM(tokens.shape, F32),
            pltpu.SemaphoreType.DMA((4,)),
            pltpu.SemaphoreType.DMA((4,)),
        ],
        compiler_params=pltpu.CompilerParams(vmem_limit_bytes=LIMIT),
        name="finish",
    )(ffn, tokens, late, early, small)


def fast_body(
    tokens,
    norm_gain,
    norm_bias,
    in_right,
    in_left,
    short_kernel,
    filter_first,
    filter_second,
    filter_third,
    conv_bias,
    out_right,
    out_left,
    ffn_gain,
    ffn_bias,
    gate_weight,
    up_weight,
    down_weight,
    cotangent,
):
    n_seq, n_tp = lax.axis_size("seq"), lax.axis_size("tp")
    _, rows, width = tokens.shape
    chans, length = width // n_seq, rows * n_seq
    shape = (n_seq, n_tp)
    table, features = (jnp.asarray(array) for array in constants(length))
    mixed, signals, conv, wave, taps, nyquist, acts, normed, shuffled, cot_rows, columns, third = front(
        shape, tokens, cotangent, table, norm_gain, norm_bias, in_right, in_left, short_kernel.transpose(0, 2, 1), conv_bias,
        features, filter_first, filter_second, filter_third,
    )
    grad_mixed, grad_resid, shard, grad_weights, grad_vectors, output = feed(
        shape, mixed, tokens, cot_rows, ffn_gain, ffn_bias, out_right, out_left, gate_weight, up_weight, down_weight
    )
    ffn, grad_tokens, late, early, small = back(
        shape, grad_mixed, columns, norm_gain, in_right, in_left, filter_second, third, nyquist, shard, grad_weights,
        grad_vectors, features, tokens, table, signals, conv, wave, taps, acts, normed, shuffled, grad_resid,
    )
    grads = finish(chans, ffn, grad_tokens, late, early, small)
    return (output,) + grads[:5] + (grads[5].transpose(0, 2, 1),) + grads[6:]


highest = lax.Precision.HIGHEST


def norm_forward(values, gain, bias):
    centre = jnp.mean(values, axis=-1, keepdims=True)
    shifted = values - centre
    inverse = lax.rsqrt(jnp.mean(shifted * shifted, axis=-1, keepdims=True) + 1e-05)
    scaled = shifted * inverse
    return (scaled * gain + bias, scaled, inverse)


def norm_backward(upstream, scaled, inverse, gain):
    weighted = upstream * gain
    first_mean = jnp.mean(weighted, axis=-1, keepdims=True)
    second_mean = jnp.mean(weighted * scaled, axis=-1, keepdims=True)
    grad_input = inverse * (weighted - first_mean - scaled * second_mean)
    breadth = upstream.shape[-1]
    grad_gain = jnp.sum((upstream * scaled).reshape(-1, breadth), axis=0)
    grad_bias = jnp.sum(upstream.reshape(-1, breadth), axis=0)
    return (grad_input, grad_gain, grad_bias)


def shuffle(blocked):
    row_count, groups, breadth = blocked.shape
    return (
        blocked.reshape(row_count, groups, groups, breadth // groups)
        .transpose(0, 2, 1, 3)
        .reshape(row_count, groups, breadth)
    )


def rows_monarch_forward(operand, right_factor, left_factor):
    row_count = operand.shape[0]
    groups = right_factor.shape[0]
    blocked = operand.reshape(row_count, groups, -1)
    middle = jnp.einsum(
        "tbi,bij->tbj", blocked, right_factor, preferred_element_type=jnp.float32
    ).astype(jnp.bfloat16)
    shuffled = shuffle(middle)
    result = jnp.einsum("tbi,bij->tbj", shuffled, left_factor, preferred_element_type=jnp.float32)
    return (shuffled, result.reshape(row_count, -1))


def rows_monarch_backward(grad_result, operand, shuffled, right_factor, left_factor):
    row_count = operand.shape[0]
    groups = right_factor.shape[0]
    grad_blocked = grad_result.reshape(row_count, groups, -1)
    grad_left = jnp.einsum(
        "tbi,tbj->bij", shuffled, grad_blocked, preferred_element_type=jnp.float32
    )
    grad_shuffled = jnp.einsum(
        "tbj,bij->tbi", grad_blocked, left_factor, preferred_element_type=jnp.float32
    )
    grad_middle = shuffle(grad_shuffled).astype(jnp.bfloat16)
    blocked = operand.reshape(row_count, groups, -1)
    grad_right = jnp.einsum(
        "tbi,tbj->bij", blocked, grad_middle, preferred_element_type=jnp.float32
    )
    grad_operand = jnp.einsum(
        "tbj,bij->tbi", grad_middle, right_factor, preferred_element_type=jnp.float32
    )
    return (grad_operand.reshape(row_count, -1), grad_right, grad_left)


def roots(row_count, col_count, period):
    product = jnp.arange(row_count)[:, None] * jnp.arange(col_count)[None, :] % period
    angle = product.astype(jnp.float32) * (2.0 * math.pi / period)
    return (jnp.cos(angle), jnp.sin(angle))


def complex_step(real_part, imag_part, cos_table, sin_table, sign, form):
    real_out = jnp.einsum(form, real_part, cos_table, precision=highest) - sign * jnp.einsum(
        form, imag_part, sin_table, precision=highest
    )
    imag_out = jnp.einsum(form, imag_part, cos_table, precision=highest) + sign * jnp.einsum(
        form, real_part, sin_table, precision=highest
    )
    return (real_out, imag_out)


def real_step(real_part, cos_table, sin_table, sign, form):
    real_out = jnp.einsum(form, real_part, cos_table, precision=highest)
    imag_out = sign * jnp.einsum(form, real_part, sin_table, precision=highest)
    return (real_out, imag_out)


def twiddle(real_part, imag_part, cos_table, sin_table, sign):
    real_out = real_part * cos_table - sign * imag_part * sin_table
    imag_out = imag_part * cos_table + sign * real_part * sin_table
    return (real_out, imag_out)


def spectrum_of(real_part):
    total = real_part.shape[-1]
    first = math.gcd(total, 128)
    second = total // first
    leading = real_part.shape[:-1]
    real_part = real_part.reshape(leading + (first, second))
    cos_first, sin_first = roots(first, first, first)
    real_part, imag_part = real_step(real_part, cos_first, sin_first, -1.0, "...ab,ak->...kb")
    cos_twist, sin_twist = roots(first, second, total)
    real_part, imag_part = twiddle(real_part, imag_part, cos_twist, sin_twist, -1.0)
    cos_second, sin_second = roots(second, second, second)
    return complex_step(real_part, imag_part, cos_second, sin_second, -1.0, "...kb,bm->...km")


def signal_of(real_part, imag_part):
    first = real_part.shape[-2]
    second = real_part.shape[-1]
    total = first * second
    leading = real_part.shape[:-2]
    cos_second, sin_second = roots(second, second, second)
    real_part, imag_part = complex_step(
        real_part, imag_part, cos_second, sin_second, 1.0, "...kb,bm->...km"
    )
    cos_twist, sin_twist = roots(first, second, total)
    real_part, imag_part = twiddle(real_part, imag_part, cos_twist, sin_twist, 1.0)
    cos_first, sin_first = roots(first, first, first)
    real_part, imag_part = complex_step(
        real_part, imag_part, cos_first, sin_first, 1.0, "...ab,ak->...kb"
    )
    return real_part.reshape(leading + (total,)) / total


def filter_parts(filter_first, filter_second, third_cols, seq_length):
    total = 2 * seq_length
    index = jnp.arange(total)
    offset = jnp.where(index < seq_length, index, index - total).astype(jnp.float32)
    scaled = offset / seq_length
    features = jnp.stack(
        [
            scaled,
            jnp.sin(math.pi * scaled),
            jnp.cos(math.pi * scaled),
            jnp.sin(7.0 * math.pi * scaled),
            jnp.cos(7.0 * math.pi * scaled),
        ],
        axis=1,
    )
    pre_one = jnp.dot(features, filter_first, precision=highest)
    act_one = jnp.sin(pre_one)
    pre_two = jnp.dot(act_one, filter_second, precision=highest)
    act_two = jnp.sin(pre_two)
    tap_mask = (index != seq_length).astype(jnp.float32)[:, None] * seq_length ** (-0.5)
    taps = jnp.dot(act_two, third_cols, precision=highest) * tap_mask
    filt_real, filt_imag = spectrum_of(taps.T)
    return (features, pre_one, act_one, pre_two, act_two, tap_mask, filt_real, filt_imag)


def general_body(
    tokens,
    norm_gain,
    norm_bias,
    in_right,
    in_left,
    short_kernel,
    filter_first,
    filter_second,
    filter_third,
    conv_bias,
    out_right,
    out_left,
    ffn_gain,
    ffn_bias,
    gate_weight,
    up_weight,
    down_weight,
    cotangent,
):
    seq_count, pos_count, model_width = tokens.shape
    row_count = seq_count * pos_count
    axis_count = lax.axis_size("seq")
    my_index = lax.axis_index("seq")
    chan_count = model_width // axis_count
    seq_length = pos_count * axis_count
    part_rows = cotangent.shape[1]
    tp_index = lax.axis_index("tp")
    tp_count = lax.axis_size("tp")
    chan_start = my_index * chan_count
    mix_count = seq_count // tp_count
    mix_tokens = lax.dynamic_slice_in_dim(tokens, tp_index * mix_count, mix_count, 0)
    mix_rows = mix_count * pos_count
    flat = mix_tokens.reshape(mix_rows, model_width).astype(jnp.float32)
    normed, scaled_one, inverse_one = norm_forward(flat, norm_gain, norm_bias)
    normed_low = normed.astype(jnp.bfloat16)
    shuffled_in, projected = rows_monarch_forward(normed_low, in_right, in_left)
    projected_low = (
        projected.astype(jnp.bfloat16)
        .reshape(mix_count, pos_count, 3, model_width)
        .transpose(2, 3, 0, 1)
    )
    channels = lax.all_to_all(projected_low, "seq", split_axis=1, concat_axis=3, tiled=True)
    signals = channels.astype(jnp.float32)
    kernel = lax.dynamic_slice_in_dim(short_kernel, chan_start, chan_count, 1).astype(jnp.float32)
    tap_zero = kernel[:, :, 0][:, :, None, None]
    tap_one = kernel[:, :, 1][:, :, None, None]
    tap_two = kernel[:, :, 2][:, :, None, None]
    padded = jnp.pad(signals, ((0, 0), (0, 0), (0, 0), (1, 1)))
    shorted = padded[..., :-2] * tap_zero + padded[..., 1:-1] * tap_one + padded[..., 2:] * tap_two
    first_f = filter_first.astype(jnp.float32)
    second_f = filter_second.astype(jnp.float32)
    third_cols = lax.dynamic_slice_in_dim(filter_third, chan_start, chan_count, 1).astype(
        jnp.float32
    )
    kept = filter_parts(first_f, second_f, third_cols, seq_length)
    filt_real = kept[6][:, None]
    filt_imag = kept[7][:, None]
    bias_cols = lax.dynamic_slice_in_dim(conv_bias, chan_start, chan_count, 0)[:, None, None]
    product = shorted[0] * shorted[2]
    product_pad = jnp.pad(product, ((0, 0), (0, 0), (0, seq_length)))
    spec_real, spec_imag = spectrum_of(product_pad)
    conv_real = spec_real * filt_real - spec_imag * filt_imag
    conv_imag = spec_real * filt_imag + spec_imag * filt_real
    convolved = signal_of(conv_real, conv_imag)[..., :seq_length] + bias_cols * product
    mixed_low = (shorted[1] * convolved).astype(jnp.bfloat16)
    back_rows = lax.all_to_all(mixed_low, "seq", split_axis=2, concat_axis=0, tiled=True)
    mixed_rows = back_rows.transpose(1, 2, 0).reshape(mix_rows, model_width)
    shuffled_out, branch = rows_monarch_forward(mixed_rows, out_right, out_left)
    residual_mine = (flat + branch).reshape(mix_count, pos_count, model_width)
    residual = lax.all_gather(residual_mine, "tp", axis=0, tiled=True)
    part_resid = lax.dynamic_slice_in_dim(residual, tp_index * part_rows, part_rows, 1)
    normed_two, scaled_two, inverse_two = norm_forward(part_resid, ffn_gain, ffn_bias)
    normed_rows = lax.all_gather(normed_two.astype(jnp.bfloat16), "tp", axis=1, tiled=True).reshape(
        row_count, model_width
    )
    gate = jnp.dot(normed_rows, gate_weight, preferred_element_type=jnp.float32)
    upward = jnp.dot(normed_rows, up_weight, preferred_element_type=jnp.float32)
    sigma = jax.nn.sigmoid(gate)
    hidden_low = (gate * sigma * upward).astype(jnp.bfloat16)
    partial_down = jnp.dot(hidden_low, down_weight, preferred_element_type=jnp.float32).reshape(
        seq_count, pos_count, model_width
    )
    glu_part = lax.psum_scatter(
        partial_down.astype(jnp.bfloat16), "tp", scatter_dimension=1, tiled=True
    ).astype(jnp.float32)
    output = (part_resid + glu_part).astype(jnp.bfloat16)
    grad_out_rows = lax.all_gather(cotangent, "tp", axis=1, tiled=True).reshape(
        row_count, model_width
    )
    grad_hidden = jnp.dot(grad_out_rows, down_weight.T, preferred_element_type=jnp.float32)
    grad_gate = (grad_hidden * upward * (sigma + gate * sigma * (1.0 - sigma))).astype(jnp.bfloat16)
    grad_up = (grad_hidden * gate * sigma).astype(jnp.bfloat16)
    grad_down_w = jnp.dot(hidden_low.T, grad_out_rows, preferred_element_type=jnp.float32)
    grad_gate_w = jnp.dot(normed_rows.T, grad_gate, preferred_element_type=jnp.float32)
    grad_up_w = jnp.dot(normed_rows.T, grad_up, preferred_element_type=jnp.float32)
    grad_normed = jnp.dot(grad_gate, gate_weight.T, preferred_element_type=jnp.float32) + jnp.dot(
        grad_up, up_weight.T, preferred_element_type=jnp.float32
    )
    grad_normed_part = lax.psum_scatter(
        grad_normed.reshape(seq_count, pos_count, model_width),
        "tp",
        scatter_dimension=1,
        tiled=True,
    )
    grad_in_two, grad_gain_two, grad_bias_two = norm_backward(
        grad_normed_part, scaled_two, inverse_two, ffn_gain
    )
    gain_total = lax.psum((grad_gain_two, grad_bias_two), ("seq", "tp"))
    grad_resid_part = cotangent.astype(jnp.float32) + grad_in_two
    grad_resid = lax.all_gather(
        grad_resid_part.astype(jnp.bfloat16), "tp", axis=1, tiled=True
    ).astype(grad_resid_part.dtype)
    grad_resid_mix = lax.dynamic_slice_in_dim(
        grad_resid, tp_index * mix_count, mix_count, 0
    ).reshape(mix_rows, model_width)
    grad_mixed_rows, grad_out_right, grad_out_left = rows_monarch_backward(
        grad_resid_mix.astype(jnp.bfloat16), mixed_rows, shuffled_out, out_right, out_left
    )
    grad_mixed_low = (
        grad_mixed_rows.astype(jnp.bfloat16)
        .reshape(mix_count, pos_count, model_width)
        .transpose(2, 0, 1)
    )
    grad_mixed = lax.all_to_all(
        grad_mixed_low, "seq", split_axis=0, concat_axis=2, tiled=True
    ).astype(jnp.float32)
    grad_conv = grad_mixed * shorted[1]
    grad_key = grad_mixed * convolved
    again = lax.optimization_barrier((first_f, second_f, third_cols))
    kept = filter_parts(again[0], again[1], again[2], seq_length)
    filt_real = kept[6][:, None]
    filt_imag = kept[7][:, None]
    features, pre_one, act_one, pre_two, act_two, tap_mask = (
        kept[0],
        kept[1],
        kept[2],
        kept[3],
        kept[4],
        kept[5],
    )
    grad_pad = jnp.pad(grad_conv, ((0, 0), (0, 0), (0, seq_length)))
    grad_spec_real, grad_spec_imag = spectrum_of(grad_pad)
    back_real = grad_spec_real * filt_real + grad_spec_imag * filt_imag
    back_imag = grad_spec_imag * filt_real - grad_spec_real * filt_imag
    grad_product = signal_of(back_real, back_imag)[..., :seq_length] + bias_cols * grad_conv
    grad_bias_cols = jnp.sum(grad_conv * product, axis=(1, 2))
    taps_real = jnp.sum(grad_spec_real * spec_real + grad_spec_imag * spec_imag, axis=1)
    taps_imag = jnp.sum(grad_spec_imag * spec_real - grad_spec_real * spec_imag, axis=1)
    grad_taps = signal_of(taps_real, taps_imag)
    grad_pre = grad_taps.T * tap_mask
    grad_third_cols = jnp.dot(act_two.T, grad_pre, precision=highest)
    grad_pre_two = jnp.dot(grad_pre, third_cols.T, precision=highest) * jnp.cos(pre_two)
    grad_second = jnp.dot(act_one.T, grad_pre_two, precision=highest)
    grad_pre_one = jnp.dot(grad_pre_two, second_f.T, precision=highest) * jnp.cos(pre_one)
    grad_first = jnp.dot(features.T, grad_pre_one, precision=highest)
    grad_shorted = jnp.stack([grad_product * shorted[2], grad_key, grad_product * shorted[0]])
    grad_short_pad = jnp.pad(grad_shorted, ((0, 0), (0, 0), (0, 0), (1, 1)))
    grad_signals = (
        grad_short_pad[..., 2:] * tap_zero
        + grad_short_pad[..., 1:-1] * tap_one
        + grad_short_pad[..., :-2] * tap_two
    )
    grad_kernel = jnp.stack(
        [
            jnp.sum(grad_shorted * padded[..., :-2], axis=(2, 3)),
            jnp.sum(grad_shorted * padded[..., 1:-1], axis=(2, 3)),
            jnp.sum(grad_shorted * padded[..., 2:], axis=(2, 3)),
        ],
        axis=-1,
    )
    grad_proj = lax.all_to_all(
        grad_signals.astype(jnp.bfloat16), "seq", split_axis=3, concat_axis=1, tiled=True
    )
    grad_proj_rows = grad_proj.transpose(2, 3, 0, 1).reshape(mix_rows, 3 * model_width)
    grad_normed_one, grad_in_right, grad_in_left = rows_monarch_backward(
        grad_proj_rows, normed_low, shuffled_in, in_right, in_left
    )
    grad_in_one, grad_gain_one, grad_bias_one = norm_backward(
        grad_normed_one, scaled_one, inverse_one, norm_gain
    )
    grad_mine = (grad_resid_mix + grad_in_one).reshape(mix_count, pos_count, model_width)
    short_full = lax.dynamic_update_slice_in_dim(
        jnp.zeros(short_kernel.shape, jnp.float32), grad_kernel, chan_start, 1
    )
    third_full = lax.dynamic_update_slice_in_dim(
        jnp.zeros(filter_third.shape, jnp.float32), grad_third_cols, chan_start, 1
    )
    bias_full = lax.dynamic_update_slice_in_dim(
        jnp.zeros(conv_bias.shape, jnp.float32), grad_bias_cols, chan_start, 0
    )
    mixer_grads = (
        grad_gain_one,
        grad_bias_one,
        grad_in_right,
        grad_in_left,
        short_full,
        grad_first,
        grad_second,
        third_full,
        bias_full,
        grad_out_right,
        grad_out_left,
    )
    grad_tokens = lax.all_gather(grad_mine.astype(jnp.bfloat16), "tp", axis=0, tiled=True).astype(
        grad_mine.dtype
    )
    mixer_grads = (
        lax.psum(mixer_grads[0].astype(jnp.bfloat16), "tp").astype(jnp.float32),
        lax.psum(mixer_grads[1].astype(jnp.bfloat16), "tp").astype(jnp.float32),
        lax.psum(mixer_grads[2].astype(jnp.bfloat16), "tp").astype(jnp.float32),
        lax.psum(mixer_grads[3].astype(jnp.bfloat16), "tp").astype(jnp.float32),
        lax.psum(mixer_grads[4].astype(jnp.bfloat16), "tp").astype(jnp.float32),
        lax.psum(mixer_grads[5].astype(jnp.bfloat16), "tp").astype(jnp.float32),
        lax.psum(mixer_grads[6].astype(jnp.bfloat16), "tp").astype(jnp.float32),
        lax.psum(mixer_grads[7].astype(jnp.bfloat16), "tp").astype(jnp.float32),
        lax.psum(mixer_grads[8].astype(jnp.bfloat16), "tp").astype(jnp.float32),
        lax.psum(mixer_grads[9].astype(jnp.bfloat16), "tp").astype(jnp.float32),
        lax.psum(mixer_grads[10].astype(jnp.bfloat16), "tp").astype(jnp.float32),
    )
    all_total = lax.psum(
        (
            mixer_grads[0],
            mixer_grads[1],
            mixer_grads[2],
            mixer_grads[3],
            mixer_grads[4],
            mixer_grads[5],
            mixer_grads[6],
            mixer_grads[7],
            mixer_grads[8],
            mixer_grads[9],
            mixer_grads[10],
            grad_gate_w,
            grad_up_w,
            grad_down_w,
        ),
        "seq",
    )
    return (
        output,
        grad_tokens,
        all_total[0],
        all_total[1],
        all_total[2],
        all_total[3],
        all_total[4],
        all_total[5],
        all_total[6],
        all_total[7],
        all_total[8],
        all_total[9],
        all_total[10],
        gain_total[0],
        gain_total[1],
        all_total[11],
        all_total[12],
        all_total[13],
    )


def choose_body(mesh, *arrays):
    tokens = arrays[0]
    chans = tokens.shape[2] // mesh.shape["seq"]
    fits = mesh.shape["seq"] == 8 and mesh.shape["tp"] == 4 and tokens.shape[:2] == (4, 128) and chans == 96
    return (fast_body if fits else general_body)(*arrays)


def solution(mesh):
    mapped = jax.shard_map(
        functools.partial(choose_body, mesh),
        mesh=mesh,
        in_specs=(
            P(None, "seq", None),
            P(),
            P(),
            P(),
            P(),
            P(),
            P(),
            P(),
            P(),
            P(),
            P(),
            P(),
            P(),
            P(),
            P(None, "tp"),
            P(None, "tp"),
            P("tp", None),
            P(None, ("seq", "tp"), None),
        ),
        out_specs=(
            P(None, ("seq", "tp"), None),
            P(None, "seq", None),
            P(),
            P(),
            P(),
            P(),
            P(),
            P(),
            P(),
            P(),
            P(),
            P(),
            P(),
            P(),
            P(),
            P(None, "tp"),
            P(None, "tp"),
            P("tp", None),
        ),
        check_vma=False,
    )

    def program(*arrays):
        with jax.sharding.use_abstract_mesh(mesh.abstract_mesh):
            return mapped(*arrays)

    return program
```

```python
import functools
import math
import types
import typing

import numpy as np
import jax
import jax.numpy as jnp
from jax import lax
from jax.experimental import pallas as pl
from jax.experimental.pallas import tpu as pltpu
from jax.sharding import PartitionSpec as P

BF = jnp.bfloat16
F32 = jnp.float32
MESH = pl.DeviceIdType.MESH
NN = ((1,), (0,))
NT = ((1,), (1,))
TN = ((0,), (0,))
LIMIT = 56 * 1024 * 1024


def dot(first, second, form=NN):
    return lax.dot_general(first, second, (form, ((), ())), preferred_element_type=F32)


def any_spec():
    return pl.BlockSpec(memory_space=pl.ANY)


def vmem_spec():
    return pl.BlockSpec(memory_space=pltpu.VMEM)


def sin_cos(value):
    turns = jnp.floor(value * (1.0 / math.pi) + 0.5)
    rest = value - turns * 3.140625
    rest = rest - turns * 9.67502593994140625e-4
    rest = rest - turns * 1.509957990978376432e-7
    half = turns * 0.5
    sign = 1.0 - 4.0 * (half - jnp.floor(half))
    square = rest * rest
    sine = 1.0 / 362880 - square * (1.0 / 39916800)
    sine = -1.0 / 5040 + square * sine
    sine = 1.0 / 120 + square * sine
    sine = -1.0 / 6 + square * sine
    sine = rest + rest * square * sine
    cosine = 1.0 / 40320 - square * (1.0 / 3628800 - square * (1.0 / 479001600))
    cosine = -1.0 / 720 + square * cosine
    cosine = 1.0 / 24 + square * cosine
    cosine = -0.5 + square * cosine
    cosine = 1.0 + square * cosine
    return sign * sine, sign * cosine


def flip(index, bits):
    result = 0
    for place in range(3):
        digit = lax.rem(index // (1 << place), 2)
        if (bits >> place) & 1:
            digit = 1 - digit
        result = result + digit * (1 << place)
    return result


def greet(n_seq, n_tp):
    me, plane = lax.axis_index("seq"), lax.axis_index("tp")
    barrier = pltpu.get_barrier_semaphore()
    for k in range(1, n_seq):
        pl.semaphore_signal(barrier, inc=1, device_id={"seq": flip(me, k)}, device_id_type=MESH)
    for k in range(1, n_tp):
        pl.semaphore_signal(barrier, inc=1, device_id={"tp": flip(plane, k)}, device_id_type=MESH)
    return lambda: pl.semaphore_wait(barrier, n_seq + n_tp - 2)


def sign_rows(count, width):
    row = lax.broadcasted_iota(jnp.int32, (count, width), 0)
    return (1 - 2 * lax.rem(row, 2)).astype(F32)


def sign_lanes(count, width):
    lane = lax.broadcasted_iota(jnp.int32, (count, width), 1)
    return (1 - 2 * lax.rem(lane, 2)).astype(F32)


def previous(values):
    lane = lax.broadcasted_iota(jnp.int32, values.shape, 1)
    return jnp.where(lane == 0, 0.0, pltpu.roll(values, 1, 1))


def following(values):
    last = values.shape[1] - 1
    lane = lax.broadcasted_iota(jnp.int32, values.shape, 1)
    return jnp.where(lane == last, 0.0, pltpu.roll(values, last, 1))


def monarch_forward(load, right, left, shuffled, store):
    groups, width, _ = right.shape
    part = width // groups
    for b in range(groups):
        middle = dot(right[b], load(b), TN).astype(BF)
        for g in range(groups):
            shuffled[pl.ds(g * width + b * part, part), :] = middle[g * part : (g + 1) * part]
    for g in range(groups):
        store(g, dot(left[g], shuffled[pl.ds(g * width, width), :], TN))


SEQ_ORDER = (6, 7, 2, 3, 4, 5, 1)


def front_kernel(n_seq, n_tp, dims, *refs):
    (tokens, cotangent, table, gain, bias, right, left, short, conv_bias, features, first, second, third) = refs[:13]
    (mixed_out, signals_out, conv_out, wave_out, taps_out, nyquist_out, acts_out, normed_out, shuffled_out, cot_out,
     columns_out, third_out) = refs[13:25]
    (token_v, table_v, normed, shuffled, projected, signals, acts, spread, taps_v, padded, product, keyed, wave, spectrum, conv,
     mixed, mixed_rows, nyquist, totals, columns, tall, turned, third_v,
     local_sems, seq_send, seq_recv, back_send, back_recv, tp_send, tp_recv) = refs[25:]
    width, chans, length, rows = dims
    me, plane = lax.axis_index("seq"), lax.axis_index("tp")
    entered = greet(n_seq, n_tp)
    token_load = pltpu.make_async_copy(tokens.at[plane], token_v, local_sems.at[0])
    token_load.start()
    table_load = pltpu.make_async_copy(table, table_v, local_sems.at[1])
    table_load.start()
    token_load.wait()
    value = token_v[...].astype(F32)
    shifted = value - jnp.mean(value, axis=-1, keepdims=True)
    inverse = lax.rsqrt(jnp.mean(shifted * shifted, axis=-1, keepdims=True) + 1e-05)
    value = shifted * inverse * gain[...].reshape(1, width) + bias[...].reshape(1, width)
    normed[...] = value.T.astype(BF)
    groups = right.shape[0]
    block = width // groups
    fan = left.shape[2]

    def keep(g, result):
        projected[pl.ds(g * fan, fan), :] = result.astype(BF)

    monarch_forward(lambda b: normed[pl.ds(b * block, block), :], right, left, shuffled, keep)
    entered()
    sends = []
    mine = pl.ds(pl.multiple_of(me * rows, rows), rows)
    for k in SEQ_ORDER:
        other = flip(me, k)
        for s in range(3):
            copy = pltpu.make_async_remote_copy(
                src_ref=projected.at[pl.ds(pl.multiple_of(s * width + other * chans, 16), chans), :],
                dst_ref=signals.at[s, :, mine],
                send_sem=seq_send.at[k, s],
                recv_sem=seq_recv.at[k, s],
                device_id={"seq": other},
                device_id_type=MESH,
            )
            copy.start()
            sends.append(copy)
    for s in range(3):
        signals[s, :, mine] = projected[pl.ds(pl.multiple_of(s * width + me * chans, 16), chans), :]
    part = rows // n_tp
    spot = pl.ds(pl.multiple_of(plane * part, part), part)
    cot_copies = []
    for k in range(1, n_tp):
        copy = pltpu.make_async_remote_copy(
            src_ref=cotangent,
            dst_ref=cot_out.at[:, spot, :],
            send_sem=tp_send.at[k],
            recv_sem=tp_recv.at[k],
            device_id={"tp": flip(plane, k)},
            device_id_type=MESH,
        )
        copy.start()
        cot_copies.append(copy)
    own_cot = pltpu.make_async_copy(cotangent, cot_out.at[:, spot, :], local_sems.at[2])
    own_cot.start()
    out_copies = [
        pltpu.make_async_copy(normed, normed_out, local_sems.at[3]),
        pltpu.make_async_copy(shuffled, shuffled_out, local_sems.at[4]),
    ]
    for copy in out_copies:
        copy.start()

    own = pl.ds(pl.multiple_of(me * chans, 16), chans)
    lines = [short[s].astype(F32) for s in range(3)]
    lines += [conv_bias[...].reshape(1, width), jnp.zeros((6, width), F32)]
    tall[...] = jnp.concatenate(lines, axis=0).T
    columns[...] = tall[own, :]
    columns_out[...] = columns[...]
    turned[...] = third[...].T
    third_v[pl.ds(0, chans), :] = turned[own, :]
    third_v[pl.ds(chans, 128 - chans), :] = jnp.zeros((128 - chans, 128), BF)
    third_out[...] = third_v[...]
    lead = jnp.concatenate([first[...].astype(F32), jnp.zeros((3, 128), F32)], axis=0)
    lead = jnp.concatenate([lead, lead], axis=0).astype(BF)

    chunk = 256
    per = length // chunk
    totals[...] = jnp.zeros_like(totals)
    for half in range(2):

        def tap_step(at, carry, half=half):
            row = pl.multiple_of(half * length + at * chunk, chunk)
            here = pl.ds(row, chunk)
            sine, cosine = sin_cos(dot(features[here, :], lead))
            high = sine.astype(BF)
            acts[0, here, :] = high
            acts[1, here, :] = cosine.astype(BF)
            low = (sine - high.astype(F32)).astype(BF)
            sine, cosine = sin_cos(dot(high, second[...]) + dot(low, second[...]))
            high = sine.astype(BF)
            acts[2, here, :] = high
            acts[3, here, :] = cosine.astype(BF)
            taps = dot(high, third_v[...], NT) * (length**-0.5)
            if half == 1:
                index = lax.broadcasted_iota(jnp.int32, taps.shape, 0) + at * chunk
                taps = jnp.where(index == 0, 0.0, taps)
            totals[...] += jnp.sum(taps * sign_rows(*taps.shape), axis=0, keepdims=True)
            spread[pl.ds(pl.multiple_of(at * chunk, chunk), chunk), pl.ds(half * 128, 128)] = taps.astype(BF)
            return carry

        lax.fori_loop(0, per, tap_step, 0)
    acts_copy = pltpu.make_async_copy(acts, acts_out, local_sems.at[5])
    acts_copy.start()
    out_copies.append(acts_copy)
    table_load.wait()

    def spectrum_step(at, carry):
        here = pl.ds(pl.multiple_of(at * chunk, chunk), chunk)
        sign = sign_rows(chunk, 128)
        index = lax.broadcasted_iota(jnp.int32, (chunk, 128), 0) + at * chunk
        weight = jnp.where(index == 0, 0.5 / length, 1.0 / length)
        for which in range(2):
            result = dot(table_v[which, here, :], spread[...])
            taps_v[which, here, :] = ((result[:, :128] + sign * result[:, 128:]) * weight).astype(BF)
        return carry

    lax.fori_loop(0, per, spectrum_step, 0)
    copy = pltpu.make_async_copy(taps_v, taps_out, local_sems.at[6])
    copy.start()
    out_copies.append(copy)
    tap_total = jnp.broadcast_to(totals[...], (128, 128)).T[:chans, 0:1]

    for copy in sends:
        copy.wait_recv()
    copy = pltpu.make_async_copy(signals, signals_out, local_sems.at[7])
    copy.start()
    out_copies.append(copy)

    step = 16
    padded[pl.ds(chans, 128 - chans), :] = jnp.zeros((128 - chans, length), BF)

    def short_step(at, carry):
        here = pl.ds(pl.multiple_of(at * step, step), step)
        shorted = []
        for s in range(3):
            value = signals[s, here, :].astype(F32)
            shorted.append(
                previous(value) * columns[here, 3 * s : 3 * s + 1]
                + value * columns[here, 3 * s + 1 : 3 * s + 2]
                + following(value) * columns[here, 3 * s + 2 : 3 * s + 3]
            )
        result = shorted[0] * shorted[2]
        product[here, :] = result
        keyed[here, :] = shorted[1]
        padded[here, :] = result.astype(BF)
        nyquist[here, 0:1] = jnp.sum(result * sign_lanes(step, length), axis=1, keepdims=True)
        return carry

    lax.fori_loop(0, chans // step, short_step, 0)
    nyquist[:, 1:2] = tap_total

    def wave_step(at, carry):
        here = pl.ds(pl.multiple_of(at * chunk, chunk), chunk)
        cos_part = dot(table_v[0, here, :], padded[...], NT)
        sin_part = dot(table_v[1, here, :], padded[...], NT)
        wave[0, here, :] = cos_part.astype(BF)
        wave[1, here, :] = sin_part.astype(BF)
        tap_cos = taps_v[0, here, :].astype(F32)
        tap_sin = taps_v[1, here, :].astype(F32)
        spectrum[0, here, :] = (cos_part * tap_cos - sin_part * tap_sin).astype(BF)
        spectrum[1, here, :] = (cos_part * tap_sin + sin_part * tap_cos).astype(BF)
        return carry

    lax.fori_loop(0, per, wave_step, 0)

    def conv_step(at, carry):
        here = pl.ds(pl.multiple_of(at * chunk, chunk), chunk)
        result = dot(table_v[0, here, :], spectrum[0]) + dot(table_v[1, here, :], spectrum[1])
        result = result.T[:chans]
        result = (
            result
            + sign_lanes(chans, chunk) * (nyquist[:, 0:1] * nyquist[:, 1:2] * (0.5 / length))
            + columns[:, 9:10] * product[:, here]
        )
        conv[:, here] = result
        mixed[:, here] = (keyed[:, here] * result).astype(BF)
        return carry

    lax.fori_loop(0, per, conv_step, 0)
    backs = []
    slot = pl.ds(pl.multiple_of(me * chans, 16), chans)
    for k in SEQ_ORDER:
        other = flip(me, k)
        copy = pltpu.make_async_remote_copy(
            src_ref=mixed.at[:, pl.ds(pl.multiple_of(other * rows, rows), rows)],
            dst_ref=mixed_rows.at[slot, :],
            send_sem=back_send.at[k],
            recv_sem=back_recv.at[k],
            device_id={"seq": other},
            device_id_type=MESH,
        )
        copy.start()
        backs.append(copy)
    mixed_rows[slot, :] = mixed[:, mine]
    for at, pair in enumerate(((wave, wave_out), (conv, conv_out), (nyquist, nyquist_out))):
        copy = pltpu.make_async_copy(pair[0], pair[1], local_sems.at[8 + at])
        copy.start()
        out_copies.append(copy)
    for copy in sends:
        copy.wait_send()
    for copy in cot_copies:
        copy.wait()
    own_cot.wait()
    for copy in backs:
        copy.wait()
    mixed_out[...] = mixed_rows[...]
    for copy in out_copies:
        copy.wait()


def front(mesh_shape, *operands):
    n_seq, n_tp = mesh_shape
    _, rows, width = operands[0].shape
    chans, length = width // n_seq, rows * n_seq
    shape = jax.ShapeDtypeStruct
    return pl.pallas_call(
        functools.partial(front_kernel, n_seq, n_tp, (width, chans, length, rows)),
        out_shape=(
            shape((width, rows), BF),
            shape((3, chans, length), BF),
            shape((chans, length), F32),
            shape((2, length, 128), BF),
            shape((2, length, 128), BF),
            shape((chans, 128), F32),
            shape((4, 2 * length, 128), BF),
            shape((width, rows), BF),
            shape((width, rows), BF),
            shape((n_tp, rows, width), BF),
            shape((chans, 16), F32),
            shape((128, 128), BF),
        ),
        in_specs=[any_spec()] * 3 + [vmem_spec()] * 10,
        out_specs=(vmem_spec(),) + (any_spec(),) * 9 + (vmem_spec(),) * 2,
        scratch_shapes=[
            pltpu.VMEM((rows, width), BF),
            pltpu.VMEM((2, length, length), BF),
            pltpu.VMEM((width, rows), BF),
            pltpu.VMEM((width, rows), BF),
            pltpu.VMEM((3 * width, rows), BF),
            pltpu.VMEM((3, chans, length), BF),
            pltpu.VMEM((4, 2 * length, 128), BF),
            pltpu.VMEM((length, 256), BF),
            pltpu.VMEM((2, length, 128), BF),
            pltpu.VMEM((128, length), BF),
            pltpu.VMEM((chans, length), F32),
            pltpu.VMEM((chans, length), F32),
            pltpu.VMEM((2, length, 128), BF),
            pltpu.VMEM((2, length, 128), BF),
            pltpu.VMEM((chans, length), F32),
            pltpu.VMEM((chans, length), BF),
            pltpu.VMEM((width, rows), BF),
            pltpu.VMEM((chans, 128), F32),
            pltpu.VMEM((1, 128), F32),
            pltpu.VMEM((chans, 16), F32),
            pltpu.VMEM((width, 16), F32),
            pltpu.VMEM((width, 128), BF),
            pltpu.VMEM((128, 128), BF),
            pltpu.SemaphoreType.DMA((12,)),
            pltpu.SemaphoreType.DMA((n_seq, 3)),
            pltpu.SemaphoreType.DMA((n_seq, 3)),
            pltpu.SemaphoreType.DMA((n_seq,)),
            pltpu.SemaphoreType.DMA((n_seq,)),
            pltpu.SemaphoreType.DMA((n_tp,)),
            pltpu.SemaphoreType.DMA((n_tp,)),
        ],
        compiler_params=pltpu.CompilerParams(collective_id=0, has_side_effects=True, vmem_limit_bytes=LIMIT),
        name="front",
    )(*operands)


def split_table(values):
    high = values.astype(BF)
    low = (values - high.astype(np.float32)).astype(BF)
    return high, low


def constants(length):
    index = np.arange(length)
    angle = (index[:, None] * index[None, :] % (2 * length)) * (math.pi / length)
    table = np.stack([np.cos(angle), np.sin(angle)]).astype(np.float32).astype(BF)
    place = np.arange(2 * length)
    scaled = np.where(place < length, place, place - 2 * length) / length
    features = np.zeros((2 * length, 8), np.float32)
    features[:, 0] = scaled
    features[:, 1] = np.sin(math.pi * scaled)
    features[:, 2] = np.cos(math.pi * scaled)
    features[:, 3] = np.sin(7.0 * math.pi * scaled)
    features[:, 4] = np.cos(7.0 * math.pi * scaled)
    return table, np.concatenate(split_table(features), axis=1)


def monarch_backward(upstream, operand, shuffled, right, left, middle, keep_right, keep_left, store):
    groups, width, _ = right.shape
    part = width // groups
    for g in range(groups):
        above = upstream(g)
        keep_left(g, dot(shuffled[pl.ds(g * width, width), :], above, NT))
        below = dot(left[g], above).astype(BF)
        for b in range(groups):
            middle[pl.ds(b * width + g * part, part), :] = below[b * part : (b + 1) * part]
    for b in range(groups):
        above = middle[pl.ds(b * width, width), :]
        keep_right(b, dot(operand(b), above, NT))
        store(b, dot(right[b], above))


CHIPS = (6, 2, 4)


class Reduce:
    def __init__(self, n_seq, n_tp, own, full, core_in, halves, chip_in, quarter, plane_in, send, recv):
        self.own, self.full, self.core_in, self.halves = own, full, core_in, halves
        self.chip_in, self.quarter, self.plane_in = chip_in, quarter, plane_in
        self.send, self.recv, self.n_tp = send, recv, n_tp
        rows, width = own.shape
        self.rows, self.width = rows, width
        self.per_chip, self.per_plane = rows // (n_seq // 2), rows // (n_seq // 2) // n_tp
        self.me, self.plane = lax.axis_index("seq"), lax.axis_index("tp")
        core = lax.rem(self.me, 2)
        self.mine = pl.ds(pl.multiple_of(core * (width // 2), 128), width // 2)
        self.theirs = pl.ds(pl.multiple_of((1 - core) * (width // 2), 128), width // 2)
        self.started = []

    def chip_rows(self, index):
        return pl.ds(pl.multiple_of(index // 2 * self.per_chip, 16), self.per_chip)

    def copy(self, source, target, at, where):
        result = pltpu.make_async_remote_copy(
            src_ref=source, dst_ref=target, send_sem=self.send.at[at], recv_sem=self.recv.at[at],
            device_id=where, device_id_type=MESH,
        )
        result.start()
        self.started.append(result)
        return result

    def start_core(self):
        self.phase = [self.copy(self.own.at[:, self.theirs], self.core_in, 0, {"seq": flip(self.me, 1)})]

    def arrived(self):
        for copy in self.phase:
            copy.wait_recv()
        self.phase = []

    def start_chip(self):
        self.arrived()
        self.halves[...] = (self.own[:, self.mine].astype(F32) + self.core_in[...].astype(F32)).astype(BF)
        for k in CHIPS:
            other = flip(self.me, k)
            self.phase.append(
                self.copy(self.halves.at[self.chip_rows(other), :], self.chip_in.at[k // 2], k // 2, {"seq": other})
            )

    def start_plane(self):
        self.arrived()
        total = self.halves[self.chip_rows(self.me), :].astype(F32)
        for k in CHIPS:
            total = total + self.chip_in[k // 2].astype(F32)
        self.quarter[...] = total.astype(BF)
        for k in range(1, self.n_tp):
            other = flip(self.plane, k)
            here = pl.ds(pl.multiple_of(other * self.per_plane, 16), self.per_plane)
            self.phase.append(self.copy(self.quarter.at[here, :], self.plane_in.at[k], 3 + k, {"tp": other}))

    def start_plane_back(self):
        self.arrived()
        here = pl.ds(pl.multiple_of(self.plane * self.per_plane, 16), self.per_plane)
        total = self.quarter[here, :].astype(F32)
        for k in range(1, self.n_tp):
            total = total + self.plane_in[k].astype(F32)
        rows = pl.ds(
            pl.multiple_of(self.me // 2 * self.per_chip + self.plane * self.per_plane, 16), self.per_plane
        )
        self.full[rows, self.mine] = total.astype(BF)
        spot = self.full.at[rows, self.mine]
        for k in range(1, self.n_tp):
            self.phase.append(self.copy(spot, spot, 6 + k, {"tp": flip(self.plane, k)}))

    def start_chip_back(self):
        self.arrived()
        spot = self.full.at[self.chip_rows(self.me), self.mine]
        for k in CHIPS:
            self.phase.append(self.copy(spot, spot, 9 + k // 2, {"seq": flip(self.me, k)}))

    def start_core_back(self):
        self.arrived()
        spot = self.full.at[:, self.mine]
        self.phase.append(self.copy(spot, spot, 13, {"seq": flip(self.me, 1)}))

    def finish(self):
        self.arrived()
        for copy in self.started:
            copy.wait_send()


def neighbour_order(plane, at):
    upper = plane // 2
    near = plane + upper * (3 - 2 * plane)
    result = at * (1 - near) + (0, 0, 2, 3)[at] * near
    return result + upper * (3 - 2 * result)


class Line:
    def __init__(self, n_tp, slots, send, recv):
        self.n_tp, self.slots, self.send, self.recv = n_tp, slots, send, recv
        self.plane = lax.axis_index("tp")
        self.sent = []

    def copy(self, block, source, way):
        return pltpu.make_async_remote_copy(
            src_ref=source, dst_ref=self.slots.at[block], send_sem=self.send.at[way, block], recv_sem=self.recv.at[block],
            device_id={"tp": self.plane + (1, -1)[way]}, device_id_type=MESH,
        )

    def start(self, block, source, way, here):
        @pl.when(here)
        def _():
            self.copy(block, source, way).start()

        self.sent.append((block, source, way, here))

    def begin(self, source):
        self.start(self.plane, source, 0, self.plane < self.n_tp - 1)
        self.start(self.plane, source, 1, self.plane > 0)

    def take(self, block):
        pltpu.make_async_remote_copy(
            src_ref=self.slots.at[block], dst_ref=self.slots.at[block], send_sem=self.send.at[0, block],
            recv_sem=self.recv.at[block], device_id={"tp": block}, device_id_type=MESH,
        ).wait_recv()
        source = self.slots.at[block]
        self.start(block, source, 0, jnp.logical_and(block < self.plane, self.plane < self.n_tp - 1))
        self.start(block, source, 1, jnp.logical_and(block > self.plane, self.plane > 0))

    def finish(self):
        for block, source, way, here in self.sent:

            @pl.when(here)
            def _(block=block, source=source, way=way):
                self.copy(block, source, way).wait_send()


class Square:
    def __init__(self, own, full, core_in, half, first_in, second_in, send, recv):
        self.own, self.full, self.core_in, self.half = own, full, core_in, half
        self.first_in, self.second_in, self.send, self.recv = first_in, second_in, send, recv
        me = lax.axis_index("seq")
        self.me = me
        rows = own.shape[0]
        self.rows = rows
        self.core = lax.rem(me, 2)
        y, x = me // 4, lax.rem(me // 2, 2)
        quarter, part = rows // 8, rows // 16
        base = rows // 4
        self.ways = ((2, x, y, 0), (4, y, x, base))
        self.quarter, self.part = quarter, part
        self.started = []
        self.phase = []

    def copy(self, source, target, at, k):
        result = pltpu.make_async_remote_copy(
            src_ref=source, dst_ref=target, send_sem=self.send.at[at], recv_sem=self.recv.at[at],
            device_id={"seq": flip(self.me, k)}, device_id_type=MESH,
        )
        result.start()
        self.started.append(result)
        self.phase.append(result)

    def arrived(self):
        for copy in self.phase:
            copy.wait_recv()
        self.phase = []

    def span(self, start, size):
        return pl.ds(pl.multiple_of(start, 16), size)

    def start_core(self):
        half = self.rows // 2
        self.copy(self.own.at[self.span((1 - self.core) * half, half), :], self.core_in, 0, 1)

    def start_first(self):
        self.arrived()
        half = self.rows // 2
        own = self.own[self.span(self.core * half, half), :]
        self.half[...] = (own.astype(F32) + self.core_in[...].astype(F32)).astype(BF)
        for way, (k, near, far, base) in enumerate(self.ways):
            source = self.half.at[self.span(base + (1 - near) * self.quarter, self.quarter), :]
            self.copy(source, self.first_in.at[way], 1 + way, k)

    def start_second(self):
        self.arrived()
        for way, (k, near, far, base) in enumerate(self.ways):
            here = self.span(base + near * self.quarter, self.quarter)
            self.half[here, :] = (self.half[here, :].astype(F32) + self.first_in[way].astype(F32)).astype(BF)
            source = self.half.at[self.span(base + near * self.quarter + (1 - far) * self.part, self.part), :]
            self.copy(source, self.second_in.at[way], 3 + way, 6 - k)

    def start_second_back(self):
        self.arrived()
        for way, (k, near, far, base) in enumerate(self.ways):
            place = base + near * self.quarter + far * self.part
            total = self.half[self.span(place, self.part), :].astype(F32) + self.second_in[way].astype(F32)
            here = self.span(self.core * (self.rows // 2) + place, self.part)
            self.full[here, :] = total.astype(BF)
            spot = self.full.at[here, :]
            self.copy(spot, spot, 5 + way, 6 - k)

    def start_first_back(self):
        self.arrived()
        for way, (k, near, far, base) in enumerate(self.ways):
            spot = self.full.at[self.span(self.core * (self.rows // 2) + base + near * self.quarter, self.quarter), :]
            self.copy(spot, spot, 7 + way, k)

    def start_core_back(self):
        self.arrived()
        spot = self.full.at[self.span(self.core * (self.rows // 2), self.rows // 2), :]
        self.copy(spot, spot, 9, 1)

    def finish(self):
        for copy in self.started:
            copy.wait_send()


class Inputs(typing.NamedTuple):
    mixed: typing.Any
    feed_gain: typing.Any
    feed_bias: typing.Any
    out_right: typing.Any
    out_left: typing.Any
    columns: typing.Any
    gain: typing.Any
    in_right: typing.Any
    in_left: typing.Any
    second: typing.Any
    third: typing.Any
    nyquist: typing.Any
    features: typing.Any
    cot_rows: typing.Any
    tokens: typing.Any
    gate_w: typing.Any
    up_w: typing.Any
    down_w: typing.Any
    table: typing.Any
    signals_in: typing.Any
    conv_in: typing.Any
    wave_in: typing.Any
    taps_in: typing.Any
    acts_in: typing.Any
    normed_in: typing.Any
    shuffled_in: typing.Any


class Outputs(typing.NamedTuple):
    output_out: typing.Any
    ffn_out: typing.Any
    tokens_out: typing.Any
    late_out: typing.Any
    early_out: typing.Any
    small_out: typing.Any


def core_scratch(n_seq, n_tp, width, chans, length, rows):
    result = dict(
        token_v=pltpu.VMEM((rows, width), BF),
        cot_v=pltpu.VMEM((n_tp, rows, width), BF),
        gate_v=pltpu.VMEM((width, width), BF),
        up_v=pltpu.VMEM((width, width), BF),
        down_v=pltpu.VMEM((width, width), BF),
        out_shuffled=pltpu.VMEM((width, rows), BF),
        branch=pltpu.VMEM((width, rows), F32),
        resid=pltpu.VMEM((rows, width), F32),
        scaled=pltpu.VMEM((rows, width), F32),
        inverse=pltpu.VMEM((rows, 1), F32),
        normed=pltpu.VMEM((n_tp, rows, width), BF),
        hidden=pltpu.VMEM((n_tp, rows, width), BF),
        grad_hidden=pltpu.VMEM((n_tp, rows, width), F32),
        grad_gate=pltpu.VMEM((n_tp, rows, width), BF),
        grad_up=pltpu.VMEM((n_tp, rows, width), BF),
        grad_normed=pltpu.VMEM((rows, width), F32),
        grad_send=pltpu.VMEM((n_tp, rows, width), BF),
        grad_recv=pltpu.VMEM((n_tp, rows, width), BF),
        glu_own=pltpu.VMEM((rows, width), F32),
        glu_send=pltpu.VMEM((n_tp, rows, width), BF),
        glu_recv=pltpu.VMEM((n_tp, rows, width), BF),
        turned=pltpu.VMEM((width, n_tp*rows), BF),
        grads=pltpu.VMEM((3, width, width), BF),
        ffn_v=pltpu.VMEM((3, width, width), BF),
        core_in=pltpu.VMEM((3, width//2, width), BF),
        halves=pltpu.VMEM((3, width//2, width), BF),
        first_in=pltpu.VMEM((3, 2, width//8, width), BF),
        second_in=pltpu.VMEM((3, 2, width//16, width), BF),
        grad_branch=pltpu.VMEM((width, rows), BF),
        middle=pltpu.VMEM((width, rows), BF),
        grad_mixed_own=pltpu.VMEM((width, rows), BF),
        grad_mixed=pltpu.VMEM((chans, length), BF),
        out_rows=pltpu.VMEM((rows, width), BF),
        output_v=pltpu.VMEM((n_tp, rows//n_tp, width), BF),
        grad_vectors=pltpu.VMEM((2, width), F32),
        grad_resid=pltpu.VMEM((rows, width), F32),
        table_v=pltpu.VMEM((2, length, length), BF),
        signals=pltpu.VMEM((3, chans, length), BF),
        conv=pltpu.VMEM((chans, length), F32),
        wave=pltpu.VMEM((2, length, 128), BF),
        taps_v=pltpu.VMEM((2, length, 128), BF),
        acts=pltpu.VMEM((4, 2*length, 128), BF),
        in_normed=pltpu.VMEM((width, rows), BF),
        in_shuffled=pltpu.VMEM((width, rows), BF),
        grad_short=pltpu.VMEM((3, chans, length), F32),
        query=pltpu.VMEM((chans, length), F32),
        value_v=pltpu.VMEM((chans, length), F32),
        grad_conv=pltpu.VMEM((chans, length), F32),
        padded=pltpu.VMEM((128, length), BF),
        back_wave=pltpu.VMEM((2, length, 128), BF),
        cross=pltpu.VMEM((2, length, 256), BF),
        sums=pltpu.VMEM((128, 128), F32),
        grad_signals=pltpu.VMEM((3, chans, length), BF),
        grad_proj=pltpu.VMEM((3*width, rows), BF),
        grad_rows=pltpu.VMEM((width, rows), F32),
        grad_tok=pltpu.VMEM((rows, width), BF),
        grad_second=pltpu.VMEM((128, 128), F32),
        grad_first=pltpu.VMEM((16, 128), F32),
        grad_third=pltpu.VMEM((128, 128), F32),
        local_sems=pltpu.SemaphoreType.DMA((20,)),
        line_send=pltpu.SemaphoreType.DMA((2,n_tp)),
        line_recv=pltpu.SemaphoreType.DMA((n_tp,)),
        tok_send=pltpu.SemaphoreType.DMA((2,n_tp)),
        tok_recv=pltpu.SemaphoreType.DMA((n_tp,)),
        back_send=pltpu.SemaphoreType.DMA((n_tp,)),
        back_recv=pltpu.SemaphoreType.DMA((n_tp,)),
        glu_ssem=pltpu.SemaphoreType.DMA((n_tp,)),
        glu_rsem=pltpu.SemaphoreType.DMA((n_tp,)),
        out_send=pltpu.SemaphoreType.DMA((n_tp,)),
        out_recv=pltpu.SemaphoreType.DMA((n_tp,)),
        mixed_send=pltpu.SemaphoreType.DMA((n_seq,)),
        mixed_recv=pltpu.SemaphoreType.DMA((n_seq,)),
        seq_send=pltpu.SemaphoreType.DMA((n_seq,3)),
        seq_recv=pltpu.SemaphoreType.DMA((n_seq,3)),
        ffn_send=pltpu.SemaphoreType.DMA((3,10)),
        ffn_recv=pltpu.SemaphoreType.DMA((3,10)),
        late_own=pltpu.VMEM((width, width), BF),
        late_full=pltpu.VMEM((width, width), BF),
        early_own=pltpu.VMEM((width, 512), BF),
        early_full=pltpu.VMEM((width, 512), BF),
        small_own=pltpu.VMEM((256, 256), BF),
        small_full=pltpu.VMEM((256, 256), BF),
    )
    groups = []
    for count, breadth in ((256, width), (256, width), (256, width), (width, 512), (256, 256)):
        half, chip = breadth // 2, count // (n_seq // 2)
        groups.append(
            [
                pltpu.VMEM((count, half), BF),
                pltpu.VMEM((count, half), BF),
                pltpu.VMEM((n_seq // 2, chip, half), BF),
                pltpu.VMEM((chip, half), BF),
                pltpu.VMEM((n_tp, chip // n_tp, half), BF),
                pltpu.SemaphoreType.DMA((14,)),
                pltpu.SemaphoreType.DMA((14,)),
            ]
        )
    return result, groups


def core_kernel(n_seq, n_tp, dims, *refs):
    width, chans, length, rows = dims
    scratch, groups = core_scratch(n_seq, n_tp, width, chans, length, rows)
    named = dict(zip(Inputs._fields + Outputs._fields + tuple(scratch), refs))
    r = types.SimpleNamespace(**named)
    spare = list(refs[len(named) :])
    reduce_refs = [[spare.pop(0) for _ in group] for group in groups]
    me, plane = lax.axis_index("seq"), lax.axis_index("tp")
    entered = greet(n_seq, n_tp)
    sources = dict(
        token=(r.tokens.at[plane], r.token_v),
        cot=(r.cot_rows, r.cot_v),
        down=(r.down_w, r.down_v),
        gate=(r.gate_w, r.gate_v),
        up=(r.up_w, r.up_v),
        signals=(r.signals_in, r.signals),
        conv=(r.conv_in, r.conv),
        table=(r.table, r.table_v),
        wave=(r.wave_in, r.wave),
        taps=(r.taps_in, r.taps_v),
        acts=(r.acts_in, r.acts),
        normed=(r.normed_in, r.in_normed),
        shuffled=(r.shuffled_in, r.in_shuffled),
    )
    copies = {
        name: pltpu.make_async_copy(*pair, r.local_sems.at[at]) for at, (name, pair) in enumerate(sources.items())
    }
    for copy in copies.values():
        copy.start()
    loads = types.SimpleNamespace(**copies)
    _, block, _ = r.out_right.shape
    chunk = 256
    pieces = width // chunk
    per = length // chunk
    step = 16

    lates = []
    for at in range(3):
        here = pl.ds(256 * at, 256)
        lates.append(Reduce(n_seq, n_tp, r.late_own.at[here, :], r.late_full.at[here, :], *reduce_refs[at]))
    early = Reduce(n_seq, n_tp, r.early_own, r.early_full, *reduce_refs[3])
    small = Reduce(n_seq, n_tp, r.small_own, r.small_full, *reduce_refs[4])
    squares = [
        Square(
            r.grads.at[which], r.ffn_v.at[which], r.core_in.at[which], r.halves.at[which], r.first_in.at[which],
            r.second_in.at[which], r.ffn_send.at[which], r.ffn_recv.at[which],
        )
        for which in range(3)
    ]

    def keep_branch(g, result):
        r.branch[pl.ds(g * block, block), :] = result

    monarch_forward(lambda b: r.mixed[pl.ds(b * block, block), :], r.out_right, r.out_left, r.out_shuffled, keep_branch)
    loads.token.wait()
    tokens = r.token_v[...].astype(F32)
    value = tokens + r.branch[...].T
    r.resid[...] = value
    shifted = value - jnp.mean(value, axis=-1, keepdims=True)
    r.inverse[...] = lax.rsqrt(jnp.mean(shifted * shifted, axis=-1, keepdims=True) + 1e-05)
    value = shifted * r.inverse[...]
    r.scaled[...] = value
    r.normed[plane] = (value * r.feed_gain[...].reshape(1, width) + r.feed_bias[...].reshape(1, width)).astype(BF)
    entered()
    line = Line(n_tp, r.normed, r.line_send, r.line_recv)
    line.begin(r.normed.at[plane])
    loads.cot.wait()
    loads.down.wait()

    def hidden_step(at, carry):
        cols = pl.ds(pl.multiple_of(at * chunk, chunk), chunk)
        result = dot(r.cot_v[...].reshape(n_tp * rows, width), r.down_v[cols, :], NT)
        r.grad_hidden[:, :, cols] = result.reshape(n_tp, rows, chunk)
        return carry

    lax.fori_loop(0, pieces, hidden_step, 0)
    loads.gate.wait()
    loads.up.wait()
    backs = []
    for k in range(n_tp):
        other = plane if k == 0 else neighbour_order(plane, k)
        if k > 0:
            line.take(other)

        def gate_step(at, carry, other=other):
            cols = pl.ds(pl.multiple_of(at * chunk, chunk), chunk)
            value = r.normed[other]
            gate = dot(value, r.gate_v[:, cols])
            upward = dot(value, r.up_v[:, cols])
            sigma = 1.0 / (1.0 + jnp.exp(-gate))
            active = gate * sigma
            r.hidden[other, :, cols] = (active * upward).astype(BF)
            above = r.grad_hidden[other, :, cols]
            r.grad_gate[other, :, cols] = (above * upward * (sigma + active * (1.0 - sigma))).astype(BF)
            r.grad_up[other, :, cols] = (above * active).astype(BF)
            return carry

        lax.fori_loop(0, pieces, gate_step, 0)

        def back_step(at, carry, k=k, other=other):
            cols = pl.ds(pl.multiple_of(at * chunk, chunk), chunk)
            result = dot(r.grad_gate[other], r.gate_v[cols, :], NT) + dot(r.grad_up[other], r.up_v[cols, :], NT)
            if k == 0:
                r.grad_normed[:, cols] = result
            else:
                r.grad_send[other, :, cols] = result.astype(BF)
            return carry

        lax.fori_loop(0, pieces, back_step, 0)
        if k > 0:
            copy = pltpu.make_async_remote_copy(
                src_ref=r.grad_send.at[other],
                dst_ref=r.grad_recv.at[plane],
                send_sem=r.back_send.at[other],
                recv_sem=r.back_recv.at[plane],
                device_id={"tp": other},
                device_id_type=MESH,
            )
            copy.start()
            backs.append(copy)

    def turn(source):
        for s in range(n_tp):
            r.turned[:, s * rows : (s + 1) * rows] = source[s].T

    def weight_grad(which, factor):
        def grad_step(at, carry):
            here = pl.ds(pl.multiple_of(at * chunk, chunk), chunk)
            result = dot(r.turned[here, :], factor[...].reshape(n_tp * rows, width))
            r.grads[which, here, :] = result.astype(BF)
            return carry

        lax.fori_loop(0, pieces, grad_step, 0)
        squares[which].start_core()

    turn(r.normed)
    weight_grad(0, r.grad_gate)
    weight_grad(1, r.grad_up)
    squares[0].start_first()
    turn(r.hidden)
    weight_grad(2, r.cot_v)
    squares[1].start_first()
    squares[2].start_first()

    def from_planes(recv, slots):
        total = 0.0
        for k in range(1, n_tp):
            other = flip(plane, k)
            pltpu.make_async_remote_copy(
                src_ref=slots.at[other], dst_ref=slots.at[other], send_sem=recv.at[other], recv_sem=recv.at[other],
                device_id={"tp": other}, device_id_type=MESH,
            ).wait_recv()
            total = total + slots[other].astype(F32)
        return total

    total = r.grad_normed[...] + from_planes(r.back_recv, r.grad_recv)
    value = r.scaled[...]
    r.grad_vectors[0:1, :] = jnp.sum(total * value, axis=0, keepdims=True)
    r.grad_vectors[1:2, :] = jnp.sum(total, axis=0, keepdims=True)
    total = total * r.feed_gain[...].reshape(1, width)
    first_mean = jnp.mean(total, axis=-1, keepdims=True)
    second_mean = jnp.mean(total * value, axis=-1, keepdims=True)
    total = r.cot_v[plane].astype(F32) + r.inverse[...] * (total - first_mean - value * second_mean)
    r.grad_resid[...] = total
    r.grad_branch[...] = total.T.astype(BF)
    out_parts = {}

    def keep_out_left(g, result):
        out_parts[g] = result.astype(BF)

    def keep_out_right(b, result):
        both = jnp.concatenate([result.astype(BF), out_parts[b]], axis=1)
        r.early_own[pl.ds(b * block, block), 0 : 2 * block] = both

    def keep_mixed(b, result):
        r.grad_mixed_own[pl.ds(b * block, block), :] = result.astype(BF)

    monarch_backward(
        lambda g: r.grad_branch[pl.ds(g * block, block), :],
        lambda b: r.mixed[pl.ds(b * block, block), :],
        r.out_shuffled, r.out_right, r.out_left, r.middle, keep_out_right, keep_out_left, keep_mixed,
    )
    mine = pl.ds(pl.multiple_of(me * rows, rows), rows)
    own_chans = pl.ds(pl.multiple_of(me * chans, 16), chans)
    mixed_copies = []
    for k in SEQ_ORDER:
        other = flip(me, k)
        copy = pltpu.make_async_remote_copy(
            src_ref=r.grad_mixed_own.at[pl.ds(pl.multiple_of(other * chans, 16), chans), :],
            dst_ref=r.grad_mixed.at[:, mine],
            send_sem=r.mixed_send.at[k],
            recv_sem=r.mixed_recv.at[k],
            device_id={"seq": other},
            device_id_type=MESH,
        )
        copy.start()
        mixed_copies.append(copy)
    r.grad_mixed[:, mine] = r.grad_mixed_own[own_chans, :]
    squares[0].start_second()

    glus = []
    for k in range(n_tp):
        other = plane if k == 0 else neighbour_order(plane, n_tp - k)

        def glu_step(at, carry, k=k, other=other):
            cols = pl.ds(pl.multiple_of(at * chunk, chunk), chunk)
            result = dot(r.hidden[other], r.down_v[:, cols])
            if k == 0:
                r.glu_own[:, cols] = result
            else:
                r.glu_send[other, :, cols] = result.astype(BF)
            return carry

        lax.fori_loop(0, pieces, glu_step, 0)
        if k > 0:
            copy = pltpu.make_async_remote_copy(
                src_ref=r.glu_send.at[other],
                dst_ref=r.glu_recv.at[plane],
                send_sem=r.glu_ssem.at[other],
                recv_sem=r.glu_rsem.at[plane],
                device_id={"tp": other},
                device_id_type=MESH,
            )
            copy.start()
            glus.append(copy)
    squares[1].start_second()
    r.sums[...] = jnp.zeros_like(r.sums)
    r.small_own[...] = jnp.zeros_like(r.small_own)
    r.early_own[:, 384:512] = jnp.zeros((width, 128), BF)
    r.padded[pl.ds(chans, 128 - chans), :] = jnp.zeros((128 - chans, length), BF)
    loads.signals.wait()
    loads.conv.wait()
    for copy in mixed_copies:
        copy.wait_recv()

    def short_step(at, carry):
        here = pl.ds(pl.multiple_of(at * step, step), step)
        shorted = []
        for s in range(3):
            value = r.signals[s, here, :].astype(F32)
            shorted.append(
                previous(value) * r.columns[here, 3 * s : 3 * s + 1]
                + value * r.columns[here, 3 * s + 1 : 3 * s + 2]
                + following(value) * r.columns[here, 3 * s + 2 : 3 * s + 3]
            )
        r.query[here, :] = shorted[0]
        r.value_v[here, :] = shorted[2]
        above = r.grad_mixed[here, :].astype(F32)
        r.grad_short[1, here, :] = above * r.conv[here, :]
        above = above * shorted[1]
        r.grad_conv[here, :] = above
        r.padded[here, :] = above.astype(BF)
        r.sums[here, 9:10] = jnp.sum(above * shorted[0] * shorted[2], axis=1, keepdims=True)
        r.sums[here, 10:11] = jnp.sum(above * sign_lanes(step, length), axis=1, keepdims=True)
        return carry

    lax.fori_loop(0, chans // step, short_step, 0)
    for copy in (loads.table, loads.wave, loads.taps):
        copy.wait()
    squares[2].start_second()

    def wave_step(at, carry):
        here = pl.ds(pl.multiple_of(at * chunk, chunk), chunk)
        sign = sign_rows(chunk, 128)
        index = lax.broadcasted_iota(jnp.int32, (chunk, 128), 0) + at * chunk
        weight = jnp.where(index == 0, 0.5 / length, 1.0 / length)
        cos_part = dot(r.table_v[0, here, :], r.padded[...], NT)
        sin_part = dot(r.table_v[1, here, :], r.padded[...], NT)
        tap_cos = r.taps_v[0, here, :].astype(F32)
        tap_sin = r.taps_v[1, here, :].astype(F32)
        r.back_wave[0, here, :] = (cos_part * tap_cos + sin_part * tap_sin).astype(BF)
        r.back_wave[1, here, :] = (sin_part * tap_cos - cos_part * tap_sin).astype(BF)
        wave_cos = r.wave[0, here, :].astype(F32) * weight
        wave_sin = r.wave[1, here, :].astype(F32) * weight
        result = cos_part * wave_cos + sin_part * wave_sin
        r.cross[0, here, 0:128] = result.astype(BF)
        r.cross[0, here, 128:256] = (result * sign).astype(BF)
        result = sin_part * wave_cos - cos_part * wave_sin
        r.cross[1, here, 0:128] = result.astype(BF)
        r.cross[1, here, 128:256] = (result * sign).astype(BF)
        return carry

    lax.fori_loop(0, per, wave_step, 0)
    squares[0].start_second_back()
    squares[1].start_second_back()

    def product_step(at, carry):
        here = pl.ds(pl.multiple_of(at * chunk, chunk), chunk)
        result = dot(r.table_v[0, here, :], r.back_wave[0]) + dot(r.table_v[1, here, :], r.back_wave[1])
        result = (
            result.T[:chans]
            + sign_lanes(chans, chunk) * (r.sums[:chans, 10:11] * r.nyquist[:, 1:2] * (0.5 / length))
            + r.columns[:, 9:10] * r.grad_conv[:, here]
        )
        r.grad_short[0, :, here] = result * r.value_v[:, here]
        r.grad_short[2, :, here] = result * r.query[:, here]
        return carry

    lax.fori_loop(0, per, product_step, 0)

    def signal_step(at, carry):
        here = pl.ds(pl.multiple_of(at * step, step), step)
        for s in range(3):
            above = r.grad_short[s, here, :]
            value = r.signals[s, here, :].astype(F32)
            before, after = previous(above), following(above)
            r.grad_signals[s, here, :] = (
                after * r.columns[here, 3 * s : 3 * s + 1]
                + above * r.columns[here, 3 * s + 1 : 3 * s + 2]
                + before * r.columns[here, 3 * s + 2 : 3 * s + 3]
            ).astype(BF)
            r.sums[here, 3 * s : 3 * s + 1] = jnp.sum(after * value, axis=1, keepdims=True)
            r.sums[here, 3 * s + 1 : 3 * s + 2] = jnp.sum(above * value, axis=1, keepdims=True)
            r.sums[here, 3 * s + 2 : 3 * s + 3] = jnp.sum(before * value, axis=1, keepdims=True)
        return carry

    lax.fori_loop(0, chans // step, signal_step, 0)
    seq_copies = []
    for k in SEQ_ORDER:
        other = flip(me, k)
        for s in range(3):
            copy = pltpu.make_async_remote_copy(
                src_ref=r.grad_signals.at[s, :, pl.ds(pl.multiple_of(other * rows, rows), rows)],
                dst_ref=r.grad_proj.at[pl.ds(pl.multiple_of(s * width + me * chans, 16), chans), :],
                send_sem=r.seq_send.at[k, s],
                recv_sem=r.seq_recv.at[k, s],
                device_id={"seq": other},
                device_id_type=MESH,
            )
            copy.start()
            seq_copies.append(copy)
    for s in range(3):
        r.grad_proj[pl.ds(pl.multiple_of(s * width + me * chans, 16), chans), :] = r.grad_signals[s, :, mine]
    squares[2].start_second_back()

    total = r.resid[...] + r.glu_own[...] + from_planes(r.glu_rsem, r.glu_recv)
    r.out_rows[...] = total.astype(BF)
    part = rows // n_tp
    out_copies = []
    for k in range(1, n_tp):
        other = flip(plane, k)
        copy = pltpu.make_async_remote_copy(
            src_ref=r.out_rows.at[pl.ds(pl.multiple_of(other * part, part), part), :],
            dst_ref=r.output_v.at[plane],
            send_sem=r.out_send.at[k],
            recv_sem=r.out_recv.at[k],
            device_id={"tp": other},
            device_id_type=MESH,
        )
        copy.start()
        out_copies.append(copy)
    r.output_v[plane] = r.out_rows[pl.ds(pl.multiple_of(plane * part, part), part), :]

    loads.acts.wait()
    tap_total = jnp.broadcast_to(r.sums[:, 10:11], (128, 128)).T[0:1, :]
    pad_nyquist = jnp.concatenate([r.nyquist[:, 0:1], jnp.zeros((128 - chans, 1), F32)], axis=0)
    tap_total = tap_total * jnp.broadcast_to(pad_nyquist, (128, 128)).T[0:1, :] * (0.5 / length)
    r.grad_second[...] = jnp.zeros_like(r.grad_second)
    r.grad_first[...] = jnp.zeros_like(r.grad_first)
    r.grad_third[...] = jnp.zeros_like(r.grad_third)

    def filter_step(at, carry):
        here = pl.ds(pl.multiple_of(at * chunk, chunk), chunk)
        result = dot(r.table_v[0, here, :], r.cross[0]) + dot(r.table_v[1, here, :], r.cross[1])
        sign = sign_rows(chunk, 128)
        for half in range(2):
            above = (result[:, half * 128 : (half + 1) * 128] + sign * tap_total) * (length**-0.5)
            if half == 1:
                index = lax.broadcasted_iota(jnp.int32, above.shape, 0) + at * chunk
                above = jnp.where(index == 0, 0.0, above)
            above = above.astype(BF)
            spot = pl.ds(pl.multiple_of(half * length + at * chunk, chunk), chunk)
            r.grad_third[...] += dot(above, r.acts[2, spot, :], TN)
            below = (dot(above, r.third[...]) * r.acts[3, spot, :].astype(F32)).astype(BF)
            r.grad_second[...] += dot(r.acts[0, spot, :], below, TN)
            below = (dot(below, r.second[...], NT) * r.acts[1, spot, :].astype(F32)).astype(BF)
            r.grad_first[...] += dot(r.features[spot, :], below, TN)
        return carry

    lax.fori_loop(0, per, filter_step, 0)
    r.early_own[own_chans, 384:512] = r.grad_third[:chans, :].astype(BF)
    r.small_own[0:128, 0:128] = r.grad_second[...].astype(BF)
    r.small_own[128:136, 0:128] = (r.grad_first[0:8, :] + r.grad_first[8:16, :]).astype(BF)
    r.small_own[pl.ds(pl.multiple_of(me * 16, 16), 16), 128:256] = r.sums[...].T[0:16, :].astype(BF)
    early.start_core()
    shifted = tokens - jnp.mean(tokens, axis=-1, keepdims=True)
    inverse = lax.rsqrt(jnp.mean(shifted * shifted, axis=-1, keepdims=True) + 1e-05)
    r.scaled[...] = shifted * inverse
    loads.normed.wait()
    loads.shuffled.wait()
    fan = r.in_left.shape[2]
    for copy in seq_copies:
        copy.wait_recv()
    squares[0].start_first_back()
    squares[1].start_first_back()
    early.start_chip()

    in_parts = {}

    def keep_left(g, result):
        r.late_own[pl.ds(g * block, block), 0:512] = result[:, 0:512].astype(BF)
        in_parts[g] = result[:, 512:576].astype(BF)

    def keep_right(b, result):
        r.late_own[pl.ds(b * block, block), 512:768] = jnp.concatenate([in_parts[b], result.astype(BF)], axis=1)

    def keep_rows(b, result):
        r.grad_rows[pl.ds(b * block, block), :] = result

    monarch_backward(
        lambda g: r.grad_proj[pl.ds(g * fan, fan), :],
        lambda b: r.in_normed[pl.ds(b * block, block), :],
        r.in_shuffled, r.in_right, r.in_left, r.middle, keep_right, keep_left, keep_rows,
    )
    for late in lates:
        late.start_core()
    squares[2].start_first_back()
    early.start_plane()
    for late in lates:
        late.start_chip()
    total = r.grad_rows[...].T
    scaled = r.scaled[...]
    lines = [jnp.sum(total * scaled, axis=0, keepdims=True), jnp.sum(total, axis=0, keepdims=True)]
    total = total * r.gain[...].reshape(1, width)
    first_mean = jnp.mean(total, axis=-1, keepdims=True)
    second_mean = jnp.mean(total * scaled, axis=-1, keepdims=True)
    total = r.grad_resid[...] + inverse * (total - first_mean - scaled * second_mean)
    r.grad_tok[...] = total.astype(BF)
    token_line = Line(n_tp, r.tokens_out, r.tok_send, r.tok_recv)
    token_line.begin(r.grad_tok)
    own_tok = pltpu.make_async_copy(r.grad_tok, r.tokens_out.at[plane], r.local_sems.at[13])
    own_tok.start()
    lines += [r.grad_vectors[0:1, :], r.grad_vectors[1:2, :]]
    packed = [row[:, at * 128 : (at + 1) * 128] for row in lines for at in range(width // 128)]
    r.small_own[128:160, 128:256] = jnp.concatenate(packed + [jnp.zeros((8, 128), F32)], axis=0).astype(BF)
    small.start_core()
    early.start_plane_back()
    small.start_chip()
    token_line.take(neighbour_order(plane, 1))
    for late in lates:
        late.start_plane()
    small.start_plane()
    early.start_chip_back()
    for square in squares:
        square.start_core_back()
    token_line.take(neighbour_order(plane, 2))
    for late in lates:
        late.start_plane_back()
    small.start_plane_back()
    for late in lates:
        late.start_chip_back()
    small.start_chip_back()
    early.start_core_back()
    token_line.take(neighbour_order(plane, 3))
    ffn_copies = []
    for which, square in enumerate(squares):
        square.arrived()
        copy = pltpu.make_async_copy(r.ffn_v.at[which], r.ffn_out.at[which], r.local_sems.at[14 + which])
        copy.start()
        ffn_copies.append(copy)
    for late in lates:
        late.start_core_back()
    small.start_core_back()
    early.finish()
    r.early_out[...] = r.early_full[...]
    small.finish()
    r.small_out[...] = r.small_full[...]
    for copy in out_copies:
        copy.wait()
    r.output_out[...] = r.output_v[...]
    for late in lates:
        late.finish()
    r.late_out[...] = r.late_full[...]
    for copy in mixed_copies + seq_copies + backs + glus:
        copy.wait_send()
    for square in squares:
        square.finish()
    line.finish()
    token_line.finish()
    own_tok.wait()
    for copy in ffn_copies:
        copy.wait()


def core(mesh_shape, *operands):
    n_seq, n_tp = mesh_shape
    tokens = Inputs(*operands).tokens
    _, rows, width = tokens.shape
    chans, length = width // n_seq, rows * n_seq
    scratch, groups = core_scratch(n_seq, n_tp, width, chans, length, rows)
    shape = jax.ShapeDtypeStruct
    return pl.pallas_call(
        functools.partial(core_kernel, n_seq, n_tp, (width, chans, length, rows)),
        out_shape=(
            shape((n_tp, rows // n_tp, width), BF),
            shape((3, width, width), BF),
            shape((n_tp, rows, width), BF),
            shape((width, width), BF),
            shape((width, 512), BF),
            shape((256, 256), BF),
        ),
        in_specs=[vmem_spec()] * 13 + [any_spec()] * (len(Inputs._fields) - 13),
        out_specs=(vmem_spec(), any_spec(), any_spec(), vmem_spec(), vmem_spec(), vmem_spec()),
        scratch_shapes=list(scratch.values()) + sum(groups, []),
        compiler_params=pltpu.CompilerParams(collective_id=1, has_side_effects=True, vmem_limit_bytes=60 * 1024 * 1024),
        name="core",
    )(*operands)


def finish_kernel(width, chans, *refs):
    (ffn, tokens, late, early, small) = refs[:5]
    (grad_tokens, norm_gain, norm_bias, in_right, in_left, short, first, second, third, conv_bias, out_right, out_left,
     ffn_gain, ffn_bias, gate, up, down) = refs[5:22]
    (ffn_v, ffn_f, token_v, token_f, in_sems, out_sems) = refs[22:]
    loads = [pltpu.make_async_copy(ffn.at[which], ffn_v.at[which], in_sems.at[which]) for which in range(3)]
    loads.append(pltpu.make_async_copy(tokens, token_v, in_sems.at[3]))
    for copy in loads:
        copy.start()
    stores = [
        pltpu.make_async_copy(ffn_f.at[which], target, out_sems.at[which]) for which, target in enumerate((gate, up, down))
    ]
    stores.append(pltpu.make_async_copy(token_f, grad_tokens, out_sems.at[3]))
    chunk = 64
    for which in range(3):
        loads[which].wait()

        def step(at, carry, which=which):
            here = pl.ds(pl.multiple_of(at * chunk, chunk), chunk)
            ffn_f[which, here, :] = ffn_v[which, here, :].astype(F32)
            return carry

        lax.fori_loop(0, width // chunk, step, 0)
        stores[which].start()
    loads[3].wait()

    def token_step(at, carry):
        token_f[at] = token_v[at].astype(F32)
        return carry

    lax.fori_loop(0, token_v.shape[0], token_step, 0)
    stores[3].start()
    groups, block, _ = in_right.shape
    for b in range(groups):
        here = pl.ds(b * block, block)
        in_left[b] = late[here, 0 : 3 * block].astype(F32)
        in_right[b] = late[here, 3 * block : 4 * block].astype(F32)
        out_right[b] = early[here, 0:block].astype(F32)
        out_left[b] = early[here, block : 2 * block].astype(F32)
    third[...] = early[:, 384:512].astype(F32).T
    values = small[...].astype(F32)
    second[...] = values[0:128, 0:128]
    first[...] = values[128:133, 0:128]
    for at, target in enumerate((norm_gain, norm_bias, ffn_gain, ffn_bias)):
        row = 128 + at * (width // 128)
        target[...] = jnp.concatenate([values[row + k : row + k + 1, 128:256] for k in range(width // 128)], axis=1).reshape(width)
    parts = [values[16 * at : 16 * at + 16, 128 : 128 + chans] for at in range(width // chans)]
    lines = jnp.concatenate(parts, axis=1)
    for s in range(3):
        short[s] = lines[3 * s : 3 * s + 3]
    conv_bias[...] = lines[9:10].reshape(width)
    for copy in stores:
        copy.wait()


def finish(chans, ffn, tokens, late, early, small):
    width = ffn.shape[1]
    block = width // 4
    shape = jax.ShapeDtypeStruct
    vector = shape((width,), F32)
    square = shape((4, block, block), F32)
    return pl.pallas_call(
        functools.partial(finish_kernel, width, chans),
        out_shape=(
            shape(tokens.shape, F32), vector, vector, square, shape((4, block, 3 * block), F32), shape((3, 3, width), F32),
            shape((5, 128), F32), shape((128, 128), F32), shape((128, width), F32), vector, square, square, vector, vector,
        )
        + (shape((width, width), F32),) * 3,
        in_specs=[any_spec()] * 2 + [vmem_spec()] * 3,
        out_specs=(any_spec(),) + (vmem_spec(),) * 13 + (any_spec(),) * 3,
        scratch_shapes=[
            pltpu.VMEM(ffn.shape, BF),
            pltpu.VMEM(ffn.shape, F32),
            pltpu.VMEM(tokens.shape, BF),
            pltpu.VMEM(tokens.shape, F32),
            pltpu.SemaphoreType.DMA((4,)),
            pltpu.SemaphoreType.DMA((4,)),
        ],
        compiler_params=pltpu.CompilerParams(vmem_limit_bytes=LIMIT),
        name="finish",
    )(ffn, tokens, late, early, small)


def fast_body(
    tokens,
    norm_gain,
    norm_bias,
    in_right,
    in_left,
    short_kernel,
    filter_first,
    filter_second,
    filter_third,
    conv_bias,
    out_right,
    out_left,
    ffn_gain,
    ffn_bias,
    gate_weight,
    up_weight,
    down_weight,
    cotangent,
):
    n_seq, n_tp = lax.axis_size("seq"), lax.axis_size("tp")
    _, rows, width = tokens.shape
    chans, length = width // n_seq, rows * n_seq
    shape = (n_seq, n_tp)
    table, features = (jnp.asarray(array) for array in constants(length))
    mixed, signals, conv, wave, taps, nyquist, acts, normed, shuffled, cot_rows, columns, third = front(
        shape, tokens, cotangent, table, norm_gain, norm_bias, in_right, in_left, short_kernel.transpose(0, 2, 1), conv_bias,
        features, filter_first, filter_second, filter_third,
    )
    output, ffn, grad_tokens, late, early, small = core(
        shape, mixed, ffn_gain, ffn_bias, out_right, out_left, columns, norm_gain, in_right, in_left, filter_second, third,
        nyquist, features, cot_rows, tokens, gate_weight, up_weight, down_weight, table, signals, conv, wave, taps, acts, normed,
        shuffled,
    )
    grads = finish(chans, ffn, grad_tokens, late, early, small)
    return (output,) + grads[:5] + (grads[5].transpose(0, 2, 1),) + grads[6:]


highest = lax.Precision.HIGHEST


def norm_forward(values, gain, bias):
    centre = jnp.mean(values, axis=-1, keepdims=True)
    shifted = values - centre
    inverse = lax.rsqrt(jnp.mean(shifted * shifted, axis=-1, keepdims=True) + 1e-05)
    scaled = shifted * inverse
    return (scaled * gain + bias, scaled, inverse)


def norm_backward(upstream, scaled, inverse, gain):
    weighted = upstream * gain
    first_mean = jnp.mean(weighted, axis=-1, keepdims=True)
    second_mean = jnp.mean(weighted * scaled, axis=-1, keepdims=True)
    grad_input = inverse * (weighted - first_mean - scaled * second_mean)
    breadth = upstream.shape[-1]
    grad_gain = jnp.sum((upstream * scaled).reshape(-1, breadth), axis=0)
    grad_bias = jnp.sum(upstream.reshape(-1, breadth), axis=0)
    return (grad_input, grad_gain, grad_bias)


def shuffle(blocked):
    row_count, groups, breadth = blocked.shape
    return (
        blocked.reshape(row_count, groups, groups, breadth // groups)
        .transpose(0, 2, 1, 3)
        .reshape(row_count, groups, breadth)
    )


def rows_monarch_forward(operand, right_factor, left_factor):
    row_count = operand.shape[0]
    groups = right_factor.shape[0]
    blocked = operand.reshape(row_count, groups, -1)
    middle = jnp.einsum(
        "tbi,bij->tbj", blocked, right_factor, preferred_element_type=jnp.float32
    ).astype(jnp.bfloat16)
    shuffled = shuffle(middle)
    result = jnp.einsum("tbi,bij->tbj", shuffled, left_factor, preferred_element_type=jnp.float32)
    return (shuffled, result.reshape(row_count, -1))


def rows_monarch_backward(grad_result, operand, shuffled, right_factor, left_factor):
    row_count = operand.shape[0]
    groups = right_factor.shape[0]
    grad_blocked = grad_result.reshape(row_count, groups, -1)
    grad_left = jnp.einsum(
        "tbi,tbj->bij", shuffled, grad_blocked, preferred_element_type=jnp.float32
    )
    grad_shuffled = jnp.einsum(
        "tbj,bij->tbi", grad_blocked, left_factor, preferred_element_type=jnp.float32
    )
    grad_middle = shuffle(grad_shuffled).astype(jnp.bfloat16)
    blocked = operand.reshape(row_count, groups, -1)
    grad_right = jnp.einsum(
        "tbi,tbj->bij", blocked, grad_middle, preferred_element_type=jnp.float32
    )
    grad_operand = jnp.einsum(
        "tbj,bij->tbi", grad_middle, right_factor, preferred_element_type=jnp.float32
    )
    return (grad_operand.reshape(row_count, -1), grad_right, grad_left)


def roots(row_count, col_count, period):
    product = jnp.arange(row_count)[:, None] * jnp.arange(col_count)[None, :] % period
    angle = product.astype(jnp.float32) * (2.0 * math.pi / period)
    return (jnp.cos(angle), jnp.sin(angle))


def complex_step(real_part, imag_part, cos_table, sin_table, sign, form):
    real_out = jnp.einsum(form, real_part, cos_table, precision=highest) - sign * jnp.einsum(
        form, imag_part, sin_table, precision=highest
    )
    imag_out = jnp.einsum(form, imag_part, cos_table, precision=highest) + sign * jnp.einsum(
        form, real_part, sin_table, precision=highest
    )
    return (real_out, imag_out)


def real_step(real_part, cos_table, sin_table, sign, form):
    real_out = jnp.einsum(form, real_part, cos_table, precision=highest)
    imag_out = sign * jnp.einsum(form, real_part, sin_table, precision=highest)
    return (real_out, imag_out)


def twiddle(real_part, imag_part, cos_table, sin_table, sign):
    real_out = real_part * cos_table - sign * imag_part * sin_table
    imag_out = imag_part * cos_table + sign * real_part * sin_table
    return (real_out, imag_out)


def spectrum_of(real_part):
    total = real_part.shape[-1]
    first = math.gcd(total, 128)
    second = total // first
    leading = real_part.shape[:-1]
    real_part = real_part.reshape(leading + (first, second))
    cos_first, sin_first = roots(first, first, first)
    real_part, imag_part = real_step(real_part, cos_first, sin_first, -1.0, "...ab,ak->...kb")
    cos_twist, sin_twist = roots(first, second, total)
    real_part, imag_part = twiddle(real_part, imag_part, cos_twist, sin_twist, -1.0)
    cos_second, sin_second = roots(second, second, second)
    return complex_step(real_part, imag_part, cos_second, sin_second, -1.0, "...kb,bm->...km")


def signal_of(real_part, imag_part):
    first = real_part.shape[-2]
    second = real_part.shape[-1]
    total = first * second
    leading = real_part.shape[:-2]
    cos_second, sin_second = roots(second, second, second)
    real_part, imag_part = complex_step(
        real_part, imag_part, cos_second, sin_second, 1.0, "...kb,bm->...km"
    )
    cos_twist, sin_twist = roots(first, second, total)
    real_part, imag_part = twiddle(real_part, imag_part, cos_twist, sin_twist, 1.0)
    cos_first, sin_first = roots(first, first, first)
    real_part, imag_part = complex_step(
        real_part, imag_part, cos_first, sin_first, 1.0, "...ab,ak->...kb"
    )
    return real_part.reshape(leading + (total,)) / total


def filter_parts(filter_first, filter_second, third_cols, seq_length):
    total = 2 * seq_length
    index = jnp.arange(total)
    offset = jnp.where(index < seq_length, index, index - total).astype(jnp.float32)
    scaled = offset / seq_length
    features = jnp.stack(
        [
            scaled,
            jnp.sin(math.pi * scaled),
            jnp.cos(math.pi * scaled),
            jnp.sin(7.0 * math.pi * scaled),
            jnp.cos(7.0 * math.pi * scaled),
        ],
        axis=1,
    )
    pre_one = jnp.dot(features, filter_first, precision=highest)
    act_one = jnp.sin(pre_one)
    pre_two = jnp.dot(act_one, filter_second, precision=highest)
    act_two = jnp.sin(pre_two)
    tap_mask = (index != seq_length).astype(jnp.float32)[:, None] * seq_length ** (-0.5)
    taps = jnp.dot(act_two, third_cols, precision=highest) * tap_mask
    filt_real, filt_imag = spectrum_of(taps.T)
    return (features, pre_one, act_one, pre_two, act_two, tap_mask, filt_real, filt_imag)


def general_body(
    tokens,
    norm_gain,
    norm_bias,
    in_right,
    in_left,
    short_kernel,
    filter_first,
    filter_second,
    filter_third,
    conv_bias,
    out_right,
    out_left,
    ffn_gain,
    ffn_bias,
    gate_weight,
    up_weight,
    down_weight,
    cotangent,
):
    seq_count, pos_count, model_width = tokens.shape
    row_count = seq_count * pos_count
    axis_count = lax.axis_size("seq")
    my_index = lax.axis_index("seq")
    chan_count = model_width // axis_count
    seq_length = pos_count * axis_count
    part_rows = cotangent.shape[1]
    tp_index = lax.axis_index("tp")
    tp_count = lax.axis_size("tp")
    chan_start = my_index * chan_count
    mix_count = seq_count // tp_count
    mix_tokens = lax.dynamic_slice_in_dim(tokens, tp_index * mix_count, mix_count, 0)
    mix_rows = mix_count * pos_count
    flat = mix_tokens.reshape(mix_rows, model_width).astype(jnp.float32)
    normed, scaled_one, inverse_one = norm_forward(flat, norm_gain, norm_bias)
    normed_low = normed.astype(jnp.bfloat16)
    shuffled_in, projected = rows_monarch_forward(normed_low, in_right, in_left)
    projected_low = (
        projected.astype(jnp.bfloat16)
        .reshape(mix_count, pos_count, 3, model_width)
        .transpose(2, 3, 0, 1)
    )
    channels = lax.all_to_all(projected_low, "seq", split_axis=1, concat_axis=3, tiled=True)
    signals = channels.astype(jnp.float32)
    kernel = lax.dynamic_slice_in_dim(short_kernel, chan_start, chan_count, 1).astype(jnp.float32)
    tap_zero = kernel[:, :, 0][:, :, None, None]
    tap_one = kernel[:, :, 1][:, :, None, None]
    tap_two = kernel[:, :, 2][:, :, None, None]
    padded = jnp.pad(signals, ((0, 0), (0, 0), (0, 0), (1, 1)))
    shorted = padded[..., :-2] * tap_zero + padded[..., 1:-1] * tap_one + padded[..., 2:] * tap_two
    first_f = filter_first.astype(jnp.float32)
    second_f = filter_second.astype(jnp.float32)
    third_cols = lax.dynamic_slice_in_dim(filter_third, chan_start, chan_count, 1).astype(
        jnp.float32
    )
    kept = filter_parts(first_f, second_f, third_cols, seq_length)
    filt_real = kept[6][:, None]
    filt_imag = kept[7][:, None]
    bias_cols = lax.dynamic_slice_in_dim(conv_bias, chan_start, chan_count, 0)[:, None, None]
    product = shorted[0] * shorted[2]
    product_pad = jnp.pad(product, ((0, 0), (0, 0), (0, seq_length)))
    spec_real, spec_imag = spectrum_of(product_pad)
    conv_real = spec_real * filt_real - spec_imag * filt_imag
    conv_imag = spec_real * filt_imag + spec_imag * filt_real
    convolved = signal_of(conv_real, conv_imag)[..., :seq_length] + bias_cols * product
    mixed_low = (shorted[1] * convolved).astype(jnp.bfloat16)
    back_rows = lax.all_to_all(mixed_low, "seq", split_axis=2, concat_axis=0, tiled=True)
    mixed_rows = back_rows.transpose(1, 2, 0).reshape(mix_rows, model_width)
    shuffled_out, branch = rows_monarch_forward(mixed_rows, out_right, out_left)
    residual_mine = (flat + branch).reshape(mix_count, pos_count, model_width)
    residual = lax.all_gather(residual_mine, "tp", axis=0, tiled=True)
    part_resid = lax.dynamic_slice_in_dim(residual, tp_index * part_rows, part_rows, 1)
    normed_two, scaled_two, inverse_two = norm_forward(part_resid, ffn_gain, ffn_bias)
    normed_rows = lax.all_gather(normed_two.astype(jnp.bfloat16), "tp", axis=1, tiled=True).reshape(
        row_count, model_width
    )
    gate = jnp.dot(normed_rows, gate_weight, preferred_element_type=jnp.float32)
    upward = jnp.dot(normed_rows, up_weight, preferred_element_type=jnp.float32)
    sigma = jax.nn.sigmoid(gate)
    hidden_low = (gate * sigma * upward).astype(jnp.bfloat16)
    partial_down = jnp.dot(hidden_low, down_weight, preferred_element_type=jnp.float32).reshape(
        seq_count, pos_count, model_width
    )
    glu_part = lax.psum_scatter(
        partial_down.astype(jnp.bfloat16), "tp", scatter_dimension=1, tiled=True
    ).astype(jnp.float32)
    output = (part_resid + glu_part).astype(jnp.bfloat16)
    grad_out_rows = lax.all_gather(cotangent, "tp", axis=1, tiled=True).reshape(
        row_count, model_width
    )
    grad_hidden = jnp.dot(grad_out_rows, down_weight.T, preferred_element_type=jnp.float32)
    grad_gate = (grad_hidden * upward * (sigma + gate * sigma * (1.0 - sigma))).astype(jnp.bfloat16)
    grad_up = (grad_hidden * gate * sigma).astype(jnp.bfloat16)
    grad_down_w = jnp.dot(hidden_low.T, grad_out_rows, preferred_element_type=jnp.float32)
    grad_gate_w = jnp.dot(normed_rows.T, grad_gate, preferred_element_type=jnp.float32)
    grad_up_w = jnp.dot(normed_rows.T, grad_up, preferred_element_type=jnp.float32)
    grad_normed = jnp.dot(grad_gate, gate_weight.T, preferred_element_type=jnp.float32) + jnp.dot(
        grad_up, up_weight.T, preferred_element_type=jnp.float32
    )
    grad_normed_part = lax.psum_scatter(
        grad_normed.reshape(seq_count, pos_count, model_width),
        "tp",
        scatter_dimension=1,
        tiled=True,
    )
    grad_in_two, grad_gain_two, grad_bias_two = norm_backward(
        grad_normed_part, scaled_two, inverse_two, ffn_gain
    )
    gain_total = lax.psum((grad_gain_two, grad_bias_two), ("seq", "tp"))
    grad_resid_part = cotangent.astype(jnp.float32) + grad_in_two
    grad_resid = lax.all_gather(
        grad_resid_part.astype(jnp.bfloat16), "tp", axis=1, tiled=True
    ).astype(grad_resid_part.dtype)
    grad_resid_mix = lax.dynamic_slice_in_dim(
        grad_resid, tp_index * mix_count, mix_count, 0
    ).reshape(mix_rows, model_width)
    grad_mixed_rows, grad_out_right, grad_out_left = rows_monarch_backward(
        grad_resid_mix.astype(jnp.bfloat16), mixed_rows, shuffled_out, out_right, out_left
    )
    grad_mixed_low = (
        grad_mixed_rows.astype(jnp.bfloat16)
        .reshape(mix_count, pos_count, model_width)
        .transpose(2, 0, 1)
    )
    grad_mixed = lax.all_to_all(
        grad_mixed_low, "seq", split_axis=0, concat_axis=2, tiled=True
    ).astype(jnp.float32)
    grad_conv = grad_mixed * shorted[1]
    grad_key = grad_mixed * convolved
    again = lax.optimization_barrier((first_f, second_f, third_cols))
    kept = filter_parts(again[0], again[1], again[2], seq_length)
    filt_real = kept[6][:, None]
    filt_imag = kept[7][:, None]
    features, pre_one, act_one, pre_two, act_two, tap_mask = (
        kept[0],
        kept[1],
        kept[2],
        kept[3],
        kept[4],
        kept[5],
    )
    grad_pad = jnp.pad(grad_conv, ((0, 0), (0, 0), (0, seq_length)))
    grad_spec_real, grad_spec_imag = spectrum_of(grad_pad)
    back_real = grad_spec_real * filt_real + grad_spec_imag * filt_imag
    back_imag = grad_spec_imag * filt_real - grad_spec_real * filt_imag
    grad_product = signal_of(back_real, back_imag)[..., :seq_length] + bias_cols * grad_conv
    grad_bias_cols = jnp.sum(grad_conv * product, axis=(1, 2))
    taps_real = jnp.sum(grad_spec_real * spec_real + grad_spec_imag * spec_imag, axis=1)
    taps_imag = jnp.sum(grad_spec_imag * spec_real - grad_spec_real * spec_imag, axis=1)
    grad_taps = signal_of(taps_real, taps_imag)
    grad_pre = grad_taps.T * tap_mask
    grad_third_cols = jnp.dot(act_two.T, grad_pre, precision=highest)
    grad_pre_two = jnp.dot(grad_pre, third_cols.T, precision=highest) * jnp.cos(pre_two)
    grad_second = jnp.dot(act_one.T, grad_pre_two, precision=highest)
    grad_pre_one = jnp.dot(grad_pre_two, second_f.T, precision=highest) * jnp.cos(pre_one)
    grad_first = jnp.dot(features.T, grad_pre_one, precision=highest)
    grad_shorted = jnp.stack([grad_product * shorted[2], grad_key, grad_product * shorted[0]])
    grad_short_pad = jnp.pad(grad_shorted, ((0, 0), (0, 0), (0, 0), (1, 1)))
    grad_signals = (
        grad_short_pad[..., 2:] * tap_zero
        + grad_short_pad[..., 1:-1] * tap_one
        + grad_short_pad[..., :-2] * tap_two
    )
    grad_kernel = jnp.stack(
        [
            jnp.sum(grad_shorted * padded[..., :-2], axis=(2, 3)),
            jnp.sum(grad_shorted * padded[..., 1:-1], axis=(2, 3)),
            jnp.sum(grad_shorted * padded[..., 2:], axis=(2, 3)),
        ],
        axis=-1,
    )
    grad_proj = lax.all_to_all(
        grad_signals.astype(jnp.bfloat16), "seq", split_axis=3, concat_axis=1, tiled=True
    )
    grad_proj_rows = grad_proj.transpose(2, 3, 0, 1).reshape(mix_rows, 3 * model_width)
    grad_normed_one, grad_in_right, grad_in_left = rows_monarch_backward(
        grad_proj_rows, normed_low, shuffled_in, in_right, in_left
    )
    grad_in_one, grad_gain_one, grad_bias_one = norm_backward(
        grad_normed_one, scaled_one, inverse_one, norm_gain
    )
    grad_mine = (grad_resid_mix + grad_in_one).reshape(mix_count, pos_count, model_width)
    short_full = lax.dynamic_update_slice_in_dim(
        jnp.zeros(short_kernel.shape, jnp.float32), grad_kernel, chan_start, 1
    )
    third_full = lax.dynamic_update_slice_in_dim(
        jnp.zeros(filter_third.shape, jnp.float32), grad_third_cols, chan_start, 1
    )
    bias_full = lax.dynamic_update_slice_in_dim(
        jnp.zeros(conv_bias.shape, jnp.float32), grad_bias_cols, chan_start, 0
    )
    mixer_grads = (
        grad_gain_one,
        grad_bias_one,
        grad_in_right,
        grad_in_left,
        short_full,
        grad_first,
        grad_second,
        third_full,
        bias_full,
        grad_out_right,
        grad_out_left,
    )
    grad_tokens = lax.all_gather(grad_mine.astype(jnp.bfloat16), "tp", axis=0, tiled=True).astype(
        grad_mine.dtype
    )
    mixer_grads = (
        lax.psum(mixer_grads[0].astype(jnp.bfloat16), "tp").astype(jnp.float32),
        lax.psum(mixer_grads[1].astype(jnp.bfloat16), "tp").astype(jnp.float32),
        lax.psum(mixer_grads[2].astype(jnp.bfloat16), "tp").astype(jnp.float32),
        lax.psum(mixer_grads[3].astype(jnp.bfloat16), "tp").astype(jnp.float32),
        lax.psum(mixer_grads[4].astype(jnp.bfloat16), "tp").astype(jnp.float32),
        lax.psum(mixer_grads[5].astype(jnp.bfloat16), "tp").astype(jnp.float32),
        lax.psum(mixer_grads[6].astype(jnp.bfloat16), "tp").astype(jnp.float32),
        lax.psum(mixer_grads[7].astype(jnp.bfloat16), "tp").astype(jnp.float32),
        lax.psum(mixer_grads[8].astype(jnp.bfloat16), "tp").astype(jnp.float32),
        lax.psum(mixer_grads[9].astype(jnp.bfloat16), "tp").astype(jnp.float32),
        lax.psum(mixer_grads[10].astype(jnp.bfloat16), "tp").astype(jnp.float32),
    )
    all_total = lax.psum(
        (
            mixer_grads[0],
            mixer_grads[1],
            mixer_grads[2],
            mixer_grads[3],
            mixer_grads[4],
            mixer_grads[5],
            mixer_grads[6],
            mixer_grads[7],
            mixer_grads[8],
            mixer_grads[9],
            mixer_grads[10],
            grad_gate_w,
            grad_up_w,
            grad_down_w,
        ),
        "seq",
    )
    return (
        output,
        grad_tokens,
        all_total[0],
        all_total[1],
        all_total[2],
        all_total[3],
        all_total[4],
        all_total[5],
        all_total[6],
        all_total[7],
        all_total[8],
        all_total[9],
        all_total[10],
        gain_total[0],
        gain_total[1],
        all_total[11],
        all_total[12],
        all_total[13],
    )


def choose_body(mesh, *arrays):
    tokens = arrays[0]
    chans = tokens.shape[2] // mesh.shape["seq"]
    fits = mesh.shape["seq"] == 8 and mesh.shape["tp"] == 4 and tokens.shape[:2] == (4, 128) and chans == 96
    return (fast_body if fits else general_body)(*arrays)


def solution(mesh):
    mapped = jax.shard_map(
        functools.partial(choose_body, mesh),
        mesh=mesh,
        in_specs=(
            P(None, "seq", None),
            P(),
            P(),
            P(),
            P(),
            P(),
            P(),
            P(),
            P(),
            P(),
            P(),
            P(),
            P(),
            P(),
            P(None, "tp"),
            P(None, "tp"),
            P("tp", None),
            P(None, ("seq", "tp"), None),
        ),
        out_specs=(
            P(None, ("seq", "tp"), None),
            P(None, "seq", None),
            P(),
            P(),
            P(),
            P(),
            P(),
            P(),
            P(),
            P(),
            P(),
            P(),
            P(),
            P(),
            P(),
            P(None, "tp"),
            P(None, "tp"),
            P("tp", None),
        ),
        check_vma=False,
    )

    def program(*arrays):
        with jax.sharding.use_abstract_mesh(mesh.abstract_mesh):
            return mapped(*arrays)

    return program
```

```python
import functools
import math
import types
import typing

import numpy as np
import jax
import jax.numpy as jnp
from jax import lax
from jax.experimental import pallas as pl
from jax.experimental.pallas import tpu as pltpu
from jax.sharding import PartitionSpec as P

BF = jnp.bfloat16
F32 = jnp.float32
MESH = pl.DeviceIdType.MESH
NN = ((1,), (0,))
NT = ((1,), (1,))
TN = ((0,), (0,))
LIMIT = 56 * 1024 * 1024


def dot(first, second, form=NN):
    return lax.dot_general(first, second, (form, ((), ())), preferred_element_type=F32)


def any_spec():
    return pl.BlockSpec(memory_space=pl.ANY)


def vmem_spec():
    return pl.BlockSpec(memory_space=pltpu.VMEM)


def sin_cos(value):
    turns = jnp.floor(value * (1.0 / math.pi) + 0.5)
    rest = value - turns * 3.140625
    rest = rest - turns * 9.67502593994140625e-4
    rest = rest - turns * 1.509957990978376432e-7
    half = turns * 0.5
    sign = 1.0 - 4.0 * (half - jnp.floor(half))
    square = rest * rest
    sine = 1.0 / 362880 - square * (1.0 / 39916800)
    sine = -1.0 / 5040 + square * sine
    sine = 1.0 / 120 + square * sine
    sine = -1.0 / 6 + square * sine
    sine = rest + rest * square * sine
    cosine = 1.0 / 40320 - square * (1.0 / 3628800 - square * (1.0 / 479001600))
    cosine = -1.0 / 720 + square * cosine
    cosine = 1.0 / 24 + square * cosine
    cosine = -0.5 + square * cosine
    cosine = 1.0 + square * cosine
    return sign * sine, sign * cosine


def flip(index, bits):
    result = 0
    for place in range(3):
        digit = lax.rem(index // (1 << place), 2)
        if (bits >> place) & 1:
            digit = 1 - digit
        result = result + digit * (1 << place)
    return result


def greet(n_seq, n_tp):
    me, plane = lax.axis_index("seq"), lax.axis_index("tp")
    barrier = pltpu.get_barrier_semaphore()
    for k in range(1, n_seq):
        pl.semaphore_signal(barrier, inc=1, device_id={"seq": flip(me, k)}, device_id_type=MESH)
    for k in range(1, n_tp):
        pl.semaphore_signal(barrier, inc=1, device_id={"tp": flip(plane, k)}, device_id_type=MESH)
    return lambda: pl.semaphore_wait(barrier, n_seq + n_tp - 2)


def sign_rows(count, width):
    row = lax.broadcasted_iota(jnp.int32, (count, width), 0)
    return (1 - 2 * lax.rem(row, 2)).astype(F32)


def sign_lanes(count, width):
    lane = lax.broadcasted_iota(jnp.int32, (count, width), 1)
    return (1 - 2 * lax.rem(lane, 2)).astype(F32)


def previous(values):
    lane = lax.broadcasted_iota(jnp.int32, values.shape, 1)
    return jnp.where(lane == 0, 0.0, pltpu.roll(values, 1, 1))


def following(values):
    last = values.shape[1] - 1
    lane = lax.broadcasted_iota(jnp.int32, values.shape, 1)
    return jnp.where(lane == last, 0.0, pltpu.roll(values, last, 1))


def monarch_forward(load, right, left, shuffled, store):
    groups, width, _ = right.shape
    part = width // groups
    for b in range(groups):
        middle = dot(right[b], load(b), TN).astype(BF)
        for g in range(groups):
            shuffled[pl.ds(g * width + b * part, part), :] = middle[g * part : (g + 1) * part]
    for g in range(groups):
        store(g, dot(left[g], shuffled[pl.ds(g * width, width), :], TN))


SEQ_ORDER = (6, 7, 2, 3, 4, 5, 1)


def front_part(n_seq, n_tp, dims, r, entered, loads):
    width, chans, length, rows = dims
    me, plane = lax.axis_index("seq"), lax.axis_index("tp")
    cotangent, right, left, features = r.cotangent, r.in_right, r.in_left, r.features
    token_v, table_v, normed, shuffled, signals = r.token_v, r.table_v, r.in_normed, r.in_shuffled, r.signals
    acts, taps_v, padded, wave, conv, nyquist, columns, third_v = (
        r.acts, r.taps_v, r.padded, r.wave, r.conv, r.nyquist, r.columns, r.third_v
    )
    projected, spread, product, keyed, spectrum, mixed, totals = (
        r.projected, r.spread, r.product, r.query, r.back_wave, r.front_mixed, r.totals
    )
    loads.token.wait()
    value = token_v[...].astype(F32)
    shifted = value - jnp.mean(value, axis=-1, keepdims=True)
    inverse = lax.rsqrt(jnp.mean(shifted * shifted, axis=-1, keepdims=True) + 1e-05)
    value = shifted * inverse * r.gain[...].reshape(1, width) + r.bias[...].reshape(1, width)
    normed[...] = value.T.astype(BF)
    groups = right.shape[0]
    block = width // groups
    fan = left.shape[2]

    def keep(g, result):
        projected[pl.ds(g * fan, fan), :] = result.astype(BF)

    monarch_forward(lambda b: normed[pl.ds(b * block, block), :], right, left, shuffled, keep)
    entered()
    sends = []
    mine = pl.ds(pl.multiple_of(me * rows, rows), rows)
    for k in SEQ_ORDER:
        other = flip(me, k)
        for s in range(3):
            copy = pltpu.make_async_remote_copy(
                src_ref=projected.at[pl.ds(pl.multiple_of(s * width + other * chans, 16), chans), :],
                dst_ref=signals.at[s, :, mine],
                send_sem=r.front_send.at[k, s],
                recv_sem=r.front_recv.at[k, s],
                device_id={"seq": other},
                device_id_type=MESH,
            )
            copy.start()
            sends.append(copy)
    for s in range(3):
        signals[s, :, mine] = projected[pl.ds(pl.multiple_of(s * width + me * chans, 16), chans), :]
    part = rows // n_tp
    spot = pl.ds(pl.multiple_of(plane * part, part), part)
    cot_copies = []
    for k in range(1, n_tp):
        copy = pltpu.make_async_remote_copy(
            src_ref=cotangent,
            dst_ref=r.cot_v.at[:, spot, :],
            send_sem=r.cot_send.at[k],
            recv_sem=r.cot_recv.at[k],
            device_id={"tp": flip(plane, k)},
            device_id_type=MESH,
        )
        copy.start()
        cot_copies.append(copy)
    own_cot = pltpu.make_async_copy(cotangent, r.cot_v.at[:, spot, :], r.local_sems.at[17])
    own_cot.start()

    own = pl.ds(pl.multiple_of(me * chans, 16), chans)
    lines = [r.short[s].astype(F32) for s in range(3)]
    lines += [r.conv_bias[...].reshape(1, width), jnp.zeros((6, width), F32)]
    r.tall[...] = jnp.concatenate(lines, axis=0).T
    columns[...] = r.tall[own, :]
    r.third_turned[...] = r.third[...].T
    third_v[pl.ds(0, chans), :] = r.third_turned[own, :]
    third_v[pl.ds(chans, 128 - chans), :] = jnp.zeros((128 - chans, 128), BF)
    lead = jnp.concatenate([r.first[...].astype(F32), jnp.zeros((3, 128), F32)], axis=0)
    lead = jnp.concatenate([lead, lead], axis=0).astype(BF)

    chunk = 256
    per = length // chunk
    totals[...] = jnp.zeros_like(totals)
    for half in range(2):

        def tap_step(at, carry, half=half):
            row = pl.multiple_of(half * length + at * chunk, chunk)
            here = pl.ds(row, chunk)
            sine, cosine = sin_cos(dot(features[here, :], lead))
            high = sine.astype(BF)
            acts[0, here, :] = high
            acts[1, here, :] = cosine.astype(BF)
            low = (sine - high.astype(F32)).astype(BF)
            sine, cosine = sin_cos(dot(high, r.second[...]) + dot(low, r.second[...]))
            high = sine.astype(BF)
            acts[2, here, :] = high
            acts[3, here, :] = cosine.astype(BF)
            taps = dot(high, third_v[...], NT) * (length**-0.5)
            if half == 1:
                index = lax.broadcasted_iota(jnp.int32, taps.shape, 0) + at * chunk
                taps = jnp.where(index == 0, 0.0, taps)
            totals[...] += jnp.sum(taps * sign_rows(*taps.shape), axis=0, keepdims=True)
            spread[pl.ds(pl.multiple_of(at * chunk, chunk), chunk), pl.ds(half * 128, 128)] = taps.astype(BF)
            return carry

        lax.fori_loop(0, per, tap_step, 0)
    loads.table.wait()

    def spectrum_step(at, carry):
        here = pl.ds(pl.multiple_of(at * chunk, chunk), chunk)
        sign = sign_rows(chunk, 128)
        index = lax.broadcasted_iota(jnp.int32, (chunk, 128), 0) + at * chunk
        weight = jnp.where(index == 0, 0.5 / length, 1.0 / length)
        for which in range(2):
            result = dot(table_v[which, here, :], spread[...])
            taps_v[which, here, :] = ((result[:, :128] + sign * result[:, 128:]) * weight).astype(BF)
        return carry

    lax.fori_loop(0, per, spectrum_step, 0)
    tap_total = jnp.broadcast_to(totals[...], (128, 128)).T[:chans, 0:1]

    for copy in sends:
        copy.wait_recv()

    step = 16
    padded[pl.ds(chans, 128 - chans), :] = jnp.zeros((128 - chans, length), BF)

    def short_step(at, carry):
        here = pl.ds(pl.multiple_of(at * step, step), step)
        shorted = []
        for s in range(3):
            value = signals[s, here, :].astype(F32)
            shorted.append(
                previous(value) * columns[here, 3 * s : 3 * s + 1]
                + value * columns[here, 3 * s + 1 : 3 * s + 2]
                + following(value) * columns[here, 3 * s + 2 : 3 * s + 3]
            )
        result = shorted[0] * shorted[2]
        product[here, :] = result
        keyed[here, :] = shorted[1]
        padded[here, :] = result.astype(BF)
        nyquist[here, 0:1] = jnp.sum(result * sign_lanes(step, length), axis=1, keepdims=True)
        return carry

    lax.fori_loop(0, chans // step, short_step, 0)
    nyquist[:, 1:2] = tap_total

    def wave_step(at, carry):
        here = pl.ds(pl.multiple_of(at * chunk, chunk), chunk)
        cos_part = dot(table_v[0, here, :], padded[...], NT)
        sin_part = dot(table_v[1, here, :], padded[...], NT)
        wave[0, here, :] = cos_part.astype(BF)
        wave[1, here, :] = sin_part.astype(BF)
        tap_cos = taps_v[0, here, :].astype(F32)
        tap_sin = taps_v[1, here, :].astype(F32)
        spectrum[0, here, :] = (cos_part * tap_cos - sin_part * tap_sin).astype(BF)
        spectrum[1, here, :] = (cos_part * tap_sin + sin_part * tap_cos).astype(BF)
        return carry

    lax.fori_loop(0, per, wave_step, 0)

    def conv_step(at, carry):
        here = pl.ds(pl.multiple_of(at * chunk, chunk), chunk)
        result = dot(table_v[0, here, :], spectrum[0]) + dot(table_v[1, here, :], spectrum[1])
        result = result.T[:chans]
        result = (
            result
            + sign_lanes(chans, chunk) * (nyquist[:, 0:1] * nyquist[:, 1:2] * (0.5 / length))
            + columns[:, 9:10] * product[:, here]
        )
        conv[:, here] = result
        mixed[:, here] = (keyed[:, here] * result).astype(BF)
        return carry

    lax.fori_loop(0, per, conv_step, 0)
    backs = []
    slot = pl.ds(pl.multiple_of(me * chans, 16), chans)
    for k in SEQ_ORDER:
        other = flip(me, k)
        copy = pltpu.make_async_remote_copy(
            src_ref=mixed.at[:, pl.ds(pl.multiple_of(other * rows, rows), rows)],
            dst_ref=r.mixed.at[slot, :],
            send_sem=r.mix_send.at[k],
            recv_sem=r.mix_recv.at[k],
            device_id={"seq": other},
            device_id_type=MESH,
        )
        copy.start()
        backs.append(copy)
    r.mixed[slot, :] = mixed[:, mine]
    for copy in backs:
        copy.wait_recv()
    return sends + backs, cot_copies, own_cot


def split_table(values):
    high = values.astype(BF)
    low = (values - high.astype(np.float32)).astype(BF)
    return high, low


def constants(length):
    index = np.arange(length)
    angle = (index[:, None] * index[None, :] % (2 * length)) * (math.pi / length)
    table = np.stack([np.cos(angle), np.sin(angle)]).astype(np.float32).astype(BF)
    place = np.arange(2 * length)
    scaled = np.where(place < length, place, place - 2 * length) / length
    features = np.zeros((2 * length, 8), np.float32)
    features[:, 0] = scaled
    features[:, 1] = np.sin(math.pi * scaled)
    features[:, 2] = np.cos(math.pi * scaled)
    features[:, 3] = np.sin(7.0 * math.pi * scaled)
    features[:, 4] = np.cos(7.0 * math.pi * scaled)
    return table, np.concatenate(split_table(features), axis=1)


def monarch_backward(upstream, operand, shuffled, right, left, middle, keep_right, keep_left, store):
    groups, width, _ = right.shape
    part = width // groups
    for g in range(groups):
        above = upstream(g)
        keep_left(g, dot(shuffled[pl.ds(g * width, width), :], above, NT))
        below = dot(left[g], above).astype(BF)
        for b in range(groups):
            middle[pl.ds(b * width + g * part, part), :] = below[b * part : (b + 1) * part]
    for b in range(groups):
        above = middle[pl.ds(b * width, width), :]
        keep_right(b, dot(operand(b), above, NT))
        store(b, dot(right[b], above))


CHIPS = (6, 2, 4)


class Reduce:
    def __init__(self, n_seq, n_tp, own, full, core_in, halves, chip_in, quarter, plane_in, send, recv):
        self.own, self.full, self.core_in, self.halves = own, full, core_in, halves
        self.chip_in, self.quarter, self.plane_in = chip_in, quarter, plane_in
        self.send, self.recv, self.n_tp = send, recv, n_tp
        rows, width = own.shape
        self.rows, self.width = rows, width
        self.per_chip, self.per_plane = rows // (n_seq // 2), rows // (n_seq // 2) // n_tp
        self.me, self.plane = lax.axis_index("seq"), lax.axis_index("tp")
        core = lax.rem(self.me, 2)
        self.mine = pl.ds(pl.multiple_of(core * (width // 2), 128), width // 2)
        self.theirs = pl.ds(pl.multiple_of((1 - core) * (width // 2), 128), width // 2)
        self.started = []

    def chip_rows(self, index):
        return pl.ds(pl.multiple_of(index // 2 * self.per_chip, 16), self.per_chip)

    def copy(self, source, target, at, where):
        result = pltpu.make_async_remote_copy(
            src_ref=source, dst_ref=target, send_sem=self.send.at[at], recv_sem=self.recv.at[at],
            device_id=where, device_id_type=MESH,
        )
        result.start()
        self.started.append(result)
        return result

    def start_core(self):
        self.phase = [self.copy(self.own.at[:, self.theirs], self.core_in, 0, {"seq": flip(self.me, 1)})]

    def arrived(self):
        for copy in self.phase:
            copy.wait_recv()
        self.phase = []

    def start_chip(self):
        self.arrived()
        self.halves[...] = (self.own[:, self.mine].astype(F32) + self.core_in[...].astype(F32)).astype(BF)
        for k in CHIPS:
            other = flip(self.me, k)
            self.phase.append(
                self.copy(self.halves.at[self.chip_rows(other), :], self.chip_in.at[k // 2], k // 2, {"seq": other})
            )

    def start_plane(self):
        self.arrived()
        total = self.halves[self.chip_rows(self.me), :].astype(F32)
        for k in CHIPS:
            total = total + self.chip_in[k // 2].astype(F32)
        self.quarter[...] = total.astype(BF)
        for k in range(1, self.n_tp):
            other = flip(self.plane, k)
            here = pl.ds(pl.multiple_of(other * self.per_plane, 16), self.per_plane)
            self.phase.append(self.copy(self.quarter.at[here, :], self.plane_in.at[k], 3 + k, {"tp": other}))

    def start_plane_back(self):
        self.arrived()
        here = pl.ds(pl.multiple_of(self.plane * self.per_plane, 16), self.per_plane)
        total = self.quarter[here, :].astype(F32)
        for k in range(1, self.n_tp):
            total = total + self.plane_in[k].astype(F32)
        rows = pl.ds(
            pl.multiple_of(self.me // 2 * self.per_chip + self.plane * self.per_plane, 16), self.per_plane
        )
        self.full[rows, self.mine] = total.astype(BF)
        spot = self.full.at[rows, self.mine]
        for k in range(1, self.n_tp):
            self.phase.append(self.copy(spot, spot, 6 + k, {"tp": flip(self.plane, k)}))

    def start_chip_back(self):
        self.arrived()
        spot = self.full.at[self.chip_rows(self.me), self.mine]
        for k in CHIPS:
            self.phase.append(self.copy(spot, spot, 9 + k // 2, {"seq": flip(self.me, k)}))

    def start_core_back(self):
        self.arrived()
        spot = self.full.at[:, self.mine]
        self.phase.append(self.copy(spot, spot, 13, {"seq": flip(self.me, 1)}))

    def finish(self):
        self.arrived()
        for copy in self.started:
            copy.wait_send()


def neighbour_order(plane, at):
    upper = plane // 2
    near = plane + upper * (3 - 2 * plane)
    result = at * (1 - near) + (0, 0, 2, 3)[at] * near
    return result + upper * (3 - 2 * result)


class Line:
    def __init__(self, n_tp, slots, send, recv):
        self.n_tp, self.slots, self.send, self.recv = n_tp, slots, send, recv
        self.plane = lax.axis_index("tp")
        self.sent = []

    def copy(self, block, source, way):
        return pltpu.make_async_remote_copy(
            src_ref=source, dst_ref=self.slots.at[block], send_sem=self.send.at[way, block], recv_sem=self.recv.at[block],
            device_id={"tp": self.plane + (1, -1)[way]}, device_id_type=MESH,
        )

    def start(self, block, source, way, here):
        @pl.when(here)
        def _():
            self.copy(block, source, way).start()

        self.sent.append((block, source, way, here))

    def begin(self, source):
        self.start(self.plane, source, 0, self.plane < self.n_tp - 1)
        self.start(self.plane, source, 1, self.plane > 0)

    def take(self, block):
        pltpu.make_async_remote_copy(
            src_ref=self.slots.at[block], dst_ref=self.slots.at[block], send_sem=self.send.at[0, block],
            recv_sem=self.recv.at[block], device_id={"tp": block}, device_id_type=MESH,
        ).wait_recv()
        source = self.slots.at[block]
        self.start(block, source, 0, jnp.logical_and(block < self.plane, self.plane < self.n_tp - 1))
        self.start(block, source, 1, jnp.logical_and(block > self.plane, self.plane > 0))

    def finish(self):
        for block, source, way, here in self.sent:

            @pl.when(here)
            def _(block=block, source=source, way=way):
                self.copy(block, source, way).wait_send()


class Square:
    def __init__(self, own, full, core_in, half, first_in, second_in, send, recv):
        self.own, self.full, self.core_in, self.half = own, full, core_in, half
        self.first_in, self.second_in, self.send, self.recv = first_in, second_in, send, recv
        me = lax.axis_index("seq")
        self.me = me
        rows = own.shape[0]
        self.rows = rows
        self.core = lax.rem(me, 2)
        y, x = me // 4, lax.rem(me // 2, 2)
        quarter, part = rows // 8, rows // 16
        base = rows // 4
        self.ways = ((2, x, y, 0), (4, y, x, base))
        self.quarter, self.part = quarter, part
        self.started = []
        self.phase = []

    def copy(self, source, target, at, k):
        result = pltpu.make_async_remote_copy(
            src_ref=source, dst_ref=target, send_sem=self.send.at[at], recv_sem=self.recv.at[at],
            device_id={"seq": flip(self.me, k)}, device_id_type=MESH,
        )
        result.start()
        self.started.append(result)
        self.phase.append(result)

    def arrived(self):
        for copy in self.phase:
            copy.wait_recv()
        self.phase = []

    def span(self, start, size):
        return pl.ds(pl.multiple_of(start, 16), size)

    def start_core(self):
        half = self.rows // 2
        self.copy(self.own.at[self.span((1 - self.core) * half, half), :], self.core_in, 0, 1)

    def start_first(self):
        self.arrived()
        half = self.rows // 2
        own = self.own[self.span(self.core * half, half), :]
        self.half[...] = (own.astype(F32) + self.core_in[...].astype(F32)).astype(BF)
        for way, (k, near, far, base) in enumerate(self.ways):
            source = self.half.at[self.span(base + (1 - near) * self.quarter, self.quarter), :]
            self.copy(source, self.first_in.at[way], 1 + way, k)

    def start_second(self):
        self.arrived()
        for way, (k, near, far, base) in enumerate(self.ways):
            here = self.span(base + near * self.quarter, self.quarter)
            self.half[here, :] = (self.half[here, :].astype(F32) + self.first_in[way].astype(F32)).astype(BF)
            source = self.half.at[self.span(base + near * self.quarter + (1 - far) * self.part, self.part), :]
            self.copy(source, self.second_in.at[way], 3 + way, 6 - k)

    def start_second_back(self):
        self.arrived()
        for way, (k, near, far, base) in enumerate(self.ways):
            place = base + near * self.quarter + far * self.part
            total = self.half[self.span(place, self.part), :].astype(F32) + self.second_in[way].astype(F32)
            here = self.span(self.core * (self.rows // 2) + place, self.part)
            self.full[here, :] = total.astype(BF)
            spot = self.full.at[here, :]
            self.copy(spot, spot, 5 + way, 6 - k)

    def start_first_back(self):
        self.arrived()
        for way, (k, near, far, base) in enumerate(self.ways):
            spot = self.full.at[self.span(self.core * (self.rows // 2) + base + near * self.quarter, self.quarter), :]
            self.copy(spot, spot, 7 + way, k)

    def start_core_back(self):
        self.arrived()
        spot = self.full.at[self.span(self.core * (self.rows // 2), self.rows // 2), :]
        self.copy(spot, spot, 9, 1)

    def finish(self):
        for copy in self.started:
            copy.wait_send()


class Inputs(typing.NamedTuple):
    feed_gain: typing.Any
    feed_bias: typing.Any
    out_right: typing.Any
    out_left: typing.Any
    gain: typing.Any
    bias: typing.Any
    in_right: typing.Any
    in_left: typing.Any
    short: typing.Any
    conv_bias: typing.Any
    features: typing.Any
    first: typing.Any
    second: typing.Any
    third: typing.Any
    tokens: typing.Any
    cotangent: typing.Any
    table: typing.Any
    gate_w: typing.Any
    up_w: typing.Any
    down_w: typing.Any


class Outputs(typing.NamedTuple):
    output_out: typing.Any
    ffn_out: typing.Any
    tokens_out: typing.Any
    late_out: typing.Any
    early_out: typing.Any
    small_out: typing.Any


def core_scratch(n_seq, n_tp, width, chans, length, rows):
    result = dict(
        token_v=pltpu.VMEM((rows, width), BF),
        cot_v=pltpu.VMEM((n_tp, rows, width), BF),
        gate_v=pltpu.VMEM((width, width), BF),
        up_v=pltpu.VMEM((width, width), BF),
        down_v=pltpu.VMEM((width, width), BF),
        out_shuffled=pltpu.VMEM((width, rows), BF),
        branch=pltpu.VMEM((width, rows), F32),
        resid=pltpu.VMEM((rows, width), F32),
        scaled=pltpu.VMEM((rows, width), F32),
        inverse=pltpu.VMEM((rows, 1), F32),
        normed=pltpu.VMEM((n_tp, rows, width), BF),
        hidden=pltpu.VMEM((n_tp, rows, width), BF),
        grad_hidden=pltpu.VMEM((n_tp, rows, width), F32),
        grad_gate=pltpu.VMEM((n_tp, rows, width), BF),
        grad_up=pltpu.VMEM((n_tp, rows, width), BF),
        grad_normed=pltpu.VMEM((rows, width), F32),
        grad_send=pltpu.VMEM((n_tp, rows, width), BF),
        grad_recv=pltpu.VMEM((n_tp, rows, width), BF),
        glu_own=pltpu.VMEM((rows, width), F32),
        glu_send=pltpu.VMEM((n_tp, rows, width), BF),
        glu_recv=pltpu.VMEM((n_tp, rows, width), BF),
        turned=pltpu.VMEM((width, n_tp*rows), BF),
        grads=pltpu.VMEM((3, width, width), BF),
        ffn_v=pltpu.VMEM((3, width, width), BF),
        core_in=pltpu.VMEM((3, width//2, width), BF),
        halves=pltpu.VMEM((3, width//2, width), BF),
        first_in=pltpu.VMEM((3, 2, width//8, width), BF),
        second_in=pltpu.VMEM((3, 2, width//16, width), BF),
        grad_branch=pltpu.VMEM((width, rows), BF),
        middle=pltpu.VMEM((width, rows), BF),
        grad_mixed_own=pltpu.VMEM((width, rows), BF),
        grad_mixed=pltpu.VMEM((chans, length), BF),
        out_rows=pltpu.VMEM((rows, width), BF),
        output_v=pltpu.VMEM((n_tp, rows//n_tp, width), BF),
        grad_vectors=pltpu.VMEM((2, width), F32),
        grad_resid=pltpu.VMEM((rows, width), F32),
        table_v=pltpu.VMEM((2, length, length), BF),
        signals=pltpu.VMEM((3, chans, length), BF),
        conv=pltpu.VMEM((chans, length), F32),
        wave=pltpu.VMEM((2, length, 128), BF),
        taps_v=pltpu.VMEM((2, length, 128), BF),
        acts=pltpu.VMEM((4, 2*length, 128), BF),
        in_normed=pltpu.VMEM((width, rows), BF),
        in_shuffled=pltpu.VMEM((width, rows), BF),
        grad_short=pltpu.VMEM((3, chans, length), F32),
        query=pltpu.VMEM((chans, length), F32),
        value_v=pltpu.VMEM((chans, length), F32),
        grad_conv=pltpu.VMEM((chans, length), F32),
        padded=pltpu.VMEM((128, length), BF),
        back_wave=pltpu.VMEM((2, length, 128), BF),
        cross=pltpu.VMEM((2, length, 256), BF),
        sums=pltpu.VMEM((128, 128), F32),
        grad_signals=pltpu.VMEM((3, chans, length), BF),
        grad_proj=pltpu.VMEM((3*width, rows), BF),
        grad_rows=pltpu.VMEM((width, rows), F32),
        grad_tok=pltpu.VMEM((rows, width), BF),
        grad_second=pltpu.VMEM((128, 128), F32),
        grad_first=pltpu.VMEM((16, 128), F32),
        grad_third=pltpu.VMEM((128, 128), F32),
        local_sems=pltpu.SemaphoreType.DMA((20,)),
        line_send=pltpu.SemaphoreType.DMA((2,n_tp)),
        line_recv=pltpu.SemaphoreType.DMA((n_tp,)),
        tok_send=pltpu.SemaphoreType.DMA((2,n_tp)),
        tok_recv=pltpu.SemaphoreType.DMA((n_tp,)),
        back_send=pltpu.SemaphoreType.DMA((n_tp,)),
        back_recv=pltpu.SemaphoreType.DMA((n_tp,)),
        glu_ssem=pltpu.SemaphoreType.DMA((n_tp,)),
        glu_rsem=pltpu.SemaphoreType.DMA((n_tp,)),
        out_send=pltpu.SemaphoreType.DMA((n_tp,)),
        out_recv=pltpu.SemaphoreType.DMA((n_tp,)),
        mixed_send=pltpu.SemaphoreType.DMA((n_seq,)),
        mixed_recv=pltpu.SemaphoreType.DMA((n_seq,)),
        seq_send=pltpu.SemaphoreType.DMA((n_seq,3)),
        seq_recv=pltpu.SemaphoreType.DMA((n_seq,3)),
        ffn_send=pltpu.SemaphoreType.DMA((3,10)),
        ffn_recv=pltpu.SemaphoreType.DMA((3,10)),
        mixed=pltpu.VMEM((width, rows), BF),
        front_mixed=pltpu.VMEM((chans, length), BF),
        nyquist=pltpu.VMEM((chans, 128), F32),
        columns=pltpu.VMEM((chans, 16), F32),
        third_v=pltpu.VMEM((128, 128), BF),
        projected=pltpu.VMEM((3 * width, rows), BF),
        spread=pltpu.VMEM((length, 256), BF),
        product=pltpu.VMEM((chans, length), F32),
        totals=pltpu.VMEM((1, 128), F32),
        tall=pltpu.VMEM((width, 16), F32),
        third_turned=pltpu.VMEM((width, 128), BF),
        front_send=pltpu.SemaphoreType.DMA((n_seq, 3)),
        front_recv=pltpu.SemaphoreType.DMA((n_seq, 3)),
        mix_send=pltpu.SemaphoreType.DMA((n_seq,)),
        mix_recv=pltpu.SemaphoreType.DMA((n_seq,)),
        cot_send=pltpu.SemaphoreType.DMA((n_tp,)),
        cot_recv=pltpu.SemaphoreType.DMA((n_tp,)),
        late_own=pltpu.VMEM((width, width), BF),
        late_full=pltpu.VMEM((width, width), BF),
        early_own=pltpu.VMEM((width, 512), BF),
        early_full=pltpu.VMEM((width, 512), BF),
        small_own=pltpu.VMEM((256, 256), BF),
        small_full=pltpu.VMEM((256, 256), BF),
    )
    groups = []
    for count, breadth in ((256, width), (256, width), (256, width), (width, 512), (256, 256)):
        half, chip = breadth // 2, count // (n_seq // 2)
        groups.append(
            [
                pltpu.VMEM((count, half), BF),
                pltpu.VMEM((count, half), BF),
                pltpu.VMEM((n_seq // 2, chip, half), BF),
                pltpu.VMEM((chip, half), BF),
                pltpu.VMEM((n_tp, chip // n_tp, half), BF),
                pltpu.SemaphoreType.DMA((14,)),
                pltpu.SemaphoreType.DMA((14,)),
            ]
        )
    return result, groups


def core_kernel(n_seq, n_tp, dims, *refs):
    width, chans, length, rows = dims
    scratch, groups = core_scratch(n_seq, n_tp, width, chans, length, rows)
    named = dict(zip(Inputs._fields + Outputs._fields + tuple(scratch), refs))
    r = types.SimpleNamespace(**named)
    spare = list(refs[len(named) :])
    reduce_refs = [[spare.pop(0) for _ in group] for group in groups]
    me, plane = lax.axis_index("seq"), lax.axis_index("tp")
    entered = greet(n_seq, n_tp)
    sources = dict(
        token=(r.tokens.at[plane], r.token_v),
        down=(r.down_w, r.down_v),
        gate=(r.gate_w, r.gate_v),
        up=(r.up_w, r.up_v),
        table=(r.table, r.table_v),
    )
    copies = {
        name: pltpu.make_async_copy(*pair, r.local_sems.at[at]) for at, (name, pair) in enumerate(sources.items())
    }
    for copy in copies.values():
        copy.start()
    loads = types.SimpleNamespace(**copies)
    front_sends, cot_copies, own_cot = front_part(n_seq, n_tp, dims, r, entered, loads)
    _, block, _ = r.out_right.shape
    chunk = 256
    pieces = width // chunk
    per = length // chunk
    step = 16

    lates = []
    for at in range(3):
        here = pl.ds(256 * at, 256)
        lates.append(Reduce(n_seq, n_tp, r.late_own.at[here, :], r.late_full.at[here, :], *reduce_refs[at]))
    early = Reduce(n_seq, n_tp, r.early_own, r.early_full, *reduce_refs[3])
    small = Reduce(n_seq, n_tp, r.small_own, r.small_full, *reduce_refs[4])
    squares = [
        Square(
            r.grads.at[which], r.ffn_v.at[which], r.core_in.at[which], r.halves.at[which], r.first_in.at[which],
            r.second_in.at[which], r.ffn_send.at[which], r.ffn_recv.at[which],
        )
        for which in range(3)
    ]

    def keep_branch(g, result):
        r.branch[pl.ds(g * block, block), :] = result

    monarch_forward(lambda b: r.mixed[pl.ds(b * block, block), :], r.out_right, r.out_left, r.out_shuffled, keep_branch)
    tokens = r.token_v[...].astype(F32)
    value = tokens + r.branch[...].T
    r.resid[...] = value
    shifted = value - jnp.mean(value, axis=-1, keepdims=True)
    r.inverse[...] = lax.rsqrt(jnp.mean(shifted * shifted, axis=-1, keepdims=True) + 1e-05)
    value = shifted * r.inverse[...]
    r.scaled[...] = value
    r.normed[plane] = (value * r.feed_gain[...].reshape(1, width) + r.feed_bias[...].reshape(1, width)).astype(BF)
    line = Line(n_tp, r.normed, r.line_send, r.line_recv)
    line.begin(r.normed.at[plane])
    for copy in cot_copies:
        copy.wait_recv()
    own_cot.wait()
    loads.down.wait()

    def hidden_step(at, carry):
        cols = pl.ds(pl.multiple_of(at * chunk, chunk), chunk)
        result = dot(r.cot_v[...].reshape(n_tp * rows, width), r.down_v[cols, :], NT)
        r.grad_hidden[:, :, cols] = result.reshape(n_tp, rows, chunk)
        return carry

    lax.fori_loop(0, pieces, hidden_step, 0)
    loads.gate.wait()
    loads.up.wait()
    backs = []
    for k in range(n_tp):
        other = plane if k == 0 else neighbour_order(plane, k)
        if k > 0:
            line.take(other)

        def gate_step(at, carry, other=other):
            cols = pl.ds(pl.multiple_of(at * chunk, chunk), chunk)
            value = r.normed[other]
            gate = dot(value, r.gate_v[:, cols])
            upward = dot(value, r.up_v[:, cols])
            sigma = 1.0 / (1.0 + jnp.exp(-gate))
            active = gate * sigma
            r.hidden[other, :, cols] = (active * upward).astype(BF)
            above = r.grad_hidden[other, :, cols]
            r.grad_gate[other, :, cols] = (above * upward * (sigma + active * (1.0 - sigma))).astype(BF)
            r.grad_up[other, :, cols] = (above * active).astype(BF)
            return carry

        lax.fori_loop(0, pieces, gate_step, 0)

        def back_step(at, carry, k=k, other=other):
            cols = pl.ds(pl.multiple_of(at * chunk, chunk), chunk)
            result = dot(r.grad_gate[other], r.gate_v[cols, :], NT) + dot(r.grad_up[other], r.up_v[cols, :], NT)
            if k == 0:
                r.grad_normed[:, cols] = result
            else:
                r.grad_send[other, :, cols] = result.astype(BF)
            return carry

        lax.fori_loop(0, pieces, back_step, 0)
        if k > 0:
            copy = pltpu.make_async_remote_copy(
                src_ref=r.grad_send.at[other],
                dst_ref=r.grad_recv.at[plane],
                send_sem=r.back_send.at[other],
                recv_sem=r.back_recv.at[plane],
                device_id={"tp": other},
                device_id_type=MESH,
            )
            copy.start()
            backs.append(copy)

    def turn(source):
        for s in range(n_tp):
            r.turned[:, s * rows : (s + 1) * rows] = source[s].T

    def weight_grad(which, factor):
        def grad_step(at, carry):
            here = pl.ds(pl.multiple_of(at * chunk, chunk), chunk)
            result = dot(r.turned[here, :], factor[...].reshape(n_tp * rows, width))
            r.grads[which, here, :] = result.astype(BF)
            return carry

        lax.fori_loop(0, pieces, grad_step, 0)
        squares[which].start_core()

    turn(r.normed)
    weight_grad(0, r.grad_gate)
    weight_grad(1, r.grad_up)
    squares[0].start_first()
    turn(r.hidden)
    weight_grad(2, r.cot_v)
    squares[1].start_first()
    squares[2].start_first()

    def from_planes(recv, slots):
        total = 0.0
        for k in range(1, n_tp):
            other = flip(plane, k)
            pltpu.make_async_remote_copy(
                src_ref=slots.at[other], dst_ref=slots.at[other], send_sem=recv.at[other], recv_sem=recv.at[other],
                device_id={"tp": other}, device_id_type=MESH,
            ).wait_recv()
            total = total + slots[other].astype(F32)
        return total

    total = r.grad_normed[...] + from_planes(r.back_recv, r.grad_recv)
    value = r.scaled[...]
    r.grad_vectors[0:1, :] = jnp.sum(total * value, axis=0, keepdims=True)
    r.grad_vectors[1:2, :] = jnp.sum(total, axis=0, keepdims=True)
    total = total * r.feed_gain[...].reshape(1, width)
    first_mean = jnp.mean(total, axis=-1, keepdims=True)
    second_mean = jnp.mean(total * value, axis=-1, keepdims=True)
    total = r.cot_v[plane].astype(F32) + r.inverse[...] * (total - first_mean - value * second_mean)
    r.grad_resid[...] = total
    r.grad_branch[...] = total.T.astype(BF)
    out_parts = {}

    def keep_out_left(g, result):
        out_parts[g] = result.astype(BF)

    def keep_out_right(b, result):
        both = jnp.concatenate([result.astype(BF), out_parts[b]], axis=1)
        r.early_own[pl.ds(b * block, block), 0 : 2 * block] = both

    def keep_mixed(b, result):
        r.grad_mixed_own[pl.ds(b * block, block), :] = result.astype(BF)

    monarch_backward(
        lambda g: r.grad_branch[pl.ds(g * block, block), :],
        lambda b: r.mixed[pl.ds(b * block, block), :],
        r.out_shuffled, r.out_right, r.out_left, r.middle, keep_out_right, keep_out_left, keep_mixed,
    )
    mine = pl.ds(pl.multiple_of(me * rows, rows), rows)
    own_chans = pl.ds(pl.multiple_of(me * chans, 16), chans)
    mixed_copies = []
    for k in SEQ_ORDER:
        other = flip(me, k)
        copy = pltpu.make_async_remote_copy(
            src_ref=r.grad_mixed_own.at[pl.ds(pl.multiple_of(other * chans, 16), chans), :],
            dst_ref=r.grad_mixed.at[:, mine],
            send_sem=r.mixed_send.at[k],
            recv_sem=r.mixed_recv.at[k],
            device_id={"seq": other},
            device_id_type=MESH,
        )
        copy.start()
        mixed_copies.append(copy)
    r.grad_mixed[:, mine] = r.grad_mixed_own[own_chans, :]
    squares[0].start_second()

    glus = []
    for k in range(n_tp):
        other = plane if k == 0 else neighbour_order(plane, n_tp - k)

        def glu_step(at, carry, k=k, other=other):
            cols = pl.ds(pl.multiple_of(at * chunk, chunk), chunk)
            result = dot(r.hidden[other], r.down_v[:, cols])
            if k == 0:
                r.glu_own[:, cols] = result
            else:
                r.glu_send[other, :, cols] = result.astype(BF)
            return carry

        lax.fori_loop(0, pieces, glu_step, 0)
        if k > 0:
            copy = pltpu.make_async_remote_copy(
                src_ref=r.glu_send.at[other],
                dst_ref=r.glu_recv.at[plane],
                send_sem=r.glu_ssem.at[other],
                recv_sem=r.glu_rsem.at[plane],
                device_id={"tp": other},
                device_id_type=MESH,
            )
            copy.start()
            glus.append(copy)
    squares[1].start_second()
    r.sums[...] = jnp.zeros_like(r.sums)
    r.small_own[...] = jnp.zeros_like(r.small_own)
    r.early_own[:, 384:512] = jnp.zeros((width, 128), BF)
    r.padded[pl.ds(chans, 128 - chans), :] = jnp.zeros((128 - chans, length), BF)
    for copy in mixed_copies:
        copy.wait_recv()

    def short_step(at, carry):
        here = pl.ds(pl.multiple_of(at * step, step), step)
        shorted = []
        for s in range(3):
            value = r.signals[s, here, :].astype(F32)
            shorted.append(
                previous(value) * r.columns[here, 3 * s : 3 * s + 1]
                + value * r.columns[here, 3 * s + 1 : 3 * s + 2]
                + following(value) * r.columns[here, 3 * s + 2 : 3 * s + 3]
            )
        r.query[here, :] = shorted[0]
        r.value_v[here, :] = shorted[2]
        above = r.grad_mixed[here, :].astype(F32)
        r.grad_short[1, here, :] = above * r.conv[here, :]
        above = above * shorted[1]
        r.grad_conv[here, :] = above
        r.padded[here, :] = above.astype(BF)
        r.sums[here, 9:10] = jnp.sum(above * shorted[0] * shorted[2], axis=1, keepdims=True)
        r.sums[here, 10:11] = jnp.sum(above * sign_lanes(step, length), axis=1, keepdims=True)
        return carry

    lax.fori_loop(0, chans // step, short_step, 0)
    squares[2].start_second()

    def wave_step(at, carry):
        here = pl.ds(pl.multiple_of(at * chunk, chunk), chunk)
        sign = sign_rows(chunk, 128)
        index = lax.broadcasted_iota(jnp.int32, (chunk, 128), 0) + at * chunk
        weight = jnp.where(index == 0, 0.5 / length, 1.0 / length)
        cos_part = dot(r.table_v[0, here, :], r.padded[...], NT)
        sin_part = dot(r.table_v[1, here, :], r.padded[...], NT)
        tap_cos = r.taps_v[0, here, :].astype(F32)
        tap_sin = r.taps_v[1, here, :].astype(F32)
        r.back_wave[0, here, :] = (cos_part * tap_cos + sin_part * tap_sin).astype(BF)
        r.back_wave[1, here, :] = (sin_part * tap_cos - cos_part * tap_sin).astype(BF)
        wave_cos = r.wave[0, here, :].astype(F32) * weight
        wave_sin = r.wave[1, here, :].astype(F32) * weight
        result = cos_part * wave_cos + sin_part * wave_sin
        r.cross[0, here, 0:128] = result.astype(BF)
        r.cross[0, here, 128:256] = (result * sign).astype(BF)
        result = sin_part * wave_cos - cos_part * wave_sin
        r.cross[1, here, 0:128] = result.astype(BF)
        r.cross[1, here, 128:256] = (result * sign).astype(BF)
        return carry

    lax.fori_loop(0, per, wave_step, 0)
    squares[0].start_second_back()
    squares[1].start_second_back()

    def product_step(at, carry):
        here = pl.ds(pl.multiple_of(at * chunk, chunk), chunk)
        result = dot(r.table_v[0, here, :], r.back_wave[0]) + dot(r.table_v[1, here, :], r.back_wave[1])
        result = (
            result.T[:chans]
            + sign_lanes(chans, chunk) * (r.sums[:chans, 10:11] * r.nyquist[:, 1:2] * (0.5 / length))
            + r.columns[:, 9:10] * r.grad_conv[:, here]
        )
        r.grad_short[0, :, here] = result * r.value_v[:, here]
        r.grad_short[2, :, here] = result * r.query[:, here]
        return carry

    lax.fori_loop(0, per, product_step, 0)

    def signal_step(at, carry):
        here = pl.ds(pl.multiple_of(at * step, step), step)
        for s in range(3):
            above = r.grad_short[s, here, :]
            value = r.signals[s, here, :].astype(F32)
            before, after = previous(above), following(above)
            r.grad_signals[s, here, :] = (
                after * r.columns[here, 3 * s : 3 * s + 1]
                + above * r.columns[here, 3 * s + 1 : 3 * s + 2]
                + before * r.columns[here, 3 * s + 2 : 3 * s + 3]
            ).astype(BF)
            r.sums[here, 3 * s : 3 * s + 1] = jnp.sum(after * value, axis=1, keepdims=True)
            r.sums[here, 3 * s + 1 : 3 * s + 2] = jnp.sum(above * value, axis=1, keepdims=True)
            r.sums[here, 3 * s + 2 : 3 * s + 3] = jnp.sum(before * value, axis=1, keepdims=True)
        return carry

    lax.fori_loop(0, chans // step, signal_step, 0)
    seq_copies = []
    for k in SEQ_ORDER:
        other = flip(me, k)
        for s in range(3):
            copy = pltpu.make_async_remote_copy(
                src_ref=r.grad_signals.at[s, :, pl.ds(pl.multiple_of(other * rows, rows), rows)],
                dst_ref=r.grad_proj.at[pl.ds(pl.multiple_of(s * width + me * chans, 16), chans), :],
                send_sem=r.seq_send.at[k, s],
                recv_sem=r.seq_recv.at[k, s],
                device_id={"seq": other},
                device_id_type=MESH,
            )
            copy.start()
            seq_copies.append(copy)
    for s in range(3):
        r.grad_proj[pl.ds(pl.multiple_of(s * width + me * chans, 16), chans), :] = r.grad_signals[s, :, mine]
    squares[2].start_second_back()

    total = r.resid[...] + r.glu_own[...] + from_planes(r.glu_rsem, r.glu_recv)
    r.out_rows[...] = total.astype(BF)
    part = rows // n_tp
    out_copies = []
    for k in range(1, n_tp):
        other = flip(plane, k)
        copy = pltpu.make_async_remote_copy(
            src_ref=r.out_rows.at[pl.ds(pl.multiple_of(other * part, part), part), :],
            dst_ref=r.output_v.at[plane],
            send_sem=r.out_send.at[k],
            recv_sem=r.out_recv.at[k],
            device_id={"tp": other},
            device_id_type=MESH,
        )
        copy.start()
        out_copies.append(copy)
    r.output_v[plane] = r.out_rows[pl.ds(pl.multiple_of(plane * part, part), part), :]

    tap_total = jnp.broadcast_to(r.sums[:, 10:11], (128, 128)).T[0:1, :]
    pad_nyquist = jnp.concatenate([r.nyquist[:, 0:1], jnp.zeros((128 - chans, 1), F32)], axis=0)
    tap_total = tap_total * jnp.broadcast_to(pad_nyquist, (128, 128)).T[0:1, :] * (0.5 / length)
    r.grad_second[...] = jnp.zeros_like(r.grad_second)
    r.grad_first[...] = jnp.zeros_like(r.grad_first)
    r.grad_third[...] = jnp.zeros_like(r.grad_third)

    def filter_step(at, carry):
        here = pl.ds(pl.multiple_of(at * chunk, chunk), chunk)
        result = dot(r.table_v[0, here, :], r.cross[0]) + dot(r.table_v[1, here, :], r.cross[1])
        sign = sign_rows(chunk, 128)
        for half in range(2):
            above = (result[:, half * 128 : (half + 1) * 128] + sign * tap_total) * (length**-0.5)
            if half == 1:
                index = lax.broadcasted_iota(jnp.int32, above.shape, 0) + at * chunk
                above = jnp.where(index == 0, 0.0, above)
            above = above.astype(BF)
            spot = pl.ds(pl.multiple_of(half * length + at * chunk, chunk), chunk)
            r.grad_third[...] += dot(above, r.acts[2, spot, :], TN)
            below = (dot(above, r.third_v[...]) * r.acts[3, spot, :].astype(F32)).astype(BF)
            r.grad_second[...] += dot(r.acts[0, spot, :], below, TN)
            below = (dot(below, r.second[...], NT) * r.acts[1, spot, :].astype(F32)).astype(BF)
            r.grad_first[...] += dot(r.features[spot, :], below, TN)
        return carry

    lax.fori_loop(0, per, filter_step, 0)
    r.early_own[own_chans, 384:512] = r.grad_third[:chans, :].astype(BF)
    r.small_own[0:128, 0:128] = r.grad_second[...].astype(BF)
    r.small_own[128:136, 0:128] = (r.grad_first[0:8, :] + r.grad_first[8:16, :]).astype(BF)
    r.small_own[pl.ds(pl.multiple_of(me * 16, 16), 16), 128:256] = r.sums[...].T[0:16, :].astype(BF)
    early.start_core()
    shifted = tokens - jnp.mean(tokens, axis=-1, keepdims=True)
    inverse = lax.rsqrt(jnp.mean(shifted * shifted, axis=-1, keepdims=True) + 1e-05)
    r.scaled[...] = shifted * inverse
    fan = r.in_left.shape[2]
    for copy in seq_copies:
        copy.wait_recv()
    squares[0].start_first_back()
    squares[1].start_first_back()
    early.start_chip()

    in_parts = {}

    def keep_left(g, result):
        r.late_own[pl.ds(g * block, block), 0:512] = result[:, 0:512].astype(BF)
        in_parts[g] = result[:, 512:576].astype(BF)

    def keep_right(b, result):
        r.late_own[pl.ds(b * block, block), 512:768] = jnp.concatenate([in_parts[b], result.astype(BF)], axis=1)

    def keep_rows(b, result):
        r.grad_rows[pl.ds(b * block, block), :] = result

    part = block // 4
    for g in range(4):
        below = dot(r.in_left[g], r.grad_proj[pl.ds(g * fan, fan), :]).astype(BF)
        for b in range(4):
            r.middle[pl.ds(b * block + g * part, part), :] = below[b * part : (b + 1) * part]
    for b in range(4):
        keep_rows(b, dot(r.in_right[b], r.middle[pl.ds(b * block, block), :]))
    total = r.grad_rows[...].T
    scaled = r.scaled[...]
    lines = [jnp.sum(total * scaled, axis=0, keepdims=True), jnp.sum(total, axis=0, keepdims=True)]
    total = total * r.gain[...].reshape(1, width)
    first_mean = jnp.mean(total, axis=-1, keepdims=True)
    second_mean = jnp.mean(total * scaled, axis=-1, keepdims=True)
    total = r.grad_resid[...] + inverse * (total - first_mean - scaled * second_mean)
    r.grad_tok[...] = total.astype(BF)
    token_line = Line(n_tp, r.tokens_out, r.tok_send, r.tok_recv)
    token_line.begin(r.grad_tok)
    own_tok = pltpu.make_async_copy(r.grad_tok, r.tokens_out.at[plane], r.local_sems.at[13])
    own_tok.start()
    for g in range(4):
        keep_left(g, dot(r.in_shuffled[pl.ds(g * block, block), :], r.grad_proj[pl.ds(g * fan, fan), :], NT))
    for b in range(4):
        keep_right(b, dot(r.in_normed[pl.ds(b * block, block), :], r.middle[pl.ds(b * block, block), :], NT))
    for late in lates:
        late.start_core()
    squares[2].start_first_back()
    early.start_plane()
    for late in lates:
        late.start_chip()
    lines += [r.grad_vectors[0:1, :], r.grad_vectors[1:2, :]]
    packed = [row[:, at * 128 : (at + 1) * 128] for row in lines for at in range(width // 128)]
    r.small_own[128:160, 128:256] = jnp.concatenate(packed + [jnp.zeros((8, 128), F32)], axis=0).astype(BF)
    small.start_core()
    early.start_plane_back()
    small.start_chip()
    token_line.take(neighbour_order(plane, 1))
    for late in lates:
        late.start_plane()
    small.start_plane()
    early.start_chip_back()
    for square in squares:
        square.start_core_back()
    token_line.take(neighbour_order(plane, 2))
    for late in lates:
        late.start_plane_back()
    small.start_plane_back()
    for late in lates:
        late.start_chip_back()
    small.start_chip_back()
    early.start_core_back()
    token_line.take(neighbour_order(plane, 3))
    ffn_copies = []
    for which, square in enumerate(squares):
        square.arrived()
        copy = pltpu.make_async_copy(r.ffn_v.at[which], r.ffn_out.at[which], r.local_sems.at[14 + which])
        copy.start()
        ffn_copies.append(copy)
    for late in lates:
        late.start_core_back()
    small.start_core_back()
    early.finish()
    r.early_out[...] = r.early_full[...]
    small.finish()
    r.small_out[...] = r.small_full[...]
    for copy in out_copies:
        copy.wait()
    r.output_out[...] = r.output_v[...]
    for late in lates:
        late.finish()
    r.late_out[...] = r.late_full[...]
    for copy in mixed_copies + seq_copies + backs + glus + front_sends + cot_copies:
        copy.wait_send()
    for square in squares:
        square.finish()
    line.finish()
    token_line.finish()
    own_tok.wait()
    for copy in ffn_copies:
        copy.wait()


def core(mesh_shape, *operands):
    n_seq, n_tp = mesh_shape
    tokens = Inputs(*operands).tokens
    _, rows, width = tokens.shape
    chans, length = width // n_seq, rows * n_seq
    scratch, groups = core_scratch(n_seq, n_tp, width, chans, length, rows)
    shape = jax.ShapeDtypeStruct
    return pl.pallas_call(
        functools.partial(core_kernel, n_seq, n_tp, (width, chans, length, rows)),
        out_shape=(
            shape((n_tp, rows // n_tp, width), BF),
            shape((3, width, width), BF),
            shape((n_tp, rows, width), BF),
            shape((width, width), BF),
            shape((width, 512), BF),
            shape((256, 256), BF),
        ),
        in_specs=[vmem_spec()] * 14 + [any_spec()] * (len(Inputs._fields) - 14),
        out_specs=(vmem_spec(), any_spec(), any_spec(), vmem_spec(), vmem_spec(), vmem_spec()),
        scratch_shapes=list(scratch.values()) + sum(groups, []),
        compiler_params=pltpu.CompilerParams(collective_id=0, has_side_effects=True, vmem_limit_bytes=60 * 1024 * 1024),
        name="layer",
    )(*operands)


def finish_kernel(width, chans, *refs):
    (ffn, tokens, late, early, small) = refs[:5]
    (grad_tokens, norm_gain, norm_bias, in_right, in_left, short, first, second, third, conv_bias, out_right, out_left,
     ffn_gain, ffn_bias, gate, up, down) = refs[5:22]
    (ffn_v, ffn_f, token_v, token_f, late_v, early_v, in_right_f, in_left_f, out_right_f, out_left_f, in_sems, out_sems) = refs[22:]
    pairs = [(ffn.at[which], ffn_v.at[which]) for which in range(3)] + [(tokens, token_v), (late, late_v), (early, early_v)]
    loads = [pltpu.make_async_copy(*pair, in_sems.at[at]) for at, pair in enumerate(pairs)]
    for copy in loads:
        copy.start()
    pairs = [(ffn_f.at[which], target) for which, target in enumerate((gate, up, down))]
    pairs += [
        (token_f, grad_tokens), (in_right_f, in_right), (in_left_f, in_left), (out_right_f, out_right), (out_left_f, out_left)
    ]
    stores = [pltpu.make_async_copy(*pair, out_sems.at[at]) for at, pair in enumerate(pairs)]
    chunk = 64
    for which in range(3):
        loads[which].wait()

        def step(at, carry, which=which):
            here = pl.ds(pl.multiple_of(at * chunk, chunk), chunk)
            ffn_f[which, here, :] = ffn_v[which, here, :].astype(F32)
            return carry

        lax.fori_loop(0, width // chunk, step, 0)
        stores[which].start()
    loads[3].wait()

    def token_step(at, carry):
        token_f[at] = token_v[at].astype(F32)
        return carry

    lax.fori_loop(0, token_v.shape[0], token_step, 0)
    stores[3].start()
    groups, block, _ = in_right.shape
    loads[4].wait()
    for b in range(groups):
        here = pl.ds(b * block, block)
        in_left_f[b] = late_v[here, 0 : 3 * block].astype(F32)
        in_right_f[b] = late_v[here, 3 * block : 4 * block].astype(F32)
    stores[4].start()
    stores[5].start()
    loads[5].wait()
    for b in range(groups):
        here = pl.ds(b * block, block)
        out_right_f[b] = early_v[here, 0:block].astype(F32)
        out_left_f[b] = early_v[here, block : 2 * block].astype(F32)
    stores[6].start()
    stores[7].start()
    third[...] = early_v[:, 384:512].astype(F32).T
    values = small[...].astype(F32)
    second[...] = values[0:128, 0:128]
    first[...] = values[128:133, 0:128]
    for at, target in enumerate((norm_gain, norm_bias, ffn_gain, ffn_bias)):
        row = 128 + at * (width // 128)
        target[...] = jnp.concatenate([values[row + k : row + k + 1, 128:256] for k in range(width // 128)], axis=1).reshape(width)
    parts = [values[16 * at : 16 * at + 16, 128 : 128 + chans] for at in range(width // chans)]
    lines = jnp.concatenate(parts, axis=1)
    for s in range(3):
        short[s] = lines[3 * s : 3 * s + 3]
    conv_bias[...] = lines[9:10].reshape(width)
    for copy in stores:
        copy.wait()


def finish(chans, ffn, tokens, late, early, small):
    width = ffn.shape[1]
    block = width // 4
    shape = jax.ShapeDtypeStruct
    vector = shape((width,), F32)
    square = shape((4, block, block), F32)
    wide = shape((4, block, 3 * block), F32)
    return pl.pallas_call(
        functools.partial(finish_kernel, width, chans),
        out_shape=(
            shape(tokens.shape, F32), vector, vector, square, wide, shape((3, 3, width), F32),
            shape((5, 128), F32), shape((128, 128), F32), shape((128, width), F32), vector, square, square, vector, vector,
        )
        + (shape((width, width), F32),) * 3,
        in_specs=[any_spec()] * 4 + [vmem_spec()],
        out_specs=(any_spec(), vmem_spec(), vmem_spec(), any_spec(), any_spec())
        + (vmem_spec(),) * 5
        + (any_spec(), any_spec(), vmem_spec(), vmem_spec())
        + (any_spec(),) * 3,
        scratch_shapes=[
            pltpu.VMEM(ffn.shape, BF),
            pltpu.VMEM(ffn.shape, F32),
            pltpu.VMEM(tokens.shape, BF),
            pltpu.VMEM(tokens.shape, F32),
            pltpu.VMEM(late.shape, BF),
            pltpu.VMEM(early.shape, BF),
            pltpu.VMEM(square.shape, F32),
            pltpu.VMEM(wide.shape, F32),
            pltpu.VMEM(square.shape, F32),
            pltpu.VMEM(square.shape, F32),
            pltpu.SemaphoreType.DMA((6,)),
            pltpu.SemaphoreType.DMA((8,)),
        ],
        compiler_params=pltpu.CompilerParams(vmem_limit_bytes=LIMIT),
        name="finish",
    )(ffn, tokens, late, early, small)


def fast_body(
    tokens,
    norm_gain,
    norm_bias,
    in_right,
    in_left,
    short_kernel,
    filter_first,
    filter_second,
    filter_third,
    conv_bias,
    out_right,
    out_left,
    ffn_gain,
    ffn_bias,
    gate_weight,
    up_weight,
    down_weight,
    cotangent,
):
    n_seq, n_tp = lax.axis_size("seq"), lax.axis_size("tp")
    _, rows, width = tokens.shape
    chans, length = width // n_seq, rows * n_seq
    shape = (n_seq, n_tp)
    table, features = (jnp.asarray(array) for array in constants(length))
    output, ffn, grad_tokens, late, early, small = core(
        shape, ffn_gain, ffn_bias, out_right, out_left, norm_gain, norm_bias, in_right, in_left, short_kernel.transpose(0, 2, 1),
        conv_bias, features, filter_first, filter_second, filter_third, tokens, cotangent, table, gate_weight, up_weight,
        down_weight,
    )
    grads = finish(chans, ffn, grad_tokens, late, early, small)
    return (output,) + grads[:5] + (grads[5].transpose(0, 2, 1),) + grads[6:]


highest = lax.Precision.HIGHEST


def norm_forward(values, gain, bias):
    centre = jnp.mean(values, axis=-1, keepdims=True)
    shifted = values - centre
    inverse = lax.rsqrt(jnp.mean(shifted * shifted, axis=-1, keepdims=True) + 1e-05)
    scaled = shifted * inverse
    return (scaled * gain + bias, scaled, inverse)


def norm_backward(upstream, scaled, inverse, gain):
    weighted = upstream * gain
    first_mean = jnp.mean(weighted, axis=-1, keepdims=True)
    second_mean = jnp.mean(weighted * scaled, axis=-1, keepdims=True)
    grad_input = inverse * (weighted - first_mean - scaled * second_mean)
    breadth = upstream.shape[-1]
    grad_gain = jnp.sum((upstream * scaled).reshape(-1, breadth), axis=0)
    grad_bias = jnp.sum(upstream.reshape(-1, breadth), axis=0)
    return (grad_input, grad_gain, grad_bias)


def shuffle(blocked):
    row_count, groups, breadth = blocked.shape
    return (
        blocked.reshape(row_count, groups, groups, breadth // groups)
        .transpose(0, 2, 1, 3)
        .reshape(row_count, groups, breadth)
    )


def rows_monarch_forward(operand, right_factor, left_factor):
    row_count = operand.shape[0]
    groups = right_factor.shape[0]
    blocked = operand.reshape(row_count, groups, -1)
    middle = jnp.einsum(
        "tbi,bij->tbj", blocked, right_factor, preferred_element_type=jnp.float32
    ).astype(jnp.bfloat16)
    shuffled = shuffle(middle)
    result = jnp.einsum("tbi,bij->tbj", shuffled, left_factor, preferred_element_type=jnp.float32)
    return (shuffled, result.reshape(row_count, -1))


def rows_monarch_backward(grad_result, operand, shuffled, right_factor, left_factor):
    row_count = operand.shape[0]
    groups = right_factor.shape[0]
    grad_blocked = grad_result.reshape(row_count, groups, -1)
    grad_left = jnp.einsum(
        "tbi,tbj->bij", shuffled, grad_blocked, preferred_element_type=jnp.float32
    )
    grad_shuffled = jnp.einsum(
        "tbj,bij->tbi", grad_blocked, left_factor, preferred_element_type=jnp.float32
    )
    grad_middle = shuffle(grad_shuffled).astype(jnp.bfloat16)
    blocked = operand.reshape(row_count, groups, -1)
    grad_right = jnp.einsum(
        "tbi,tbj->bij", blocked, grad_middle, preferred_element_type=jnp.float32
    )
    grad_operand = jnp.einsum(
        "tbj,bij->tbi", grad_middle, right_factor, preferred_element_type=jnp.float32
    )
    return (grad_operand.reshape(row_count, -1), grad_right, grad_left)


def roots(row_count, col_count, period):
    product = jnp.arange(row_count)[:, None] * jnp.arange(col_count)[None, :] % period
    angle = product.astype(jnp.float32) * (2.0 * math.pi / period)
    return (jnp.cos(angle), jnp.sin(angle))


def complex_step(real_part, imag_part, cos_table, sin_table, sign, form):
    real_out = jnp.einsum(form, real_part, cos_table, precision=highest) - sign * jnp.einsum(
        form, imag_part, sin_table, precision=highest
    )
    imag_out = jnp.einsum(form, imag_part, cos_table, precision=highest) + sign * jnp.einsum(
        form, real_part, sin_table, precision=highest
    )
    return (real_out, imag_out)


def real_step(real_part, cos_table, sin_table, sign, form):
    real_out = jnp.einsum(form, real_part, cos_table, precision=highest)
    imag_out = sign * jnp.einsum(form, real_part, sin_table, precision=highest)
    return (real_out, imag_out)


def twiddle(real_part, imag_part, cos_table, sin_table, sign):
    real_out = real_part * cos_table - sign * imag_part * sin_table
    imag_out = imag_part * cos_table + sign * real_part * sin_table
    return (real_out, imag_out)


def spectrum_of(real_part):
    total = real_part.shape[-1]
    first = math.gcd(total, 128)
    second = total // first
    leading = real_part.shape[:-1]
    real_part = real_part.reshape(leading + (first, second))
    cos_first, sin_first = roots(first, first, first)
    real_part, imag_part = real_step(real_part, cos_first, sin_first, -1.0, "...ab,ak->...kb")
    cos_twist, sin_twist = roots(first, second, total)
    real_part, imag_part = twiddle(real_part, imag_part, cos_twist, sin_twist, -1.0)
    cos_second, sin_second = roots(second, second, second)
    return complex_step(real_part, imag_part, cos_second, sin_second, -1.0, "...kb,bm->...km")


def signal_of(real_part, imag_part):
    first = real_part.shape[-2]
    second = real_part.shape[-1]
    total = first * second
    leading = real_part.shape[:-2]
    cos_second, sin_second = roots(second, second, second)
    real_part, imag_part = complex_step(
        real_part, imag_part, cos_second, sin_second, 1.0, "...kb,bm->...km"
    )
    cos_twist, sin_twist = roots(first, second, total)
    real_part, imag_part = twiddle(real_part, imag_part, cos_twist, sin_twist, 1.0)
    cos_first, sin_first = roots(first, first, first)
    real_part, imag_part = complex_step(
        real_part, imag_part, cos_first, sin_first, 1.0, "...ab,ak->...kb"
    )
    return real_part.reshape(leading + (total,)) / total


def filter_parts(filter_first, filter_second, third_cols, seq_length):
    total = 2 * seq_length
    index = jnp.arange(total)
    offset = jnp.where(index < seq_length, index, index - total).astype(jnp.float32)
    scaled = offset / seq_length
    features = jnp.stack(
        [
            scaled,
            jnp.sin(math.pi * scaled),
            jnp.cos(math.pi * scaled),
            jnp.sin(7.0 * math.pi * scaled),
            jnp.cos(7.0 * math.pi * scaled),
        ],
        axis=1,
    )
    pre_one = jnp.dot(features, filter_first, precision=highest)
    act_one = jnp.sin(pre_one)
    pre_two = jnp.dot(act_one, filter_second, precision=highest)
    act_two = jnp.sin(pre_two)
    tap_mask = (index != seq_length).astype(jnp.float32)[:, None] * seq_length ** (-0.5)
    taps = jnp.dot(act_two, third_cols, precision=highest) * tap_mask
    filt_real, filt_imag = spectrum_of(taps.T)
    return (features, pre_one, act_one, pre_two, act_two, tap_mask, filt_real, filt_imag)


def general_body(
    tokens,
    norm_gain,
    norm_bias,
    in_right,
    in_left,
    short_kernel,
    filter_first,
    filter_second,
    filter_third,
    conv_bias,
    out_right,
    out_left,
    ffn_gain,
    ffn_bias,
    gate_weight,
    up_weight,
    down_weight,
    cotangent,
):
    seq_count, pos_count, model_width = tokens.shape
    row_count = seq_count * pos_count
    axis_count = lax.axis_size("seq")
    my_index = lax.axis_index("seq")
    chan_count = model_width // axis_count
    seq_length = pos_count * axis_count
    part_rows = cotangent.shape[1]
    tp_index = lax.axis_index("tp")
    tp_count = lax.axis_size("tp")
    chan_start = my_index * chan_count
    mix_count = seq_count // tp_count
    mix_tokens = lax.dynamic_slice_in_dim(tokens, tp_index * mix_count, mix_count, 0)
    mix_rows = mix_count * pos_count
    flat = mix_tokens.reshape(mix_rows, model_width).astype(jnp.float32)
    normed, scaled_one, inverse_one = norm_forward(flat, norm_gain, norm_bias)
    normed_low = normed.astype(jnp.bfloat16)
    shuffled_in, projected = rows_monarch_forward(normed_low, in_right, in_left)
    projected_low = (
        projected.astype(jnp.bfloat16)
        .reshape(mix_count, pos_count, 3, model_width)
        .transpose(2, 3, 0, 1)
    )
    channels = lax.all_to_all(projected_low, "seq", split_axis=1, concat_axis=3, tiled=True)
    signals = channels.astype(jnp.float32)
    kernel = lax.dynamic_slice_in_dim(short_kernel, chan_start, chan_count, 1).astype(jnp.float32)
    tap_zero = kernel[:, :, 0][:, :, None, None]
    tap_one = kernel[:, :, 1][:, :, None, None]
    tap_two = kernel[:, :, 2][:, :, None, None]
    padded = jnp.pad(signals, ((0, 0), (0, 0), (0, 0), (1, 1)))
    shorted = padded[..., :-2] * tap_zero + padded[..., 1:-1] * tap_one + padded[..., 2:] * tap_two
    first_f = filter_first.astype(jnp.float32)
    second_f = filter_second.astype(jnp.float32)
    third_cols = lax.dynamic_slice_in_dim(filter_third, chan_start, chan_count, 1).astype(
        jnp.float32
    )
    kept = filter_parts(first_f, second_f, third_cols, seq_length)
    filt_real = kept[6][:, None]
    filt_imag = kept[7][:, None]
    bias_cols = lax.dynamic_slice_in_dim(conv_bias, chan_start, chan_count, 0)[:, None, None]
    product = shorted[0] * shorted[2]
    product_pad = jnp.pad(product, ((0, 0), (0, 0), (0, seq_length)))
    spec_real, spec_imag = spectrum_of(product_pad)
    conv_real = spec_real * filt_real - spec_imag * filt_imag
    conv_imag = spec_real * filt_imag + spec_imag * filt_real
    convolved = signal_of(conv_real, conv_imag)[..., :seq_length] + bias_cols * product
    mixed_low = (shorted[1] * convolved).astype(jnp.bfloat16)
    back_rows = lax.all_to_all(mixed_low, "seq", split_axis=2, concat_axis=0, tiled=True)
    mixed_rows = back_rows.transpose(1, 2, 0).reshape(mix_rows, model_width)
    shuffled_out, branch = rows_monarch_forward(mixed_rows, out_right, out_left)
    residual_mine = (flat + branch).reshape(mix_count, pos_count, model_width)
    residual = lax.all_gather(residual_mine, "tp", axis=0, tiled=True)
    part_resid = lax.dynamic_slice_in_dim(residual, tp_index * part_rows, part_rows, 1)
    normed_two, scaled_two, inverse_two = norm_forward(part_resid, ffn_gain, ffn_bias)
    normed_rows = lax.all_gather(normed_two.astype(jnp.bfloat16), "tp", axis=1, tiled=True).reshape(
        row_count, model_width
    )
    gate = jnp.dot(normed_rows, gate_weight, preferred_element_type=jnp.float32)
    upward = jnp.dot(normed_rows, up_weight, preferred_element_type=jnp.float32)
    sigma = jax.nn.sigmoid(gate)
    hidden_low = (gate * sigma * upward).astype(jnp.bfloat16)
    partial_down = jnp.dot(hidden_low, down_weight, preferred_element_type=jnp.float32).reshape(
        seq_count, pos_count, model_width
    )
    glu_part = lax.psum_scatter(
        partial_down.astype(jnp.bfloat16), "tp", scatter_dimension=1, tiled=True
    ).astype(jnp.float32)
    output = (part_resid + glu_part).astype(jnp.bfloat16)
    grad_out_rows = lax.all_gather(cotangent, "tp", axis=1, tiled=True).reshape(
        row_count, model_width
    )
    grad_hidden = jnp.dot(grad_out_rows, down_weight.T, preferred_element_type=jnp.float32)
    grad_gate = (grad_hidden * upward * (sigma + gate * sigma * (1.0 - sigma))).astype(jnp.bfloat16)
    grad_up = (grad_hidden * gate * sigma).astype(jnp.bfloat16)
    grad_down_w = jnp.dot(hidden_low.T, grad_out_rows, preferred_element_type=jnp.float32)
    grad_gate_w = jnp.dot(normed_rows.T, grad_gate, preferred_element_type=jnp.float32)
    grad_up_w = jnp.dot(normed_rows.T, grad_up, preferred_element_type=jnp.float32)
    grad_normed = jnp.dot(grad_gate, gate_weight.T, preferred_element_type=jnp.float32) + jnp.dot(
        grad_up, up_weight.T, preferred_element_type=jnp.float32
    )
    grad_normed_part = lax.psum_scatter(
        grad_normed.reshape(seq_count, pos_count, model_width),
        "tp",
        scatter_dimension=1,
        tiled=True,
    )
    grad_in_two, grad_gain_two, grad_bias_two = norm_backward(
        grad_normed_part, scaled_two, inverse_two, ffn_gain
    )
    gain_total = lax.psum((grad_gain_two, grad_bias_two), ("seq", "tp"))
    grad_resid_part = cotangent.astype(jnp.float32) + grad_in_two
    grad_resid = lax.all_gather(
        grad_resid_part.astype(jnp.bfloat16), "tp", axis=1, tiled=True
    ).astype(grad_resid_part.dtype)
    grad_resid_mix = lax.dynamic_slice_in_dim(
        grad_resid, tp_index * mix_count, mix_count, 0
    ).reshape(mix_rows, model_width)
    grad_mixed_rows, grad_out_right, grad_out_left = rows_monarch_backward(
        grad_resid_mix.astype(jnp.bfloat16), mixed_rows, shuffled_out, out_right, out_left
    )
    grad_mixed_low = (
        grad_mixed_rows.astype(jnp.bfloat16)
        .reshape(mix_count, pos_count, model_width)
        .transpose(2, 0, 1)
    )
    grad_mixed = lax.all_to_all(
        grad_mixed_low, "seq", split_axis=0, concat_axis=2, tiled=True
    ).astype(jnp.float32)
    grad_conv = grad_mixed * shorted[1]
    grad_key = grad_mixed * convolved
    again = lax.optimization_barrier((first_f, second_f, third_cols))
    kept = filter_parts(again[0], again[1], again[2], seq_length)
    filt_real = kept[6][:, None]
    filt_imag = kept[7][:, None]
    features, pre_one, act_one, pre_two, act_two, tap_mask = (
        kept[0],
        kept[1],
        kept[2],
        kept[3],
        kept[4],
        kept[5],
    )
    grad_pad = jnp.pad(grad_conv, ((0, 0), (0, 0), (0, seq_length)))
    grad_spec_real, grad_spec_imag = spectrum_of(grad_pad)
    back_real = grad_spec_real * filt_real + grad_spec_imag * filt_imag
    back_imag = grad_spec_imag * filt_real - grad_spec_real * filt_imag
    grad_product = signal_of(back_real, back_imag)[..., :seq_length] + bias_cols * grad_conv
    grad_bias_cols = jnp.sum(grad_conv * product, axis=(1, 2))
    taps_real = jnp.sum(grad_spec_real * spec_real + grad_spec_imag * spec_imag, axis=1)
    taps_imag = jnp.sum(grad_spec_imag * spec_real - grad_spec_real * spec_imag, axis=1)
    grad_taps = signal_of(taps_real, taps_imag)
    grad_pre = grad_taps.T * tap_mask
    grad_third_cols = jnp.dot(act_two.T, grad_pre, precision=highest)
    grad_pre_two = jnp.dot(grad_pre, third_cols.T, precision=highest) * jnp.cos(pre_two)
    grad_second = jnp.dot(act_one.T, grad_pre_two, precision=highest)
    grad_pre_one = jnp.dot(grad_pre_two, second_f.T, precision=highest) * jnp.cos(pre_one)
    grad_first = jnp.dot(features.T, grad_pre_one, precision=highest)
    grad_shorted = jnp.stack([grad_product * shorted[2], grad_key, grad_product * shorted[0]])
    grad_short_pad = jnp.pad(grad_shorted, ((0, 0), (0, 0), (0, 0), (1, 1)))
    grad_signals = (
        grad_short_pad[..., 2:] * tap_zero
        + grad_short_pad[..., 1:-1] * tap_one
        + grad_short_pad[..., :-2] * tap_two
    )
    grad_kernel = jnp.stack(
        [
            jnp.sum(grad_shorted * padded[..., :-2], axis=(2, 3)),
            jnp.sum(grad_shorted * padded[..., 1:-1], axis=(2, 3)),
            jnp.sum(grad_shorted * padded[..., 2:], axis=(2, 3)),
        ],
        axis=-1,
    )
    grad_proj = lax.all_to_all(
        grad_signals.astype(jnp.bfloat16), "seq", split_axis=3, concat_axis=1, tiled=True
    )
    grad_proj_rows = grad_proj.transpose(2, 3, 0, 1).reshape(mix_rows, 3 * model_width)
    grad_normed_one, grad_in_right, grad_in_left = rows_monarch_backward(
        grad_proj_rows, normed_low, shuffled_in, in_right, in_left
    )
    grad_in_one, grad_gain_one, grad_bias_one = norm_backward(
        grad_normed_one, scaled_one, inverse_one, norm_gain
    )
    grad_mine = (grad_resid_mix + grad_in_one).reshape(mix_count, pos_count, model_width)
    short_full = lax.dynamic_update_slice_in_dim(
        jnp.zeros(short_kernel.shape, jnp.float32), grad_kernel, chan_start, 1
    )
    third_full = lax.dynamic_update_slice_in_dim(
        jnp.zeros(filter_third.shape, jnp.float32), grad_third_cols, chan_start, 1
    )
    bias_full = lax.dynamic_update_slice_in_dim(
        jnp.zeros(conv_bias.shape, jnp.float32), grad_bias_cols, chan_start, 0
    )
    mixer_grads = (
        grad_gain_one,
        grad_bias_one,
        grad_in_right,
        grad_in_left,
        short_full,
        grad_first,
        grad_second,
        third_full,
        bias_full,
        grad_out_right,
        grad_out_left,
    )
    grad_tokens = lax.all_gather(grad_mine.astype(jnp.bfloat16), "tp", axis=0, tiled=True).astype(
        grad_mine.dtype
    )
    mixer_grads = (
        lax.psum(mixer_grads[0].astype(jnp.bfloat16), "tp").astype(jnp.float32),
        lax.psum(mixer_grads[1].astype(jnp.bfloat16), "tp").astype(jnp.float32),
        lax.psum(mixer_grads[2].astype(jnp.bfloat16), "tp").astype(jnp.float32),
        lax.psum(mixer_grads[3].astype(jnp.bfloat16), "tp").astype(jnp.float32),
        lax.psum(mixer_grads[4].astype(jnp.bfloat16), "tp").astype(jnp.float32),
        lax.psum(mixer_grads[5].astype(jnp.bfloat16), "tp").astype(jnp.float32),
        lax.psum(mixer_grads[6].astype(jnp.bfloat16), "tp").astype(jnp.float32),
        lax.psum(mixer_grads[7].astype(jnp.bfloat16), "tp").astype(jnp.float32),
        lax.psum(mixer_grads[8].astype(jnp.bfloat16), "tp").astype(jnp.float32),
        lax.psum(mixer_grads[9].astype(jnp.bfloat16), "tp").astype(jnp.float32),
        lax.psum(mixer_grads[10].astype(jnp.bfloat16), "tp").astype(jnp.float32),
    )
    all_total = lax.psum(
        (
            mixer_grads[0],
            mixer_grads[1],
            mixer_grads[2],
            mixer_grads[3],
            mixer_grads[4],
            mixer_grads[5],
            mixer_grads[6],
            mixer_grads[7],
            mixer_grads[8],
            mixer_grads[9],
            mixer_grads[10],
            grad_gate_w,
            grad_up_w,
            grad_down_w,
        ),
        "seq",
    )
    return (
        output,
        grad_tokens,
        all_total[0],
        all_total[1],
        all_total[2],
        all_total[3],
        all_total[4],
        all_total[5],
        all_total[6],
        all_total[7],
        all_total[8],
        all_total[9],
        all_total[10],
        gain_total[0],
        gain_total[1],
        all_total[11],
        all_total[12],
        all_total[13],
    )


def choose_body(mesh, *arrays):
    tokens = arrays[0]
    chans = tokens.shape[2] // mesh.shape["seq"]
    fits = mesh.shape["seq"] == 8 and mesh.shape["tp"] == 4 and tokens.shape[:2] == (4, 128) and chans == 96
    return (fast_body if fits else general_body)(*arrays)


def solution(mesh):
    mapped = jax.shard_map(
        functools.partial(choose_body, mesh),
        mesh=mesh,
        in_specs=(
            P(None, "seq", None),
            P(),
            P(),
            P(),
            P(),
            P(),
            P(),
            P(),
            P(),
            P(),
            P(),
            P(),
            P(),
            P(),
            P(None, "tp"),
            P(None, "tp"),
            P("tp", None),
            P(None, ("seq", "tp"), None),
        ),
        out_specs=(
            P(None, ("seq", "tp"), None),
            P(None, "seq", None),
            P(),
            P(),
            P(),
            P(),
            P(),
            P(),
            P(),
            P(),
            P(),
            P(),
            P(),
            P(),
            P(),
            P(None, "tp"),
            P(None, "tp"),
            P("tp", None),
        ),
        check_vma=False,
    )

    def program(*arrays):
        with jax.sharding.use_abstract_mesh(mesh.abstract_mesh):
            return mapped(*arrays)

    return program
```

```python
import functools
import math
import types
import typing

import numpy as np
import jax
import jax.numpy as jnp
from jax import lax
from jax.experimental import pallas as pl
from jax.experimental.pallas import tpu as pltpu
from jax.sharding import PartitionSpec as P

BF = jnp.bfloat16
F32 = jnp.float32
MESH = pl.DeviceIdType.MESH
NN = ((1,), (0,))
NT = ((1,), (1,))
TN = ((0,), (0,))
LIMIT = 56 * 1024 * 1024


def dot(first, second, form=NN):
    return lax.dot_general(first, second, (form, ((), ())), preferred_element_type=F32)


def any_spec():
    return pl.BlockSpec(memory_space=pl.ANY)


def vmem_spec():
    return pl.BlockSpec(memory_space=pltpu.VMEM)


def sin_cos(value):
    turns = jnp.floor(value * (1.0 / math.pi) + 0.5)
    rest = value - turns * 3.140625
    rest = rest - turns * 9.67502593994140625e-4
    rest = rest - turns * 1.509957990978376432e-7
    half = turns * 0.5
    sign = 1.0 - 4.0 * (half - jnp.floor(half))
    square = rest * rest
    sine = 1.0 / 362880 - square * (1.0 / 39916800)
    sine = -1.0 / 5040 + square * sine
    sine = 1.0 / 120 + square * sine
    sine = -1.0 / 6 + square * sine
    sine = rest + rest * square * sine
    cosine = 1.0 / 40320 - square * (1.0 / 3628800 - square * (1.0 / 479001600))
    cosine = -1.0 / 720 + square * cosine
    cosine = 1.0 / 24 + square * cosine
    cosine = -0.5 + square * cosine
    cosine = 1.0 + square * cosine
    return sign * sine, sign * cosine


def flip(index, bits):
    result = 0
    for place in range(3):
        digit = lax.rem(index // (1 << place), 2)
        if (bits >> place) & 1:
            digit = 1 - digit
        result = result + digit * (1 << place)
    return result


def greet(n_seq, n_tp):
    me, plane = lax.axis_index("seq"), lax.axis_index("tp")
    barrier = pltpu.get_barrier_semaphore()
    for k in range(1, n_seq):
        pl.semaphore_signal(barrier, inc=1, device_id={"seq": flip(me, k)}, device_id_type=MESH)
    for k in range(1, n_tp):
        pl.semaphore_signal(barrier, inc=1, device_id={"tp": flip(plane, k)}, device_id_type=MESH)
    return lambda: pl.semaphore_wait(barrier, n_seq + n_tp - 2)


def sign_rows(count, width):
    row = lax.broadcasted_iota(jnp.int32, (count, width), 0)
    return (1 - 2 * lax.rem(row, 2)).astype(F32)


def sign_lanes(count, width):
    lane = lax.broadcasted_iota(jnp.int32, (count, width), 1)
    return (1 - 2 * lax.rem(lane, 2)).astype(F32)


def previous(values):
    lane = lax.broadcasted_iota(jnp.int32, values.shape, 1)
    return jnp.where(lane == 0, 0.0, pltpu.roll(values, 1, 1))


def following(values):
    last = values.shape[1] - 1
    lane = lax.broadcasted_iota(jnp.int32, values.shape, 1)
    return jnp.where(lane == last, 0.0, pltpu.roll(values, last, 1))


def monarch_forward(load, right, left, shuffled, store):
    groups, width, _ = right.shape
    part = width // groups
    for b in range(groups):
        middle = dot(right[b], load(b), TN).astype(BF)
        for g in range(groups):
            shuffled[pl.ds(g * width + b * part, part), :] = middle[g * part : (g + 1) * part]
    for g in range(groups):
        store(g, dot(left[g], shuffled[pl.ds(g * width, width), :], TN))


SEQ_ORDER = (6, 7, 2, 3, 4, 5, 1)


def front_part(n_seq, n_tp, dims, r, entered, loads):
    width, chans, length, rows = dims
    me, plane = lax.axis_index("seq"), lax.axis_index("tp")
    cotangent, right, left, features = r.cotangent, r.in_right, r.in_left, r.features
    token_v, table_v, normed, shuffled, signals = r.token_v, r.table_v, r.in_normed, r.in_shuffled, r.signals
    acts, taps_v, padded, wave, conv, nyquist, columns, third_v = (
        r.acts, r.taps_v, r.padded, r.wave, r.conv, r.nyquist, r.columns, r.third_v
    )
    projected, spread, product, keyed, spectrum, mixed, totals = (
        r.projected, r.spread, r.product, r.query, r.back_wave, r.front_mixed, r.totals
    )
    loads.token.wait()
    value = token_v[...].astype(F32)
    shifted = value - jnp.mean(value, axis=-1, keepdims=True)
    inverse = lax.rsqrt(jnp.mean(shifted * shifted, axis=-1, keepdims=True) + 1e-05)
    value = shifted * inverse * r.gain[...].reshape(1, width) + r.bias[...].reshape(1, width)
    normed[...] = value.T.astype(BF)
    groups = right.shape[0]
    block = width // groups
    fan = left.shape[2]

    def keep(g, result):
        projected[pl.ds(g * fan, fan), :] = result.astype(BF)

    monarch_forward(lambda b: normed[pl.ds(b * block, block), :], right, left, shuffled, keep)
    entered()
    sends = []
    mine = pl.ds(pl.multiple_of(me * rows, rows), rows)
    for k in SEQ_ORDER:
        other = flip(me, k)
        for s in range(3):
            copy = pltpu.make_async_remote_copy(
                src_ref=projected.at[pl.ds(pl.multiple_of(s * width + other * chans, 16), chans), :],
                dst_ref=signals.at[s, :, mine],
                send_sem=r.front_send.at[k, s],
                recv_sem=r.front_recv.at[k, s],
                device_id={"seq": other},
                device_id_type=MESH,
            )
            copy.start()
            sends.append(copy)
    for s in range(3):
        signals[s, :, mine] = projected[pl.ds(pl.multiple_of(s * width + me * chans, 16), chans), :]
    part = rows // n_tp
    spot = pl.ds(pl.multiple_of(plane * part, part), part)
    cot_copies = []
    for k in range(1, n_tp):
        copy = pltpu.make_async_remote_copy(
            src_ref=cotangent,
            dst_ref=r.cot_v.at[:, spot, :],
            send_sem=r.cot_send.at[k],
            recv_sem=r.cot_recv.at[k],
            device_id={"tp": flip(plane, k)},
            device_id_type=MESH,
        )
        copy.start()
        cot_copies.append(copy)
    own_cot = pltpu.make_async_copy(cotangent, r.cot_v.at[:, spot, :], r.local_sems.at[17])
    own_cot.start()

    own = pl.ds(pl.multiple_of(me * chans, 16), chans)
    lines = [r.short[s].astype(F32) for s in range(3)]
    lines += [r.conv_bias[...].reshape(1, width), jnp.zeros((6, width), F32)]
    r.tall[...] = jnp.concatenate(lines, axis=0).T
    columns[...] = r.tall[own, :]
    r.third_turned[...] = r.third[...].T
    third_v[pl.ds(0, chans), :] = r.third_turned[own, :]
    third_v[pl.ds(chans, 128 - chans), :] = jnp.zeros((128 - chans, 128), BF)
    lead = jnp.concatenate([r.first[...].astype(F32), jnp.zeros((3, 128), F32)], axis=0)
    lead = jnp.concatenate([lead, lead], axis=0).astype(BF)

    chunk = 256
    per = length // chunk
    totals[...] = jnp.zeros_like(totals)
    for half in range(2):

        def tap_step(at, carry, half=half):
            row = pl.multiple_of(half * length + at * chunk, chunk)
            here = pl.ds(row, chunk)
            sine, cosine = sin_cos(dot(features[here, :], lead))
            high = sine.astype(BF)
            acts[0, here, :] = high
            acts[1, here, :] = cosine.astype(BF)
            low = (sine - high.astype(F32)).astype(BF)
            sine, cosine = sin_cos(dot(high, r.second[...]) + dot(low, r.second[...]))
            high = sine.astype(BF)
            acts[2, here, :] = high
            acts[3, here, :] = cosine.astype(BF)
            taps = dot(high, third_v[...], NT) * (length**-0.5)
            if half == 1:
                index = lax.broadcasted_iota(jnp.int32, taps.shape, 0) + at * chunk
                taps = jnp.where(index == 0, 0.0, taps)
            totals[...] += jnp.sum(taps * sign_rows(*taps.shape), axis=0, keepdims=True)
            spread[pl.ds(pl.multiple_of(at * chunk, chunk), chunk), pl.ds(half * 128, 128)] = taps.astype(BF)
            return carry

        lax.fori_loop(0, per, tap_step, 0)
    loads.table.wait()

    def spectrum_step(at, carry):
        here = pl.ds(pl.multiple_of(at * chunk, chunk), chunk)
        sign = sign_rows(chunk, 128)
        index = lax.broadcasted_iota(jnp.int32, (chunk, 128), 0) + at * chunk
        weight = jnp.where(index == 0, 0.5 / length, 1.0 / length)
        for which in range(2):
            result = dot(table_v[which, here, :], spread[...])
            taps_v[which, here, :] = ((result[:, :128] + sign * result[:, 128:]) * weight).astype(BF)
        return carry

    lax.fori_loop(0, per, spectrum_step, 0)
    tap_total = jnp.broadcast_to(totals[...], (128, 128)).T[:chans, 0:1]

    for copy in sends:
        copy.wait_recv()

    step = 16
    padded[pl.ds(chans, 128 - chans), :] = jnp.zeros((128 - chans, length), BF)

    def short_step(at, carry):
        here = pl.ds(pl.multiple_of(at * step, step), step)
        shorted = []
        for s in range(3):
            value = signals[s, here, :].astype(F32)
            shorted.append(
                previous(value) * columns[here, 3 * s : 3 * s + 1]
                + value * columns[here, 3 * s + 1 : 3 * s + 2]
                + following(value) * columns[here, 3 * s + 2 : 3 * s + 3]
            )
        result = shorted[0] * shorted[2]
        product[here, :] = result
        keyed[here, :] = shorted[1]
        padded[here, :] = result.astype(BF)
        nyquist[here, 0:1] = jnp.sum(result * sign_lanes(step, length), axis=1, keepdims=True)
        return carry

    lax.fori_loop(0, chans // step, short_step, 0)
    nyquist[:, 1:2] = tap_total

    def wave_step(at, carry):
        here = pl.ds(pl.multiple_of(at * chunk, chunk), chunk)
        cos_part = dot(table_v[0, here, :], padded[...], NT)
        sin_part = dot(table_v[1, here, :], padded[...], NT)
        wave[0, here, :] = cos_part.astype(BF)
        wave[1, here, :] = sin_part.astype(BF)
        tap_cos = taps_v[0, here, :].astype(F32)
        tap_sin = taps_v[1, here, :].astype(F32)
        spectrum[0, here, :] = (cos_part * tap_cos - sin_part * tap_sin).astype(BF)
        spectrum[1, here, :] = (cos_part * tap_sin + sin_part * tap_cos).astype(BF)
        return carry

    lax.fori_loop(0, per, wave_step, 0)

    def conv_step(at, carry):
        here = pl.ds(pl.multiple_of(at * chunk, chunk), chunk)
        result = dot(table_v[0, here, :], spectrum[0]) + dot(table_v[1, here, :], spectrum[1])
        result = result.T[:chans]
        result = (
            result
            + sign_lanes(chans, chunk) * (nyquist[:, 0:1] * nyquist[:, 1:2] * (0.5 / length))
            + columns[:, 9:10] * product[:, here]
        )
        conv[:, here] = result
        mixed[:, here] = (keyed[:, here] * result).astype(BF)
        return carry

    lax.fori_loop(0, per, conv_step, 0)
    backs = []
    slot = pl.ds(pl.multiple_of(me * chans, 16), chans)
    for k in SEQ_ORDER:
        other = flip(me, k)
        copy = pltpu.make_async_remote_copy(
            src_ref=mixed.at[:, pl.ds(pl.multiple_of(other * rows, rows), rows)],
            dst_ref=r.mixed.at[slot, :],
            send_sem=r.mix_send.at[k],
            recv_sem=r.mix_recv.at[k],
            device_id={"seq": other},
            device_id_type=MESH,
        )
        copy.start()
        backs.append(copy)
    r.mixed[slot, :] = mixed[:, mine]
    for copy in backs:
        copy.wait_recv()
    return sends + backs, cot_copies, own_cot


def split_table(values):
    high = values.astype(BF)
    low = (values - high.astype(np.float32)).astype(BF)
    return high, low


def constants(length):
    index = np.arange(length)
    angle = (index[:, None] * index[None, :] % (2 * length)) * (math.pi / length)
    table = np.stack([np.cos(angle), np.sin(angle)]).astype(np.float32).astype(BF)
    place = np.arange(2 * length)
    scaled = np.where(place < length, place, place - 2 * length) / length
    features = np.zeros((2 * length, 8), np.float32)
    features[:, 0] = scaled
    features[:, 1] = np.sin(math.pi * scaled)
    features[:, 2] = np.cos(math.pi * scaled)
    features[:, 3] = np.sin(7.0 * math.pi * scaled)
    features[:, 4] = np.cos(7.0 * math.pi * scaled)
    return table, np.concatenate(split_table(features), axis=1)


def monarch_backward(upstream, operand, shuffled, right, left, middle, keep_right, keep_left, store):
    groups, width, _ = right.shape
    part = width // groups
    for g in range(groups):
        above = upstream(g)
        keep_left(g, dot(shuffled[pl.ds(g * width, width), :], above, NT))
        below = dot(left[g], above).astype(BF)
        for b in range(groups):
            middle[pl.ds(b * width + g * part, part), :] = below[b * part : (b + 1) * part]
    for b in range(groups):
        above = middle[pl.ds(b * width, width), :]
        keep_right(b, dot(operand(b), above, NT))
        store(b, dot(right[b], above))


CHIPS = (6, 2, 4)


class Reduce:
    def __init__(self, n_seq, n_tp, own, full, core_in, halves, chip_in, quarter, plane_in, send, recv):
        self.own, self.full, self.core_in, self.halves = own, full, core_in, halves
        self.chip_in, self.quarter, self.plane_in = chip_in, quarter, plane_in
        self.send, self.recv, self.n_tp = send, recv, n_tp
        rows, width = own.shape
        self.rows, self.width = rows, width
        self.per_chip, self.per_plane = rows // (n_seq // 2), rows // (n_seq // 2) // n_tp
        self.me, self.plane = lax.axis_index("seq"), lax.axis_index("tp")
        core = lax.rem(self.me, 2)
        self.mine = pl.ds(pl.multiple_of(core * (width // 2), 128), width // 2)
        self.theirs = pl.ds(pl.multiple_of((1 - core) * (width // 2), 128), width // 2)
        self.started = []

    def chip_rows(self, index):
        return pl.ds(pl.multiple_of(index // 2 * self.per_chip, 16), self.per_chip)

    def copy(self, source, target, at, where):
        result = pltpu.make_async_remote_copy(
            src_ref=source, dst_ref=target, send_sem=self.send.at[at], recv_sem=self.recv.at[at],
            device_id=where, device_id_type=MESH,
        )
        result.start()
        self.started.append(result)
        return result

    def start_core(self):
        self.phase = [self.copy(self.own.at[:, self.theirs], self.core_in, 0, {"seq": flip(self.me, 1)})]

    def arrived(self):
        for copy in self.phase:
            copy.wait_recv()
        self.phase = []

    def start_chip(self):
        self.arrived()
        self.halves[...] = (self.own[:, self.mine].astype(F32) + self.core_in[...].astype(F32)).astype(BF)
        for k in CHIPS:
            other = flip(self.me, k)
            self.phase.append(
                self.copy(self.halves.at[self.chip_rows(other), :], self.chip_in.at[k // 2], k // 2, {"seq": other})
            )

    def start_plane(self):
        self.arrived()
        total = self.halves[self.chip_rows(self.me), :].astype(F32)
        for k in CHIPS:
            total = total + self.chip_in[k // 2].astype(F32)
        self.quarter[...] = total.astype(BF)
        for k in range(1, self.n_tp):
            other = flip(self.plane, k)
            here = pl.ds(pl.multiple_of(other * self.per_plane, 16), self.per_plane)
            self.phase.append(self.copy(self.quarter.at[here, :], self.plane_in.at[k], 3 + k, {"tp": other}))

    def start_plane_back(self):
        self.arrived()
        here = pl.ds(pl.multiple_of(self.plane * self.per_plane, 16), self.per_plane)
        total = self.quarter[here, :].astype(F32)
        for k in range(1, self.n_tp):
            total = total + self.plane_in[k].astype(F32)
        rows = pl.ds(
            pl.multiple_of(self.me // 2 * self.per_chip + self.plane * self.per_plane, 16), self.per_plane
        )
        self.full[rows, self.mine] = total.astype(BF)
        spot = self.full.at[rows, self.mine]
        for k in range(1, self.n_tp):
            self.phase.append(self.copy(spot, spot, 6 + k, {"tp": flip(self.plane, k)}))

    def start_chip_back(self):
        self.arrived()
        spot = self.full.at[self.chip_rows(self.me), self.mine]
        for k in CHIPS:
            self.phase.append(self.copy(spot, spot, 9 + k // 2, {"seq": flip(self.me, k)}))

    def start_core_back(self):
        self.arrived()
        spot = self.full.at[:, self.mine]
        self.phase.append(self.copy(spot, spot, 13, {"seq": flip(self.me, 1)}))

    def finish(self):
        self.arrived()
        for copy in self.started:
            copy.wait_send()


def neighbour_order(plane, at):
    upper = plane // 2
    near = plane + upper * (3 - 2 * plane)
    result = at * (1 - near) + (0, 0, 2, 3)[at] * near
    return result + upper * (3 - 2 * result)


def work_order(plane):
    odd = lax.rem(plane, 2)
    return 1 + odd, lax.rem(plane + 2, 4), 3 - 3 * odd


class Line:
    def __init__(self, n_tp, slots, send, recv):
        self.n_tp, self.slots, self.send, self.recv = n_tp, slots, send, recv
        self.plane = lax.axis_index("tp")
        self.sent = []

    def copy(self, block, source, way):
        return pltpu.make_async_remote_copy(
            src_ref=source, dst_ref=self.slots.at[block], send_sem=self.send.at[way, block], recv_sem=self.recv.at[block],
            device_id={"tp": self.plane + (1, -1)[way]}, device_id_type=MESH,
        )

    def start(self, block, source, way, here):
        @pl.when(here)
        def _():
            self.copy(block, source, way).start()

        self.sent.append((block, source, way, here))

    def begin(self, source):
        self.start(self.plane, source, 0, self.plane < self.n_tp - 1)
        self.start(self.plane, source, 1, self.plane > 0)

    def take(self, block, here=None):
        arrival = pltpu.make_async_remote_copy(
            src_ref=self.slots.at[block], dst_ref=self.slots.at[block], send_sem=self.send.at[0, block],
            recv_sem=self.recv.at[block], device_id={"tp": block}, device_id_type=MESH,
        )
        up = jnp.logical_and(block < self.plane, self.plane < self.n_tp - 1)
        down = jnp.logical_and(block > self.plane, self.plane > 0)
        if here is None:
            arrival.wait_recv()
        else:
            pl.when(here)(arrival.wait_recv)
            up, down = jnp.logical_and(up, here), jnp.logical_and(down, here)
        source = self.slots.at[block]
        self.start(block, source, 0, up)
        self.start(block, source, 1, down)

    def finish(self):
        for block, source, way, here in self.sent:

            @pl.when(here)
            def _(block=block, source=source, way=way):
                self.copy(block, source, way).wait_send()


class Square:
    def __init__(self, own, full, core_in, half, first_in, second_in, send, recv):
        self.own, self.full, self.core_in, self.half = own, full, core_in, half
        self.first_in, self.second_in, self.send, self.recv = first_in, second_in, send, recv
        me = lax.axis_index("seq")
        self.me = me
        rows = own.shape[0]
        self.rows = rows
        self.core = lax.rem(me, 2)
        y, x = me // 4, lax.rem(me // 2, 2)
        quarter, part = rows // 8, rows // 16
        base = rows // 4
        self.ways = ((2, x, y, 0), (4, y, x, base))
        self.quarter, self.part = quarter, part
        self.started = []
        self.phase = []

    def copy(self, source, target, at, k):
        result = pltpu.make_async_remote_copy(
            src_ref=source, dst_ref=target, send_sem=self.send.at[at], recv_sem=self.recv.at[at],
            device_id={"seq": flip(self.me, k)}, device_id_type=MESH,
        )
        result.start()
        self.started.append(result)
        self.phase.append(result)

    def arrived(self):
        for copy in self.phase:
            copy.wait_recv()
        self.phase = []

    def span(self, start, size):
        return pl.ds(pl.multiple_of(start, 16), size)

    def start_core(self):
        half = self.rows // 2
        self.copy(self.own.at[self.span((1 - self.core) * half, half), :], self.core_in, 0, 1)

    def start_first(self):
        self.arrived()
        half = self.rows // 2
        own = self.own[self.span(self.core * half, half), :]
        self.half[...] = (own.astype(F32) + self.core_in[...].astype(F32)).astype(BF)
        for way, (k, near, far, base) in enumerate(self.ways):
            source = self.half.at[self.span(base + (1 - near) * self.quarter, self.quarter), :]
            self.copy(source, self.first_in.at[way], 1 + way, k)

    def start_second(self):
        self.arrived()
        for way, (k, near, far, base) in enumerate(self.ways):
            here = self.span(base + near * self.quarter, self.quarter)
            self.half[here, :] = (self.half[here, :].astype(F32) + self.first_in[way].astype(F32)).astype(BF)
            source = self.half.at[self.span(base + near * self.quarter + (1 - far) * self.part, self.part), :]
            self.copy(source, self.second_in.at[way], 3 + way, 6 - k)

    def start_second_back(self):
        self.arrived()
        for way, (k, near, far, base) in enumerate(self.ways):
            place = base + near * self.quarter + far * self.part
            total = self.half[self.span(place, self.part), :].astype(F32) + self.second_in[way].astype(F32)
            here = self.span(self.core * (self.rows // 2) + place, self.part)
            self.full[here, :] = total.astype(BF)
            spot = self.full.at[here, :]
            self.copy(spot, spot, 5 + way, 6 - k)

    def start_first_back(self):
        self.arrived()
        for way, (k, near, far, base) in enumerate(self.ways):
            spot = self.full.at[self.span(self.core * (self.rows // 2) + base + near * self.quarter, self.quarter), :]
            self.copy(spot, spot, 7 + way, k)

    def start_core_back(self):
        self.arrived()
        spot = self.full.at[self.span(self.core * (self.rows // 2), self.rows // 2), :]
        self.copy(spot, spot, 9, 1)

    def finish(self):
        for copy in self.started:
            copy.wait_send()


class Inputs(typing.NamedTuple):
    feed_gain: typing.Any
    feed_bias: typing.Any
    out_right: typing.Any
    out_left: typing.Any
    gain: typing.Any
    bias: typing.Any
    in_right: typing.Any
    in_left: typing.Any
    short: typing.Any
    conv_bias: typing.Any
    features: typing.Any
    first: typing.Any
    second: typing.Any
    third: typing.Any
    tokens: typing.Any
    cotangent: typing.Any
    table: typing.Any
    gate_w: typing.Any
    up_w: typing.Any
    down_w: typing.Any


class Outputs(typing.NamedTuple):
    output_out: typing.Any
    ffn_out: typing.Any
    tokens_out: typing.Any
    late_out: typing.Any
    early_out: typing.Any
    small_out: typing.Any


def core_scratch(n_seq, n_tp, width, chans, length, rows):
    result = dict(
        token_v=pltpu.VMEM((rows, width), BF),
        cot_v=pltpu.VMEM((n_tp, rows, width), BF),
        gate_v=pltpu.VMEM((width, width), BF),
        up_v=pltpu.VMEM((width, width), BF),
        down_v=pltpu.VMEM((width, width), BF),
        out_shuffled=pltpu.VMEM((width, rows), BF),
        branch=pltpu.VMEM((width, rows), F32),
        resid=pltpu.VMEM((rows, width), F32),
        scaled=pltpu.VMEM((rows, width), F32),
        inverse=pltpu.VMEM((rows, 1), F32),
        normed=pltpu.VMEM((n_tp, rows, width), BF),
        hidden=pltpu.VMEM((n_tp, rows, width), BF),
        grad_hidden=pltpu.VMEM((n_tp, rows, width), F32),
        grad_gate=pltpu.VMEM((n_tp, rows, width), BF),
        grad_up=pltpu.VMEM((n_tp, rows, width), BF),
        grad_normed=pltpu.VMEM((rows, width), F32),
        grad_send=pltpu.VMEM((n_tp, rows, width), BF),
        grad_recv=pltpu.VMEM((n_tp, rows, width), BF),
        glu_own=pltpu.VMEM((rows, width), F32),
        glu_send=pltpu.VMEM((n_tp, rows, width), BF),
        glu_recv=pltpu.VMEM((n_tp, rows, width), BF),
        turned=pltpu.VMEM((width, n_tp*rows), BF),
        grads=pltpu.VMEM((3, width, width), BF),
        ffn_v=pltpu.VMEM((3, width, width), BF),
        core_in=pltpu.VMEM((3, width//2, width), BF),
        halves=pltpu.VMEM((3, width//2, width), BF),
        first_in=pltpu.VMEM((3, 2, width//8, width), BF),
        second_in=pltpu.VMEM((3, 2, width//16, width), BF),
        grad_branch=pltpu.VMEM((width, rows), BF),
        middle=pltpu.VMEM((width, rows), BF),
        grad_mixed_own=pltpu.VMEM((width, rows), BF),
        grad_mixed=pltpu.VMEM((chans, length), BF),
        out_rows=pltpu.VMEM((rows, width), BF),
        output_v=pltpu.VMEM((n_tp, rows//n_tp, width), BF),
        grad_vectors=pltpu.VMEM((2, width), F32),
        grad_resid=pltpu.VMEM((rows, width), F32),
        table_v=pltpu.VMEM((2, length, length), BF),
        signals=pltpu.VMEM((3, chans, length), BF),
        conv=pltpu.VMEM((chans, length), F32),
        wave=pltpu.VMEM((2, length, 128), BF),
        taps_v=pltpu.VMEM((2, length, 128), BF),
        acts=pltpu.VMEM((4, 2*length, 128), BF),
        in_normed=pltpu.VMEM((width, rows), BF),
        in_shuffled=pltpu.VMEM((width, rows), BF),
        grad_short=pltpu.VMEM((3, chans, length), F32),
        query=pltpu.VMEM((chans, length), F32),
        value_v=pltpu.VMEM((chans, length), F32),
        grad_conv=pltpu.VMEM((chans, length), F32),
        padded=pltpu.VMEM((128, length), BF),
        back_wave=pltpu.VMEM((2, length, 128), BF),
        cross=pltpu.VMEM((2, length, 256), BF),
        sums=pltpu.VMEM((128, 128), F32),
        grad_signals=pltpu.VMEM((3, chans, length), BF),
        grad_proj=pltpu.VMEM((3*width, rows), BF),
        grad_rows=pltpu.VMEM((width, rows), F32),
        grad_tok=pltpu.VMEM((rows, width), BF),
        grad_second=pltpu.VMEM((128, 128), F32),
        grad_first=pltpu.VMEM((16, 128), F32),
        grad_third=pltpu.VMEM((128, 128), F32),
        local_sems=pltpu.SemaphoreType.DMA((20,)),
        line_send=pltpu.SemaphoreType.DMA((2,n_tp)),
        line_recv=pltpu.SemaphoreType.DMA((n_tp,)),
        tok_send=pltpu.SemaphoreType.DMA((2,n_tp)),
        tok_recv=pltpu.SemaphoreType.DMA((n_tp,)),
        back_send=pltpu.SemaphoreType.DMA((n_tp,)),
        back_recv=pltpu.SemaphoreType.DMA((n_tp,)),
        glu_ssem=pltpu.SemaphoreType.DMA((n_tp,)),
        glu_rsem=pltpu.SemaphoreType.DMA((n_tp,)),
        out_send=pltpu.SemaphoreType.DMA((n_tp,)),
        out_recv=pltpu.SemaphoreType.DMA((n_tp,)),
        mixed_send=pltpu.SemaphoreType.DMA((n_seq,)),
        mixed_recv=pltpu.SemaphoreType.DMA((n_seq,)),
        seq_send=pltpu.SemaphoreType.DMA((n_seq,3)),
        seq_recv=pltpu.SemaphoreType.DMA((n_seq,3)),
        ffn_send=pltpu.SemaphoreType.DMA((3,10)),
        ffn_recv=pltpu.SemaphoreType.DMA((3,10)),
        mixed=pltpu.VMEM((width, rows), BF),
        front_mixed=pltpu.VMEM((chans, length), BF),
        nyquist=pltpu.VMEM((chans, 128), F32),
        columns=pltpu.VMEM((chans, 16), F32),
        third_v=pltpu.VMEM((128, 128), BF),
        projected=pltpu.VMEM((3 * width, rows), BF),
        spread=pltpu.VMEM((length, 256), BF),
        product=pltpu.VMEM((chans, length), F32),
        totals=pltpu.VMEM((1, 128), F32),
        tall=pltpu.VMEM((width, 16), F32),
        third_turned=pltpu.VMEM((width, 128), BF),
        front_send=pltpu.SemaphoreType.DMA((n_seq, 3)),
        front_recv=pltpu.SemaphoreType.DMA((n_seq, 3)),
        mix_send=pltpu.SemaphoreType.DMA((n_seq,)),
        mix_recv=pltpu.SemaphoreType.DMA((n_seq,)),
        cot_send=pltpu.SemaphoreType.DMA((n_tp,)),
        cot_recv=pltpu.SemaphoreType.DMA((n_tp,)),
        late_own=pltpu.VMEM((width, width), BF),
        late_full=pltpu.VMEM((width, width), BF),
        early_own=pltpu.VMEM((width, 512), BF),
        early_full=pltpu.VMEM((width, 512), BF),
        small_own=pltpu.VMEM((256, 256), BF),
        small_full=pltpu.VMEM((256, 256), BF),
    )
    groups = []
    for count, breadth in ((256, width), (256, width), (256, width), (width, 512), (256, 256)):
        half, chip = breadth // 2, count // (n_seq // 2)
        groups.append(
            [
                pltpu.VMEM((count, half), BF),
                pltpu.VMEM((count, half), BF),
                pltpu.VMEM((n_seq // 2, chip, half), BF),
                pltpu.VMEM((chip, half), BF),
                pltpu.VMEM((n_tp, chip // n_tp, half), BF),
                pltpu.SemaphoreType.DMA((14,)),
                pltpu.SemaphoreType.DMA((14,)),
            ]
        )
    return result, groups


def core_kernel(n_seq, n_tp, dims, *refs):
    width, chans, length, rows = dims
    scratch, groups = core_scratch(n_seq, n_tp, width, chans, length, rows)
    named = dict(zip(Inputs._fields + Outputs._fields + tuple(scratch), refs))
    r = types.SimpleNamespace(**named)
    spare = list(refs[len(named) :])
    reduce_refs = [[spare.pop(0) for _ in group] for group in groups]
    me, plane = lax.axis_index("seq"), lax.axis_index("tp")
    entered = greet(n_seq, n_tp)
    sources = dict(
        token=(r.tokens.at[plane], r.token_v),
        down=(r.down_w, r.down_v),
        gate=(r.gate_w, r.gate_v),
        up=(r.up_w, r.up_v),
        table=(r.table, r.table_v),
    )
    copies = {
        name: pltpu.make_async_copy(*pair, r.local_sems.at[at]) for at, (name, pair) in enumerate(sources.items())
    }
    for copy in copies.values():
        copy.start()
    loads = types.SimpleNamespace(**copies)
    front_sends, cot_copies, own_cot = front_part(n_seq, n_tp, dims, r, entered, loads)
    _, block, _ = r.out_right.shape
    chunk = 256
    pieces = width // chunk
    per = length // chunk
    step = 16

    lates = []
    for at in range(3):
        here = pl.ds(256 * at, 256)
        lates.append(Reduce(n_seq, n_tp, r.late_own.at[here, :], r.late_full.at[here, :], *reduce_refs[at]))
    early = Reduce(n_seq, n_tp, r.early_own, r.early_full, *reduce_refs[3])
    small = Reduce(n_seq, n_tp, r.small_own, r.small_full, *reduce_refs[4])
    squares = [
        Square(
            r.grads.at[which], r.ffn_v.at[which], r.core_in.at[which], r.halves.at[which], r.first_in.at[which],
            r.second_in.at[which], r.ffn_send.at[which], r.ffn_recv.at[which],
        )
        for which in range(3)
    ]

    def keep_branch(g, result):
        r.branch[pl.ds(g * block, block), :] = result

    monarch_forward(lambda b: r.mixed[pl.ds(b * block, block), :], r.out_right, r.out_left, r.out_shuffled, keep_branch)
    tokens = r.token_v[...].astype(F32)
    value = tokens + r.branch[...].T
    r.resid[...] = value
    shifted = value - jnp.mean(value, axis=-1, keepdims=True)
    r.inverse[...] = lax.rsqrt(jnp.mean(shifted * shifted, axis=-1, keepdims=True) + 1e-05)
    value = shifted * r.inverse[...]
    r.scaled[...] = value
    r.normed[plane] = (value * r.feed_gain[...].reshape(1, width) + r.feed_bias[...].reshape(1, width)).astype(BF)
    line = Line(n_tp, r.normed, r.line_send, r.line_recv)
    line.begin(r.normed.at[plane])
    for copy in cot_copies:
        copy.wait_recv()
    own_cot.wait()
    loads.down.wait()

    def hidden_step(at, carry):
        cols = pl.ds(pl.multiple_of(at * chunk, chunk), chunk)
        result = dot(r.cot_v[...].reshape(n_tp * rows, width), r.down_v[cols, :], NT)
        r.grad_hidden[:, :, cols] = result.reshape(n_tp, rows, chunk)
        return carry

    lax.fori_loop(0, pieces, hidden_step, 0)
    loads.gate.wait()
    loads.up.wait()
    backs = []
    def send_back(other):
        copy = pltpu.make_async_remote_copy(
            src_ref=r.grad_send.at[other],
            dst_ref=r.grad_recv.at[plane],
            send_sem=r.back_send.at[other],
            recv_sem=r.back_recv.at[plane],
            device_id={"tp": other},
            device_id_type=MESH,
        )
        copy.start()
        backs.append(copy)

    order = work_order(plane)
    inner = jnp.logical_and(plane > 0, plane < n_tp - 1)
    outer = jnp.logical_not(inner)
    for k in range(n_tp):
        other = plane if k == 0 else order[k - 1]
        if k == 1:
            line.take(order[2], inner)
            line.take(order[0])
        if k == 2:
            line.take(order[1])
        if k == 3:
            line.take(order[2], outer)
        if k > 1:
            send_back(order[k - 2])

        def gate_step(at, carry, other=other):
            cols = pl.ds(pl.multiple_of(at * chunk, chunk), chunk)
            value = r.normed[other]
            gate = dot(value, r.gate_v[:, cols])
            upward = dot(value, r.up_v[:, cols])
            sigma = 1.0 / (1.0 + jnp.exp(-gate))
            active = gate * sigma
            r.hidden[other, :, cols] = (active * upward).astype(BF)
            above = r.grad_hidden[other, :, cols]
            r.grad_gate[other, :, cols] = (above * upward * (sigma + active * (1.0 - sigma))).astype(BF)
            r.grad_up[other, :, cols] = (above * active).astype(BF)
            return carry

        lax.fori_loop(0, pieces, gate_step, 0)

        def back_step(at, carry, k=k, other=other):
            cols = pl.ds(pl.multiple_of(at * chunk, chunk), chunk)
            result = dot(r.grad_gate[other], r.gate_v[cols, :], NT) + dot(r.grad_up[other], r.up_v[cols, :], NT)
            if k == 0:
                r.grad_normed[:, cols] = result
            else:
                r.grad_send[other, :, cols] = result.astype(BF)
            return carry

        lax.fori_loop(0, pieces, back_step, 0)
    send_back(order[2])

    def turn(source):
        for s in range(n_tp):
            r.turned[:, s * rows : (s + 1) * rows] = source[s].T

    def weight_grad(which, factor):
        def grad_step(at, carry):
            here = pl.ds(pl.multiple_of(at * chunk, chunk), chunk)
            result = dot(r.turned[here, :], factor[...].reshape(n_tp * rows, width))
            r.grads[which, here, :] = result.astype(BF)
            return carry

        lax.fori_loop(0, pieces, grad_step, 0)
        squares[which].start_core()

    turn(r.normed)
    weight_grad(0, r.grad_gate)
    weight_grad(1, r.grad_up)
    squares[0].start_first()
    turn(r.hidden)
    weight_grad(2, r.cot_v)
    squares[1].start_first()
    squares[2].start_first()

    def from_planes(recv, slots):
        total = 0.0
        for k in range(1, n_tp):
            other = flip(plane, k)
            pltpu.make_async_remote_copy(
                src_ref=slots.at[other], dst_ref=slots.at[other], send_sem=recv.at[other], recv_sem=recv.at[other],
                device_id={"tp": other}, device_id_type=MESH,
            ).wait_recv()
            total = total + slots[other].astype(F32)
        return total

    total = r.grad_normed[...] + from_planes(r.back_recv, r.grad_recv)
    value = r.scaled[...]
    r.grad_vectors[0:1, :] = jnp.sum(total * value, axis=0, keepdims=True)
    r.grad_vectors[1:2, :] = jnp.sum(total, axis=0, keepdims=True)
    total = total * r.feed_gain[...].reshape(1, width)
    first_mean = jnp.mean(total, axis=-1, keepdims=True)
    second_mean = jnp.mean(total * value, axis=-1, keepdims=True)
    total = r.cot_v[plane].astype(F32) + r.inverse[...] * (total - first_mean - value * second_mean)
    r.grad_resid[...] = total
    r.grad_branch[...] = total.T.astype(BF)
    out_parts = {}

    def keep_out_left(g, result):
        out_parts[g] = result.astype(BF)

    def keep_out_right(b, result):
        both = jnp.concatenate([result.astype(BF), out_parts[b]], axis=1)
        r.early_own[pl.ds(b * block, block), 0 : 2 * block] = both

    def keep_mixed(b, result):
        r.grad_mixed_own[pl.ds(b * block, block), :] = result.astype(BF)

    monarch_backward(
        lambda g: r.grad_branch[pl.ds(g * block, block), :],
        lambda b: r.mixed[pl.ds(b * block, block), :],
        r.out_shuffled, r.out_right, r.out_left, r.middle, keep_out_right, keep_out_left, keep_mixed,
    )
    mine = pl.ds(pl.multiple_of(me * rows, rows), rows)
    own_chans = pl.ds(pl.multiple_of(me * chans, 16), chans)
    mixed_copies = []
    for k in SEQ_ORDER:
        other = flip(me, k)
        copy = pltpu.make_async_remote_copy(
            src_ref=r.grad_mixed_own.at[pl.ds(pl.multiple_of(other * chans, 16), chans), :],
            dst_ref=r.grad_mixed.at[:, mine],
            send_sem=r.mixed_send.at[k],
            recv_sem=r.mixed_recv.at[k],
            device_id={"seq": other},
            device_id_type=MESH,
        )
        copy.start()
        mixed_copies.append(copy)
    r.grad_mixed[:, mine] = r.grad_mixed_own[own_chans, :]
    squares[0].start_second()

    glus = []
    for k in range(n_tp):
        other = plane if k == 0 else neighbour_order(plane, n_tp - k)

        def glu_step(at, carry, k=k, other=other):
            cols = pl.ds(pl.multiple_of(at * chunk, chunk), chunk)
            result = dot(r.hidden[other], r.down_v[:, cols])
            if k == 0:
                r.glu_own[:, cols] = result
            else:
                r.glu_send[other, :, cols] = result.astype(BF)
            return carry

        lax.fori_loop(0, pieces, glu_step, 0)
        if k > 0:
            copy = pltpu.make_async_remote_copy(
                src_ref=r.glu_send.at[other],
                dst_ref=r.glu_recv.at[plane],
                send_sem=r.glu_ssem.at[other],
                recv_sem=r.glu_rsem.at[plane],
                device_id={"tp": other},
                device_id_type=MESH,
            )
            copy.start()
            glus.append(copy)
    squares[1].start_second()
    r.sums[...] = jnp.zeros_like(r.sums)
    r.small_own[...] = jnp.zeros_like(r.small_own)
    r.early_own[:, 384:512] = jnp.zeros((width, 128), BF)
    r.padded[pl.ds(chans, 128 - chans), :] = jnp.zeros((128 - chans, length), BF)
    for copy in mixed_copies:
        copy.wait_recv()

    def short_step(at, carry):
        here = pl.ds(pl.multiple_of(at * step, step), step)
        shorted = []
        for s in range(3):
            value = r.signals[s, here, :].astype(F32)
            shorted.append(
                previous(value) * r.columns[here, 3 * s : 3 * s + 1]
                + value * r.columns[here, 3 * s + 1 : 3 * s + 2]
                + following(value) * r.columns[here, 3 * s + 2 : 3 * s + 3]
            )
        r.query[here, :] = shorted[0]
        r.value_v[here, :] = shorted[2]
        above = r.grad_mixed[here, :].astype(F32)
        r.grad_short[1, here, :] = above * r.conv[here, :]
        above = above * shorted[1]
        r.grad_conv[here, :] = above
        r.padded[here, :] = above.astype(BF)
        r.sums[here, 9:10] = jnp.sum(above * shorted[0] * shorted[2], axis=1, keepdims=True)
        r.sums[here, 10:11] = jnp.sum(above * sign_lanes(step, length), axis=1, keepdims=True)
        return carry

    lax.fori_loop(0, chans // step, short_step, 0)
    squares[2].start_second()

    def wave_step(at, carry):
        here = pl.ds(pl.multiple_of(at * chunk, chunk), chunk)
        sign = sign_rows(chunk, 128)
        index = lax.broadcasted_iota(jnp.int32, (chunk, 128), 0) + at * chunk
        weight = jnp.where(index == 0, 0.5 / length, 1.0 / length)
        cos_part = dot(r.table_v[0, here, :], r.padded[...], NT)
        sin_part = dot(r.table_v[1, here, :], r.padded[...], NT)
        tap_cos = r.taps_v[0, here, :].astype(F32)
        tap_sin = r.taps_v[1, here, :].astype(F32)
        r.back_wave[0, here, :] = (cos_part * tap_cos + sin_part * tap_sin).astype(BF)
        r.back_wave[1, here, :] = (sin_part * tap_cos - cos_part * tap_sin).astype(BF)
        wave_cos = r.wave[0, here, :].astype(F32) * weight
        wave_sin = r.wave[1, here, :].astype(F32) * weight
        result = cos_part * wave_cos + sin_part * wave_sin
        r.cross[0, here, 0:128] = result.astype(BF)
        r.cross[0, here, 128:256] = (result * sign).astype(BF)
        result = sin_part * wave_cos - cos_part * wave_sin
        r.cross[1, here, 0:128] = result.astype(BF)
        r.cross[1, here, 128:256] = (result * sign).astype(BF)
        return carry

    lax.fori_loop(0, per, wave_step, 0)
    squares[0].start_second_back()
    squares[1].start_second_back()

    def product_step(at, carry):
        here = pl.ds(pl.multiple_of(at * chunk, chunk), chunk)
        result = dot(r.table_v[0, here, :], r.back_wave[0]) + dot(r.table_v[1, here, :], r.back_wave[1])
        result = (
            result.T[:chans]
            + sign_lanes(chans, chunk) * (r.sums[:chans, 10:11] * r.nyquist[:, 1:2] * (0.5 / length))
            + r.columns[:, 9:10] * r.grad_conv[:, here]
        )
        r.grad_short[0, :, here] = result * r.value_v[:, here]
        r.grad_short[2, :, here] = result * r.query[:, here]
        return carry

    lax.fori_loop(0, per, product_step, 0)

    def signal_step(at, carry):
        here = pl.ds(pl.multiple_of(at * step, step), step)
        for s in range(3):
            above = r.grad_short[s, here, :]
            value = r.signals[s, here, :].astype(F32)
            before, after = previous(above), following(above)
            r.grad_signals[s, here, :] = (
                after * r.columns[here, 3 * s : 3 * s + 1]
                + above * r.columns[here, 3 * s + 1 : 3 * s + 2]
                + before * r.columns[here, 3 * s + 2 : 3 * s + 3]
            ).astype(BF)
            r.sums[here, 3 * s : 3 * s + 1] = jnp.sum(after * value, axis=1, keepdims=True)
            r.sums[here, 3 * s + 1 : 3 * s + 2] = jnp.sum(above * value, axis=1, keepdims=True)
            r.sums[here, 3 * s + 2 : 3 * s + 3] = jnp.sum(before * value, axis=1, keepdims=True)
        return carry

    lax.fori_loop(0, chans // step, signal_step, 0)
    seq_copies = []
    for k in SEQ_ORDER:
        other = flip(me, k)
        for s in range(3):
            copy = pltpu.make_async_remote_copy(
                src_ref=r.grad_signals.at[s, :, pl.ds(pl.multiple_of(other * rows, rows), rows)],
                dst_ref=r.grad_proj.at[pl.ds(pl.multiple_of(s * width + me * chans, 16), chans), :],
                send_sem=r.seq_send.at[k, s],
                recv_sem=r.seq_recv.at[k, s],
                device_id={"seq": other},
                device_id_type=MESH,
            )
            copy.start()
            seq_copies.append(copy)
    for s in range(3):
        r.grad_proj[pl.ds(pl.multiple_of(s * width + me * chans, 16), chans), :] = r.grad_signals[s, :, mine]
    squares[2].start_second_back()

    total = r.resid[...] + r.glu_own[...] + from_planes(r.glu_rsem, r.glu_recv)
    r.out_rows[...] = total.astype(BF)
    part = rows // n_tp
    out_copies = []
    for k in range(1, n_tp):
        other = flip(plane, k)
        copy = pltpu.make_async_remote_copy(
            src_ref=r.out_rows.at[pl.ds(pl.multiple_of(other * part, part), part), :],
            dst_ref=r.output_v.at[plane],
            send_sem=r.out_send.at[k],
            recv_sem=r.out_recv.at[k],
            device_id={"tp": other},
            device_id_type=MESH,
        )
        copy.start()
        out_copies.append(copy)
    r.output_v[plane] = r.out_rows[pl.ds(pl.multiple_of(plane * part, part), part), :]

    tap_total = jnp.broadcast_to(r.sums[:, 10:11], (128, 128)).T[0:1, :]
    pad_nyquist = jnp.concatenate([r.nyquist[:, 0:1], jnp.zeros((128 - chans, 1), F32)], axis=0)
    tap_total = tap_total * jnp.broadcast_to(pad_nyquist, (128, 128)).T[0:1, :] * (0.5 / length)
    r.grad_second[...] = jnp.zeros_like(r.grad_second)
    r.grad_first[...] = jnp.zeros_like(r.grad_first)
    r.grad_third[...] = jnp.zeros_like(r.grad_third)

    def filter_step(at, carry):
        here = pl.ds(pl.multiple_of(at * chunk, chunk), chunk)
        result = dot(r.table_v[0, here, :], r.cross[0]) + dot(r.table_v[1, here, :], r.cross[1])
        sign = sign_rows(chunk, 128)
        for half in range(2):
            above = (result[:, half * 128 : (half + 1) * 128] + sign * tap_total) * (length**-0.5)
            if half == 1:
                index = lax.broadcasted_iota(jnp.int32, above.shape, 0) + at * chunk
                above = jnp.where(index == 0, 0.0, above)
            above = above.astype(BF)
            spot = pl.ds(pl.multiple_of(half * length + at * chunk, chunk), chunk)
            r.grad_third[...] += dot(above, r.acts[2, spot, :], TN)
            below = (dot(above, r.third_v[...]) * r.acts[3, spot, :].astype(F32)).astype(BF)
            r.grad_second[...] += dot(r.acts[0, spot, :], below, TN)
            below = (dot(below, r.second[...], NT) * r.acts[1, spot, :].astype(F32)).astype(BF)
            r.grad_first[...] += dot(r.features[spot, :], below, TN)
        return carry

    lax.fori_loop(0, per, filter_step, 0)
    r.early_own[own_chans, 384:512] = r.grad_third[:chans, :].astype(BF)
    r.small_own[0:128, 0:128] = r.grad_second[...].astype(BF)
    r.small_own[128:136, 0:128] = (r.grad_first[0:8, :] + r.grad_first[8:16, :]).astype(BF)
    r.small_own[pl.ds(pl.multiple_of(me * 16, 16), 16), 128:256] = r.sums[...].T[0:16, :].astype(BF)
    early.start_core()
    shifted = tokens - jnp.mean(tokens, axis=-1, keepdims=True)
    inverse = lax.rsqrt(jnp.mean(shifted * shifted, axis=-1, keepdims=True) + 1e-05)
    r.scaled[...] = shifted * inverse
    fan = r.in_left.shape[2]
    for copy in seq_copies:
        copy.wait_recv()
    squares[0].start_first_back()
    squares[1].start_first_back()
    early.start_chip()

    in_parts = {}

    def keep_left(g, result):
        r.late_own[pl.ds(g * block, block), 0:512] = result[:, 0:512].astype(BF)
        in_parts[g] = result[:, 512:576].astype(BF)

    def keep_right(b, result):
        r.late_own[pl.ds(b * block, block), 512:768] = jnp.concatenate([in_parts[b], result.astype(BF)], axis=1)

    def keep_rows(b, result):
        r.grad_rows[pl.ds(b * block, block), :] = result

    part = block // 4
    for g in range(4):
        below = dot(r.in_left[g], r.grad_proj[pl.ds(g * fan, fan), :]).astype(BF)
        for b in range(4):
            r.middle[pl.ds(b * block + g * part, part), :] = below[b * part : (b + 1) * part]
    for b in range(4):
        keep_rows(b, dot(r.in_right[b], r.middle[pl.ds(b * block, block), :]))
    total = r.grad_rows[...].T
    scaled = r.scaled[...]
    lines = [jnp.sum(total * scaled, axis=0, keepdims=True), jnp.sum(total, axis=0, keepdims=True)]
    total = total * r.gain[...].reshape(1, width)
    first_mean = jnp.mean(total, axis=-1, keepdims=True)
    second_mean = jnp.mean(total * scaled, axis=-1, keepdims=True)
    total = r.grad_resid[...] + inverse * (total - first_mean - scaled * second_mean)
    r.grad_tok[...] = total.astype(BF)
    token_line = Line(n_tp, r.tokens_out, r.tok_send, r.tok_recv)
    token_line.begin(r.grad_tok)
    own_tok = pltpu.make_async_copy(r.grad_tok, r.tokens_out.at[plane], r.local_sems.at[13])
    own_tok.start()
    for g in range(4):
        keep_left(g, dot(r.in_shuffled[pl.ds(g * block, block), :], r.grad_proj[pl.ds(g * fan, fan), :], NT))
    for b in range(4):
        keep_right(b, dot(r.in_normed[pl.ds(b * block, block), :], r.middle[pl.ds(b * block, block), :], NT))
    for late in lates:
        late.start_core()
    squares[2].start_first_back()
    early.start_plane()
    for late in lates:
        late.start_chip()
    lines += [r.grad_vectors[0:1, :], r.grad_vectors[1:2, :]]
    packed = [row[:, at * 128 : (at + 1) * 128] for row in lines for at in range(width // 128)]
    r.small_own[128:160, 128:256] = jnp.concatenate(packed + [jnp.zeros((8, 128), F32)], axis=0).astype(BF)
    small.start_core()
    early.start_plane_back()
    small.start_chip()
    token_line.take(neighbour_order(plane, 1))
    for late in lates:
        late.start_plane()
    small.start_plane()
    early.start_chip_back()
    for square in squares:
        square.start_core_back()
    token_line.take(neighbour_order(plane, 2))
    for late in lates:
        late.start_plane_back()
    small.start_plane_back()
    for late in lates:
        late.start_chip_back()
    small.start_chip_back()
    early.start_core_back()
    token_line.take(neighbour_order(plane, 3))
    ffn_copies = []
    for which, square in enumerate(squares):
        square.arrived()
        copy = pltpu.make_async_copy(r.ffn_v.at[which], r.ffn_out.at[which], r.local_sems.at[14 + which])
        copy.start()
        ffn_copies.append(copy)
    for late in lates:
        late.start_core_back()
    small.start_core_back()
    early.finish()
    r.early_out[...] = r.early_full[...]
    small.finish()
    r.small_out[...] = r.small_full[...]
    for copy in out_copies:
        copy.wait()
    r.output_out[...] = r.output_v[...]
    for late in lates:
        late.finish()
    r.late_out[...] = r.late_full[...]
    for copy in mixed_copies + seq_copies + backs + glus + front_sends + cot_copies:
        copy.wait_send()
    for square in squares:
        square.finish()
    line.finish()
    token_line.finish()
    own_tok.wait()
    for copy in ffn_copies:
        copy.wait()


def core(mesh_shape, *operands):
    n_seq, n_tp = mesh_shape
    tokens = Inputs(*operands).tokens
    _, rows, width = tokens.shape
    chans, length = width // n_seq, rows * n_seq
    scratch, groups = core_scratch(n_seq, n_tp, width, chans, length, rows)
    shape = jax.ShapeDtypeStruct
    return pl.pallas_call(
        functools.partial(core_kernel, n_seq, n_tp, (width, chans, length, rows)),
        out_shape=(
            shape((n_tp, rows // n_tp, width), BF),
            shape((3, width, width), BF),
            shape((n_tp, rows, width), BF),
            shape((width, width), BF),
            shape((width, 512), BF),
            shape((256, 256), BF),
        ),
        in_specs=[vmem_spec()] * 14 + [any_spec()] * (len(Inputs._fields) - 14),
        out_specs=(vmem_spec(), any_spec(), any_spec(), vmem_spec(), vmem_spec(), vmem_spec()),
        scratch_shapes=list(scratch.values()) + sum(groups, []),
        compiler_params=pltpu.CompilerParams(collective_id=0, has_side_effects=True, vmem_limit_bytes=60 * 1024 * 1024),
        name="layer",
    )(*operands)


def finish_kernel(width, chans, *refs):
    (ffn, tokens, late, early, small) = refs[:5]
    (grad_tokens, norm_gain, norm_bias, in_right, in_left, short, first, second, third, conv_bias, out_right, out_left,
     ffn_gain, ffn_bias, gate, up, down) = refs[5:22]
    (ffn_v, ffn_f, token_v, token_f, late_v, early_v, in_right_f, in_left_f, out_right_f, out_left_f, in_sems, out_sems) = refs[22:]
    pairs = [(ffn.at[which], ffn_v.at[which]) for which in range(3)] + [(tokens, token_v), (late, late_v), (early, early_v)]
    loads = [pltpu.make_async_copy(*pair, in_sems.at[at]) for at, pair in enumerate(pairs)]
    for copy in loads:
        copy.start()
    pairs = [(ffn_f.at[which], target) for which, target in enumerate((gate, up, down))]
    pairs += [
        (token_f, grad_tokens), (in_right_f, in_right), (in_left_f, in_left), (out_right_f, out_right), (out_left_f, out_left)
    ]
    stores = [pltpu.make_async_copy(*pair, out_sems.at[at]) for at, pair in enumerate(pairs)]
    chunk = 64
    for which in range(3):
        loads[which].wait()

        def step(at, carry, which=which):
            here = pl.ds(pl.multiple_of(at * chunk, chunk), chunk)
            ffn_f[which, here, :] = ffn_v[which, here, :].astype(F32)
            return carry

        lax.fori_loop(0, width // chunk, step, 0)
        stores[which].start()
    loads[3].wait()

    def token_step(at, carry):
        token_f[at] = token_v[at].astype(F32)
        return carry

    lax.fori_loop(0, token_v.shape[0], token_step, 0)
    stores[3].start()
    groups, block, _ = in_right.shape
    loads[4].wait()
    for b in range(groups):
        here = pl.ds(b * block, block)
        in_left_f[b] = late_v[here, 0 : 3 * block].astype(F32)
        in_right_f[b] = late_v[here, 3 * block : 4 * block].astype(F32)
    stores[4].start()
    stores[5].start()
    loads[5].wait()
    for b in range(groups):
        here = pl.ds(b * block, block)
        out_right_f[b] = early_v[here, 0:block].astype(F32)
        out_left_f[b] = early_v[here, block : 2 * block].astype(F32)
    stores[6].start()
    stores[7].start()
    third[...] = early_v[:, 384:512].astype(F32).T
    values = small[...].astype(F32)
    second[...] = values[0:128, 0:128]
    first[...] = values[128:133, 0:128]
    for at, target in enumerate((norm_gain, norm_bias, ffn_gain, ffn_bias)):
        row = 128 + at * (width // 128)
        target[...] = jnp.concatenate([values[row + k : row + k + 1, 128:256] for k in range(width // 128)], axis=1).reshape(width)
    parts = [values[16 * at : 16 * at + 16, 128 : 128 + chans] for at in range(width // chans)]
    lines = jnp.concatenate(parts, axis=1)
    for s in range(3):
        short[s] = lines[3 * s : 3 * s + 3]
    conv_bias[...] = lines[9:10].reshape(width)
    for copy in stores:
        copy.wait()


def finish(chans, ffn, tokens, late, early, small):
    width = ffn.shape[1]
    block = width // 4
    shape = jax.ShapeDtypeStruct
    vector = shape((width,), F32)
    square = shape((4, block, block), F32)
    wide = shape((4, block, 3 * block), F32)
    return pl.pallas_call(
        functools.partial(finish_kernel, width, chans),
        out_shape=(
            shape(tokens.shape, F32), vector, vector, square, wide, shape((3, 3, width), F32),
            shape((5, 128), F32), shape((128, 128), F32), shape((128, width), F32), vector, square, square, vector, vector,
        )
        + (shape((width, width), F32),) * 3,
        in_specs=[any_spec()] * 4 + [vmem_spec()],
        out_specs=(any_spec(), vmem_spec(), vmem_spec(), any_spec(), any_spec())
        + (vmem_spec(),) * 5
        + (any_spec(), any_spec(), vmem_spec(), vmem_spec())
        + (any_spec(),) * 3,
        scratch_shapes=[
            pltpu.VMEM(ffn.shape, BF),
            pltpu.VMEM(ffn.shape, F32),
            pltpu.VMEM(tokens.shape, BF),
            pltpu.VMEM(tokens.shape, F32),
            pltpu.VMEM(late.shape, BF),
            pltpu.VMEM(early.shape, BF),
            pltpu.VMEM(square.shape, F32),
            pltpu.VMEM(wide.shape, F32),
            pltpu.VMEM(square.shape, F32),
            pltpu.VMEM(square.shape, F32),
            pltpu.SemaphoreType.DMA((6,)),
            pltpu.SemaphoreType.DMA((8,)),
        ],
        compiler_params=pltpu.CompilerParams(vmem_limit_bytes=LIMIT),
        name="finish",
    )(ffn, tokens, late, early, small)


def fast_body(
    tokens,
    norm_gain,
    norm_bias,
    in_right,
    in_left,
    short_kernel,
    filter_first,
    filter_second,
    filter_third,
    conv_bias,
    out_right,
    out_left,
    ffn_gain,
    ffn_bias,
    gate_weight,
    up_weight,
    down_weight,
    cotangent,
):
    n_seq, n_tp = lax.axis_size("seq"), lax.axis_size("tp")
    _, rows, width = tokens.shape
    chans, length = width // n_seq, rows * n_seq
    shape = (n_seq, n_tp)
    table, features = (jnp.asarray(array) for array in constants(length))
    output, ffn, grad_tokens, late, early, small = core(
        shape, ffn_gain, ffn_bias, out_right, out_left, norm_gain, norm_bias, in_right, in_left, short_kernel.transpose(0, 2, 1),
        conv_bias, features, filter_first, filter_second, filter_third, tokens, cotangent, table, gate_weight, up_weight,
        down_weight,
    )
    grads = finish(chans, ffn, grad_tokens, late, early, small)
    return (output,) + grads[:5] + (grads[5].transpose(0, 2, 1),) + grads[6:]


highest = lax.Precision.HIGHEST


def norm_forward(values, gain, bias):
    centre = jnp.mean(values, axis=-1, keepdims=True)
    shifted = values - centre
    inverse = lax.rsqrt(jnp.mean(shifted * shifted, axis=-1, keepdims=True) + 1e-05)
    scaled = shifted * inverse
    return (scaled * gain + bias, scaled, inverse)


def norm_backward(upstream, scaled, inverse, gain):
    weighted = upstream * gain
    first_mean = jnp.mean(weighted, axis=-1, keepdims=True)
    second_mean = jnp.mean(weighted * scaled, axis=-1, keepdims=True)
    grad_input = inverse * (weighted - first_mean - scaled * second_mean)
    breadth = upstream.shape[-1]
    grad_gain = jnp.sum((upstream * scaled).reshape(-1, breadth), axis=0)
    grad_bias = jnp.sum(upstream.reshape(-1, breadth), axis=0)
    return (grad_input, grad_gain, grad_bias)


def shuffle(blocked):
    row_count, groups, breadth = blocked.shape
    return (
        blocked.reshape(row_count, groups, groups, breadth // groups)
        .transpose(0, 2, 1, 3)
        .reshape(row_count, groups, breadth)
    )


def rows_monarch_forward(operand, right_factor, left_factor):
    row_count = operand.shape[0]
    groups = right_factor.shape[0]
    blocked = operand.reshape(row_count, groups, -1)
    middle = jnp.einsum(
        "tbi,bij->tbj", blocked, right_factor, preferred_element_type=jnp.float32
    ).astype(jnp.bfloat16)
    shuffled = shuffle(middle)
    result = jnp.einsum("tbi,bij->tbj", shuffled, left_factor, preferred_element_type=jnp.float32)
    return (shuffled, result.reshape(row_count, -1))


def rows_monarch_backward(grad_result, operand, shuffled, right_factor, left_factor):
    row_count = operand.shape[0]
    groups = right_factor.shape[0]
    grad_blocked = grad_result.reshape(row_count, groups, -1)
    grad_left = jnp.einsum(
        "tbi,tbj->bij", shuffled, grad_blocked, preferred_element_type=jnp.float32
    )
    grad_shuffled = jnp.einsum(
        "tbj,bij->tbi", grad_blocked, left_factor, preferred_element_type=jnp.float32
    )
    grad_middle = shuffle(grad_shuffled).astype(jnp.bfloat16)
    blocked = operand.reshape(row_count, groups, -1)
    grad_right = jnp.einsum(
        "tbi,tbj->bij", blocked, grad_middle, preferred_element_type=jnp.float32
    )
    grad_operand = jnp.einsum(
        "tbj,bij->tbi", grad_middle, right_factor, preferred_element_type=jnp.float32
    )
    return (grad_operand.reshape(row_count, -1), grad_right, grad_left)


def roots(row_count, col_count, period):
    product = jnp.arange(row_count)[:, None] * jnp.arange(col_count)[None, :] % period
    angle = product.astype(jnp.float32) * (2.0 * math.pi / period)
    return (jnp.cos(angle), jnp.sin(angle))


def complex_step(real_part, imag_part, cos_table, sin_table, sign, form):
    real_out = jnp.einsum(form, real_part, cos_table, precision=highest) - sign * jnp.einsum(
        form, imag_part, sin_table, precision=highest
    )
    imag_out = jnp.einsum(form, imag_part, cos_table, precision=highest) + sign * jnp.einsum(
        form, real_part, sin_table, precision=highest
    )
    return (real_out, imag_out)


def real_step(real_part, cos_table, sin_table, sign, form):
    real_out = jnp.einsum(form, real_part, cos_table, precision=highest)
    imag_out = sign * jnp.einsum(form, real_part, sin_table, precision=highest)
    return (real_out, imag_out)


def twiddle(real_part, imag_part, cos_table, sin_table, sign):
    real_out = real_part * cos_table - sign * imag_part * sin_table
    imag_out = imag_part * cos_table + sign * real_part * sin_table
    return (real_out, imag_out)


def spectrum_of(real_part):
    total = real_part.shape[-1]
    first = math.gcd(total, 128)
    second = total // first
    leading = real_part.shape[:-1]
    real_part = real_part.reshape(leading + (first, second))
    cos_first, sin_first = roots(first, first, first)
    real_part, imag_part = real_step(real_part, cos_first, sin_first, -1.0, "...ab,ak->...kb")
    cos_twist, sin_twist = roots(first, second, total)
    real_part, imag_part = twiddle(real_part, imag_part, cos_twist, sin_twist, -1.0)
    cos_second, sin_second = roots(second, second, second)
    return complex_step(real_part, imag_part, cos_second, sin_second, -1.0, "...kb,bm->...km")


def signal_of(real_part, imag_part):
    first = real_part.shape[-2]
    second = real_part.shape[-1]
    total = first * second
    leading = real_part.shape[:-2]
    cos_second, sin_second = roots(second, second, second)
    real_part, imag_part = complex_step(
        real_part, imag_part, cos_second, sin_second, 1.0, "...kb,bm->...km"
    )
    cos_twist, sin_twist = roots(first, second, total)
    real_part, imag_part = twiddle(real_part, imag_part, cos_twist, sin_twist, 1.0)
    cos_first, sin_first = roots(first, first, first)
    real_part, imag_part = complex_step(
        real_part, imag_part, cos_first, sin_first, 1.0, "...ab,ak->...kb"
    )
    return real_part.reshape(leading + (total,)) / total


def filter_parts(filter_first, filter_second, third_cols, seq_length):
    total = 2 * seq_length
    index = jnp.arange(total)
    offset = jnp.where(index < seq_length, index, index - total).astype(jnp.float32)
    scaled = offset / seq_length
    features = jnp.stack(
        [
            scaled,
            jnp.sin(math.pi * scaled),
            jnp.cos(math.pi * scaled),
            jnp.sin(7.0 * math.pi * scaled),
            jnp.cos(7.0 * math.pi * scaled),
        ],
        axis=1,
    )
    pre_one = jnp.dot(features, filter_first, precision=highest)
    act_one = jnp.sin(pre_one)
    pre_two = jnp.dot(act_one, filter_second, precision=highest)
    act_two = jnp.sin(pre_two)
    tap_mask = (index != seq_length).astype(jnp.float32)[:, None] * seq_length ** (-0.5)
    taps = jnp.dot(act_two, third_cols, precision=highest) * tap_mask
    filt_real, filt_imag = spectrum_of(taps.T)
    return (features, pre_one, act_one, pre_two, act_two, tap_mask, filt_real, filt_imag)


def general_body(
    tokens,
    norm_gain,
    norm_bias,
    in_right,
    in_left,
    short_kernel,
    filter_first,
    filter_second,
    filter_third,
    conv_bias,
    out_right,
    out_left,
    ffn_gain,
    ffn_bias,
    gate_weight,
    up_weight,
    down_weight,
    cotangent,
):
    seq_count, pos_count, model_width = tokens.shape
    row_count = seq_count * pos_count
    axis_count = lax.axis_size("seq")
    my_index = lax.axis_index("seq")
    chan_count = model_width // axis_count
    seq_length = pos_count * axis_count
    part_rows = cotangent.shape[1]
    tp_index = lax.axis_index("tp")
    tp_count = lax.axis_size("tp")
    chan_start = my_index * chan_count
    mix_count = seq_count // tp_count
    mix_tokens = lax.dynamic_slice_in_dim(tokens, tp_index * mix_count, mix_count, 0)
    mix_rows = mix_count * pos_count
    flat = mix_tokens.reshape(mix_rows, model_width).astype(jnp.float32)
    normed, scaled_one, inverse_one = norm_forward(flat, norm_gain, norm_bias)
    normed_low = normed.astype(jnp.bfloat16)
    shuffled_in, projected = rows_monarch_forward(normed_low, in_right, in_left)
    projected_low = (
        projected.astype(jnp.bfloat16)
        .reshape(mix_count, pos_count, 3, model_width)
        .transpose(2, 3, 0, 1)
    )
    channels = lax.all_to_all(projected_low, "seq", split_axis=1, concat_axis=3, tiled=True)
    signals = channels.astype(jnp.float32)
    kernel = lax.dynamic_slice_in_dim(short_kernel, chan_start, chan_count, 1).astype(jnp.float32)
    tap_zero = kernel[:, :, 0][:, :, None, None]
    tap_one = kernel[:, :, 1][:, :, None, None]
    tap_two = kernel[:, :, 2][:, :, None, None]
    padded = jnp.pad(signals, ((0, 0), (0, 0), (0, 0), (1, 1)))
    shorted = padded[..., :-2] * tap_zero + padded[..., 1:-1] * tap_one + padded[..., 2:] * tap_two
    first_f = filter_first.astype(jnp.float32)
    second_f = filter_second.astype(jnp.float32)
    third_cols = lax.dynamic_slice_in_dim(filter_third, chan_start, chan_count, 1).astype(
        jnp.float32
    )
    kept = filter_parts(first_f, second_f, third_cols, seq_length)
    filt_real = kept[6][:, None]
    filt_imag = kept[7][:, None]
    bias_cols = lax.dynamic_slice_in_dim(conv_bias, chan_start, chan_count, 0)[:, None, None]
    product = shorted[0] * shorted[2]
    product_pad = jnp.pad(product, ((0, 0), (0, 0), (0, seq_length)))
    spec_real, spec_imag = spectrum_of(product_pad)
    conv_real = spec_real * filt_real - spec_imag * filt_imag
    conv_imag = spec_real * filt_imag + spec_imag * filt_real
    convolved = signal_of(conv_real, conv_imag)[..., :seq_length] + bias_cols * product
    mixed_low = (shorted[1] * convolved).astype(jnp.bfloat16)
    back_rows = lax.all_to_all(mixed_low, "seq", split_axis=2, concat_axis=0, tiled=True)
    mixed_rows = back_rows.transpose(1, 2, 0).reshape(mix_rows, model_width)
    shuffled_out, branch = rows_monarch_forward(mixed_rows, out_right, out_left)
    residual_mine = (flat + branch).reshape(mix_count, pos_count, model_width)
    residual = lax.all_gather(residual_mine, "tp", axis=0, tiled=True)
    part_resid = lax.dynamic_slice_in_dim(residual, tp_index * part_rows, part_rows, 1)
    normed_two, scaled_two, inverse_two = norm_forward(part_resid, ffn_gain, ffn_bias)
    normed_rows = lax.all_gather(normed_two.astype(jnp.bfloat16), "tp", axis=1, tiled=True).reshape(
        row_count, model_width
    )
    gate = jnp.dot(normed_rows, gate_weight, preferred_element_type=jnp.float32)
    upward = jnp.dot(normed_rows, up_weight, preferred_element_type=jnp.float32)
    sigma = jax.nn.sigmoid(gate)
    hidden_low = (gate * sigma * upward).astype(jnp.bfloat16)
    partial_down = jnp.dot(hidden_low, down_weight, preferred_element_type=jnp.float32).reshape(
        seq_count, pos_count, model_width
    )
    glu_part = lax.psum_scatter(
        partial_down.astype(jnp.bfloat16), "tp", scatter_dimension=1, tiled=True
    ).astype(jnp.float32)
    output = (part_resid + glu_part).astype(jnp.bfloat16)
    grad_out_rows = lax.all_gather(cotangent, "tp", axis=1, tiled=True).reshape(
        row_count, model_width
    )
    grad_hidden = jnp.dot(grad_out_rows, down_weight.T, preferred_element_type=jnp.float32)
    grad_gate = (grad_hidden * upward * (sigma + gate * sigma * (1.0 - sigma))).astype(jnp.bfloat16)
    grad_up = (grad_hidden * gate * sigma).astype(jnp.bfloat16)
    grad_down_w = jnp.dot(hidden_low.T, grad_out_rows, preferred_element_type=jnp.float32)
    grad_gate_w = jnp.dot(normed_rows.T, grad_gate, preferred_element_type=jnp.float32)
    grad_up_w = jnp.dot(normed_rows.T, grad_up, preferred_element_type=jnp.float32)
    grad_normed = jnp.dot(grad_gate, gate_weight.T, preferred_element_type=jnp.float32) + jnp.dot(
        grad_up, up_weight.T, preferred_element_type=jnp.float32
    )
    grad_normed_part = lax.psum_scatter(
        grad_normed.reshape(seq_count, pos_count, model_width),
        "tp",
        scatter_dimension=1,
        tiled=True,
    )
    grad_in_two, grad_gain_two, grad_bias_two = norm_backward(
        grad_normed_part, scaled_two, inverse_two, ffn_gain
    )
    gain_total = lax.psum((grad_gain_two, grad_bias_two), ("seq", "tp"))
    grad_resid_part = cotangent.astype(jnp.float32) + grad_in_two
    grad_resid = lax.all_gather(
        grad_resid_part.astype(jnp.bfloat16), "tp", axis=1, tiled=True
    ).astype(grad_resid_part.dtype)
    grad_resid_mix = lax.dynamic_slice_in_dim(
        grad_resid, tp_index * mix_count, mix_count, 0
    ).reshape(mix_rows, model_width)
    grad_mixed_rows, grad_out_right, grad_out_left = rows_monarch_backward(
        grad_resid_mix.astype(jnp.bfloat16), mixed_rows, shuffled_out, out_right, out_left
    )
    grad_mixed_low = (
        grad_mixed_rows.astype(jnp.bfloat16)
        .reshape(mix_count, pos_count, model_width)
        .transpose(2, 0, 1)
    )
    grad_mixed = lax.all_to_all(
        grad_mixed_low, "seq", split_axis=0, concat_axis=2, tiled=True
    ).astype(jnp.float32)
    grad_conv = grad_mixed * shorted[1]
    grad_key = grad_mixed * convolved
    again = lax.optimization_barrier((first_f, second_f, third_cols))
    kept = filter_parts(again[0], again[1], again[2], seq_length)
    filt_real = kept[6][:, None]
    filt_imag = kept[7][:, None]
    features, pre_one, act_one, pre_two, act_two, tap_mask = (
        kept[0],
        kept[1],
        kept[2],
        kept[3],
        kept[4],
        kept[5],
    )
    grad_pad = jnp.pad(grad_conv, ((0, 0), (0, 0), (0, seq_length)))
    grad_spec_real, grad_spec_imag = spectrum_of(grad_pad)
    back_real = grad_spec_real * filt_real + grad_spec_imag * filt_imag
    back_imag = grad_spec_imag * filt_real - grad_spec_real * filt_imag
    grad_product = signal_of(back_real, back_imag)[..., :seq_length] + bias_cols * grad_conv
    grad_bias_cols = jnp.sum(grad_conv * product, axis=(1, 2))
    taps_real = jnp.sum(grad_spec_real * spec_real + grad_spec_imag * spec_imag, axis=1)
    taps_imag = jnp.sum(grad_spec_imag * spec_real - grad_spec_real * spec_imag, axis=1)
    grad_taps = signal_of(taps_real, taps_imag)
    grad_pre = grad_taps.T * tap_mask
    grad_third_cols = jnp.dot(act_two.T, grad_pre, precision=highest)
    grad_pre_two = jnp.dot(grad_pre, third_cols.T, precision=highest) * jnp.cos(pre_two)
    grad_second = jnp.dot(act_one.T, grad_pre_two, precision=highest)
    grad_pre_one = jnp.dot(grad_pre_two, second_f.T, precision=highest) * jnp.cos(pre_one)
    grad_first = jnp.dot(features.T, grad_pre_one, precision=highest)
    grad_shorted = jnp.stack([grad_product * shorted[2], grad_key, grad_product * shorted[0]])
    grad_short_pad = jnp.pad(grad_shorted, ((0, 0), (0, 0), (0, 0), (1, 1)))
    grad_signals = (
        grad_short_pad[..., 2:] * tap_zero
        + grad_short_pad[..., 1:-1] * tap_one
        + grad_short_pad[..., :-2] * tap_two
    )
    grad_kernel = jnp.stack(
        [
            jnp.sum(grad_shorted * padded[..., :-2], axis=(2, 3)),
            jnp.sum(grad_shorted * padded[..., 1:-1], axis=(2, 3)),
            jnp.sum(grad_shorted * padded[..., 2:], axis=(2, 3)),
        ],
        axis=-1,
    )
    grad_proj = lax.all_to_all(
        grad_signals.astype(jnp.bfloat16), "seq", split_axis=3, concat_axis=1, tiled=True
    )
    grad_proj_rows = grad_proj.transpose(2, 3, 0, 1).reshape(mix_rows, 3 * model_width)
    grad_normed_one, grad_in_right, grad_in_left = rows_monarch_backward(
        grad_proj_rows, normed_low, shuffled_in, in_right, in_left
    )
    grad_in_one, grad_gain_one, grad_bias_one = norm_backward(
        grad_normed_one, scaled_one, inverse_one, norm_gain
    )
    grad_mine = (grad_resid_mix + grad_in_one).reshape(mix_count, pos_count, model_width)
    short_full = lax.dynamic_update_slice_in_dim(
        jnp.zeros(short_kernel.shape, jnp.float32), grad_kernel, chan_start, 1
    )
    third_full = lax.dynamic_update_slice_in_dim(
        jnp.zeros(filter_third.shape, jnp.float32), grad_third_cols, chan_start, 1
    )
    bias_full = lax.dynamic_update_slice_in_dim(
        jnp.zeros(conv_bias.shape, jnp.float32), grad_bias_cols, chan_start, 0
    )
    mixer_grads = (
        grad_gain_one,
        grad_bias_one,
        grad_in_right,
        grad_in_left,
        short_full,
        grad_first,
        grad_second,
        third_full,
        bias_full,
        grad_out_right,
        grad_out_left,
    )
    grad_tokens = lax.all_gather(grad_mine.astype(jnp.bfloat16), "tp", axis=0, tiled=True).astype(
        grad_mine.dtype
    )
    mixer_grads = (
        lax.psum(mixer_grads[0].astype(jnp.bfloat16), "tp").astype(jnp.float32),
        lax.psum(mixer_grads[1].astype(jnp.bfloat16), "tp").astype(jnp.float32),
        lax.psum(mixer_grads[2].astype(jnp.bfloat16), "tp").astype(jnp.float32),
        lax.psum(mixer_grads[3].astype(jnp.bfloat16), "tp").astype(jnp.float32),
        lax.psum(mixer_grads[4].astype(jnp.bfloat16), "tp").astype(jnp.float32),
        lax.psum(mixer_grads[5].astype(jnp.bfloat16), "tp").astype(jnp.float32),
        lax.psum(mixer_grads[6].astype(jnp.bfloat16), "tp").astype(jnp.float32),
        lax.psum(mixer_grads[7].astype(jnp.bfloat16), "tp").astype(jnp.float32),
        lax.psum(mixer_grads[8].astype(jnp.bfloat16), "tp").astype(jnp.float32),
        lax.psum(mixer_grads[9].astype(jnp.bfloat16), "tp").astype(jnp.float32),
        lax.psum(mixer_grads[10].astype(jnp.bfloat16), "tp").astype(jnp.float32),
    )
    all_total = lax.psum(
        (
            mixer_grads[0],
            mixer_grads[1],
            mixer_grads[2],
            mixer_grads[3],
            mixer_grads[4],
            mixer_grads[5],
            mixer_grads[6],
            mixer_grads[7],
            mixer_grads[8],
            mixer_grads[9],
            mixer_grads[10],
            grad_gate_w,
            grad_up_w,
            grad_down_w,
        ),
        "seq",
    )
    return (
        output,
        grad_tokens,
        all_total[0],
        all_total[1],
        all_total[2],
        all_total[3],
        all_total[4],
        all_total[5],
        all_total[6],
        all_total[7],
        all_total[8],
        all_total[9],
        all_total[10],
        gain_total[0],
        gain_total[1],
        all_total[11],
        all_total[12],
        all_total[13],
    )


def choose_body(mesh, *arrays):
    tokens = arrays[0]
    chans = tokens.shape[2] // mesh.shape["seq"]
    fits = mesh.shape["seq"] == 8 and mesh.shape["tp"] == 4 and tokens.shape[:2] == (4, 128) and chans == 96
    return (fast_body if fits else general_body)(*arrays)


def solution(mesh):
    mapped = jax.shard_map(
        functools.partial(choose_body, mesh),
        mesh=mesh,
        in_specs=(
            P(None, "seq", None),
            P(),
            P(),
            P(),
            P(),
            P(),
            P(),
            P(),
            P(),
            P(),
            P(),
            P(),
            P(),
            P(),
            P(None, "tp"),
            P(None, "tp"),
            P("tp", None),
            P(None, ("seq", "tp"), None),
        ),
        out_specs=(
            P(None, ("seq", "tp"), None),
            P(None, "seq", None),
            P(),
            P(),
            P(),
            P(),
            P(),
            P(),
            P(),
            P(),
            P(),
            P(),
            P(),
            P(),
            P(),
            P(None, "tp"),
            P(None, "tp"),
            P("tp", None),
        ),
        check_vma=False,
    )

    def program(*arrays):
        with jax.sharding.use_abstract_mesh(mesh.abstract_mesh):
            return mapped(*arrays)

    return program
```

```python
import functools
import math
import types
import typing

import numpy as np
import jax
import jax.numpy as jnp
from jax import lax
from jax.experimental import pallas as pl
from jax.experimental.pallas import tpu as pltpu
from jax.sharding import PartitionSpec as P

BF = jnp.bfloat16
F32 = jnp.float32
MESH = pl.DeviceIdType.MESH
NN = ((1,), (0,))
NT = ((1,), (1,))
TN = ((0,), (0,))
LIMIT = 56 * 1024 * 1024


def dot(first, second, form=NN):
    return lax.dot_general(first, second, (form, ((), ())), preferred_element_type=F32)


def any_spec():
    return pl.BlockSpec(memory_space=pl.ANY)


def vmem_spec():
    return pl.BlockSpec(memory_space=pltpu.VMEM)


def sin_cos(value):
    turns = jnp.floor(value * (1.0 / math.pi) + 0.5)
    rest = value - turns * 3.140625
    rest = rest - turns * 9.67502593994140625e-4
    rest = rest - turns * 1.509957990978376432e-7
    half = turns * 0.5
    sign = 1.0 - 4.0 * (half - jnp.floor(half))
    square = rest * rest
    sine = 1.0 / 362880 - square * (1.0 / 39916800)
    sine = -1.0 / 5040 + square * sine
    sine = 1.0 / 120 + square * sine
    sine = -1.0 / 6 + square * sine
    sine = rest + rest * square * sine
    cosine = 1.0 / 40320 - square * (1.0 / 3628800 - square * (1.0 / 479001600))
    cosine = -1.0 / 720 + square * cosine
    cosine = 1.0 / 24 + square * cosine
    cosine = -0.5 + square * cosine
    cosine = 1.0 + square * cosine
    return sign * sine, sign * cosine


def flip(index, bits):
    result = 0
    for place in range(3):
        digit = lax.rem(index // (1 << place), 2)
        if (bits >> place) & 1:
            digit = 1 - digit
        result = result + digit * (1 << place)
    return result


def greet(n_seq, n_tp):
    me, plane = lax.axis_index("seq"), lax.axis_index("tp")
    barrier = pltpu.get_barrier_semaphore()
    for k in range(1, n_seq):
        pl.semaphore_signal(barrier, inc=1, device_id={"seq": flip(me, k)}, device_id_type=MESH)
    for k in range(1, n_tp):
        pl.semaphore_signal(barrier, inc=1, device_id={"tp": flip(plane, k)}, device_id_type=MESH)
    return lambda: pl.semaphore_wait(barrier, n_seq + n_tp - 2)


def sign_rows(count, width):
    row = lax.broadcasted_iota(jnp.int32, (count, width), 0)
    return (1 - 2 * lax.rem(row, 2)).astype(F32)


def sign_lanes(count, width):
    lane = lax.broadcasted_iota(jnp.int32, (count, width), 1)
    return (1 - 2 * lax.rem(lane, 2)).astype(F32)


def previous(values):
    lane = lax.broadcasted_iota(jnp.int32, values.shape, 1)
    return jnp.where(lane == 0, 0.0, pltpu.roll(values, 1, 1))


def following(values):
    last = values.shape[1] - 1
    lane = lax.broadcasted_iota(jnp.int32, values.shape, 1)
    return jnp.where(lane == last, 0.0, pltpu.roll(values, last, 1))


def monarch_forward(load, right, left, shuffled, store):
    groups, width, _ = right.shape
    part = width // groups
    for b in range(groups):
        middle = dot(right[b], load(b), TN).astype(BF)
        for g in range(groups):
            shuffled[pl.ds(g * width + b * part, part), :] = middle[g * part : (g + 1) * part]
    for g in range(groups):
        store(g, dot(left[g], shuffled[pl.ds(g * width, width), :], TN))


SEQ_ORDER = (6, 7, 2, 3, 4, 5, 1)


def front_part(n_seq, n_tp, dims, r, entered, loads):
    width, chans, length, rows = dims
    me, plane = lax.axis_index("seq"), lax.axis_index("tp")
    cotangent, right, left, features = r.cotangent, r.in_right, r.in_left, r.features
    token_v, table_v, normed, shuffled, signals = r.token_v, r.table_v, r.in_normed, r.in_shuffled, r.signals
    acts, taps_v, padded, wave, conv, nyquist, columns, third_v = (
        r.acts, r.taps_v, r.padded, r.wave, r.conv, r.nyquist, r.columns, r.third_v
    )
    projected, spread, product, keyed, spectrum, mixed, totals = (
        r.projected, r.spread, r.product, r.query, r.back_wave, r.front_mixed, r.totals
    )
    loads.token.wait()
    value = token_v[...].astype(F32)
    shifted = value - jnp.mean(value, axis=-1, keepdims=True)
    inverse = lax.rsqrt(jnp.mean(shifted * shifted, axis=-1, keepdims=True) + 1e-05)
    value = shifted * inverse * r.gain[...].reshape(1, width) + r.bias[...].reshape(1, width)
    normed[...] = value.T.astype(BF)
    groups = right.shape[0]
    block = width // groups
    fan = left.shape[2]

    def keep(g, result):
        projected[pl.ds(g * fan, fan), :] = result.astype(BF)

    monarch_forward(lambda b: normed[pl.ds(b * block, block), :], right, left, shuffled, keep)
    entered()
    sends = []
    mine = pl.ds(pl.multiple_of(me * rows, rows), rows)
    for k in SEQ_ORDER:
        other = flip(me, k)
        for s in range(3):
            copy = pltpu.make_async_remote_copy(
                src_ref=projected.at[pl.ds(pl.multiple_of(s * width + other * chans, 16), chans), :],
                dst_ref=signals.at[s, :, mine],
                send_sem=r.front_send.at[k, s],
                recv_sem=r.front_recv.at[k, s],
                device_id={"seq": other},
                device_id_type=MESH,
            )
            copy.start()
            sends.append(copy)
    for s in range(3):
        signals[s, :, mine] = projected[pl.ds(pl.multiple_of(s * width + me * chans, 16), chans), :]
    part = rows // n_tp
    spot = pl.ds(pl.multiple_of(plane * part, part), part)
    cot_copies = []
    for k in range(1, n_tp):
        copy = pltpu.make_async_remote_copy(
            src_ref=cotangent,
            dst_ref=r.cot_v.at[:, spot, :],
            send_sem=r.cot_send.at[k],
            recv_sem=r.cot_recv.at[k],
            device_id={"tp": flip(plane, k)},
            device_id_type=MESH,
        )
        copy.start()
        cot_copies.append(copy)
    own_cot = pltpu.make_async_copy(cotangent, r.cot_v.at[:, spot, :], r.local_sems.at[17])
    own_cot.start()

    own = pl.ds(pl.multiple_of(me * chans, 16), chans)
    lines = [r.short[s].astype(F32) for s in range(3)]
    lines += [r.conv_bias[...].reshape(1, width), jnp.zeros((6, width), F32)]
    r.tall[...] = jnp.concatenate(lines, axis=0).T
    columns[...] = r.tall[own, :]
    r.third_turned[...] = r.third[...].T
    third_v[pl.ds(0, chans), :] = r.third_turned[own, :]
    third_v[pl.ds(chans, 128 - chans), :] = jnp.zeros((128 - chans, 128), BF)
    lead = jnp.concatenate([r.first[...].astype(F32), jnp.zeros((3, 128), F32)], axis=0)
    lead = jnp.concatenate([lead, lead], axis=0).astype(BF)

    chunk = 256
    per = length // chunk
    totals[...] = jnp.zeros_like(totals)
    for half in range(2):

        def tap_step(at, carry, half=half):
            row = pl.multiple_of(half * length + at * chunk, chunk)
            here = pl.ds(row, chunk)
            sine, cosine = sin_cos(dot(features[here, :], lead))
            high = sine.astype(BF)
            acts[0, here, :] = high
            acts[1, here, :] = cosine.astype(BF)
            low = (sine - high.astype(F32)).astype(BF)
            sine, cosine = sin_cos(dot(high, r.second[...]) + dot(low, r.second[...]))
            high = sine.astype(BF)
            acts[2, here, :] = high
            acts[3, here, :] = cosine.astype(BF)
            taps = dot(high, third_v[...], NT) * (length**-0.5)
            if half == 1:
                index = lax.broadcasted_iota(jnp.int32, taps.shape, 0) + at * chunk
                taps = jnp.where(index == 0, 0.0, taps)
            totals[...] += jnp.sum(taps * sign_rows(*taps.shape), axis=0, keepdims=True)
            spread[pl.ds(pl.multiple_of(at * chunk, chunk), chunk), pl.ds(half * 128, 128)] = taps.astype(BF)
            return carry

        lax.fori_loop(0, per, tap_step, 0)
    loads.table.wait()

    def spectrum_step(at, carry):
        here = pl.ds(pl.multiple_of(at * chunk, chunk), chunk)
        sign = sign_rows(chunk, 128)
        index = lax.broadcasted_iota(jnp.int32, (chunk, 128), 0) + at * chunk
        weight = jnp.where(index == 0, 0.5 / length, 1.0 / length)
        for which in range(2):
            result = dot(table_v[which, here, :], spread[...])
            taps_v[which, here, :] = ((result[:, :128] + sign * result[:, 128:]) * weight).astype(BF)
        return carry

    lax.fori_loop(0, per, spectrum_step, 0)
    tap_total = jnp.broadcast_to(totals[...], (128, 128)).T[:chans, 0:1]

    for copy in sends:
        copy.wait_recv()

    step = 16
    padded[pl.ds(chans, 128 - chans), :] = jnp.zeros((128 - chans, length), BF)

    def short_step(at, carry):
        here = pl.ds(pl.multiple_of(at * step, step), step)
        shorted = []
        for s in range(3):
            value = signals[s, here, :].astype(F32)
            shorted.append(
                previous(value) * columns[here, 3 * s : 3 * s + 1]
                + value * columns[here, 3 * s + 1 : 3 * s + 2]
                + following(value) * columns[here, 3 * s + 2 : 3 * s + 3]
            )
        result = shorted[0] * shorted[2]
        product[here, :] = result
        keyed[here, :] = shorted[1]
        padded[here, :] = result.astype(BF)
        nyquist[here, 0:1] = jnp.sum(result * sign_lanes(step, length), axis=1, keepdims=True)
        return carry

    lax.fori_loop(0, chans // step, short_step, 0)
    nyquist[:, 1:2] = tap_total

    def wave_step(at, carry):
        here = pl.ds(pl.multiple_of(at * chunk, chunk), chunk)
        cos_part = dot(table_v[0, here, :], padded[...], NT)
        sin_part = dot(table_v[1, here, :], padded[...], NT)
        wave[0, here, :] = cos_part.astype(BF)
        wave[1, here, :] = sin_part.astype(BF)
        tap_cos = taps_v[0, here, :].astype(F32)
        tap_sin = taps_v[1, here, :].astype(F32)
        spectrum[0, here, :] = (cos_part * tap_cos - sin_part * tap_sin).astype(BF)
        spectrum[1, here, :] = (cos_part * tap_sin + sin_part * tap_cos).astype(BF)
        return carry

    lax.fori_loop(0, per, wave_step, 0)

    def conv_step(at, carry):
        here = pl.ds(pl.multiple_of(at * chunk, chunk), chunk)
        result = dot(table_v[0, here, :], spectrum[0]) + dot(table_v[1, here, :], spectrum[1])
        result = result.T[:chans]
        result = (
            result
            + sign_lanes(chans, chunk) * (nyquist[:, 0:1] * nyquist[:, 1:2] * (0.5 / length))
            + columns[:, 9:10] * product[:, here]
        )
        conv[:, here] = result
        mixed[:, here] = (keyed[:, here] * result).astype(BF)
        return carry

    lax.fori_loop(0, per, conv_step, 0)
    backs = []
    slot = pl.ds(pl.multiple_of(me * chans, 16), chans)
    for k in SEQ_ORDER:
        other = flip(me, k)
        copy = pltpu.make_async_remote_copy(
            src_ref=mixed.at[:, pl.ds(pl.multiple_of(other * rows, rows), rows)],
            dst_ref=r.mixed.at[slot, :],
            send_sem=r.mix_send.at[k],
            recv_sem=r.mix_recv.at[k],
            device_id={"seq": other},
            device_id_type=MESH,
        )
        copy.start()
        backs.append(copy)
    r.mixed[slot, :] = mixed[:, mine]
    for copy in backs:
        copy.wait_recv()
    return sends + backs, cot_copies, own_cot


def split_table(values):
    high = values.astype(BF)
    low = (values - high.astype(np.float32)).astype(BF)
    return high, low


def constants(length):
    index = np.arange(length)
    angle = (index[:, None] * index[None, :] % (2 * length)) * (math.pi / length)
    table = np.stack([np.cos(angle), np.sin(angle)]).astype(np.float32).astype(BF)
    place = np.arange(2 * length)
    scaled = np.where(place < length, place, place - 2 * length) / length
    features = np.zeros((2 * length, 8), np.float32)
    features[:, 0] = scaled
    features[:, 1] = np.sin(math.pi * scaled)
    features[:, 2] = np.cos(math.pi * scaled)
    features[:, 3] = np.sin(7.0 * math.pi * scaled)
    features[:, 4] = np.cos(7.0 * math.pi * scaled)
    return table, np.concatenate(split_table(features), axis=1)


def monarch_backward(upstream, operand, shuffled, right, left, middle, keep_right, keep_left, store):
    groups, width, _ = right.shape
    part = width // groups
    for g in range(groups):
        above = upstream(g)
        keep_left(g, dot(shuffled[pl.ds(g * width, width), :], above, NT))
        below = dot(left[g], above).astype(BF)
        for b in range(groups):
            middle[pl.ds(b * width + g * part, part), :] = below[b * part : (b + 1) * part]
    for b in range(groups):
        above = middle[pl.ds(b * width, width), :]
        keep_right(b, dot(operand(b), above, NT))
        store(b, dot(right[b], above))


CHIPS = (6, 2, 4)


class Reduce:
    def __init__(self, n_seq, n_tp, own, full, core_in, halves, chip_in, quarter, plane_in, send, recv):
        self.own, self.full, self.core_in, self.halves = own, full, core_in, halves
        self.chip_in, self.quarter, self.plane_in = chip_in, quarter, plane_in
        self.send, self.recv, self.n_tp = send, recv, n_tp
        rows, width = own.shape
        self.rows, self.width = rows, width
        self.per_chip, self.per_plane = rows // (n_seq // 2), rows // (n_seq // 2) // n_tp
        self.me, self.plane = lax.axis_index("seq"), lax.axis_index("tp")
        core = lax.rem(self.me, 2)
        self.mine = pl.ds(pl.multiple_of(core * (width // 2), 128), width // 2)
        self.theirs = pl.ds(pl.multiple_of((1 - core) * (width // 2), 128), width // 2)
        self.started = []

    def chip_rows(self, index):
        return pl.ds(pl.multiple_of(index // 2 * self.per_chip, 16), self.per_chip)

    def copy(self, source, target, at, where):
        result = pltpu.make_async_remote_copy(
            src_ref=source, dst_ref=target, send_sem=self.send.at[at], recv_sem=self.recv.at[at],
            device_id=where, device_id_type=MESH,
        )
        result.start()
        self.started.append(result)
        return result

    def start_core(self):
        self.phase = [self.copy(self.own.at[:, self.theirs], self.core_in, 0, {"seq": flip(self.me, 1)})]

    def arrived(self):
        for copy in self.phase:
            copy.wait_recv()
        self.phase = []

    def start_chip(self):
        self.arrived()
        self.halves[...] = (self.own[:, self.mine].astype(F32) + self.core_in[...].astype(F32)).astype(BF)
        for k in CHIPS:
            other = flip(self.me, k)
            self.phase.append(
                self.copy(self.halves.at[self.chip_rows(other), :], self.chip_in.at[k // 2], k // 2, {"seq": other})
            )

    def start_plane(self):
        self.arrived()
        total = self.halves[self.chip_rows(self.me), :].astype(F32)
        for k in CHIPS:
            total = total + self.chip_in[k // 2].astype(F32)
        self.quarter[...] = total.astype(BF)
        for k in range(1, self.n_tp):
            other = flip(self.plane, k)
            here = pl.ds(pl.multiple_of(other * self.per_plane, 16), self.per_plane)
            self.phase.append(self.copy(self.quarter.at[here, :], self.plane_in.at[k], 3 + k, {"tp": other}))

    def start_plane_back(self):
        self.arrived()
        here = pl.ds(pl.multiple_of(self.plane * self.per_plane, 16), self.per_plane)
        total = self.quarter[here, :].astype(F32)
        for k in range(1, self.n_tp):
            total = total + self.plane_in[k].astype(F32)
        rows = pl.ds(
            pl.multiple_of(self.me // 2 * self.per_chip + self.plane * self.per_plane, 16), self.per_plane
        )
        self.full[rows, self.mine] = total.astype(BF)
        spot = self.full.at[rows, self.mine]
        for k in range(1, self.n_tp):
            self.phase.append(self.copy(spot, spot, 6 + k, {"tp": flip(self.plane, k)}))

    def start_chip_back(self):
        self.arrived()
        spot = self.full.at[self.chip_rows(self.me), self.mine]
        for k in CHIPS:
            self.phase.append(self.copy(spot, spot, 9 + k // 2, {"seq": flip(self.me, k)}))

    def start_core_back(self):
        self.arrived()
        spot = self.full.at[:, self.mine]
        self.phase.append(self.copy(spot, spot, 13, {"seq": flip(self.me, 1)}))

    def finish(self):
        self.arrived()
        for copy in self.started:
            copy.wait_send()


def neighbour_order(plane, at):
    upper = plane // 2
    near = plane + upper * (3 - 2 * plane)
    result = at * (1 - near) + (0, 0, 2, 3)[at] * near
    return result + upper * (3 - 2 * result)


def work_order(plane):
    odd = lax.rem(plane, 2)
    return 1 + odd, lax.rem(plane + 2, 4), 3 - 3 * odd


class Line:
    def __init__(self, n_tp, slots, send, recv):
        self.n_tp, self.slots, self.send, self.recv = n_tp, slots, send, recv
        self.plane = lax.axis_index("tp")
        self.sent = []

    def copy(self, block, source, way):
        return pltpu.make_async_remote_copy(
            src_ref=source, dst_ref=self.slots.at[block], send_sem=self.send.at[way, block], recv_sem=self.recv.at[block],
            device_id={"tp": self.plane + (1, -1)[way]}, device_id_type=MESH,
        )

    def start(self, block, source, way, here):
        @pl.when(here)
        def _():
            self.copy(block, source, way).start()

        self.sent.append((block, source, way, here))

    def begin(self, source):
        self.start(self.plane, source, 0, self.plane < self.n_tp - 1)
        self.start(self.plane, source, 1, self.plane > 0)

    def take(self, block, here=None):
        arrival = pltpu.make_async_remote_copy(
            src_ref=self.slots.at[block], dst_ref=self.slots.at[block], send_sem=self.send.at[0, block],
            recv_sem=self.recv.at[block], device_id={"tp": block}, device_id_type=MESH,
        )
        up = jnp.logical_and(block < self.plane, self.plane < self.n_tp - 1)
        down = jnp.logical_and(block > self.plane, self.plane > 0)
        if here is None:
            arrival.wait_recv()
        else:
            pl.when(here)(arrival.wait_recv)
            up, down = jnp.logical_and(up, here), jnp.logical_and(down, here)
        source = self.slots.at[block]
        self.start(block, source, 0, up)
        self.start(block, source, 1, down)

    def finish(self):
        for block, source, way, here in self.sent:

            @pl.when(here)
            def _(block=block, source=source, way=way):
                self.copy(block, source, way).wait_send()


class Square:
    def __init__(self, own, full, core_in, half, first_in, second_in, send, recv):
        self.own, self.full, self.core_in, self.half = own, full, core_in, half
        self.first_in, self.second_in, self.send, self.recv = first_in, second_in, send, recv
        me = lax.axis_index("seq")
        self.me = me
        rows = own.shape[0]
        self.rows = rows
        self.core = lax.rem(me, 2)
        y, x = me // 4, lax.rem(me // 2, 2)
        quarter, part = rows // 8, rows // 16
        base = rows // 4
        self.ways = ((2, x, y, 0), (4, y, x, base))
        self.quarter, self.part = quarter, part
        self.started = []
        self.phase = []

    def copy(self, source, target, at, k):
        result = pltpu.make_async_remote_copy(
            src_ref=source, dst_ref=target, send_sem=self.send.at[at], recv_sem=self.recv.at[at],
            device_id={"seq": flip(self.me, k)}, device_id_type=MESH,
        )
        result.start()
        self.started.append(result)
        self.phase.append(result)

    def arrived(self):
        for copy in self.phase:
            copy.wait_recv()
        self.phase = []

    def span(self, start, size):
        return pl.ds(pl.multiple_of(start, 16), size)

    def start_core(self):
        half = self.rows // 2
        self.copy(self.own.at[self.span((1 - self.core) * half, half), :], self.core_in, 0, 1)

    def start_first(self):
        self.arrived()
        half = self.rows // 2
        own = self.own[self.span(self.core * half, half), :]
        self.half[...] = (own.astype(F32) + self.core_in[...].astype(F32)).astype(BF)
        for way, (k, near, far, base) in enumerate(self.ways):
            source = self.half.at[self.span(base + (1 - near) * self.quarter, self.quarter), :]
            self.copy(source, self.first_in.at[way], 1 + way, k)

    def start_second(self):
        self.arrived()
        for way, (k, near, far, base) in enumerate(self.ways):
            here = self.span(base + near * self.quarter, self.quarter)
            self.half[here, :] = (self.half[here, :].astype(F32) + self.first_in[way].astype(F32)).astype(BF)
            source = self.half.at[self.span(base + near * self.quarter + (1 - far) * self.part, self.part), :]
            self.copy(source, self.second_in.at[way], 3 + way, 6 - k)

    def start_second_back(self):
        self.arrived()
        for way, (k, near, far, base) in enumerate(self.ways):
            place = base + near * self.quarter + far * self.part
            total = self.half[self.span(place, self.part), :].astype(F32) + self.second_in[way].astype(F32)
            here = self.span(self.core * (self.rows // 2) + place, self.part)
            self.full[here, :] = total.astype(BF)
            spot = self.full.at[here, :]
            self.copy(spot, spot, 5 + way, 6 - k)

    def start_first_back(self):
        self.arrived()
        for way, (k, near, far, base) in enumerate(self.ways):
            spot = self.full.at[self.span(self.core * (self.rows // 2) + base + near * self.quarter, self.quarter), :]
            self.copy(spot, spot, 7 + way, k)

    def start_core_back(self):
        self.arrived()
        spot = self.full.at[self.span(self.core * (self.rows // 2), self.rows // 2), :]
        self.copy(spot, spot, 9, 1)

    def finish(self):
        for copy in self.started:
            copy.wait_send()


class Inputs(typing.NamedTuple):
    feed_gain: typing.Any
    feed_bias: typing.Any
    out_right: typing.Any
    out_left: typing.Any
    gain: typing.Any
    bias: typing.Any
    in_right: typing.Any
    in_left: typing.Any
    short: typing.Any
    conv_bias: typing.Any
    features: typing.Any
    first: typing.Any
    second: typing.Any
    third: typing.Any
    tokens: typing.Any
    cotangent: typing.Any
    table: typing.Any
    gate_w: typing.Any
    up_w: typing.Any
    down_w: typing.Any


class Outputs(typing.NamedTuple):
    output_out: typing.Any
    ffn_out: typing.Any
    tokens_out: typing.Any
    late_out: typing.Any
    early_out: typing.Any
    small_out: typing.Any


def core_scratch(n_seq, n_tp, width, chans, length, rows):
    result = dict(
        token_v=pltpu.VMEM((rows, width), BF),
        cot_v=pltpu.VMEM((n_tp, rows, width), BF),
        gate_v=pltpu.VMEM((width, width), BF),
        up_v=pltpu.VMEM((width, width), BF),
        down_v=pltpu.VMEM((width, width), BF),
        out_shuffled=pltpu.VMEM((width, rows), BF),
        branch=pltpu.VMEM((width, rows), F32),
        resid=pltpu.VMEM((rows, width), F32),
        scaled=pltpu.VMEM((rows, width), F32),
        inverse=pltpu.VMEM((rows, 1), F32),
        normed=pltpu.VMEM((n_tp, rows, width), BF),
        hidden=pltpu.VMEM((n_tp, rows, width), BF),
        grad_hidden=pltpu.VMEM((n_tp, rows, width), F32),
        grad_gate=pltpu.VMEM((n_tp, rows, width), BF),
        grad_up=pltpu.VMEM((n_tp, rows, width), BF),
        grad_normed=pltpu.VMEM((rows, width), F32),
        grad_send=pltpu.VMEM((n_tp, rows, width), BF),
        grad_recv=pltpu.VMEM((n_tp, rows, width), BF),
        glu_own=pltpu.VMEM((rows, width), F32),
        glu_send=pltpu.VMEM((n_tp, rows, width), BF),
        glu_recv=pltpu.VMEM((n_tp, rows, width), BF),
        turned=pltpu.VMEM((width, n_tp*rows), BF),
        grads=pltpu.VMEM((3, width, width), BF),
        ffn_v=pltpu.VMEM((3, width, width), BF),
        core_in=pltpu.VMEM((3, width//2, width), BF),
        halves=pltpu.VMEM((3, width//2, width), BF),
        first_in=pltpu.VMEM((3, 2, width//8, width), BF),
        second_in=pltpu.VMEM((3, 2, width//16, width), BF),
        grad_branch=pltpu.VMEM((width, rows), BF),
        middle=pltpu.VMEM((width, rows), BF),
        grad_mixed_own=pltpu.VMEM((width, rows), BF),
        grad_mixed=pltpu.VMEM((chans, length), BF),
        out_rows=pltpu.VMEM((rows, width), BF),
        output_v=pltpu.VMEM((n_tp, rows//n_tp, width), BF),
        grad_vectors=pltpu.VMEM((2, width), F32),
        grad_resid=pltpu.VMEM((rows, width), F32),
        table_v=pltpu.VMEM((2, length, length), BF),
        signals=pltpu.VMEM((3, chans, length), BF),
        conv=pltpu.VMEM((chans, length), F32),
        wave=pltpu.VMEM((2, length, 128), BF),
        taps_v=pltpu.VMEM((2, length, 128), BF),
        acts=pltpu.VMEM((4, 2*length, 128), BF),
        in_normed=pltpu.VMEM((width, rows), BF),
        in_shuffled=pltpu.VMEM((width, rows), BF),
        grad_short=pltpu.VMEM((3, chans, length), F32),
        query=pltpu.VMEM((chans, length), F32),
        value_v=pltpu.VMEM((chans, length), F32),
        grad_conv=pltpu.VMEM((chans, length), F32),
        padded=pltpu.VMEM((128, length), BF),
        back_wave=pltpu.VMEM((2, length, 128), BF),
        cross=pltpu.VMEM((2, length, 256), BF),
        sums=pltpu.VMEM((128, 128), F32),
        grad_signals=pltpu.VMEM((3, chans, length), BF),
        grad_proj=pltpu.VMEM((3*width, rows), BF),
        grad_rows=pltpu.VMEM((width, rows), F32),
        grad_tok=pltpu.VMEM((rows, width), BF),
        grad_second=pltpu.VMEM((128, 128), F32),
        grad_first=pltpu.VMEM((16, 128), F32),
        grad_third=pltpu.VMEM((128, 128), F32),
        local_sems=pltpu.SemaphoreType.DMA((20,)),
        line_send=pltpu.SemaphoreType.DMA((2,n_tp)),
        line_recv=pltpu.SemaphoreType.DMA((n_tp,)),
        tok_send=pltpu.SemaphoreType.DMA((2,n_tp)),
        tok_recv=pltpu.SemaphoreType.DMA((n_tp,)),
        back_send=pltpu.SemaphoreType.DMA((n_tp,)),
        back_recv=pltpu.SemaphoreType.DMA((n_tp,)),
        glu_ssem=pltpu.SemaphoreType.DMA((n_tp,)),
        glu_rsem=pltpu.SemaphoreType.DMA((n_tp,)),
        out_send=pltpu.SemaphoreType.DMA((n_tp,)),
        out_recv=pltpu.SemaphoreType.DMA((n_tp,)),
        mixed_send=pltpu.SemaphoreType.DMA((n_seq,)),
        mixed_recv=pltpu.SemaphoreType.DMA((n_seq,)),
        seq_send=pltpu.SemaphoreType.DMA((n_seq,3)),
        seq_recv=pltpu.SemaphoreType.DMA((n_seq,3)),
        ffn_send=pltpu.SemaphoreType.DMA((3,10)),
        ffn_recv=pltpu.SemaphoreType.DMA((3,10)),
        mixed=pltpu.VMEM((width, rows), BF),
        front_mixed=pltpu.VMEM((chans, length), BF),
        nyquist=pltpu.VMEM((chans, 128), F32),
        columns=pltpu.VMEM((chans, 16), F32),
        third_v=pltpu.VMEM((128, 128), BF),
        projected=pltpu.VMEM((3 * width, rows), BF),
        spread=pltpu.VMEM((length, 256), BF),
        product=pltpu.VMEM((chans, length), F32),
        totals=pltpu.VMEM((1, 128), F32),
        tall=pltpu.VMEM((width, 16), F32),
        third_turned=pltpu.VMEM((width, 128), BF),
        front_send=pltpu.SemaphoreType.DMA((n_seq, 3)),
        front_recv=pltpu.SemaphoreType.DMA((n_seq, 3)),
        mix_send=pltpu.SemaphoreType.DMA((n_seq,)),
        mix_recv=pltpu.SemaphoreType.DMA((n_seq,)),
        cot_send=pltpu.SemaphoreType.DMA((n_tp,)),
        cot_recv=pltpu.SemaphoreType.DMA((n_tp,)),
        late_own=pltpu.VMEM((width, width), BF),
        late_full=pltpu.VMEM((width, width), BF),
        early_own=pltpu.VMEM((width, 512), BF),
        early_full=pltpu.VMEM((width, 512), BF),
        small_own=pltpu.VMEM((256, 256), BF),
        small_full=pltpu.VMEM((256, 256), BF),
    )
    groups = []
    for count, breadth in ((256, width), (256, width), (256, width), (width, 512), (256, 256)):
        half, chip = breadth // 2, count // (n_seq // 2)
        groups.append(
            [
                pltpu.VMEM((count, half), BF),
                pltpu.VMEM((count, half), BF),
                pltpu.VMEM((n_seq // 2, chip, half), BF),
                pltpu.VMEM((chip, half), BF),
                pltpu.VMEM((n_tp, chip // n_tp, half), BF),
                pltpu.SemaphoreType.DMA((14,)),
                pltpu.SemaphoreType.DMA((14,)),
            ]
        )
    return result, groups


def core_kernel(n_seq, n_tp, dims, *refs):
    width, chans, length, rows = dims
    scratch, groups = core_scratch(n_seq, n_tp, width, chans, length, rows)
    named = dict(zip(Inputs._fields + Outputs._fields + tuple(scratch), refs))
    r = types.SimpleNamespace(**named)
    spare = list(refs[len(named) :])
    reduce_refs = [[spare.pop(0) for _ in group] for group in groups]
    me, plane = lax.axis_index("seq"), lax.axis_index("tp")
    entered = greet(n_seq, n_tp)
    sources = dict(
        token=(r.tokens.at[plane], r.token_v),
        down=(r.down_w, r.down_v),
        gate=(r.gate_w, r.gate_v),
        up=(r.up_w, r.up_v),
        table=(r.table, r.table_v),
    )
    copies = {
        name: pltpu.make_async_copy(*pair, r.local_sems.at[at]) for at, (name, pair) in enumerate(sources.items())
    }
    for copy in copies.values():
        copy.start()
    loads = types.SimpleNamespace(**copies)
    front_sends, cot_copies, own_cot = front_part(n_seq, n_tp, dims, r, entered, loads)
    _, block, _ = r.out_right.shape
    chunk = 256
    pieces = width // chunk
    per = length // chunk
    step = 16

    lates = []
    for at in range(3):
        here = pl.ds(256 * at, 256)
        lates.append(Reduce(n_seq, n_tp, r.late_own.at[here, :], r.late_full.at[here, :], *reduce_refs[at]))
    early = Reduce(n_seq, n_tp, r.early_own, r.early_full, *reduce_refs[3])
    small = Reduce(n_seq, n_tp, r.small_own, r.small_full, *reduce_refs[4])
    squares = [
        Square(
            r.grads.at[which], r.ffn_v.at[which], r.core_in.at[which], r.halves.at[which], r.first_in.at[which],
            r.second_in.at[which], r.ffn_send.at[which], r.ffn_recv.at[which],
        )
        for which in range(3)
    ]

    def keep_branch(g, result):
        r.branch[pl.ds(g * block, block), :] = result

    monarch_forward(lambda b: r.mixed[pl.ds(b * block, block), :], r.out_right, r.out_left, r.out_shuffled, keep_branch)
    tokens = r.token_v[...].astype(F32)
    value = tokens + r.branch[...].T
    r.resid[...] = value
    shifted = value - jnp.mean(value, axis=-1, keepdims=True)
    r.inverse[...] = lax.rsqrt(jnp.mean(shifted * shifted, axis=-1, keepdims=True) + 1e-05)
    value = shifted * r.inverse[...]
    r.scaled[...] = value
    r.normed[plane] = (value * r.feed_gain[...].reshape(1, width) + r.feed_bias[...].reshape(1, width)).astype(BF)
    line = Line(n_tp, r.normed, r.line_send, r.line_recv)
    line.begin(r.normed.at[plane])
    for copy in cot_copies:
        copy.wait_recv()
    own_cot.wait()
    loads.down.wait()

    def hidden_step(at, carry):
        cols = pl.ds(pl.multiple_of(at * chunk, chunk), chunk)
        result = dot(r.cot_v[...].reshape(n_tp * rows, width), r.down_v[cols, :], NT)
        r.grad_hidden[:, :, cols] = result.reshape(n_tp, rows, chunk)
        return carry

    lax.fori_loop(0, pieces, hidden_step, 0)
    loads.gate.wait()
    loads.up.wait()
    backs = []
    def send_back(other):
        copy = pltpu.make_async_remote_copy(
            src_ref=r.grad_send.at[other],
            dst_ref=r.grad_recv.at[plane],
            send_sem=r.back_send.at[other],
            recv_sem=r.back_recv.at[plane],
            device_id={"tp": other},
            device_id_type=MESH,
        )
        copy.start()
        backs.append(copy)

    order = work_order(plane)
    inner = jnp.logical_and(plane > 0, plane < n_tp - 1)
    outer = jnp.logical_not(inner)
    for k in range(n_tp):
        other = plane if k == 0 else order[k - 1]
        if k == 1:
            line.take(order[2], inner)
            line.take(order[0])
        if k == 2:
            line.take(order[1])
        if k == 3:
            line.take(order[2], outer)
        if k > 1:
            send_back(order[k - 2])

        def gate_step(at, carry, other=other):
            cols = pl.ds(pl.multiple_of(at * chunk, chunk), chunk)
            value = r.normed[other]
            gate = dot(value, r.gate_v[:, cols])
            upward = dot(value, r.up_v[:, cols])
            sigma = 1.0 / (1.0 + jnp.exp(-gate))
            active = gate * sigma
            r.hidden[other, :, cols] = (active * upward).astype(BF)
            above = r.grad_hidden[other, :, cols]
            r.grad_gate[other, :, cols] = (above * upward * (sigma + active * (1.0 - sigma))).astype(BF)
            r.grad_up[other, :, cols] = (above * active).astype(BF)
            return carry

        lax.fori_loop(0, pieces, gate_step, 0)

        def back_step(at, carry, k=k, other=other):
            cols = pl.ds(pl.multiple_of(at * chunk, chunk), chunk)
            result = dot(r.grad_gate[other], r.gate_v[cols, :], NT) + dot(r.grad_up[other], r.up_v[cols, :], NT)
            if k == 0:
                r.grad_normed[:, cols] = result
            else:
                r.grad_send[other, :, cols] = result.astype(BF)
            return carry

        lax.fori_loop(0, pieces, back_step, 0)
    send_back(order[2])

    def turn(source):
        for s in range(n_tp):
            r.turned[:, s * rows : (s + 1) * rows] = source[s].T

    def weight_grad(which, factor):
        def grad_step(at, carry):
            here = pl.ds(pl.multiple_of(at * chunk, chunk), chunk)
            result = dot(r.turned[here, :], factor[...].reshape(n_tp * rows, width))
            r.grads[which, here, :] = result.astype(BF)
            return carry

        lax.fori_loop(0, pieces, grad_step, 0)
        squares[which].start_core()

    turn(r.normed)
    weight_grad(0, r.grad_gate)
    weight_grad(1, r.grad_up)
    squares[0].start_first()
    turn(r.hidden)
    weight_grad(2, r.cot_v)
    squares[1].start_first()
    squares[2].start_first()

    def from_planes(recv, slots):
        total = 0.0
        for k in range(1, n_tp):
            other = flip(plane, k)
            pltpu.make_async_remote_copy(
                src_ref=slots.at[other], dst_ref=slots.at[other], send_sem=recv.at[other], recv_sem=recv.at[other],
                device_id={"tp": other}, device_id_type=MESH,
            ).wait_recv()
            total = total + slots[other].astype(F32)
        return total

    total = r.grad_normed[...] + from_planes(r.back_recv, r.grad_recv)
    value = r.scaled[...]
    r.grad_vectors[0:1, :] = jnp.sum(total * value, axis=0, keepdims=True)
    r.grad_vectors[1:2, :] = jnp.sum(total, axis=0, keepdims=True)
    total = total * r.feed_gain[...].reshape(1, width)
    first_mean = jnp.mean(total, axis=-1, keepdims=True)
    second_mean = jnp.mean(total * value, axis=-1, keepdims=True)
    total = r.cot_v[plane].astype(F32) + r.inverse[...] * (total - first_mean - value * second_mean)
    r.grad_resid[...] = total
    r.grad_branch[...] = total.T.astype(BF)
    out_parts = {}

    def keep_out_left(g, result):
        out_parts[g] = result.astype(BF)

    def keep_out_right(b, result):
        both = jnp.concatenate([result.astype(BF), out_parts[b]], axis=1)
        r.early_own[pl.ds(b * block, block), 0 : 2 * block] = both

    def keep_mixed(b, result):
        r.grad_mixed_own[pl.ds(b * block, block), :] = result.astype(BF)

    monarch_backward(
        lambda g: r.grad_branch[pl.ds(g * block, block), :],
        lambda b: r.mixed[pl.ds(b * block, block), :],
        r.out_shuffled, r.out_right, r.out_left, r.middle, keep_out_right, keep_out_left, keep_mixed,
    )
    mine = pl.ds(pl.multiple_of(me * rows, rows), rows)
    own_chans = pl.ds(pl.multiple_of(me * chans, 16), chans)
    mixed_copies = []
    for k in SEQ_ORDER:
        other = flip(me, k)
        copy = pltpu.make_async_remote_copy(
            src_ref=r.grad_mixed_own.at[pl.ds(pl.multiple_of(other * chans, 16), chans), :],
            dst_ref=r.grad_mixed.at[:, mine],
            send_sem=r.mixed_send.at[k],
            recv_sem=r.mixed_recv.at[k],
            device_id={"seq": other},
            device_id_type=MESH,
        )
        copy.start()
        mixed_copies.append(copy)
    r.grad_mixed[:, mine] = r.grad_mixed_own[own_chans, :]
    squares[0].start_second()

    glus = []
    for k in range(n_tp):
        other = plane if k == 0 else neighbour_order(plane, n_tp - k)

        def glu_step(at, carry, k=k, other=other):
            cols = pl.ds(pl.multiple_of(at * chunk, chunk), chunk)
            result = dot(r.hidden[other], r.down_v[:, cols])
            if k == 0:
                r.glu_own[:, cols] = result
            else:
                r.glu_send[other, :, cols] = result.astype(BF)
            return carry

        lax.fori_loop(0, pieces, glu_step, 0)
        if k > 0:
            copy = pltpu.make_async_remote_copy(
                src_ref=r.glu_send.at[other],
                dst_ref=r.glu_recv.at[plane],
                send_sem=r.glu_ssem.at[other],
                recv_sem=r.glu_rsem.at[plane],
                device_id={"tp": other},
                device_id_type=MESH,
            )
            copy.start()
            glus.append(copy)
    squares[1].start_second()
    r.sums[...] = jnp.zeros_like(r.sums)
    r.small_own[...] = jnp.zeros_like(r.small_own)
    r.early_own[:, 384:512] = jnp.zeros((width, 128), BF)
    r.padded[pl.ds(chans, 128 - chans), :] = jnp.zeros((128 - chans, length), BF)
    for copy in mixed_copies:
        copy.wait_recv()

    def short_step(at, carry):
        here = pl.ds(pl.multiple_of(at * step, step), step)
        shorted = []
        for s in range(3):
            value = r.signals[s, here, :].astype(F32)
            shorted.append(
                previous(value) * r.columns[here, 3 * s : 3 * s + 1]
                + value * r.columns[here, 3 * s + 1 : 3 * s + 2]
                + following(value) * r.columns[here, 3 * s + 2 : 3 * s + 3]
            )
        r.query[here, :] = shorted[0]
        r.value_v[here, :] = shorted[2]
        above = r.grad_mixed[here, :].astype(F32)
        r.grad_short[1, here, :] = above * r.conv[here, :]
        above = above * shorted[1]
        r.grad_conv[here, :] = above
        r.padded[here, :] = above.astype(BF)
        r.sums[here, 9:10] = jnp.sum(above * shorted[0] * shorted[2], axis=1, keepdims=True)
        r.sums[here, 10:11] = jnp.sum(above * sign_lanes(step, length), axis=1, keepdims=True)
        return carry

    lax.fori_loop(0, chans // step, short_step, 0)
    squares[2].start_second()

    def wave_step(at, carry):
        here = pl.ds(pl.multiple_of(at * chunk, chunk), chunk)
        sign = sign_rows(chunk, 128)
        index = lax.broadcasted_iota(jnp.int32, (chunk, 128), 0) + at * chunk
        weight = jnp.where(index == 0, 0.5 / length, 1.0 / length)
        cos_part = dot(r.table_v[0, here, :], r.padded[...], NT)
        sin_part = dot(r.table_v[1, here, :], r.padded[...], NT)
        tap_cos = r.taps_v[0, here, :].astype(F32)
        tap_sin = r.taps_v[1, here, :].astype(F32)
        r.back_wave[0, here, :] = (cos_part * tap_cos + sin_part * tap_sin).astype(BF)
        r.back_wave[1, here, :] = (sin_part * tap_cos - cos_part * tap_sin).astype(BF)
        wave_cos = r.wave[0, here, :].astype(F32) * weight
        wave_sin = r.wave[1, here, :].astype(F32) * weight
        result = cos_part * wave_cos + sin_part * wave_sin
        r.cross[0, here, 0:128] = result.astype(BF)
        r.cross[0, here, 128:256] = (result * sign).astype(BF)
        result = sin_part * wave_cos - cos_part * wave_sin
        r.cross[1, here, 0:128] = result.astype(BF)
        r.cross[1, here, 128:256] = (result * sign).astype(BF)
        return carry

    lax.fori_loop(0, per, wave_step, 0)
    squares[0].start_second_back()
    squares[1].start_second_back()

    def product_step(at, carry):
        here = pl.ds(pl.multiple_of(at * chunk, chunk), chunk)
        result = dot(r.table_v[0, here, :], r.back_wave[0]) + dot(r.table_v[1, here, :], r.back_wave[1])
        result = (
            result.T[:chans]
            + sign_lanes(chans, chunk) * (r.sums[:chans, 10:11] * r.nyquist[:, 1:2] * (0.5 / length))
            + r.columns[:, 9:10] * r.grad_conv[:, here]
        )
        r.grad_short[0, :, here] = result * r.value_v[:, here]
        r.grad_short[2, :, here] = result * r.query[:, here]
        return carry

    lax.fori_loop(0, per, product_step, 0)
    squares[2].start_second_back()

    def signal_step(at, carry):
        here = pl.ds(pl.multiple_of(at * step, step), step)
        for s in range(3):
            above = r.grad_short[s, here, :]
            value = r.signals[s, here, :].astype(F32)
            before, after = previous(above), following(above)
            r.grad_signals[s, here, :] = (
                after * r.columns[here, 3 * s : 3 * s + 1]
                + above * r.columns[here, 3 * s + 1 : 3 * s + 2]
                + before * r.columns[here, 3 * s + 2 : 3 * s + 3]
            ).astype(BF)
            r.sums[here, 3 * s : 3 * s + 1] = jnp.sum(after * value, axis=1, keepdims=True)
            r.sums[here, 3 * s + 1 : 3 * s + 2] = jnp.sum(above * value, axis=1, keepdims=True)
            r.sums[here, 3 * s + 2 : 3 * s + 3] = jnp.sum(before * value, axis=1, keepdims=True)
        return carry

    lax.fori_loop(0, chans // step, signal_step, 0)
    seq_copies = []
    for k in SEQ_ORDER:
        other = flip(me, k)
        for s in range(3):
            copy = pltpu.make_async_remote_copy(
                src_ref=r.grad_signals.at[s, :, pl.ds(pl.multiple_of(other * rows, rows), rows)],
                dst_ref=r.grad_proj.at[pl.ds(pl.multiple_of(s * width + me * chans, 16), chans), :],
                send_sem=r.seq_send.at[k, s],
                recv_sem=r.seq_recv.at[k, s],
                device_id={"seq": other},
                device_id_type=MESH,
            )
            copy.start()
            seq_copies.append(copy)
    for s in range(3):
        r.grad_proj[pl.ds(pl.multiple_of(s * width + me * chans, 16), chans), :] = r.grad_signals[s, :, mine]
    squares[0].start_first_back()
    squares[1].start_first_back()

    total = r.resid[...] + r.glu_own[...] + from_planes(r.glu_rsem, r.glu_recv)
    r.out_rows[...] = total.astype(BF)
    part = rows // n_tp
    out_copies = []
    for k in range(1, n_tp):
        other = flip(plane, k)
        copy = pltpu.make_async_remote_copy(
            src_ref=r.out_rows.at[pl.ds(pl.multiple_of(other * part, part), part), :],
            dst_ref=r.output_v.at[plane],
            send_sem=r.out_send.at[k],
            recv_sem=r.out_recv.at[k],
            device_id={"tp": other},
            device_id_type=MESH,
        )
        copy.start()
        out_copies.append(copy)
    r.output_v[plane] = r.out_rows[pl.ds(pl.multiple_of(plane * part, part), part), :]

    tap_total = jnp.broadcast_to(r.sums[:, 10:11], (128, 128)).T[0:1, :]
    pad_nyquist = jnp.concatenate([r.nyquist[:, 0:1], jnp.zeros((128 - chans, 1), F32)], axis=0)
    tap_total = tap_total * jnp.broadcast_to(pad_nyquist, (128, 128)).T[0:1, :] * (0.5 / length)
    r.grad_second[...] = jnp.zeros_like(r.grad_second)
    r.grad_first[...] = jnp.zeros_like(r.grad_first)
    r.grad_third[...] = jnp.zeros_like(r.grad_third)

    def filter_step(at, carry):
        here = pl.ds(pl.multiple_of(at * chunk, chunk), chunk)
        result = dot(r.table_v[0, here, :], r.cross[0]) + dot(r.table_v[1, here, :], r.cross[1])
        sign = sign_rows(chunk, 128)
        for half in range(2):
            above = (result[:, half * 128 : (half + 1) * 128] + sign * tap_total) * (length**-0.5)
            if half == 1:
                index = lax.broadcasted_iota(jnp.int32, above.shape, 0) + at * chunk
                above = jnp.where(index == 0, 0.0, above)
            above = above.astype(BF)
            spot = pl.ds(pl.multiple_of(half * length + at * chunk, chunk), chunk)
            r.grad_third[...] += dot(above, r.acts[2, spot, :], TN)
            below = (dot(above, r.third_v[...]) * r.acts[3, spot, :].astype(F32)).astype(BF)
            r.grad_second[...] += dot(r.acts[0, spot, :], below, TN)
            below = (dot(below, r.second[...], NT) * r.acts[1, spot, :].astype(F32)).astype(BF)
            r.grad_first[...] += dot(r.features[spot, :], below, TN)
        return carry

    lax.fori_loop(0, per, filter_step, 0)
    r.early_own[own_chans, 384:512] = r.grad_third[:chans, :].astype(BF)
    r.small_own[0:128, 0:128] = r.grad_second[...].astype(BF)
    r.small_own[128:136, 0:128] = (r.grad_first[0:8, :] + r.grad_first[8:16, :]).astype(BF)
    r.small_own[pl.ds(pl.multiple_of(me * 16, 16), 16), 128:256] = r.sums[...].T[0:16, :].astype(BF)
    early.start_core()
    shifted = tokens - jnp.mean(tokens, axis=-1, keepdims=True)
    inverse = lax.rsqrt(jnp.mean(shifted * shifted, axis=-1, keepdims=True) + 1e-05)
    r.scaled[...] = shifted * inverse
    fan = r.in_left.shape[2]
    for copy in seq_copies:
        copy.wait_recv()
    early.start_chip()

    in_parts = {}

    def keep_left(g, result):
        r.late_own[pl.ds(g * block, block), 0:512] = result[:, 0:512].astype(BF)
        in_parts[g] = result[:, 512:576].astype(BF)

    def keep_right(b, result):
        r.late_own[pl.ds(b * block, block), 512:768] = jnp.concatenate([in_parts[b], result.astype(BF)], axis=1)

    def keep_rows(b, result):
        r.grad_rows[pl.ds(b * block, block), :] = result

    part = block // 4
    for g in range(4):
        below = dot(r.in_left[g], r.grad_proj[pl.ds(g * fan, fan), :]).astype(BF)
        for b in range(4):
            r.middle[pl.ds(b * block + g * part, part), :] = below[b * part : (b + 1) * part]
    for b in range(4):
        keep_rows(b, dot(r.in_right[b], r.middle[pl.ds(b * block, block), :]))
    total = r.grad_rows[...].T
    scaled = r.scaled[...]
    lines = [jnp.sum(total * scaled, axis=0, keepdims=True), jnp.sum(total, axis=0, keepdims=True)]
    total = total * r.gain[...].reshape(1, width)
    first_mean = jnp.mean(total, axis=-1, keepdims=True)
    second_mean = jnp.mean(total * scaled, axis=-1, keepdims=True)
    total = r.grad_resid[...] + inverse * (total - first_mean - scaled * second_mean)
    r.grad_tok[...] = total.astype(BF)
    token_line = Line(n_tp, r.tokens_out, r.tok_send, r.tok_recv)
    token_line.begin(r.grad_tok)
    own_tok = pltpu.make_async_copy(r.grad_tok, r.tokens_out.at[plane], r.local_sems.at[13])
    own_tok.start()
    for g in range(4):
        keep_left(g, dot(r.in_shuffled[pl.ds(g * block, block), :], r.grad_proj[pl.ds(g * fan, fan), :], NT))
    for b in range(4):
        keep_right(b, dot(r.in_normed[pl.ds(b * block, block), :], r.middle[pl.ds(b * block, block), :], NT))
    for late in lates:
        late.start_core()
    squares[2].start_first_back()
    early.start_plane()
    for late in lates:
        late.start_chip()
    lines += [r.grad_vectors[0:1, :], r.grad_vectors[1:2, :]]
    packed = [row[:, at * 128 : (at + 1) * 128] for row in lines for at in range(width // 128)]
    r.small_own[128:160, 128:256] = jnp.concatenate(packed + [jnp.zeros((8, 128), F32)], axis=0).astype(BF)
    small.start_core()
    token_line.take(order[2], inner)
    token_line.take(order[0])
    early.start_plane_back()
    small.start_chip()
    for late in lates:
        late.start_plane()
    small.start_plane()
    early.start_chip_back()
    for square in squares:
        square.start_core_back()
    token_line.take(order[1])
    for late in lates:
        late.start_plane_back()
    small.start_plane_back()
    for late in lates:
        late.start_chip_back()
    small.start_chip_back()
    early.start_core_back()
    token_line.take(order[2], outer)
    ffn_copies = []
    for which, square in enumerate(squares):
        square.arrived()
        copy = pltpu.make_async_copy(r.ffn_v.at[which], r.ffn_out.at[which], r.local_sems.at[14 + which])
        copy.start()
        ffn_copies.append(copy)
    for late in lates:
        late.start_core_back()
    small.start_core_back()
    early.finish()
    r.early_out[...] = r.early_full[...]
    small.finish()
    r.small_out[...] = r.small_full[...]
    for copy in out_copies:
        copy.wait()
    r.output_out[...] = r.output_v[...]
    for late in lates:
        late.finish()
    r.late_out[...] = r.late_full[...]
    for copy in mixed_copies + seq_copies + backs + glus + front_sends + cot_copies:
        copy.wait_send()
    for square in squares:
        square.finish()
    line.finish()
    token_line.finish()
    own_tok.wait()
    for copy in ffn_copies:
        copy.wait()


def core(mesh_shape, *operands):
    n_seq, n_tp = mesh_shape
    tokens = Inputs(*operands).tokens
    _, rows, width = tokens.shape
    chans, length = width // n_seq, rows * n_seq
    scratch, groups = core_scratch(n_seq, n_tp, width, chans, length, rows)
    shape = jax.ShapeDtypeStruct
    return pl.pallas_call(
        functools.partial(core_kernel, n_seq, n_tp, (width, chans, length, rows)),
        out_shape=(
            shape((n_tp, rows // n_tp, width), BF),
            shape((3, width, width), BF),
            shape((n_tp, rows, width), BF),
            shape((width, width), BF),
            shape((width, 512), BF),
            shape((256, 256), BF),
        ),
        in_specs=[vmem_spec()] * 14 + [any_spec()] * (len(Inputs._fields) - 14),
        out_specs=(vmem_spec(), any_spec(), any_spec(), vmem_spec(), vmem_spec(), vmem_spec()),
        scratch_shapes=list(scratch.values()) + sum(groups, []),
        compiler_params=pltpu.CompilerParams(collective_id=0, has_side_effects=True, vmem_limit_bytes=60 * 1024 * 1024),
        name="layer",
    )(*operands)


def finish_kernel(width, chans, *refs):
    (ffn, tokens, late, early, small) = refs[:5]
    (grad_tokens, norm_gain, norm_bias, in_right, in_left, short, first, second, third, conv_bias, out_right, out_left,
     ffn_gain, ffn_bias, gate, up, down) = refs[5:22]
    (ffn_v, ffn_f, token_v, token_f, late_v, early_v, in_right_f, in_left_f, out_right_f, out_left_f, in_sems, out_sems) = refs[22:]
    pairs = [(ffn.at[which], ffn_v.at[which]) for which in range(3)] + [(tokens, token_v), (late, late_v), (early, early_v)]
    loads = [pltpu.make_async_copy(*pair, in_sems.at[at]) for at, pair in enumerate(pairs)]
    for copy in loads:
        copy.start()
    pairs = [(ffn_f.at[which], target) for which, target in enumerate((gate, up, down))]
    pairs += [
        (token_f, grad_tokens), (in_right_f, in_right), (in_left_f, in_left), (out_right_f, out_right), (out_left_f, out_left)
    ]
    stores = [pltpu.make_async_copy(*pair, out_sems.at[at]) for at, pair in enumerate(pairs)]
    chunk = 64
    for which in range(3):
        loads[which].wait()

        def step(at, carry, which=which):
            here = pl.ds(pl.multiple_of(at * chunk, chunk), chunk)
            ffn_f[which, here, :] = ffn_v[which, here, :].astype(F32)
            return carry

        lax.fori_loop(0, width // chunk, step, 0)
        stores[which].start()
    loads[3].wait()

    def token_step(at, carry):
        token_f[at] = token_v[at].astype(F32)
        return carry

    lax.fori_loop(0, token_v.shape[0], token_step, 0)
    stores[3].start()
    groups, block, _ = in_right.shape
    loads[4].wait()
    for b in range(groups):
        here = pl.ds(b * block, block)
        in_left_f[b] = late_v[here, 0 : 3 * block].astype(F32)
        in_right_f[b] = late_v[here, 3 * block : 4 * block].astype(F32)
    stores[4].start()
    stores[5].start()
    loads[5].wait()
    for b in range(groups):
        here = pl.ds(b * block, block)
        out_right_f[b] = early_v[here, 0:block].astype(F32)
        out_left_f[b] = early_v[here, block : 2 * block].astype(F32)
    stores[6].start()
    stores[7].start()
    third[...] = early_v[:, 384:512].astype(F32).T
    values = small[...].astype(F32)
    second[...] = values[0:128, 0:128]
    first[...] = values[128:133, 0:128]
    for at, target in enumerate((norm_gain, norm_bias, ffn_gain, ffn_bias)):
        row = 128 + at * (width // 128)
        target[...] = jnp.concatenate([values[row + k : row + k + 1, 128:256] for k in range(width // 128)], axis=1).reshape(width)
    parts = [values[16 * at : 16 * at + 16, 128 : 128 + chans] for at in range(width // chans)]
    lines = jnp.concatenate(parts, axis=1)
    for s in range(3):
        short[s] = lines[3 * s : 3 * s + 3]
    conv_bias[...] = lines[9:10].reshape(width)
    for copy in stores:
        copy.wait()


def finish(chans, ffn, tokens, late, early, small):
    width = ffn.shape[1]
    block = width // 4
    shape = jax.ShapeDtypeStruct
    vector = shape((width,), F32)
    square = shape((4, block, block), F32)
    wide = shape((4, block, 3 * block), F32)
    return pl.pallas_call(
        functools.partial(finish_kernel, width, chans),
        out_shape=(
            shape(tokens.shape, F32), vector, vector, square, wide, shape((3, 3, width), F32),
            shape((5, 128), F32), shape((128, 128), F32), shape((128, width), F32), vector, square, square, vector, vector,
        )
        + (shape((width, width), F32),) * 3,
        in_specs=[any_spec()] * 4 + [vmem_spec()],
        out_specs=(any_spec(), vmem_spec(), vmem_spec(), any_spec(), any_spec())
        + (vmem_spec(),) * 5
        + (any_spec(), any_spec(), vmem_spec(), vmem_spec())
        + (any_spec(),) * 3,
        scratch_shapes=[
            pltpu.VMEM(ffn.shape, BF),
            pltpu.VMEM(ffn.shape, F32),
            pltpu.VMEM(tokens.shape, BF),
            pltpu.VMEM(tokens.shape, F32),
            pltpu.VMEM(late.shape, BF),
            pltpu.VMEM(early.shape, BF),
            pltpu.VMEM(square.shape, F32),
            pltpu.VMEM(wide.shape, F32),
            pltpu.VMEM(square.shape, F32),
            pltpu.VMEM(square.shape, F32),
            pltpu.SemaphoreType.DMA((6,)),
            pltpu.SemaphoreType.DMA((8,)),
        ],
        compiler_params=pltpu.CompilerParams(vmem_limit_bytes=LIMIT),
        name="finish",
    )(ffn, tokens, late, early, small)


def fast_body(
    tokens,
    norm_gain,
    norm_bias,
    in_right,
    in_left,
    short_kernel,
    filter_first,
    filter_second,
    filter_third,
    conv_bias,
    out_right,
    out_left,
    ffn_gain,
    ffn_bias,
    gate_weight,
    up_weight,
    down_weight,
    cotangent,
):
    n_seq, n_tp = lax.axis_size("seq"), lax.axis_size("tp")
    _, rows, width = tokens.shape
    chans, length = width // n_seq, rows * n_seq
    shape = (n_seq, n_tp)
    table, features = (jnp.asarray(array) for array in constants(length))
    output, ffn, grad_tokens, late, early, small = core(
        shape, ffn_gain, ffn_bias, out_right, out_left, norm_gain, norm_bias, in_right, in_left, short_kernel.transpose(0, 2, 1),
        conv_bias, features, filter_first, filter_second, filter_third, tokens, cotangent, table, gate_weight, up_weight,
        down_weight,
    )
    grads = finish(chans, ffn, grad_tokens, late, early, small)
    return (output,) + grads[:5] + (grads[5].transpose(0, 2, 1),) + grads[6:]


highest = lax.Precision.HIGHEST


def norm_forward(values, gain, bias):
    centre = jnp.mean(values, axis=-1, keepdims=True)
    shifted = values - centre
    inverse = lax.rsqrt(jnp.mean(shifted * shifted, axis=-1, keepdims=True) + 1e-05)
    scaled = shifted * inverse
    return (scaled * gain + bias, scaled, inverse)


def norm_backward(upstream, scaled, inverse, gain):
    weighted = upstream * gain
    first_mean = jnp.mean(weighted, axis=-1, keepdims=True)
    second_mean = jnp.mean(weighted * scaled, axis=-1, keepdims=True)
    grad_input = inverse * (weighted - first_mean - scaled * second_mean)
    breadth = upstream.shape[-1]
    grad_gain = jnp.sum((upstream * scaled).reshape(-1, breadth), axis=0)
    grad_bias = jnp.sum(upstream.reshape(-1, breadth), axis=0)
    return (grad_input, grad_gain, grad_bias)


def shuffle(blocked):
    row_count, groups, breadth = blocked.shape
    return (
        blocked.reshape(row_count, groups, groups, breadth // groups)
        .transpose(0, 2, 1, 3)
        .reshape(row_count, groups, breadth)
    )


def rows_monarch_forward(operand, right_factor, left_factor):
    row_count = operand.shape[0]
    groups = right_factor.shape[0]
    blocked = operand.reshape(row_count, groups, -1)
    middle = jnp.einsum(
        "tbi,bij->tbj", blocked, right_factor, preferred_element_type=jnp.float32
    ).astype(jnp.bfloat16)
    shuffled = shuffle(middle)
    result = jnp.einsum("tbi,bij->tbj", shuffled, left_factor, preferred_element_type=jnp.float32)
    return (shuffled, result.reshape(row_count, -1))


def rows_monarch_backward(grad_result, operand, shuffled, right_factor, left_factor):
    row_count = operand.shape[0]
    groups = right_factor.shape[0]
    grad_blocked = grad_result.reshape(row_count, groups, -1)
    grad_left = jnp.einsum(
        "tbi,tbj->bij", shuffled, grad_blocked, preferred_element_type=jnp.float32
    )
    grad_shuffled = jnp.einsum(
        "tbj,bij->tbi", grad_blocked, left_factor, preferred_element_type=jnp.float32
    )
    grad_middle = shuffle(grad_shuffled).astype(jnp.bfloat16)
    blocked = operand.reshape(row_count, groups, -1)
    grad_right = jnp.einsum(
        "tbi,tbj->bij", blocked, grad_middle, preferred_element_type=jnp.float32
    )
    grad_operand = jnp.einsum(
        "tbj,bij->tbi", grad_middle, right_factor, preferred_element_type=jnp.float32
    )
    return (grad_operand.reshape(row_count, -1), grad_right, grad_left)


def roots(row_count, col_count, period):
    product = jnp.arange(row_count)[:, None] * jnp.arange(col_count)[None, :] % period
    angle = product.astype(jnp.float32) * (2.0 * math.pi / period)
    return (jnp.cos(angle), jnp.sin(angle))


def complex_step(real_part, imag_part, cos_table, sin_table, sign, form):
    real_out = jnp.einsum(form, real_part, cos_table, precision=highest) - sign * jnp.einsum(
        form, imag_part, sin_table, precision=highest
    )
    imag_out = jnp.einsum(form, imag_part, cos_table, precision=highest) + sign * jnp.einsum(
        form, real_part, sin_table, precision=highest
    )
    return (real_out, imag_out)


def real_step(real_part, cos_table, sin_table, sign, form):
    real_out = jnp.einsum(form, real_part, cos_table, precision=highest)
    imag_out = sign * jnp.einsum(form, real_part, sin_table, precision=highest)
    return (real_out, imag_out)


def twiddle(real_part, imag_part, cos_table, sin_table, sign):
    real_out = real_part * cos_table - sign * imag_part * sin_table
    imag_out = imag_part * cos_table + sign * real_part * sin_table
    return (real_out, imag_out)


def spectrum_of(real_part):
    total = real_part.shape[-1]
    first = math.gcd(total, 128)
    second = total // first
    leading = real_part.shape[:-1]
    real_part = real_part.reshape(leading + (first, second))
    cos_first, sin_first = roots(first, first, first)
    real_part, imag_part = real_step(real_part, cos_first, sin_first, -1.0, "...ab,ak->...kb")
    cos_twist, sin_twist = roots(first, second, total)
    real_part, imag_part = twiddle(real_part, imag_part, cos_twist, sin_twist, -1.0)
    cos_second, sin_second = roots(second, second, second)
    return complex_step(real_part, imag_part, cos_second, sin_second, -1.0, "...kb,bm->...km")


def signal_of(real_part, imag_part):
    first = real_part.shape[-2]
    second = real_part.shape[-1]
    total = first * second
    leading = real_part.shape[:-2]
    cos_second, sin_second = roots(second, second, second)
    real_part, imag_part = complex_step(
        real_part, imag_part, cos_second, sin_second, 1.0, "...kb,bm->...km"
    )
    cos_twist, sin_twist = roots(first, second, total)
    real_part, imag_part = twiddle(real_part, imag_part, cos_twist, sin_twist, 1.0)
    cos_first, sin_first = roots(first, first, first)
    real_part, imag_part = complex_step(
        real_part, imag_part, cos_first, sin_first, 1.0, "...ab,ak->...kb"
    )
    return real_part.reshape(leading + (total,)) / total


def filter_parts(filter_first, filter_second, third_cols, seq_length):
    total = 2 * seq_length
    index = jnp.arange(total)
    offset = jnp.where(index < seq_length, index, index - total).astype(jnp.float32)
    scaled = offset / seq_length
    features = jnp.stack(
        [
            scaled,
            jnp.sin(math.pi * scaled),
            jnp.cos(math.pi * scaled),
            jnp.sin(7.0 * math.pi * scaled),
            jnp.cos(7.0 * math.pi * scaled),
        ],
        axis=1,
    )
    pre_one = jnp.dot(features, filter_first, precision=highest)
    act_one = jnp.sin(pre_one)
    pre_two = jnp.dot(act_one, filter_second, precision=highest)
    act_two = jnp.sin(pre_two)
    tap_mask = (index != seq_length).astype(jnp.float32)[:, None] * seq_length ** (-0.5)
    taps = jnp.dot(act_two, third_cols, precision=highest) * tap_mask
    filt_real, filt_imag = spectrum_of(taps.T)
    return (features, pre_one, act_one, pre_two, act_two, tap_mask, filt_real, filt_imag)


def general_body(
    tokens,
    norm_gain,
    norm_bias,
    in_right,
    in_left,
    short_kernel,
    filter_first,
    filter_second,
    filter_third,
    conv_bias,
    out_right,
    out_left,
    ffn_gain,
    ffn_bias,
    gate_weight,
    up_weight,
    down_weight,
    cotangent,
):
    seq_count, pos_count, model_width = tokens.shape
    row_count = seq_count * pos_count
    axis_count = lax.axis_size("seq")
    my_index = lax.axis_index("seq")
    chan_count = model_width // axis_count
    seq_length = pos_count * axis_count
    part_rows = cotangent.shape[1]
    tp_index = lax.axis_index("tp")
    tp_count = lax.axis_size("tp")
    chan_start = my_index * chan_count
    mix_count = seq_count // tp_count
    mix_tokens = lax.dynamic_slice_in_dim(tokens, tp_index * mix_count, mix_count, 0)
    mix_rows = mix_count * pos_count
    flat = mix_tokens.reshape(mix_rows, model_width).astype(jnp.float32)
    normed, scaled_one, inverse_one = norm_forward(flat, norm_gain, norm_bias)
    normed_low = normed.astype(jnp.bfloat16)
    shuffled_in, projected = rows_monarch_forward(normed_low, in_right, in_left)
    projected_low = (
        projected.astype(jnp.bfloat16)
        .reshape(mix_count, pos_count, 3, model_width)
        .transpose(2, 3, 0, 1)
    )
    channels = lax.all_to_all(projected_low, "seq", split_axis=1, concat_axis=3, tiled=True)
    signals = channels.astype(jnp.float32)
    kernel = lax.dynamic_slice_in_dim(short_kernel, chan_start, chan_count, 1).astype(jnp.float32)
    tap_zero = kernel[:, :, 0][:, :, None, None]
    tap_one = kernel[:, :, 1][:, :, None, None]
    tap_two = kernel[:, :, 2][:, :, None, None]
    padded = jnp.pad(signals, ((0, 0), (0, 0), (0, 0), (1, 1)))
    shorted = padded[..., :-2] * tap_zero + padded[..., 1:-1] * tap_one + padded[..., 2:] * tap_two
    first_f = filter_first.astype(jnp.float32)
    second_f = filter_second.astype(jnp.float32)
    third_cols = lax.dynamic_slice_in_dim(filter_third, chan_start, chan_count, 1).astype(
        jnp.float32
    )
    kept = filter_parts(first_f, second_f, third_cols, seq_length)
    filt_real = kept[6][:, None]
    filt_imag = kept[7][:, None]
    bias_cols = lax.dynamic_slice_in_dim(conv_bias, chan_start, chan_count, 0)[:, None, None]
    product = shorted[0] * shorted[2]
    product_pad = jnp.pad(product, ((0, 0), (0, 0), (0, seq_length)))
    spec_real, spec_imag = spectrum_of(product_pad)
    conv_real = spec_real * filt_real - spec_imag * filt_imag
    conv_imag = spec_real * filt_imag + spec_imag * filt_real
    convolved = signal_of(conv_real, conv_imag)[..., :seq_length] + bias_cols * product
    mixed_low = (shorted[1] * convolved).astype(jnp.bfloat16)
    back_rows = lax.all_to_all(mixed_low, "seq", split_axis=2, concat_axis=0, tiled=True)
    mixed_rows = back_rows.transpose(1, 2, 0).reshape(mix_rows, model_width)
    shuffled_out, branch = rows_monarch_forward(mixed_rows, out_right, out_left)
    residual_mine = (flat + branch).reshape(mix_count, pos_count, model_width)
    residual = lax.all_gather(residual_mine, "tp", axis=0, tiled=True)
    part_resid = lax.dynamic_slice_in_dim(residual, tp_index * part_rows, part_rows, 1)
    normed_two, scaled_two, inverse_two = norm_forward(part_resid, ffn_gain, ffn_bias)
    normed_rows = lax.all_gather(normed_two.astype(jnp.bfloat16), "tp", axis=1, tiled=True).reshape(
        row_count, model_width
    )
    gate = jnp.dot(normed_rows, gate_weight, preferred_element_type=jnp.float32)
    upward = jnp.dot(normed_rows, up_weight, preferred_element_type=jnp.float32)
    sigma = jax.nn.sigmoid(gate)
    hidden_low = (gate * sigma * upward).astype(jnp.bfloat16)
    partial_down = jnp.dot(hidden_low, down_weight, preferred_element_type=jnp.float32).reshape(
        seq_count, pos_count, model_width
    )
    glu_part = lax.psum_scatter(
        partial_down.astype(jnp.bfloat16), "tp", scatter_dimension=1, tiled=True
    ).astype(jnp.float32)
    output = (part_resid + glu_part).astype(jnp.bfloat16)
    grad_out_rows = lax.all_gather(cotangent, "tp", axis=1, tiled=True).reshape(
        row_count, model_width
    )
    grad_hidden = jnp.dot(grad_out_rows, down_weight.T, preferred_element_type=jnp.float32)
    grad_gate = (grad_hidden * upward * (sigma + gate * sigma * (1.0 - sigma))).astype(jnp.bfloat16)
    grad_up = (grad_hidden * gate * sigma).astype(jnp.bfloat16)
    grad_down_w = jnp.dot(hidden_low.T, grad_out_rows, preferred_element_type=jnp.float32)
    grad_gate_w = jnp.dot(normed_rows.T, grad_gate, preferred_element_type=jnp.float32)
    grad_up_w = jnp.dot(normed_rows.T, grad_up, preferred_element_type=jnp.float32)
    grad_normed = jnp.dot(grad_gate, gate_weight.T, preferred_element_type=jnp.float32) + jnp.dot(
        grad_up, up_weight.T, preferred_element_type=jnp.float32
    )
    grad_normed_part = lax.psum_scatter(
        grad_normed.reshape(seq_count, pos_count, model_width),
        "tp",
        scatter_dimension=1,
        tiled=True,
    )
    grad_in_two, grad_gain_two, grad_bias_two = norm_backward(
        grad_normed_part, scaled_two, inverse_two, ffn_gain
    )
    gain_total = lax.psum((grad_gain_two, grad_bias_two), ("seq", "tp"))
    grad_resid_part = cotangent.astype(jnp.float32) + grad_in_two
    grad_resid = lax.all_gather(
        grad_resid_part.astype(jnp.bfloat16), "tp", axis=1, tiled=True
    ).astype(grad_resid_part.dtype)
    grad_resid_mix = lax.dynamic_slice_in_dim(
        grad_resid, tp_index * mix_count, mix_count, 0
    ).reshape(mix_rows, model_width)
    grad_mixed_rows, grad_out_right, grad_out_left = rows_monarch_backward(
        grad_resid_mix.astype(jnp.bfloat16), mixed_rows, shuffled_out, out_right, out_left
    )
    grad_mixed_low = (
        grad_mixed_rows.astype(jnp.bfloat16)
        .reshape(mix_count, pos_count, model_width)
        .transpose(2, 0, 1)
    )
    grad_mixed = lax.all_to_all(
        grad_mixed_low, "seq", split_axis=0, concat_axis=2, tiled=True
    ).astype(jnp.float32)
    grad_conv = grad_mixed * shorted[1]
    grad_key = grad_mixed * convolved
    again = lax.optimization_barrier((first_f, second_f, third_cols))
    kept = filter_parts(again[0], again[1], again[2], seq_length)
    filt_real = kept[6][:, None]
    filt_imag = kept[7][:, None]
    features, pre_one, act_one, pre_two, act_two, tap_mask = (
        kept[0],
        kept[1],
        kept[2],
        kept[3],
        kept[4],
        kept[5],
    )
    grad_pad = jnp.pad(grad_conv, ((0, 0), (0, 0), (0, seq_length)))
    grad_spec_real, grad_spec_imag = spectrum_of(grad_pad)
    back_real = grad_spec_real * filt_real + grad_spec_imag * filt_imag
    back_imag = grad_spec_imag * filt_real - grad_spec_real * filt_imag
    grad_product = signal_of(back_real, back_imag)[..., :seq_length] + bias_cols * grad_conv
    grad_bias_cols = jnp.sum(grad_conv * product, axis=(1, 2))
    taps_real = jnp.sum(grad_spec_real * spec_real + grad_spec_imag * spec_imag, axis=1)
    taps_imag = jnp.sum(grad_spec_imag * spec_real - grad_spec_real * spec_imag, axis=1)
    grad_taps = signal_of(taps_real, taps_imag)
    grad_pre = grad_taps.T * tap_mask
    grad_third_cols = jnp.dot(act_two.T, grad_pre, precision=highest)
    grad_pre_two = jnp.dot(grad_pre, third_cols.T, precision=highest) * jnp.cos(pre_two)
    grad_second = jnp.dot(act_one.T, grad_pre_two, precision=highest)
    grad_pre_one = jnp.dot(grad_pre_two, second_f.T, precision=highest) * jnp.cos(pre_one)
    grad_first = jnp.dot(features.T, grad_pre_one, precision=highest)
    grad_shorted = jnp.stack([grad_product * shorted[2], grad_key, grad_product * shorted[0]])
    grad_short_pad = jnp.pad(grad_shorted, ((0, 0), (0, 0), (0, 0), (1, 1)))
    grad_signals = (
        grad_short_pad[..., 2:] * tap_zero
        + grad_short_pad[..., 1:-1] * tap_one
        + grad_short_pad[..., :-2] * tap_two
    )
    grad_kernel = jnp.stack(
        [
            jnp.sum(grad_shorted * padded[..., :-2], axis=(2, 3)),
            jnp.sum(grad_shorted * padded[..., 1:-1], axis=(2, 3)),
            jnp.sum(grad_shorted * padded[..., 2:], axis=(2, 3)),
        ],
        axis=-1,
    )
    grad_proj = lax.all_to_all(
        grad_signals.astype(jnp.bfloat16), "seq", split_axis=3, concat_axis=1, tiled=True
    )
    grad_proj_rows = grad_proj.transpose(2, 3, 0, 1).reshape(mix_rows, 3 * model_width)
    grad_normed_one, grad_in_right, grad_in_left = rows_monarch_backward(
        grad_proj_rows, normed_low, shuffled_in, in_right, in_left
    )
    grad_in_one, grad_gain_one, grad_bias_one = norm_backward(
        grad_normed_one, scaled_one, inverse_one, norm_gain
    )
    grad_mine = (grad_resid_mix + grad_in_one).reshape(mix_count, pos_count, model_width)
    short_full = lax.dynamic_update_slice_in_dim(
        jnp.zeros(short_kernel.shape, jnp.float32), grad_kernel, chan_start, 1
    )
    third_full = lax.dynamic_update_slice_in_dim(
        jnp.zeros(filter_third.shape, jnp.float32), grad_third_cols, chan_start, 1
    )
    bias_full = lax.dynamic_update_slice_in_dim(
        jnp.zeros(conv_bias.shape, jnp.float32), grad_bias_cols, chan_start, 0
    )
    mixer_grads = (
        grad_gain_one,
        grad_bias_one,
        grad_in_right,
        grad_in_left,
        short_full,
        grad_first,
        grad_second,
        third_full,
        bias_full,
        grad_out_right,
        grad_out_left,
    )
    grad_tokens = lax.all_gather(grad_mine.astype(jnp.bfloat16), "tp", axis=0, tiled=True).astype(
        grad_mine.dtype
    )
    mixer_grads = (
        lax.psum(mixer_grads[0].astype(jnp.bfloat16), "tp").astype(jnp.float32),
        lax.psum(mixer_grads[1].astype(jnp.bfloat16), "tp").astype(jnp.float32),
        lax.psum(mixer_grads[2].astype(jnp.bfloat16), "tp").astype(jnp.float32),
        lax.psum(mixer_grads[3].astype(jnp.bfloat16), "tp").astype(jnp.float32),
        lax.psum(mixer_grads[4].astype(jnp.bfloat16), "tp").astype(jnp.float32),
        lax.psum(mixer_grads[5].astype(jnp.bfloat16), "tp").astype(jnp.float32),
        lax.psum(mixer_grads[6].astype(jnp.bfloat16), "tp").astype(jnp.float32),
        lax.psum(mixer_grads[7].astype(jnp.bfloat16), "tp").astype(jnp.float32),
        lax.psum(mixer_grads[8].astype(jnp.bfloat16), "tp").astype(jnp.float32),
        lax.psum(mixer_grads[9].astype(jnp.bfloat16), "tp").astype(jnp.float32),
        lax.psum(mixer_grads[10].astype(jnp.bfloat16), "tp").astype(jnp.float32),
    )
    all_total = lax.psum(
        (
            mixer_grads[0],
            mixer_grads[1],
            mixer_grads[2],
            mixer_grads[3],
            mixer_grads[4],
            mixer_grads[5],
            mixer_grads[6],
            mixer_grads[7],
            mixer_grads[8],
            mixer_grads[9],
            mixer_grads[10],
            grad_gate_w,
            grad_up_w,
            grad_down_w,
        ),
        "seq",
    )
    return (
        output,
        grad_tokens,
        all_total[0],
        all_total[1],
        all_total[2],
        all_total[3],
        all_total[4],
        all_total[5],
        all_total[6],
        all_total[7],
        all_total[8],
        all_total[9],
        all_total[10],
        gain_total[0],
        gain_total[1],
        all_total[11],
        all_total[12],
        all_total[13],
    )


def choose_body(mesh, *arrays):
    tokens = arrays[0]
    chans = tokens.shape[2] // mesh.shape["seq"]
    fits = mesh.shape["seq"] == 8 and mesh.shape["tp"] == 4 and tokens.shape[:2] == (4, 128) and chans == 96
    return (fast_body if fits else general_body)(*arrays)


def solution(mesh):
    mapped = jax.shard_map(
        functools.partial(choose_body, mesh),
        mesh=mesh,
        in_specs=(
            P(None, "seq", None),
            P(),
            P(),
            P(),
            P(),
            P(),
            P(),
            P(),
            P(),
            P(),
            P(),
            P(),
            P(),
            P(),
            P(None, "tp"),
            P(None, "tp"),
            P("tp", None),
            P(None, ("seq", "tp"), None),
        ),
        out_specs=(
            P(None, ("seq", "tp"), None),
            P(None, "seq", None),
            P(),
            P(),
            P(),
            P(),
            P(),
            P(),
            P(),
            P(),
            P(),
            P(),
            P(),
            P(),
            P(),
            P(None, "tp"),
            P(None, "tp"),
            P("tp", None),
        ),
        check_vma=False,
    )

    def program(*arrays):
        with jax.sharding.use_abstract_mesh(mesh.abstract_mesh):
            return mapped(*arrays)

    return program
```

```python
import functools
import math
import types
import typing

import numpy as np
import jax
import jax.numpy as jnp
from jax import lax
from jax.experimental import pallas as pl
from jax.experimental.pallas import tpu as pltpu
from jax.sharding import PartitionSpec as P

BF = jnp.bfloat16
F32 = jnp.float32
MESH = pl.DeviceIdType.MESH
NN = ((1,), (0,))
NT = ((1,), (1,))
TN = ((0,), (0,))
LIMIT = 56 * 1024 * 1024


def dot(first, second, form=NN):
    return lax.dot_general(first, second, (form, ((), ())), preferred_element_type=F32)


def any_spec():
    return pl.BlockSpec(memory_space=pl.ANY)


def vmem_spec():
    return pl.BlockSpec(memory_space=pltpu.VMEM)


def sin_cos(value):
    turns = jnp.floor(value * (1.0 / math.pi) + 0.5)
    rest = value - turns * 3.140625
    rest = rest - turns * 9.67502593994140625e-4
    rest = rest - turns * 1.509957990978376432e-7
    half = turns * 0.5
    sign = 1.0 - 4.0 * (half - jnp.floor(half))
    square = rest * rest
    sine = 1.0 / 362880 - square * (1.0 / 39916800)
    sine = -1.0 / 5040 + square * sine
    sine = 1.0 / 120 + square * sine
    sine = -1.0 / 6 + square * sine
    sine = rest + rest * square * sine
    cosine = 1.0 / 40320 - square * (1.0 / 3628800 - square * (1.0 / 479001600))
    cosine = -1.0 / 720 + square * cosine
    cosine = 1.0 / 24 + square * cosine
    cosine = -0.5 + square * cosine
    cosine = 1.0 + square * cosine
    return sign * sine, sign * cosine


def flip(index, bits):
    result = 0
    for place in range(3):
        digit = lax.rem(index // (1 << place), 2)
        if (bits >> place) & 1:
            digit = 1 - digit
        result = result + digit * (1 << place)
    return result


def greet(n_seq, n_tp):
    me, plane = lax.axis_index("seq"), lax.axis_index("tp")
    barrier = pltpu.get_barrier_semaphore()
    for k in range(1, n_seq):
        pl.semaphore_signal(barrier, inc=1, device_id={"seq": flip(me, k)}, device_id_type=MESH)
    for k in range(1, n_tp):
        pl.semaphore_signal(barrier, inc=1, device_id={"tp": flip(plane, k)}, device_id_type=MESH)
    return lambda: pl.semaphore_wait(barrier, n_seq + n_tp - 2)


def sign_rows(count, width):
    row = lax.broadcasted_iota(jnp.int32, (count, width), 0)
    return (1 - 2 * lax.rem(row, 2)).astype(F32)


def sign_lanes(count, width):
    lane = lax.broadcasted_iota(jnp.int32, (count, width), 1)
    return (1 - 2 * lax.rem(lane, 2)).astype(F32)


def previous(values):
    lane = lax.broadcasted_iota(jnp.int32, values.shape, 1)
    return jnp.where(lane == 0, 0.0, pltpu.roll(values, 1, 1))


def following(values):
    last = values.shape[1] - 1
    lane = lax.broadcasted_iota(jnp.int32, values.shape, 1)
    return jnp.where(lane == last, 0.0, pltpu.roll(values, last, 1))


def monarch_forward(load, right, left, shuffled, store):
    groups, width, _ = right.shape
    part = width // groups
    for b in range(groups):
        middle = dot(right[b], load(b), TN).astype(BF)
        for g in range(groups):
            shuffled[pl.ds(g * width + b * part, part), :] = middle[g * part : (g + 1) * part]
    for g in range(groups):
        store(g, dot(left[g], shuffled[pl.ds(g * width, width), :], TN))


SEQ_ORDER = (6, 7, 2, 3, 4, 5, 1)


def front_part(n_seq, n_tp, dims, r, entered, loads):
    width, chans, length, rows = dims
    me, plane = lax.axis_index("seq"), lax.axis_index("tp")
    cotangent, right, left, features = r.cotangent, r.in_right, r.in_left, r.features
    token_v, table_v, normed, shuffled, signals = r.token_v, r.table_v, r.in_normed, r.in_shuffled, r.signals
    acts, taps_v, padded, wave, conv, nyquist, columns, third_v = (
        r.acts, r.taps_v, r.padded, r.wave, r.conv, r.nyquist, r.columns, r.third_v
    )
    projected, spread, product, keyed, spectrum, mixed, totals = (
        r.projected, r.spread, r.product, r.query, r.back_wave, r.front_mixed, r.totals
    )
    loads.token.wait()
    value = token_v[...].astype(F32)
    shifted = value - jnp.mean(value, axis=-1, keepdims=True)
    inverse = lax.rsqrt(jnp.mean(shifted * shifted, axis=-1, keepdims=True) + 1e-05)
    value = shifted * inverse * r.gain[...].reshape(1, width) + r.bias[...].reshape(1, width)
    normed[...] = value.T.astype(BF)
    groups = right.shape[0]
    block = width // groups
    fan = left.shape[2]

    def keep(g, result):
        projected[pl.ds(g * fan, fan), :] = result.astype(BF)

    monarch_forward(lambda b: normed[pl.ds(b * block, block), :], right, left, shuffled, keep)
    entered()
    sends = []
    mine = pl.ds(pl.multiple_of(me * rows, rows), rows)
    for k in SEQ_ORDER:
        other = flip(me, k)
        for s in range(3):
            copy = pltpu.make_async_remote_copy(
                src_ref=projected.at[pl.ds(pl.multiple_of(s * width + other * chans, 16), chans), :],
                dst_ref=signals.at[s, :, mine],
                send_sem=r.front_send.at[k, s],
                recv_sem=r.front_recv.at[k, s],
                device_id={"seq": other},
                device_id_type=MESH,
            )
            copy.start()
            sends.append(copy)
    for s in range(3):
        signals[s, :, mine] = projected[pl.ds(pl.multiple_of(s * width + me * chans, 16), chans), :]
    part = rows // n_tp
    spot = pl.ds(pl.multiple_of(plane * part, part), part)
    cot_copies = []
    for k in range(1, n_tp):
        copy = pltpu.make_async_remote_copy(
            src_ref=cotangent,
            dst_ref=r.cot_v.at[:, spot, :],
            send_sem=r.cot_send.at[k],
            recv_sem=r.cot_recv.at[k],
            device_id={"tp": flip(plane, k)},
            device_id_type=MESH,
        )
        copy.start()
        cot_copies.append(copy)
    own_cot = pltpu.make_async_copy(cotangent, r.cot_v.at[:, spot, :], r.local_sems.at[17])
    own_cot.start()

    own = pl.ds(pl.multiple_of(me * chans, 16), chans)
    lines = [r.short[s].astype(F32) for s in range(3)]
    lines += [r.conv_bias[...].reshape(1, width), jnp.zeros((6, width), F32)]
    r.tall[...] = jnp.concatenate(lines, axis=0).T
    columns[...] = r.tall[own, :]
    r.third_turned[...] = r.third[...].T
    third_v[pl.ds(0, chans), :] = r.third_turned[own, :]
    third_v[pl.ds(chans, 128 - chans), :] = jnp.zeros((128 - chans, 128), BF)
    lead = jnp.concatenate([r.first[...].astype(F32), jnp.zeros((3, 128), F32)], axis=0)
    lead = jnp.concatenate([lead, lead], axis=0).astype(BF)

    chunk = 256
    per = length // chunk
    totals[...] = jnp.zeros_like(totals)
    for half in range(2):

        def tap_step(at, carry, half=half):
            row = pl.multiple_of(half * length + at * chunk, chunk)
            here = pl.ds(row, chunk)
            sine, cosine = sin_cos(dot(features[here, :], lead))
            high = sine.astype(BF)
            acts[0, here, :] = high
            acts[1, here, :] = cosine.astype(BF)
            low = (sine - high.astype(F32)).astype(BF)
            sine, cosine = sin_cos(dot(high, r.second[...]) + dot(low, r.second[...]))
            high = sine.astype(BF)
            acts[2, here, :] = high
            acts[3, here, :] = cosine.astype(BF)
            taps = dot(high, third_v[...], NT) * (length**-0.5)
            if half == 1:
                index = lax.broadcasted_iota(jnp.int32, taps.shape, 0) + at * chunk
                taps = jnp.where(index == 0, 0.0, taps)
            totals[...] += jnp.sum(taps * sign_rows(*taps.shape), axis=0, keepdims=True)
            spread[pl.ds(pl.multiple_of(at * chunk, chunk), chunk), pl.ds(half * 128, 128)] = taps.astype(BF)
            return carry

        lax.fori_loop(0, per, tap_step, 0)
    loads.table.wait()

    def spectrum_step(at, carry):
        here = pl.ds(pl.multiple_of(at * chunk, chunk), chunk)
        sign = sign_rows(chunk, 128)
        index = lax.broadcasted_iota(jnp.int32, (chunk, 128), 0) + at * chunk
        weight = jnp.where(index == 0, 0.5 / length, 1.0 / length)
        for which in range(2):
            result = dot(table_v[which, here, :], spread[...])
            taps_v[which, here, :] = ((result[:, :128] + sign * result[:, 128:]) * weight).astype(BF)
        return carry

    lax.fori_loop(0, per, spectrum_step, 0)
    tap_total = jnp.broadcast_to(totals[...], (128, 128)).T[:chans, 0:1]

    for copy in sends:
        copy.wait_recv()

    step = 16
    padded[pl.ds(chans, 128 - chans), :] = jnp.zeros((128 - chans, length), BF)

    def short_step(at, carry):
        here = pl.ds(pl.multiple_of(at * step, step), step)
        shorted = []
        for s in range(3):
            value = signals[s, here, :].astype(F32)
            shorted.append(
                previous(value) * columns[here, 3 * s : 3 * s + 1]
                + value * columns[here, 3 * s + 1 : 3 * s + 2]
                + following(value) * columns[here, 3 * s + 2 : 3 * s + 3]
            )
        result = shorted[0] * shorted[2]
        product[here, :] = result
        keyed[here, :] = shorted[1]
        padded[here, :] = result.astype(BF)
        nyquist[here, 0:1] = jnp.sum(result * sign_lanes(step, length), axis=1, keepdims=True)
        return carry

    lax.fori_loop(0, chans // step, short_step, 0)
    nyquist[:, 1:2] = tap_total

    def wave_step(at, carry):
        here = pl.ds(pl.multiple_of(at * chunk, chunk), chunk)
        cos_part = dot(table_v[0, here, :], padded[...], NT)
        sin_part = dot(table_v[1, here, :], padded[...], NT)
        wave[0, here, :] = cos_part.astype(BF)
        wave[1, here, :] = sin_part.astype(BF)
        tap_cos = taps_v[0, here, :].astype(F32)
        tap_sin = taps_v[1, here, :].astype(F32)
        spectrum[0, here, :] = (cos_part * tap_cos - sin_part * tap_sin).astype(BF)
        spectrum[1, here, :] = (cos_part * tap_sin + sin_part * tap_cos).astype(BF)
        return carry

    lax.fori_loop(0, per, wave_step, 0)

    def conv_step(at, carry):
        here = pl.ds(pl.multiple_of(at * chunk, chunk), chunk)
        result = dot(table_v[0, here, :], spectrum[0]) + dot(table_v[1, here, :], spectrum[1])
        result = result.T[:chans]
        result = (
            result
            + sign_lanes(chans, chunk) * (nyquist[:, 0:1] * nyquist[:, 1:2] * (0.5 / length))
            + columns[:, 9:10] * product[:, here]
        )
        conv[:, here] = result
        mixed[:, here] = (keyed[:, here] * result).astype(BF)
        return carry

    lax.fori_loop(0, per, conv_step, 0)
    backs = []
    slot = pl.ds(pl.multiple_of(me * chans, 16), chans)
    for k in SEQ_ORDER:
        other = flip(me, k)
        copy = pltpu.make_async_remote_copy(
            src_ref=mixed.at[:, pl.ds(pl.multiple_of(other * rows, rows), rows)],
            dst_ref=r.mixed.at[slot, :],
            send_sem=r.mix_send.at[k],
            recv_sem=r.mix_recv.at[k],
            device_id={"seq": other},
            device_id_type=MESH,
        )
        copy.start()
        backs.append(copy)
    r.mixed[slot, :] = mixed[:, mine]
    for copy in backs:
        copy.wait_recv()
    return sends + backs, cot_copies, own_cot


def split_table(values):
    high = values.astype(BF)
    low = (values - high.astype(np.float32)).astype(BF)
    return high, low


def constants(length):
    index = np.arange(length)
    angle = (index[:, None] * index[None, :] % (2 * length)) * (math.pi / length)
    table = np.stack([np.cos(angle), np.sin(angle)]).astype(np.float32).astype(BF)
    place = np.arange(2 * length)
    scaled = np.where(place < length, place, place - 2 * length) / length
    features = np.zeros((2 * length, 8), np.float32)
    features[:, 0] = scaled
    features[:, 1] = np.sin(math.pi * scaled)
    features[:, 2] = np.cos(math.pi * scaled)
    features[:, 3] = np.sin(7.0 * math.pi * scaled)
    features[:, 4] = np.cos(7.0 * math.pi * scaled)
    return table, np.concatenate(split_table(features), axis=1)


def monarch_backward(upstream, operand, shuffled, right, left, middle, keep_right, keep_left, store):
    groups, width, _ = right.shape
    part = width // groups
    for g in range(groups):
        above = upstream(g)
        keep_left(g, dot(shuffled[pl.ds(g * width, width), :], above, NT))
        below = dot(left[g], above).astype(BF)
        for b in range(groups):
            middle[pl.ds(b * width + g * part, part), :] = below[b * part : (b + 1) * part]
    for b in range(groups):
        above = middle[pl.ds(b * width, width), :]
        keep_right(b, dot(operand(b), above, NT))
        store(b, dot(right[b], above))


CHIPS = (6, 2, 4)


class Reduce:
    def __init__(self, n_seq, n_tp, own, full, core_in, halves, chip_in, quarter, plane_in, send, recv):
        self.own, self.full, self.core_in, self.halves = own, full, core_in, halves
        self.chip_in, self.quarter, self.plane_in = chip_in, quarter, plane_in
        self.send, self.recv, self.n_tp = send, recv, n_tp
        rows, width = own.shape
        self.rows, self.width = rows, width
        self.per_chip, self.per_plane = rows // (n_seq // 2), rows // (n_seq // 2) // n_tp
        self.me, self.plane = lax.axis_index("seq"), lax.axis_index("tp")
        core = lax.rem(self.me, 2)
        self.mine = pl.ds(pl.multiple_of(core * (width // 2), 128), width // 2)
        self.theirs = pl.ds(pl.multiple_of((1 - core) * (width // 2), 128), width // 2)
        self.started = []

    def chip_rows(self, index):
        return pl.ds(pl.multiple_of(index // 2 * self.per_chip, 16), self.per_chip)

    def copy(self, source, target, at, where):
        result = pltpu.make_async_remote_copy(
            src_ref=source, dst_ref=target, send_sem=self.send.at[at], recv_sem=self.recv.at[at],
            device_id=where, device_id_type=MESH,
        )
        result.start()
        self.started.append(result)
        return result

    def start_core(self):
        self.phase = [self.copy(self.own.at[:, self.theirs], self.core_in, 0, {"seq": flip(self.me, 1)})]

    def arrived(self):
        for copy in self.phase:
            copy.wait_recv()
        self.phase = []

    def start_chip(self):
        self.arrived()
        self.halves[...] = (self.own[:, self.mine].astype(F32) + self.core_in[...].astype(F32)).astype(BF)
        for k in CHIPS:
            other = flip(self.me, k)
            self.phase.append(
                self.copy(self.halves.at[self.chip_rows(other), :], self.chip_in.at[k // 2], k // 2, {"seq": other})
            )

    def start_plane(self):
        self.arrived()
        total = self.halves[self.chip_rows(self.me), :].astype(F32)
        for k in CHIPS:
            total = total + self.chip_in[k // 2].astype(F32)
        self.quarter[...] = total.astype(BF)
        for k in range(1, self.n_tp):
            other = flip(self.plane, k)
            here = pl.ds(pl.multiple_of(other * self.per_plane, 16), self.per_plane)
            self.phase.append(self.copy(self.quarter.at[here, :], self.plane_in.at[k], 3 + k, {"tp": other}))

    def start_plane_back(self):
        self.arrived()
        here = pl.ds(pl.multiple_of(self.plane * self.per_plane, 16), self.per_plane)
        total = self.quarter[here, :].astype(F32)
        for k in range(1, self.n_tp):
            total = total + self.plane_in[k].astype(F32)
        rows = pl.ds(
            pl.multiple_of(self.me // 2 * self.per_chip + self.plane * self.per_plane, 16), self.per_plane
        )
        self.full[rows, self.mine] = total.astype(BF)
        spot = self.full.at[rows, self.mine]
        for k in range(1, self.n_tp):
            self.phase.append(self.copy(spot, spot, 6 + k, {"tp": flip(self.plane, k)}))

    def start_chip_back(self):
        self.arrived()
        spot = self.full.at[self.chip_rows(self.me), self.mine]
        for k in CHIPS:
            self.phase.append(self.copy(spot, spot, 9 + k // 2, {"seq": flip(self.me, k)}))

    def start_core_back(self):
        self.arrived()
        spot = self.full.at[:, self.mine]
        self.phase.append(self.copy(spot, spot, 13, {"seq": flip(self.me, 1)}))

    def finish(self):
        self.arrived()
        for copy in self.started:
            copy.wait_send()


def neighbour_order(plane, at):
    upper = plane // 2
    near = plane + upper * (3 - 2 * plane)
    result = at * (1 - near) + (0, 0, 2, 3)[at] * near
    return result + upper * (3 - 2 * result)


def work_order(plane):
    odd = lax.rem(plane, 2)
    return 1 + odd, lax.rem(plane + 2, 4), 3 - 3 * odd


class Line:
    def __init__(self, n_tp, slots, send, recv):
        self.n_tp, self.slots, self.send, self.recv = n_tp, slots, send, recv
        self.plane = lax.axis_index("tp")
        self.sent = []

    def copy(self, block, source, way):
        return pltpu.make_async_remote_copy(
            src_ref=source, dst_ref=self.slots.at[block], send_sem=self.send.at[way, block], recv_sem=self.recv.at[block],
            device_id={"tp": self.plane + (1, -1)[way]}, device_id_type=MESH,
        )

    def start(self, block, source, way, here):
        @pl.when(here)
        def _():
            self.copy(block, source, way).start()

        self.sent.append((block, source, way, here))

    def begin(self, source):
        self.start(self.plane, source, 0, self.plane < self.n_tp - 1)
        self.start(self.plane, source, 1, self.plane > 0)

    def take(self, block, here=None):
        arrival = pltpu.make_async_remote_copy(
            src_ref=self.slots.at[block], dst_ref=self.slots.at[block], send_sem=self.send.at[0, block],
            recv_sem=self.recv.at[block], device_id={"tp": block}, device_id_type=MESH,
        )
        up = jnp.logical_and(block < self.plane, self.plane < self.n_tp - 1)
        down = jnp.logical_and(block > self.plane, self.plane > 0)
        if here is None:
            arrival.wait_recv()
        else:
            pl.when(here)(arrival.wait_recv)
            up, down = jnp.logical_and(up, here), jnp.logical_and(down, here)
        source = self.slots.at[block]
        self.start(block, source, 0, up)
        self.start(block, source, 1, down)

    def finish(self):
        for block, source, way, here in self.sent:

            @pl.when(here)
            def _(block=block, source=source, way=way):
                self.copy(block, source, way).wait_send()


class Square:
    def __init__(self, own, full, core_in, half, first_in, second_in, send, recv):
        self.own, self.full, self.core_in, self.half = own, full, core_in, half
        self.first_in, self.second_in, self.send, self.recv = first_in, second_in, send, recv
        me = lax.axis_index("seq")
        self.me = me
        rows = own.shape[0]
        self.rows = rows
        self.core = lax.rem(me, 2)
        y, x = me // 4, lax.rem(me // 2, 2)
        quarter, part = rows // 8, rows // 16
        base = rows // 4
        self.ways = ((2, x, y, 0), (4, y, x, base))
        self.quarter, self.part = quarter, part
        self.started = []
        self.phase = []

    def copy(self, source, target, at, k):
        result = pltpu.make_async_remote_copy(
            src_ref=source, dst_ref=target, send_sem=self.send.at[at], recv_sem=self.recv.at[at],
            device_id={"seq": flip(self.me, k)}, device_id_type=MESH,
        )
        result.start()
        self.started.append(result)
        self.phase.append(result)

    def arrived(self):
        for copy in self.phase:
            copy.wait_recv()
        self.phase = []

    def span(self, start, size):
        return pl.ds(pl.multiple_of(start, 16), size)

    def start_core(self):
        half = self.rows // 2
        self.copy(self.own.at[self.span((1 - self.core) * half, half), :], self.core_in, 0, 1)

    def start_first(self):
        self.arrived()
        half = self.rows // 2
        own = self.own[self.span(self.core * half, half), :]
        self.half[...] = (own.astype(F32) + self.core_in[...].astype(F32)).astype(BF)
        for way, (k, near, far, base) in enumerate(self.ways):
            source = self.half.at[self.span(base + (1 - near) * self.quarter, self.quarter), :]
            self.copy(source, self.first_in.at[way], 1 + way, k)

    def start_second(self):
        self.arrived()
        for way, (k, near, far, base) in enumerate(self.ways):
            here = self.span(base + near * self.quarter, self.quarter)
            self.half[here, :] = (self.half[here, :].astype(F32) + self.first_in[way].astype(F32)).astype(BF)
            source = self.half.at[self.span(base + near * self.quarter + (1 - far) * self.part, self.part), :]
            self.copy(source, self.second_in.at[way], 3 + way, 6 - k)

    def start_second_back(self):
        self.arrived()
        for way, (k, near, far, base) in enumerate(self.ways):
            place = base + near * self.quarter + far * self.part
            total = self.half[self.span(place, self.part), :].astype(F32) + self.second_in[way].astype(F32)
            here = self.span(self.core * (self.rows // 2) + place, self.part)
            self.full[here, :] = total.astype(BF)
            spot = self.full.at[here, :]
            self.copy(spot, spot, 5 + way, 6 - k)

    def start_first_back(self):
        self.arrived()
        for way, (k, near, far, base) in enumerate(self.ways):
            spot = self.full.at[self.span(self.core * (self.rows // 2) + base + near * self.quarter, self.quarter), :]
            self.copy(spot, spot, 7 + way, k)

    def start_core_back(self):
        self.arrived()
        spot = self.full.at[self.span(self.core * (self.rows // 2), self.rows // 2), :]
        self.copy(spot, spot, 9, 1)

    def finish(self):
        for copy in self.started:
            copy.wait_send()


class Inputs(typing.NamedTuple):
    feed_gain: typing.Any
    feed_bias: typing.Any
    out_right: typing.Any
    out_left: typing.Any
    gain: typing.Any
    bias: typing.Any
    in_right: typing.Any
    in_left: typing.Any
    short: typing.Any
    conv_bias: typing.Any
    features: typing.Any
    first: typing.Any
    second: typing.Any
    third: typing.Any
    tokens: typing.Any
    cotangent: typing.Any
    table: typing.Any
    gate_w: typing.Any
    up_w: typing.Any
    down_w: typing.Any


class Outputs(typing.NamedTuple):
    output_out: typing.Any
    ffn_out: typing.Any
    tokens_out: typing.Any
    late_out: typing.Any
    early_out: typing.Any
    small_out: typing.Any


def core_scratch(n_seq, n_tp, width, chans, length, rows):
    result = dict(
        token_v=pltpu.VMEM((rows, width), BF),
        cot_v=pltpu.VMEM((n_tp, rows, width), BF),
        gate_v=pltpu.VMEM((width, width), BF),
        up_v=pltpu.VMEM((width, width), BF),
        down_v=pltpu.VMEM((width, width), BF),
        out_shuffled=pltpu.VMEM((width, rows), BF),
        branch=pltpu.VMEM((width, rows), F32),
        resid=pltpu.VMEM((rows, width), F32),
        scaled=pltpu.VMEM((rows, width), F32),
        inverse=pltpu.VMEM((rows, 1), F32),
        normed=pltpu.VMEM((n_tp, rows, width), BF),
        hidden=pltpu.VMEM((n_tp, rows, width), BF),
        grad_hidden=pltpu.VMEM((n_tp, rows, width), F32),
        grad_gate=pltpu.VMEM((n_tp, rows, width), BF),
        grad_up=pltpu.VMEM((n_tp, rows, width), BF),
        grad_normed=pltpu.VMEM((rows, width), F32),
        grad_send=pltpu.VMEM((n_tp, rows, width), BF),
        grad_recv=pltpu.VMEM((n_tp, rows, width), BF),
        glu_own=pltpu.VMEM((rows, width), F32),
        glu_send=pltpu.VMEM((n_tp, rows, width), BF),
        glu_recv=pltpu.VMEM((n_tp, rows, width), BF),
        turned=pltpu.VMEM((width, n_tp*rows), BF),
        grads=pltpu.VMEM((3, width, width), BF),
        ffn_v=pltpu.VMEM((3, width, width), BF),
        core_in=pltpu.VMEM((3, width//2, width), BF),
        halves=pltpu.VMEM((3, width//2, width), BF),
        first_in=pltpu.VMEM((3, 2, width//8, width), BF),
        second_in=pltpu.VMEM((3, 2, width//16, width), BF),
        grad_branch=pltpu.VMEM((width, rows), BF),
        middle=pltpu.VMEM((width, rows), BF),
        grad_mixed_own=pltpu.VMEM((width, rows), BF),
        grad_mixed=pltpu.VMEM((chans, length), BF),
        out_rows=pltpu.VMEM((rows, width), BF),
        output_v=pltpu.VMEM((n_tp, rows//n_tp, width), BF),
        grad_vectors=pltpu.VMEM((2, width), F32),
        grad_resid=pltpu.VMEM((rows, width), F32),
        table_v=pltpu.VMEM((2, length, length), BF),
        signals=pltpu.VMEM((3, chans, length), BF),
        conv=pltpu.VMEM((chans, length), F32),
        wave=pltpu.VMEM((2, length, 128), BF),
        taps_v=pltpu.VMEM((2, length, 128), BF),
        acts=pltpu.VMEM((4, 2*length, 128), BF),
        in_normed=pltpu.VMEM((width, rows), BF),
        in_shuffled=pltpu.VMEM((width, rows), BF),
        grad_short=pltpu.VMEM((3, chans, length), F32),
        query=pltpu.VMEM((chans, length), F32),
        value_v=pltpu.VMEM((chans, length), F32),
        grad_conv=pltpu.VMEM((chans, length), F32),
        padded=pltpu.VMEM((128, length), BF),
        back_wave=pltpu.VMEM((2, length, 128), BF),
        cross=pltpu.VMEM((2, length, 256), BF),
        sums=pltpu.VMEM((128, 128), F32),
        grad_signals=pltpu.VMEM((3, chans, length), BF),
        grad_proj=pltpu.VMEM((3*width, rows), BF),
        grad_rows=pltpu.VMEM((width, rows), F32),
        grad_tok=pltpu.VMEM((rows, width), BF),
        grad_second=pltpu.VMEM((128, 128), F32),
        grad_first=pltpu.VMEM((16, 128), F32),
        grad_third=pltpu.VMEM((128, 128), F32),
        local_sems=pltpu.SemaphoreType.DMA((20,)),
        line_send=pltpu.SemaphoreType.DMA((2,n_tp)),
        line_recv=pltpu.SemaphoreType.DMA((n_tp,)),
        tok_send=pltpu.SemaphoreType.DMA((2,n_tp)),
        tok_recv=pltpu.SemaphoreType.DMA((n_tp,)),
        back_send=pltpu.SemaphoreType.DMA((n_tp,)),
        back_recv=pltpu.SemaphoreType.DMA((n_tp,)),
        glu_ssem=pltpu.SemaphoreType.DMA((n_tp,)),
        glu_rsem=pltpu.SemaphoreType.DMA((n_tp,)),
        out_send=pltpu.SemaphoreType.DMA((n_tp,)),
        out_recv=pltpu.SemaphoreType.DMA((n_tp,)),
        mixed_send=pltpu.SemaphoreType.DMA((n_seq,)),
        mixed_recv=pltpu.SemaphoreType.DMA((n_seq,)),
        seq_send=pltpu.SemaphoreType.DMA((n_seq,3)),
        seq_recv=pltpu.SemaphoreType.DMA((n_seq,3)),
        ffn_send=pltpu.SemaphoreType.DMA((3,10)),
        ffn_recv=pltpu.SemaphoreType.DMA((3,10)),
        mixed=pltpu.VMEM((width, rows), BF),
        front_mixed=pltpu.VMEM((chans, length), BF),
        nyquist=pltpu.VMEM((chans, 128), F32),
        columns=pltpu.VMEM((chans, 16), F32),
        third_v=pltpu.VMEM((128, 128), BF),
        projected=pltpu.VMEM((3 * width, rows), BF),
        spread=pltpu.VMEM((length, 256), BF),
        product=pltpu.VMEM((chans, length), F32),
        totals=pltpu.VMEM((1, 128), F32),
        tall=pltpu.VMEM((width, 16), F32),
        third_turned=pltpu.VMEM((width, 128), BF),
        front_send=pltpu.SemaphoreType.DMA((n_seq, 3)),
        front_recv=pltpu.SemaphoreType.DMA((n_seq, 3)),
        mix_send=pltpu.SemaphoreType.DMA((n_seq,)),
        mix_recv=pltpu.SemaphoreType.DMA((n_seq,)),
        cot_send=pltpu.SemaphoreType.DMA((n_tp,)),
        cot_recv=pltpu.SemaphoreType.DMA((n_tp,)),
        late_own=pltpu.VMEM((width, width), BF),
        late_full=pltpu.VMEM((width, width), BF),
        early_own=pltpu.VMEM((width, 512), BF),
        early_full=pltpu.VMEM((width, 512), BF),
        small_own=pltpu.VMEM((256, 256), BF),
        small_full=pltpu.VMEM((256, 256), BF),
    )
    groups = []
    for count, breadth in ((256, width), (256, width), (256, width), (width, 512), (256, 256)):
        half, chip = breadth // 2, count // (n_seq // 2)
        groups.append(
            [
                pltpu.VMEM((count, half), BF),
                pltpu.VMEM((count, half), BF),
                pltpu.VMEM((n_seq // 2, chip, half), BF),
                pltpu.VMEM((chip, half), BF),
                pltpu.VMEM((n_tp, chip // n_tp, half), BF),
                pltpu.SemaphoreType.DMA((14,)),
                pltpu.SemaphoreType.DMA((14,)),
            ]
        )
    return result, groups


def core_kernel(n_seq, n_tp, dims, *refs):
    width, chans, length, rows = dims
    scratch, groups = core_scratch(n_seq, n_tp, width, chans, length, rows)
    named = dict(zip(Inputs._fields + Outputs._fields + tuple(scratch), refs))
    r = types.SimpleNamespace(**named)
    spare = list(refs[len(named) :])
    reduce_refs = [[spare.pop(0) for _ in group] for group in groups]
    me, plane = lax.axis_index("seq"), lax.axis_index("tp")
    entered = greet(n_seq, n_tp)
    sources = dict(
        token=(r.tokens.at[plane], r.token_v),
        down=(r.down_w, r.down_v),
        gate=(r.gate_w, r.gate_v),
        up=(r.up_w, r.up_v),
        table=(r.table, r.table_v),
    )
    copies = {
        name: pltpu.make_async_copy(*pair, r.local_sems.at[at]) for at, (name, pair) in enumerate(sources.items())
    }
    for copy in copies.values():
        copy.start()
    loads = types.SimpleNamespace(**copies)
    front_sends, cot_copies, own_cot = front_part(n_seq, n_tp, dims, r, entered, loads)
    _, block, _ = r.out_right.shape
    chunk = 256
    pieces = width // chunk
    per = length // chunk
    step = 16

    lates = []
    for at in range(3):
        here = pl.ds(256 * at, 256)
        lates.append(Reduce(n_seq, n_tp, r.late_own.at[here, :], r.late_full.at[here, :], *reduce_refs[at]))
    early = Reduce(n_seq, n_tp, r.early_own, r.early_full, *reduce_refs[3])
    small = Reduce(n_seq, n_tp, r.small_own, r.small_full, *reduce_refs[4])
    squares = [
        Square(
            r.grads.at[which], r.ffn_v.at[which], r.core_in.at[which], r.halves.at[which], r.first_in.at[which],
            r.second_in.at[which], r.ffn_send.at[which], r.ffn_recv.at[which],
        )
        for which in range(3)
    ]

    def keep_branch(g, result):
        r.branch[pl.ds(g * block, block), :] = result

    monarch_forward(lambda b: r.mixed[pl.ds(b * block, block), :], r.out_right, r.out_left, r.out_shuffled, keep_branch)
    tokens = r.token_v[...].astype(F32)
    value = tokens + r.branch[...].T
    r.resid[...] = value
    shifted = value - jnp.mean(value, axis=-1, keepdims=True)
    r.inverse[...] = lax.rsqrt(jnp.mean(shifted * shifted, axis=-1, keepdims=True) + 1e-05)
    value = shifted * r.inverse[...]
    r.scaled[...] = value
    r.normed[plane] = (value * r.feed_gain[...].reshape(1, width) + r.feed_bias[...].reshape(1, width)).astype(BF)
    line = Line(n_tp, r.normed, r.line_send, r.line_recv)
    line.begin(r.normed.at[plane])
    for copy in cot_copies:
        copy.wait_recv()
    own_cot.wait()
    loads.down.wait()

    def hidden_step(at, carry):
        cols = pl.ds(pl.multiple_of(at * chunk, chunk), chunk)
        result = dot(r.cot_v[...].reshape(n_tp * rows, width), r.down_v[cols, :], NT)
        r.grad_hidden[:, :, cols] = result.reshape(n_tp, rows, chunk)
        return carry

    lax.fori_loop(0, pieces, hidden_step, 0)
    loads.gate.wait()
    loads.up.wait()
    backs = []
    def send_back(other):
        copy = pltpu.make_async_remote_copy(
            src_ref=r.grad_send.at[other],
            dst_ref=r.grad_recv.at[plane],
            send_sem=r.back_send.at[other],
            recv_sem=r.back_recv.at[plane],
            device_id={"tp": other},
            device_id_type=MESH,
        )
        copy.start()
        backs.append(copy)

    order = work_order(plane)
    inner = jnp.logical_and(plane > 0, plane < n_tp - 1)
    outer = jnp.logical_not(inner)
    for k in range(n_tp):
        other = plane if k == 0 else order[k - 1]
        if k == 1:
            line.take(order[2], inner)
            line.take(order[0])
        if k == 2:
            line.take(order[1])
        if k == 3:
            line.take(order[2], outer)
        if k > 1:
            send_back(order[k - 2])

        def gate_step(at, carry, other=other):
            cols = pl.ds(pl.multiple_of(at * chunk, chunk), chunk)
            value = r.normed[other]
            gate = dot(value, r.gate_v[:, cols])
            upward = dot(value, r.up_v[:, cols])
            sigma = 1.0 / (1.0 + jnp.exp(-gate))
            active = gate * sigma
            r.hidden[other, :, cols] = (active * upward).astype(BF)
            above = r.grad_hidden[other, :, cols]
            r.grad_gate[other, :, cols] = (above * upward * (sigma + active * (1.0 - sigma))).astype(BF)
            r.grad_up[other, :, cols] = (above * active).astype(BF)
            return carry

        lax.fori_loop(0, pieces, gate_step, 0)

        def back_step(at, carry, k=k, other=other):
            cols = pl.ds(pl.multiple_of(at * chunk, chunk), chunk)
            result = dot(r.grad_gate[other], r.gate_v[cols, :], NT) + dot(r.grad_up[other], r.up_v[cols, :], NT)
            if k == 0:
                r.grad_normed[:, cols] = result
            else:
                r.grad_send[other, :, cols] = result.astype(BF)
            return carry

        lax.fori_loop(0, pieces, back_step, 0)
    send_back(order[2])

    def turn(source):
        for s in range(n_tp):
            r.turned[:, s * rows : (s + 1) * rows] = source[s].T

    def weight_grad(which, factor):
        def grad_step(at, carry):
            here = pl.ds(pl.multiple_of(at * chunk, chunk), chunk)
            result = dot(r.turned[here, :], factor[...].reshape(n_tp * rows, width))
            r.grads[which, here, :] = result.astype(BF)
            return carry

        lax.fori_loop(0, pieces, grad_step, 0)
        squares[which].start_core()

    turn(r.normed)
    weight_grad(0, r.grad_gate)
    weight_grad(1, r.grad_up)
    squares[0].start_first()
    turn(r.hidden)
    weight_grad(2, r.cot_v)
    squares[1].start_first()
    squares[2].start_first()

    def from_planes(recv, slots):
        total = 0.0
        for k in range(1, n_tp):
            other = flip(plane, k)
            pltpu.make_async_remote_copy(
                src_ref=slots.at[other], dst_ref=slots.at[other], send_sem=recv.at[other], recv_sem=recv.at[other],
                device_id={"tp": other}, device_id_type=MESH,
            ).wait_recv()
            total = total + slots[other].astype(F32)
        return total

    for k in range(n_tp):
        other = plane if k == 0 else neighbour_order(plane, n_tp - k)

        def glu_step(at, carry, k=k, other=other):
            cols = pl.ds(pl.multiple_of(at * chunk, chunk), chunk)
            result = dot(r.hidden[other], r.down_v[:, cols])
            if k == 0:
                r.glu_own[:, cols] = result
            else:
                r.glu_send[other, :, cols] = result.astype(BF)
            return carry

        lax.fori_loop(0, pieces, glu_step, 0)
    total = r.grad_normed[...] + from_planes(r.back_recv, r.grad_recv)
    value = r.scaled[...]
    r.grad_vectors[0:1, :] = jnp.sum(total * value, axis=0, keepdims=True)
    r.grad_vectors[1:2, :] = jnp.sum(total, axis=0, keepdims=True)
    total = total * r.feed_gain[...].reshape(1, width)
    first_mean = jnp.mean(total, axis=-1, keepdims=True)
    second_mean = jnp.mean(total * value, axis=-1, keepdims=True)
    total = r.cot_v[plane].astype(F32) + r.inverse[...] * (total - first_mean - value * second_mean)
    r.grad_resid[...] = total
    r.grad_branch[...] = total.T.astype(BF)
    out_parts = {}

    def keep_out_left(g, result):
        out_parts[g] = result.astype(BF)

    def keep_out_right(b, result):
        both = jnp.concatenate([result.astype(BF), out_parts[b]], axis=1)
        r.early_own[pl.ds(b * block, block), 0 : 2 * block] = both

    def keep_mixed(b, result):
        r.grad_mixed_own[pl.ds(b * block, block), :] = result.astype(BF)

    monarch_backward(
        lambda g: r.grad_branch[pl.ds(g * block, block), :],
        lambda b: r.mixed[pl.ds(b * block, block), :],
        r.out_shuffled, r.out_right, r.out_left, r.middle, keep_out_right, keep_out_left, keep_mixed,
    )
    mine = pl.ds(pl.multiple_of(me * rows, rows), rows)
    own_chans = pl.ds(pl.multiple_of(me * chans, 16), chans)
    mixed_copies = []
    for k in SEQ_ORDER:
        other = flip(me, k)
        copy = pltpu.make_async_remote_copy(
            src_ref=r.grad_mixed_own.at[pl.ds(pl.multiple_of(other * chans, 16), chans), :],
            dst_ref=r.grad_mixed.at[:, mine],
            send_sem=r.mixed_send.at[k],
            recv_sem=r.mixed_recv.at[k],
            device_id={"seq": other},
            device_id_type=MESH,
        )
        copy.start()
        mixed_copies.append(copy)
    r.grad_mixed[:, mine] = r.grad_mixed_own[own_chans, :]
    squares[0].start_second()

    glus = []
    for k in range(1, n_tp):
        other = neighbour_order(plane, n_tp - k)
        copy = pltpu.make_async_remote_copy(
            src_ref=r.glu_send.at[other],
            dst_ref=r.glu_recv.at[plane],
            send_sem=r.glu_ssem.at[other],
            recv_sem=r.glu_rsem.at[plane],
            device_id={"tp": other},
            device_id_type=MESH,
        )
        copy.start()
        glus.append(copy)
    squares[1].start_second()
    r.sums[...] = jnp.zeros_like(r.sums)
    r.small_own[...] = jnp.zeros_like(r.small_own)
    r.early_own[:, 384:512] = jnp.zeros((width, 128), BF)
    r.padded[pl.ds(chans, 128 - chans), :] = jnp.zeros((128 - chans, length), BF)
    for copy in mixed_copies:
        copy.wait_recv()

    def short_step(at, carry):
        here = pl.ds(pl.multiple_of(at * step, step), step)
        shorted = []
        for s in range(3):
            value = r.signals[s, here, :].astype(F32)
            shorted.append(
                previous(value) * r.columns[here, 3 * s : 3 * s + 1]
                + value * r.columns[here, 3 * s + 1 : 3 * s + 2]
                + following(value) * r.columns[here, 3 * s + 2 : 3 * s + 3]
            )
        r.query[here, :] = shorted[0]
        r.value_v[here, :] = shorted[2]
        above = r.grad_mixed[here, :].astype(F32)
        r.grad_short[1, here, :] = above * r.conv[here, :]
        above = above * shorted[1]
        r.grad_conv[here, :] = above
        r.padded[here, :] = above.astype(BF)
        r.sums[here, 9:10] = jnp.sum(above * shorted[0] * shorted[2], axis=1, keepdims=True)
        r.sums[here, 10:11] = jnp.sum(above * sign_lanes(step, length), axis=1, keepdims=True)
        return carry

    lax.fori_loop(0, chans // step, short_step, 0)
    squares[2].start_second()

    def wave_step(at, carry):
        here = pl.ds(pl.multiple_of(at * chunk, chunk), chunk)
        sign = sign_rows(chunk, 128)
        index = lax.broadcasted_iota(jnp.int32, (chunk, 128), 0) + at * chunk
        weight = jnp.where(index == 0, 0.5 / length, 1.0 / length)
        cos_part = dot(r.table_v[0, here, :], r.padded[...], NT)
        sin_part = dot(r.table_v[1, here, :], r.padded[...], NT)
        tap_cos = r.taps_v[0, here, :].astype(F32)
        tap_sin = r.taps_v[1, here, :].astype(F32)
        r.back_wave[0, here, :] = (cos_part * tap_cos + sin_part * tap_sin).astype(BF)
        r.back_wave[1, here, :] = (sin_part * tap_cos - cos_part * tap_sin).astype(BF)
        wave_cos = r.wave[0, here, :].astype(F32) * weight
        wave_sin = r.wave[1, here, :].astype(F32) * weight
        result = cos_part * wave_cos + sin_part * wave_sin
        r.cross[0, here, 0:128] = result.astype(BF)
        r.cross[0, here, 128:256] = (result * sign).astype(BF)
        result = sin_part * wave_cos - cos_part * wave_sin
        r.cross[1, here, 0:128] = result.astype(BF)
        r.cross[1, here, 128:256] = (result * sign).astype(BF)
        return carry

    lax.fori_loop(0, per, wave_step, 0)
    squares[0].start_second_back()
    squares[1].start_second_back()

    def product_step(at, carry):
        here = pl.ds(pl.multiple_of(at * chunk, chunk), chunk)
        result = dot(r.table_v[0, here, :], r.back_wave[0]) + dot(r.table_v[1, here, :], r.back_wave[1])
        result = (
            result.T[:chans]
            + sign_lanes(chans, chunk) * (r.sums[:chans, 10:11] * r.nyquist[:, 1:2] * (0.5 / length))
            + r.columns[:, 9:10] * r.grad_conv[:, here]
        )
        r.grad_short[0, :, here] = result * r.value_v[:, here]
        r.grad_short[2, :, here] = result * r.query[:, here]
        return carry

    lax.fori_loop(0, per, product_step, 0)
    squares[2].start_second_back()

    def signal_step(at, carry):
        here = pl.ds(pl.multiple_of(at * step, step), step)
        for s in range(3):
            above = r.grad_short[s, here, :]
            value = r.signals[s, here, :].astype(F32)
            before, after = previous(above), following(above)
            r.grad_signals[s, here, :] = (
                after * r.columns[here, 3 * s : 3 * s + 1]
                + above * r.columns[here, 3 * s + 1 : 3 * s + 2]
                + before * r.columns[here, 3 * s + 2 : 3 * s + 3]
            ).astype(BF)
            r.sums[here, 3 * s : 3 * s + 1] = jnp.sum(after * value, axis=1, keepdims=True)
            r.sums[here, 3 * s + 1 : 3 * s + 2] = jnp.sum(above * value, axis=1, keepdims=True)
            r.sums[here, 3 * s + 2 : 3 * s + 3] = jnp.sum(before * value, axis=1, keepdims=True)
        return carry

    lax.fori_loop(0, chans // step, signal_step, 0)
    seq_copies = []
    for k in SEQ_ORDER:
        other = flip(me, k)
        for s in range(3):
            copy = pltpu.make_async_remote_copy(
                src_ref=r.grad_signals.at[s, :, pl.ds(pl.multiple_of(other * rows, rows), rows)],
                dst_ref=r.grad_proj.at[pl.ds(pl.multiple_of(s * width + me * chans, 16), chans), :],
                send_sem=r.seq_send.at[k, s],
                recv_sem=r.seq_recv.at[k, s],
                device_id={"seq": other},
                device_id_type=MESH,
            )
            copy.start()
            seq_copies.append(copy)
    for s in range(3):
        r.grad_proj[pl.ds(pl.multiple_of(s * width + me * chans, 16), chans), :] = r.grad_signals[s, :, mine]
    squares[0].start_first_back()
    squares[1].start_first_back()

    total = r.resid[...] + r.glu_own[...] + from_planes(r.glu_rsem, r.glu_recv)
    r.out_rows[...] = total.astype(BF)
    part = rows // n_tp
    out_copies = []
    for k in range(1, n_tp):
        other = flip(plane, k)
        copy = pltpu.make_async_remote_copy(
            src_ref=r.out_rows.at[pl.ds(pl.multiple_of(other * part, part), part), :],
            dst_ref=r.output_v.at[plane],
            send_sem=r.out_send.at[k],
            recv_sem=r.out_recv.at[k],
            device_id={"tp": other},
            device_id_type=MESH,
        )
        copy.start()
        out_copies.append(copy)
    r.output_v[plane] = r.out_rows[pl.ds(pl.multiple_of(plane * part, part), part), :]

    tap_total = jnp.broadcast_to(r.sums[:, 10:11], (128, 128)).T[0:1, :]
    pad_nyquist = jnp.concatenate([r.nyquist[:, 0:1], jnp.zeros((128 - chans, 1), F32)], axis=0)
    tap_total = tap_total * jnp.broadcast_to(pad_nyquist, (128, 128)).T[0:1, :] * (0.5 / length)
    r.grad_second[...] = jnp.zeros_like(r.grad_second)
    r.grad_first[...] = jnp.zeros_like(r.grad_first)
    r.grad_third[...] = jnp.zeros_like(r.grad_third)

    def filter_step(at, carry):
        here = pl.ds(pl.multiple_of(at * chunk, chunk), chunk)
        result = dot(r.table_v[0, here, :], r.cross[0]) + dot(r.table_v[1, here, :], r.cross[1])
        sign = sign_rows(chunk, 128)
        for half in range(2):
            above = (result[:, half * 128 : (half + 1) * 128] + sign * tap_total) * (length**-0.5)
            if half == 1:
                index = lax.broadcasted_iota(jnp.int32, above.shape, 0) + at * chunk
                above = jnp.where(index == 0, 0.0, above)
            above = above.astype(BF)
            spot = pl.ds(pl.multiple_of(half * length + at * chunk, chunk), chunk)
            r.grad_third[...] += dot(above, r.acts[2, spot, :], TN)
            below = (dot(above, r.third_v[...]) * r.acts[3, spot, :].astype(F32)).astype(BF)
            r.grad_second[...] += dot(r.acts[0, spot, :], below, TN)
            below = (dot(below, r.second[...], NT) * r.acts[1, spot, :].astype(F32)).astype(BF)
            r.grad_first[...] += dot(r.features[spot, :], below, TN)
        return carry

    lax.fori_loop(0, per, filter_step, 0)
    r.early_own[own_chans, 384:512] = r.grad_third[:chans, :].astype(BF)
    r.small_own[0:128, 0:128] = r.grad_second[...].astype(BF)
    r.small_own[128:136, 0:128] = (r.grad_first[0:8, :] + r.grad_first[8:16, :]).astype(BF)
    r.small_own[pl.ds(pl.multiple_of(me * 16, 16), 16), 128:256] = r.sums[...].T[0:16, :].astype(BF)
    early.start_core()
    shifted = tokens - jnp.mean(tokens, axis=-1, keepdims=True)
    inverse = lax.rsqrt(jnp.mean(shifted * shifted, axis=-1, keepdims=True) + 1e-05)
    r.scaled[...] = shifted * inverse
    fan = r.in_left.shape[2]
    for copy in seq_copies:
        copy.wait_recv()
    early.start_chip()

    in_parts = {}

    def keep_left(g, result):
        r.late_own[pl.ds(g * block, block), 0:512] = result[:, 0:512].astype(BF)
        in_parts[g] = result[:, 512:576].astype(BF)

    def keep_right(b, result):
        r.late_own[pl.ds(b * block, block), 512:768] = jnp.concatenate([in_parts[b], result.astype(BF)], axis=1)

    def keep_rows(b, result):
        r.grad_rows[pl.ds(b * block, block), :] = result

    part = block // 4
    for g in range(4):
        below = dot(r.in_left[g], r.grad_proj[pl.ds(g * fan, fan), :]).astype(BF)
        for b in range(4):
            r.middle[pl.ds(b * block + g * part, part), :] = below[b * part : (b + 1) * part]
    for b in range(4):
        keep_rows(b, dot(r.in_right[b], r.middle[pl.ds(b * block, block), :]))
    total = r.grad_rows[...].T
    scaled = r.scaled[...]
    lines = [jnp.sum(total * scaled, axis=0, keepdims=True), jnp.sum(total, axis=0, keepdims=True)]
    total = total * r.gain[...].reshape(1, width)
    first_mean = jnp.mean(total, axis=-1, keepdims=True)
    second_mean = jnp.mean(total * scaled, axis=-1, keepdims=True)
    total = r.grad_resid[...] + inverse * (total - first_mean - scaled * second_mean)
    r.grad_tok[...] = total.astype(BF)
    token_line = Line(n_tp, r.tokens_out, r.tok_send, r.tok_recv)
    token_line.begin(r.grad_tok)
    own_tok = pltpu.make_async_copy(r.grad_tok, r.tokens_out.at[plane], r.local_sems.at[13])
    own_tok.start()
    for g in range(4):
        keep_left(g, dot(r.in_shuffled[pl.ds(g * block, block), :], r.grad_proj[pl.ds(g * fan, fan), :], NT))
    for b in range(4):
        keep_right(b, dot(r.in_normed[pl.ds(b * block, block), :], r.middle[pl.ds(b * block, block), :], NT))
    for late in lates:
        late.start_core()
    squares[2].start_first_back()
    early.start_plane()
    for late in lates:
        late.start_chip()
    lines += [r.grad_vectors[0:1, :], r.grad_vectors[1:2, :]]
    packed = [row[:, at * 128 : (at + 1) * 128] for row in lines for at in range(width // 128)]
    r.small_own[128:160, 128:256] = jnp.concatenate(packed + [jnp.zeros((8, 128), F32)], axis=0).astype(BF)
    small.start_core()
    token_line.take(order[2], inner)
    token_line.take(order[0])
    early.start_plane_back()
    small.start_chip()
    for late in lates:
        late.start_plane()
    small.start_plane()
    early.start_chip_back()
    for square in squares:
        square.start_core_back()
    token_line.take(order[1])
    for late in lates:
        late.start_plane_back()
    small.start_plane_back()
    for late in lates:
        late.start_chip_back()
    small.start_chip_back()
    early.start_core_back()
    token_line.take(order[2], outer)
    ffn_copies = []
    for which, square in enumerate(squares):
        square.arrived()
        copy = pltpu.make_async_copy(r.ffn_v.at[which], r.ffn_out.at[which], r.local_sems.at[14 + which])
        copy.start()
        ffn_copies.append(copy)
    for late in lates:
        late.start_core_back()
    small.start_core_back()
    early.finish()
    r.early_out[...] = r.early_full[...]
    small.finish()
    r.small_out[...] = r.small_full[...]
    for copy in out_copies:
        copy.wait()
    r.output_out[...] = r.output_v[...]
    for late in lates:
        late.finish()
    r.late_out[...] = r.late_full[...]
    for copy in mixed_copies + seq_copies + backs + glus + front_sends + cot_copies:
        copy.wait_send()
    for square in squares:
        square.finish()
    line.finish()
    token_line.finish()
    own_tok.wait()
    for copy in ffn_copies:
        copy.wait()


def core(mesh_shape, *operands):
    n_seq, n_tp = mesh_shape
    tokens = Inputs(*operands).tokens
    _, rows, width = tokens.shape
    chans, length = width // n_seq, rows * n_seq
    scratch, groups = core_scratch(n_seq, n_tp, width, chans, length, rows)
    shape = jax.ShapeDtypeStruct
    return pl.pallas_call(
        functools.partial(core_kernel, n_seq, n_tp, (width, chans, length, rows)),
        out_shape=(
            shape((n_tp, rows // n_tp, width), BF),
            shape((3, width, width), BF),
            shape((n_tp, rows, width), BF),
            shape((width, width), BF),
            shape((width, 512), BF),
            shape((256, 256), BF),
        ),
        in_specs=[vmem_spec()] * 14 + [any_spec()] * (len(Inputs._fields) - 14),
        out_specs=(vmem_spec(), any_spec(), any_spec(), vmem_spec(), vmem_spec(), vmem_spec()),
        scratch_shapes=list(scratch.values()) + sum(groups, []),
        compiler_params=pltpu.CompilerParams(collective_id=0, has_side_effects=True, vmem_limit_bytes=60 * 1024 * 1024),
        name="layer",
    )(*operands)


def finish_kernel(width, chans, *refs):
    (ffn, tokens, late, early, small) = refs[:5]
    (grad_tokens, norm_gain, norm_bias, in_right, in_left, short, first, second, third, conv_bias, out_right, out_left,
     ffn_gain, ffn_bias, gate, up, down) = refs[5:22]
    (ffn_v, ffn_f, token_v, token_f, late_v, early_v, in_right_f, in_left_f, out_right_f, out_left_f, in_sems, out_sems) = refs[22:]
    pairs = [(ffn.at[which], ffn_v.at[which]) for which in range(3)] + [(tokens, token_v), (late, late_v), (early, early_v)]
    loads = [pltpu.make_async_copy(*pair, in_sems.at[at]) for at, pair in enumerate(pairs)]
    for copy in loads:
        copy.start()
    pairs = [(ffn_f.at[which], target) for which, target in enumerate((gate, up, down))]
    pairs += [
        (token_f, grad_tokens), (in_right_f, in_right), (in_left_f, in_left), (out_right_f, out_right), (out_left_f, out_left)
    ]
    stores = [pltpu.make_async_copy(*pair, out_sems.at[at]) for at, pair in enumerate(pairs)]
    chunk = 64
    for which in range(3):
        loads[which].wait()

        def step(at, carry, which=which):
            here = pl.ds(pl.multiple_of(at * chunk, chunk), chunk)
            ffn_f[which, here, :] = ffn_v[which, here, :].astype(F32)
            return carry

        lax.fori_loop(0, width // chunk, step, 0)
        stores[which].start()
    loads[3].wait()

    def token_step(at, carry):
        token_f[at] = token_v[at].astype(F32)
        return carry

    lax.fori_loop(0, token_v.shape[0], token_step, 0)
    stores[3].start()
    groups, block, _ = in_right.shape
    loads[4].wait()
    for b in range(groups):
        here = pl.ds(b * block, block)
        in_left_f[b] = late_v[here, 0 : 3 * block].astype(F32)
        in_right_f[b] = late_v[here, 3 * block : 4 * block].astype(F32)
    stores[4].start()
    stores[5].start()
    loads[5].wait()
    for b in range(groups):
        here = pl.ds(b * block, block)
        out_right_f[b] = early_v[here, 0:block].astype(F32)
        out_left_f[b] = early_v[here, block : 2 * block].astype(F32)
    stores[6].start()
    stores[7].start()
    third[...] = early_v[:, 384:512].astype(F32).T
    values = small[...].astype(F32)
    second[...] = values[0:128, 0:128]
    first[...] = values[128:133, 0:128]
    for at, target in enumerate((norm_gain, norm_bias, ffn_gain, ffn_bias)):
        row = 128 + at * (width // 128)
        target[...] = jnp.concatenate([values[row + k : row + k + 1, 128:256] for k in range(width // 128)], axis=1).reshape(width)
    parts = [values[16 * at : 16 * at + 16, 128 : 128 + chans] for at in range(width // chans)]
    lines = jnp.concatenate(parts, axis=1)
    for s in range(3):
        short[s] = lines[3 * s : 3 * s + 3]
    conv_bias[...] = lines[9:10].reshape(width)
    for copy in stores:
        copy.wait()


def finish(chans, ffn, tokens, late, early, small):
    width = ffn.shape[1]
    block = width // 4
    shape = jax.ShapeDtypeStruct
    vector = shape((width,), F32)
    square = shape((4, block, block), F32)
    wide = shape((4, block, 3 * block), F32)
    return pl.pallas_call(
        functools.partial(finish_kernel, width, chans),
        out_shape=(
            shape(tokens.shape, F32), vector, vector, square, wide, shape((3, 3, width), F32),
            shape((5, 128), F32), shape((128, 128), F32), shape((128, width), F32), vector, square, square, vector, vector,
        )
        + (shape((width, width), F32),) * 3,
        in_specs=[any_spec()] * 4 + [vmem_spec()],
        out_specs=(any_spec(), vmem_spec(), vmem_spec(), any_spec(), any_spec())
        + (vmem_spec(),) * 5
        + (any_spec(), any_spec(), vmem_spec(), vmem_spec())
        + (any_spec(),) * 3,
        scratch_shapes=[
            pltpu.VMEM(ffn.shape, BF),
            pltpu.VMEM(ffn.shape, F32),
            pltpu.VMEM(tokens.shape, BF),
            pltpu.VMEM(tokens.shape, F32),
            pltpu.VMEM(late.shape, BF),
            pltpu.VMEM(early.shape, BF),
            pltpu.VMEM(square.shape, F32),
            pltpu.VMEM(wide.shape, F32),
            pltpu.VMEM(square.shape, F32),
            pltpu.VMEM(square.shape, F32),
            pltpu.SemaphoreType.DMA((6,)),
            pltpu.SemaphoreType.DMA((8,)),
        ],
        compiler_params=pltpu.CompilerParams(vmem_limit_bytes=LIMIT),
        name="finish",
    )(ffn, tokens, late, early, small)


def fast_body(
    tokens,
    norm_gain,
    norm_bias,
    in_right,
    in_left,
    short_kernel,
    filter_first,
    filter_second,
    filter_third,
    conv_bias,
    out_right,
    out_left,
    ffn_gain,
    ffn_bias,
    gate_weight,
    up_weight,
    down_weight,
    cotangent,
):
    n_seq, n_tp = lax.axis_size("seq"), lax.axis_size("tp")
    _, rows, width = tokens.shape
    chans, length = width // n_seq, rows * n_seq
    shape = (n_seq, n_tp)
    table, features = (jnp.asarray(array) for array in constants(length))
    output, ffn, grad_tokens, late, early, small = core(
        shape, ffn_gain, ffn_bias, out_right, out_left, norm_gain, norm_bias, in_right, in_left, short_kernel.transpose(0, 2, 1),
        conv_bias, features, filter_first, filter_second, filter_third, tokens, cotangent, table, gate_weight, up_weight,
        down_weight,
    )
    grads = finish(chans, ffn, grad_tokens, late, early, small)
    return (output,) + grads[:5] + (grads[5].transpose(0, 2, 1),) + grads[6:]


highest = lax.Precision.HIGHEST


def norm_forward(values, gain, bias):
    centre = jnp.mean(values, axis=-1, keepdims=True)
    shifted = values - centre
    inverse = lax.rsqrt(jnp.mean(shifted * shifted, axis=-1, keepdims=True) + 1e-05)
    scaled = shifted * inverse
    return (scaled * gain + bias, scaled, inverse)


def norm_backward(upstream, scaled, inverse, gain):
    weighted = upstream * gain
    first_mean = jnp.mean(weighted, axis=-1, keepdims=True)
    second_mean = jnp.mean(weighted * scaled, axis=-1, keepdims=True)
    grad_input = inverse * (weighted - first_mean - scaled * second_mean)
    breadth = upstream.shape[-1]
    grad_gain = jnp.sum((upstream * scaled).reshape(-1, breadth), axis=0)
    grad_bias = jnp.sum(upstream.reshape(-1, breadth), axis=0)
    return (grad_input, grad_gain, grad_bias)


def shuffle(blocked):
    row_count, groups, breadth = blocked.shape
    return (
        blocked.reshape(row_count, groups, groups, breadth // groups)
        .transpose(0, 2, 1, 3)
        .reshape(row_count, groups, breadth)
    )


def rows_monarch_forward(operand, right_factor, left_factor):
    row_count = operand.shape[0]
    groups = right_factor.shape[0]
    blocked = operand.reshape(row_count, groups, -1)
    middle = jnp.einsum(
        "tbi,bij->tbj", blocked, right_factor, preferred_element_type=jnp.float32
    ).astype(jnp.bfloat16)
    shuffled = shuffle(middle)
    result = jnp.einsum("tbi,bij->tbj", shuffled, left_factor, preferred_element_type=jnp.float32)
    return (shuffled, result.reshape(row_count, -1))


def rows_monarch_backward(grad_result, operand, shuffled, right_factor, left_factor):
    row_count = operand.shape[0]
    groups = right_factor.shape[0]
    grad_blocked = grad_result.reshape(row_count, groups, -1)
    grad_left = jnp.einsum(
        "tbi,tbj->bij", shuffled, grad_blocked, preferred_element_type=jnp.float32
    )
    grad_shuffled = jnp.einsum(
        "tbj,bij->tbi", grad_blocked, left_factor, preferred_element_type=jnp.float32
    )
    grad_middle = shuffle(grad_shuffled).astype(jnp.bfloat16)
    blocked = operand.reshape(row_count, groups, -1)
    grad_right = jnp.einsum(
        "tbi,tbj->bij", blocked, grad_middle, preferred_element_type=jnp.float32
    )
    grad_operand = jnp.einsum(
        "tbj,bij->tbi", grad_middle, right_factor, preferred_element_type=jnp.float32
    )
    return (grad_operand.reshape(row_count, -1), grad_right, grad_left)


def roots(row_count, col_count, period):
    product = jnp.arange(row_count)[:, None] * jnp.arange(col_count)[None, :] % period
    angle = product.astype(jnp.float32) * (2.0 * math.pi / period)
    return (jnp.cos(angle), jnp.sin(angle))


def complex_step(real_part, imag_part, cos_table, sin_table, sign, form):
    real_out = jnp.einsum(form, real_part, cos_table, precision=highest) - sign * jnp.einsum(
        form, imag_part, sin_table, precision=highest
    )
    imag_out = jnp.einsum(form, imag_part, cos_table, precision=highest) + sign * jnp.einsum(
        form, real_part, sin_table, precision=highest
    )
    return (real_out, imag_out)


def real_step(real_part, cos_table, sin_table, sign, form):
    real_out = jnp.einsum(form, real_part, cos_table, precision=highest)
    imag_out = sign * jnp.einsum(form, real_part, sin_table, precision=highest)
    return (real_out, imag_out)


def twiddle(real_part, imag_part, cos_table, sin_table, sign):
    real_out = real_part * cos_table - sign * imag_part * sin_table
    imag_out = imag_part * cos_table + sign * real_part * sin_table
    return (real_out, imag_out)


def spectrum_of(real_part):
    total = real_part.shape[-1]
    first = math.gcd(total, 128)
    second = total // first
    leading = real_part.shape[:-1]
    real_part = real_part.reshape(leading + (first, second))
    cos_first, sin_first = roots(first, first, first)
    real_part, imag_part = real_step(real_part, cos_first, sin_first, -1.0, "...ab,ak->...kb")
    cos_twist, sin_twist = roots(first, second, total)
    real_part, imag_part = twiddle(real_part, imag_part, cos_twist, sin_twist, -1.0)
    cos_second, sin_second = roots(second, second, second)
    return complex_step(real_part, imag_part, cos_second, sin_second, -1.0, "...kb,bm->...km")


def signal_of(real_part, imag_part):
    first = real_part.shape[-2]
    second = real_part.shape[-1]
    total = first * second
    leading = real_part.shape[:-2]
    cos_second, sin_second = roots(second, second, second)
    real_part, imag_part = complex_step(
        real_part, imag_part, cos_second, sin_second, 1.0, "...kb,bm->...km"
    )
    cos_twist, sin_twist = roots(first, second, total)
    real_part, imag_part = twiddle(real_part, imag_part, cos_twist, sin_twist, 1.0)
    cos_first, sin_first = roots(first, first, first)
    real_part, imag_part = complex_step(
        real_part, imag_part, cos_first, sin_first, 1.0, "...ab,ak->...kb"
    )
    return real_part.reshape(leading + (total,)) / total


def filter_parts(filter_first, filter_second, third_cols, seq_length):
    total = 2 * seq_length
    index = jnp.arange(total)
    offset = jnp.where(index < seq_length, index, index - total).astype(jnp.float32)
    scaled = offset / seq_length
    features = jnp.stack(
        [
            scaled,
            jnp.sin(math.pi * scaled),
            jnp.cos(math.pi * scaled),
            jnp.sin(7.0 * math.pi * scaled),
            jnp.cos(7.0 * math.pi * scaled),
        ],
        axis=1,
    )
    pre_one = jnp.dot(features, filter_first, precision=highest)
    act_one = jnp.sin(pre_one)
    pre_two = jnp.dot(act_one, filter_second, precision=highest)
    act_two = jnp.sin(pre_two)
    tap_mask = (index != seq_length).astype(jnp.float32)[:, None] * seq_length ** (-0.5)
    taps = jnp.dot(act_two, third_cols, precision=highest) * tap_mask
    filt_real, filt_imag = spectrum_of(taps.T)
    return (features, pre_one, act_one, pre_two, act_two, tap_mask, filt_real, filt_imag)


def general_body(
    tokens,
    norm_gain,
    norm_bias,
    in_right,
    in_left,
    short_kernel,
    filter_first,
    filter_second,
    filter_third,
    conv_bias,
    out_right,
    out_left,
    ffn_gain,
    ffn_bias,
    gate_weight,
    up_weight,
    down_weight,
    cotangent,
):
    seq_count, pos_count, model_width = tokens.shape
    row_count = seq_count * pos_count
    axis_count = lax.axis_size("seq")
    my_index = lax.axis_index("seq")
    chan_count = model_width // axis_count
    seq_length = pos_count * axis_count
    part_rows = cotangent.shape[1]
    tp_index = lax.axis_index("tp")
    tp_count = lax.axis_size("tp")
    chan_start = my_index * chan_count
    mix_count = seq_count // tp_count
    mix_tokens = lax.dynamic_slice_in_dim(tokens, tp_index * mix_count, mix_count, 0)
    mix_rows = mix_count * pos_count
    flat = mix_tokens.reshape(mix_rows, model_width).astype(jnp.float32)
    normed, scaled_one, inverse_one = norm_forward(flat, norm_gain, norm_bias)
    normed_low = normed.astype(jnp.bfloat16)
    shuffled_in, projected = rows_monarch_forward(normed_low, in_right, in_left)
    projected_low = (
        projected.astype(jnp.bfloat16)
        .reshape(mix_count, pos_count, 3, model_width)
        .transpose(2, 3, 0, 1)
    )
    channels = lax.all_to_all(projected_low, "seq", split_axis=1, concat_axis=3, tiled=True)
    signals = channels.astype(jnp.float32)
    kernel = lax.dynamic_slice_in_dim(short_kernel, chan_start, chan_count, 1).astype(jnp.float32)
    tap_zero = kernel[:, :, 0][:, :, None, None]
    tap_one = kernel[:, :, 1][:, :, None, None]
    tap_two = kernel[:, :, 2][:, :, None, None]
    padded = jnp.pad(signals, ((0, 0), (0, 0), (0, 0), (1, 1)))
    shorted = padded[..., :-2] * tap_zero + padded[..., 1:-1] * tap_one + padded[..., 2:] * tap_two
    first_f = filter_first.astype(jnp.float32)
    second_f = filter_second.astype(jnp.float32)
    third_cols = lax.dynamic_slice_in_dim(filter_third, chan_start, chan_count, 1).astype(
        jnp.float32
    )
    kept = filter_parts(first_f, second_f, third_cols, seq_length)
    filt_real = kept[6][:, None]
    filt_imag = kept[7][:, None]
    bias_cols = lax.dynamic_slice_in_dim(conv_bias, chan_start, chan_count, 0)[:, None, None]
    product = shorted[0] * shorted[2]
    product_pad = jnp.pad(product, ((0, 0), (0, 0), (0, seq_length)))
    spec_real, spec_imag = spectrum_of(product_pad)
    conv_real = spec_real * filt_real - spec_imag * filt_imag
    conv_imag = spec_real * filt_imag + spec_imag * filt_real
    convolved = signal_of(conv_real, conv_imag)[..., :seq_length] + bias_cols * product
    mixed_low = (shorted[1] * convolved).astype(jnp.bfloat16)
    back_rows = lax.all_to_all(mixed_low, "seq", split_axis=2, concat_axis=0, tiled=True)
    mixed_rows = back_rows.transpose(1, 2, 0).reshape(mix_rows, model_width)
    shuffled_out, branch = rows_monarch_forward(mixed_rows, out_right, out_left)
    residual_mine = (flat + branch).reshape(mix_count, pos_count, model_width)
    residual = lax.all_gather(residual_mine, "tp", axis=0, tiled=True)
    part_resid = lax.dynamic_slice_in_dim(residual, tp_index * part_rows, part_rows, 1)
    normed_two, scaled_two, inverse_two = norm_forward(part_resid, ffn_gain, ffn_bias)
    normed_rows = lax.all_gather(normed_two.astype(jnp.bfloat16), "tp", axis=1, tiled=True).reshape(
        row_count, model_width
    )
    gate = jnp.dot(normed_rows, gate_weight, preferred_element_type=jnp.float32)
    upward = jnp.dot(normed_rows, up_weight, preferred_element_type=jnp.float32)
    sigma = jax.nn.sigmoid(gate)
    hidden_low = (gate * sigma * upward).astype(jnp.bfloat16)
    partial_down = jnp.dot(hidden_low, down_weight, preferred_element_type=jnp.float32).reshape(
        seq_count, pos_count, model_width
    )
    glu_part = lax.psum_scatter(
        partial_down.astype(jnp.bfloat16), "tp", scatter_dimension=1, tiled=True
    ).astype(jnp.float32)
    output = (part_resid + glu_part).astype(jnp.bfloat16)
    grad_out_rows = lax.all_gather(cotangent, "tp", axis=1, tiled=True).reshape(
        row_count, model_width
    )
    grad_hidden = jnp.dot(grad_out_rows, down_weight.T, preferred_element_type=jnp.float32)
    grad_gate = (grad_hidden * upward * (sigma + gate * sigma * (1.0 - sigma))).astype(jnp.bfloat16)
    grad_up = (grad_hidden * gate * sigma).astype(jnp.bfloat16)
    grad_down_w = jnp.dot(hidden_low.T, grad_out_rows, preferred_element_type=jnp.float32)
    grad_gate_w = jnp.dot(normed_rows.T, grad_gate, preferred_element_type=jnp.float32)
    grad_up_w = jnp.dot(normed_rows.T, grad_up, preferred_element_type=jnp.float32)
    grad_normed = jnp.dot(grad_gate, gate_weight.T, preferred_element_type=jnp.float32) + jnp.dot(
        grad_up, up_weight.T, preferred_element_type=jnp.float32
    )
    grad_normed_part = lax.psum_scatter(
        grad_normed.reshape(seq_count, pos_count, model_width),
        "tp",
        scatter_dimension=1,
        tiled=True,
    )
    grad_in_two, grad_gain_two, grad_bias_two = norm_backward(
        grad_normed_part, scaled_two, inverse_two, ffn_gain
    )
    gain_total = lax.psum((grad_gain_two, grad_bias_two), ("seq", "tp"))
    grad_resid_part = cotangent.astype(jnp.float32) + grad_in_two
    grad_resid = lax.all_gather(
        grad_resid_part.astype(jnp.bfloat16), "tp", axis=1, tiled=True
    ).astype(grad_resid_part.dtype)
    grad_resid_mix = lax.dynamic_slice_in_dim(
        grad_resid, tp_index * mix_count, mix_count, 0
    ).reshape(mix_rows, model_width)
    grad_mixed_rows, grad_out_right, grad_out_left = rows_monarch_backward(
        grad_resid_mix.astype(jnp.bfloat16), mixed_rows, shuffled_out, out_right, out_left
    )
    grad_mixed_low = (
        grad_mixed_rows.astype(jnp.bfloat16)
        .reshape(mix_count, pos_count, model_width)
        .transpose(2, 0, 1)
    )
    grad_mixed = lax.all_to_all(
        grad_mixed_low, "seq", split_axis=0, concat_axis=2, tiled=True
    ).astype(jnp.float32)
    grad_conv = grad_mixed * shorted[1]
    grad_key = grad_mixed * convolved
    again = lax.optimization_barrier((first_f, second_f, third_cols))
    kept = filter_parts(again[0], again[1], again[2], seq_length)
    filt_real = kept[6][:, None]
    filt_imag = kept[7][:, None]
    features, pre_one, act_one, pre_two, act_two, tap_mask = (
        kept[0],
        kept[1],
        kept[2],
        kept[3],
        kept[4],
        kept[5],
    )
    grad_pad = jnp.pad(grad_conv, ((0, 0), (0, 0), (0, seq_length)))
    grad_spec_real, grad_spec_imag = spectrum_of(grad_pad)
    back_real = grad_spec_real * filt_real + grad_spec_imag * filt_imag
    back_imag = grad_spec_imag * filt_real - grad_spec_real * filt_imag
    grad_product = signal_of(back_real, back_imag)[..., :seq_length] + bias_cols * grad_conv
    grad_bias_cols = jnp.sum(grad_conv * product, axis=(1, 2))
    taps_real = jnp.sum(grad_spec_real * spec_real + grad_spec_imag * spec_imag, axis=1)
    taps_imag = jnp.sum(grad_spec_imag * spec_real - grad_spec_real * spec_imag, axis=1)
    grad_taps = signal_of(taps_real, taps_imag)
    grad_pre = grad_taps.T * tap_mask
    grad_third_cols = jnp.dot(act_two.T, grad_pre, precision=highest)
    grad_pre_two = jnp.dot(grad_pre, third_cols.T, precision=highest) * jnp.cos(pre_two)
    grad_second = jnp.dot(act_one.T, grad_pre_two, precision=highest)
    grad_pre_one = jnp.dot(grad_pre_two, second_f.T, precision=highest) * jnp.cos(pre_one)
    grad_first = jnp.dot(features.T, grad_pre_one, precision=highest)
    grad_shorted = jnp.stack([grad_product * shorted[2], grad_key, grad_product * shorted[0]])
    grad_short_pad = jnp.pad(grad_shorted, ((0, 0), (0, 0), (0, 0), (1, 1)))
    grad_signals = (
        grad_short_pad[..., 2:] * tap_zero
        + grad_short_pad[..., 1:-1] * tap_one
        + grad_short_pad[..., :-2] * tap_two
    )
    grad_kernel = jnp.stack(
        [
            jnp.sum(grad_shorted * padded[..., :-2], axis=(2, 3)),
            jnp.sum(grad_shorted * padded[..., 1:-1], axis=(2, 3)),
            jnp.sum(grad_shorted * padded[..., 2:], axis=(2, 3)),
        ],
        axis=-1,
    )
    grad_proj = lax.all_to_all(
        grad_signals.astype(jnp.bfloat16), "seq", split_axis=3, concat_axis=1, tiled=True
    )
    grad_proj_rows = grad_proj.transpose(2, 3, 0, 1).reshape(mix_rows, 3 * model_width)
    grad_normed_one, grad_in_right, grad_in_left = rows_monarch_backward(
        grad_proj_rows, normed_low, shuffled_in, in_right, in_left
    )
    grad_in_one, grad_gain_one, grad_bias_one = norm_backward(
        grad_normed_one, scaled_one, inverse_one, norm_gain
    )
    grad_mine = (grad_resid_mix + grad_in_one).reshape(mix_count, pos_count, model_width)
    short_full = lax.dynamic_update_slice_in_dim(
        jnp.zeros(short_kernel.shape, jnp.float32), grad_kernel, chan_start, 1
    )
    third_full = lax.dynamic_update_slice_in_dim(
        jnp.zeros(filter_third.shape, jnp.float32), grad_third_cols, chan_start, 1
    )
    bias_full = lax.dynamic_update_slice_in_dim(
        jnp.zeros(conv_bias.shape, jnp.float32), grad_bias_cols, chan_start, 0
    )
    mixer_grads = (
        grad_gain_one,
        grad_bias_one,
        grad_in_right,
        grad_in_left,
        short_full,
        grad_first,
        grad_second,
        third_full,
        bias_full,
        grad_out_right,
        grad_out_left,
    )
    grad_tokens = lax.all_gather(grad_mine.astype(jnp.bfloat16), "tp", axis=0, tiled=True).astype(
        grad_mine.dtype
    )
    mixer_grads = (
        lax.psum(mixer_grads[0].astype(jnp.bfloat16), "tp").astype(jnp.float32),
        lax.psum(mixer_grads[1].astype(jnp.bfloat16), "tp").astype(jnp.float32),
        lax.psum(mixer_grads[2].astype(jnp.bfloat16), "tp").astype(jnp.float32),
        lax.psum(mixer_grads[3].astype(jnp.bfloat16), "tp").astype(jnp.float32),
        lax.psum(mixer_grads[4].astype(jnp.bfloat16), "tp").astype(jnp.float32),
        lax.psum(mixer_grads[5].astype(jnp.bfloat16), "tp").astype(jnp.float32),
        lax.psum(mixer_grads[6].astype(jnp.bfloat16), "tp").astype(jnp.float32),
        lax.psum(mixer_grads[7].astype(jnp.bfloat16), "tp").astype(jnp.float32),
        lax.psum(mixer_grads[8].astype(jnp.bfloat16), "tp").astype(jnp.float32),
        lax.psum(mixer_grads[9].astype(jnp.bfloat16), "tp").astype(jnp.float32),
        lax.psum(mixer_grads[10].astype(jnp.bfloat16), "tp").astype(jnp.float32),
    )
    all_total = lax.psum(
        (
            mixer_grads[0],
            mixer_grads[1],
            mixer_grads[2],
            mixer_grads[3],
            mixer_grads[4],
            mixer_grads[5],
            mixer_grads[6],
            mixer_grads[7],
            mixer_grads[8],
            mixer_grads[9],
            mixer_grads[10],
            grad_gate_w,
            grad_up_w,
            grad_down_w,
        ),
        "seq",
    )
    return (
        output,
        grad_tokens,
        all_total[0],
        all_total[1],
        all_total[2],
        all_total[3],
        all_total[4],
        all_total[5],
        all_total[6],
        all_total[7],
        all_total[8],
        all_total[9],
        all_total[10],
        gain_total[0],
        gain_total[1],
        all_total[11],
        all_total[12],
        all_total[13],
    )


def choose_body(mesh, *arrays):
    tokens = arrays[0]
    chans = tokens.shape[2] // mesh.shape["seq"]
    fits = mesh.shape["seq"] == 8 and mesh.shape["tp"] == 4 and tokens.shape[:2] == (4, 128) and chans == 96
    return (fast_body if fits else general_body)(*arrays)


def solution(mesh):
    mapped = jax.shard_map(
        functools.partial(choose_body, mesh),
        mesh=mesh,
        in_specs=(
            P(None, "seq", None),
            P(),
            P(),
            P(),
            P(),
            P(),
            P(),
            P(),
            P(),
            P(),
            P(),
            P(),
            P(),
            P(),
            P(None, "tp"),
            P(None, "tp"),
            P("tp", None),
            P(None, ("seq", "tp"), None),
        ),
        out_specs=(
            P(None, ("seq", "tp"), None),
            P(None, "seq", None),
            P(),
            P(),
            P(),
            P(),
            P(),
            P(),
            P(),
            P(),
            P(),
            P(),
            P(),
            P(),
            P(),
            P(None, "tp"),
            P(None, "tp"),
            P("tp", None),
        ),
        check_vma=False,
    )

    def program(*arrays):
        with jax.sharding.use_abstract_mesh(mesh.abstract_mesh):
            return mapped(*arrays)

    return program
```
